128 devices in a mesh: ctx: 32 (over x, z, y_hi), wshard: 4 (over y_lo, core).
Axes of the slice: x: 4, y: 4 (y_hi: 2, y_lo: 2; y = y_hi * 2 + y_lo), z: 4, core: 2. Of those that a mesh axis runs over, the one named last changes fastest.
Arguments:
- inputs: bfloat16 [4, 2, 2048, 2048], P('wshard', None, 'ctx'), may hold values from -6 to 6
- cotangent: bfloat16 [4, 2, 2048, 2048], P('wshard', None, 'ctx'), may hold values from -6 to 6
- norm_attn: bfloat16 [2048], replicated, may hold values from 0.5 to 1.5
- w_query: bfloat16 [2048, 2048], P('ctx', 'wshard'), may hold values from -0.125 to 0.125
- w_key: bfloat16 [2048, 256], P('ctx', 'wshard'), may hold values from -0.125 to 0.125
- w_value: bfloat16 [2048, 256], P('ctx', 'wshard'), may hold values from -0.125 to 0.125
- w_out: bfloat16 [2048, 2048], P('wshard', 'ctx'), may hold values from -3 to 3
- norm_mlp: bfloat16 [2048], replicated, may hold values from 0.5 to 1.5
- w_gate: bfloat16 [2048, 5632], P('ctx', 'wshard'), may hold values from -0.125 to 0.125
- w_up: bfloat16 [2048, 5632], P('ctx', 'wshard'), may hold values from -0.125 to 0.125
- w_down: bfloat16 [5632, 2048], P('wshard', 'ctx'), may hold values from -0.078125 to 0.078125
Outputs:
- outputs: bfloat16 [4, 2, 2048, 2048], P('wshard', None, 'ctx')
- grad_inputs: bfloat16 [4, 2, 2048, 2048], P('wshard', None, 'ctx')
- grad_norm_attn: float32 [2048], P(('ctx', 'wshard'))
- grad_query: float32 [2048, 2048], P('ctx', 'wshard')
- grad_key: float32 [2048, 256], P('ctx', 'wshard')
- grad_value: float32 [2048, 256], P('ctx', 'wshard')
- grad_out: float32 [2048, 2048], P('wshard', 'ctx')
- grad_norm_mlp: float32 [2048], P(('ctx', 'wshard'))
- grad_gate: float32 [2048, 5632], P('ctx', 'wshard')
- grad_up: float32 [2048, 5632], P('ctx', 'wshard')
- grad_down: float32 [5632, 2048], P('wshard', 'ctx')
The draws below stay inside these ranges and needn't reach their ends.
All inputs are finite; a program needn't handle non-finite values.
Results may differ from the reference program's by a relative error of at most 0.033.
Values may be sent and summed in bfloat16 or wider, within the bound.
A program may use at most 192 MiB of HBM per device.

```python
from functools import partial
import jax
import jax.numpy as jnp
from jax import lax

D = 2048
H = 32
KVH = 4
HD = 64
FF = 5632
HALF = 64
LEN = 4096
SEQS = 4
N_CTX = 32


def levels(stream_key, dims, cuts, least, top_value):
    gain, own = 1.0, jax.random.fold_in(stream_key, 6)
    for position, shards_of in cuts:
        steps = jnp.exp(jax.random.uniform(jax.random.fold_in(own, position), (shards_of,), jnp.float32, least / len(cuts), top_value / len(cuts)))
        gain = gain * jnp.repeat(steps, dims[position] // shards_of).reshape([-1 if axis == position else 1 for axis in range(len(dims))])
    return gain


def gaussian(own_key, dims, deviation, most, shards=(), held_as=jnp.bfloat16):
    level = levels(own_key, dims, shards, -0.22, 0.18) if shards else 1.0
    values = jax.random.normal(own_key, dims, jnp.float32) * deviation * level
    return jnp.minimum(jnp.maximum(values, -most), most).astype(held_as)


def setup_inputs(seed: int = 0) -> dict:
    splits = jax.random.split(jax.random.key(seed), 12)
    inputs = gaussian(splits[0], (SEQS, 2, LEN // 2, D), 1.0, 6.0, ((0, 4), (2, 32)))
    cotangent = gaussian(splits[1], (SEQS, 2, LEN // 2, D), 1.0, 6.0, ((0, 4), (2, 32)))
    norm_attn = jnp.clip(1.0 + 0.1 * jax.random.normal(splits[2], (D,), jnp.float32), 0.5, 1.5).astype(jnp.bfloat16)
    w_query = gaussian(splits[3], (D, H * HD), D ** -0.5, 0.125, ((0, 32), (1, 4)))
    w_key = gaussian(splits[4], (D, KVH * HD), D ** -0.5, 0.125, ((0, 32), (1, 4)))
    w_value = gaussian(splits[5], (D, KVH * HD), D ** -0.5, 0.125, ((0, 32), (1, 4)))
    w_out = gaussian(splits[6], (H * HD, D), (max(2, H * HD // 512)) ** -0.5, 3.0, ((0, 4), (1, 32)))
    norm_mlp = jnp.clip(1.0 + 0.1 * jax.random.normal(splits[7], (D,), jnp.float32), 0.5, 1.5).astype(jnp.bfloat16)
    w_gate = gaussian(splits[8], (D, FF), D ** -0.5, 0.125, ((0, 32), (1, 4)))
    w_up = gaussian(splits[9], (D, FF), D ** -0.5, 0.125, ((0, 32), (1, 4)))
    w_down = gaussian(splits[10], (FF, D), FF ** -0.5, 0.078125, ((0, 4), (1, 32)))
    return {"inputs": inputs, "cotangent": cotangent, "norm_attn": norm_attn, "w_query": w_query, "w_key": w_key, "w_value": w_value, "w_out": w_out, "norm_mlp": norm_mlp, "w_gate": w_gate, "w_up": w_up, "w_down": w_down}


EPS = 1e-05
NEG = -1e+30

@jax.custom_vjp
def low(v):
    return lax.optimization_barrier(v.astype(jnp.bfloat16)).astype(jnp.float32)

@jax.custom_vjp
def low_back(v):
    return v

def low_keep(v):
    return (low(v), None)

def low_pass(kept, grad):
    return (grad,)

def back_keep(v):
    return (v, None)

def back_low(kept, grad):
    return (low(grad),)
low.defvjp(low_keep, low_pass)
low_back.defvjp(back_keep, back_low)

def matmul(left, right):
    return jnp.dot(left, right, precision=lax.Precision.HIGHEST, preferred_element_type=jnp.float32)

def to_positions(values):
    first = values[:, 0]
    second = values[:, 1].reshape(SEQS, N_CTX, HALF, D)[:, ::-1].reshape(SEQS, LEN // 2, D)
    return jnp.concatenate([first, second], 1)

def to_stored(values):
    first = values[:, :LEN // 2]
    second = values[:, LEN // 2:].reshape(SEQS, N_CTX, HALF, D)[:, ::-1].reshape(SEQS, LEN // 2, D)
    return jnp.stack([first, second], 1)

def tables(positions):
    freqs = 10000.0 ** (-jnp.arange(HD // 2, dtype=jnp.float32) * 2.0 / HD)
    angles = positions[:, None] * freqs[None]
    angles = jnp.concatenate([angles, angles], -1)
    return (jnp.cos(angles), jnp.sin(angles))

def rotate(values, cosine, sine_part):
    middle = values.shape[-1] // 2
    turned = jnp.concatenate([-values[..., middle:], values[..., :middle]], -1)
    return values * cosine[:, None] + turned * sine_part[:, None]

def attend(query, keys, values, first_row):
    scores = jnp.einsum('tkgd,skd->ktgs', query, keys, precision=lax.Precision.HIGHEST) * HD ** (-0.5)
    scores = low_back(scores)
    rows = first_row + jnp.arange(query.shape[0])
    cols = jnp.arange(keys.shape[0])
    allowed = rows[:, None] >= cols[None]
    scores = jnp.where(allowed[None, :, None, :], scores, NEG)
    weights = low(jax.nn.softmax(scores, axis=-1))
    mixed = jnp.einsum('ktgs,skd->tkgd', weights, values, precision=lax.Precision.HIGHEST)
    return mixed.reshape(query.shape[0], H * HD)

def forward(inputs, norm_attn, w_query, w_key, w_value, w_out, norm_mlp, w_gate, w_up, w_down):
    ordered = to_positions(inputs)
    cosine, sine_part = tables(jnp.arange(LEN, dtype=jnp.float32))
    block_rows = min(512, LEN)

    def one(sequence):
        factor1 = lax.rsqrt(lax.optimization_barrier(jnp.mean(sequence * sequence, -1, keepdims=True)) + EPS)
        normed1 = low(sequence * factor1 * norm_attn)
        query = low(rotate(low_back(matmul(normed1, w_query)).reshape(LEN, H, HD), cosine, sine_part))
        keys = low(rotate(low_back(matmul(normed1, w_key)).reshape(LEN, KVH, HD), cosine, sine_part))
        values = low(low_back(matmul(normed1, w_value))).reshape(LEN, KVH, HD)
        grouped = query.reshape(LEN, KVH, H // KVH, HD)
        pieces = []
        for block in range(LEN // block_rows):
            stop = (block + 1) * block_rows
            step_fn = jax.checkpoint(partial(attend, first_row=block * block_rows))
            pieces.append(step_fn(grouped[block * block_rows:stop], keys[:stop], values[:stop]))
        mixed = low(low_back(jnp.concatenate(pieces, 0)))
        hidden1 = sequence + low_back(matmul(mixed, w_out))
        factor2 = lax.rsqrt(lax.optimization_barrier(jnp.mean(hidden1 * hidden1, -1, keepdims=True)) + EPS)
        normed2 = low(hidden1 * factor2 * norm_mlp)
        gate_pre = low_back(matmul(normed2, w_gate))
        up_proj = low_back(matmul(normed2, w_up))
        active = low(jax.nn.silu(gate_pre) * up_proj)
        return hidden1 + matmul(active, w_down)
    return to_stored(lax.map(jax.checkpoint(one), ordered))

def reference(inputs, cotangent, norm_attn, w_query, w_key, w_value, w_out, norm_mlp, w_gate, w_up, w_down):
    result, pull = jax.vjp(forward, inputs.astype(jnp.float32), norm_attn.astype(jnp.float32), w_query.astype(jnp.float32), w_key.astype(jnp.float32), w_value.astype(jnp.float32), w_out.astype(jnp.float32), norm_mlp.astype(jnp.float32), w_gate.astype(jnp.float32), w_up.astype(jnp.float32), w_down.astype(jnp.float32))
    grads = pull(cotangent.astype(jnp.float32))
    return (result.astype(jnp.bfloat16), grads[0].astype(jnp.bfloat16), grads[1], grads[2], grads[3], grads[4], grads[5], grads[6], grads[7], grads[8], grads[9])
```

```python
from functools import partial

import jax
import jax.numpy as jnp
from jax import lax
from jax.experimental import pallas as pl
from jax.experimental.pallas import tpu as pltpu
from jax.sharding import PartitionSpec as P

MESH = pl.DeviceIdType.MESH
HD = 64
EPS = 1e-05
NEG = -1e30
F32 = jnp.float32
BF16 = jnp.bfloat16
VMEM_LIMIT = 60 * 2**20
ANY = pl.BlockSpec(memory_space=pl.ANY)
VMEM = pl.BlockSpec(memory_space=pltpu.VMEM)


class Place:
    def __init__(self):
        ctx, shard = lax.axis_index("ctx"), lax.axis_index("wshard")
        self.x, self.z, self.y = ctx // 8, (ctx // 2) % 4, ctx % 2
        self.yl, self.co = shard // 2, shard % 2

    def at(self, x=None, z=None, y=None, yl=None, co=None):
        x, z, y = (self.x if x is None else x), (self.z if z is None else z), (self.y if y is None else y)
        yl, co = (self.yl if yl is None else yl), (self.co if co is None else co)
        return (x * 8 + z * 2 + y, yl * 2 + co)

    def step(self, axis, by):
        return self.at(**{axis: (getattr(self, axis) + by) % 4})

    def pair(self, axis):
        return self.at(**{axis: 1 - getattr(self, axis)})

    def ctx_peers(self):
        return [self.step("x", 1), self.step("x", 3), self.step("z", 1), self.step("z", 3), self.pair("y")]

    def shard_peers(self):
        return [self.pair("co"), self.pair("yl")]

    def far_peers(self):
        return [self.step("x", 2), self.step("z", 2)]


def greet(peers):
    barrier = pltpu.get_barrier_semaphore()
    for device in peers:
        pl.semaphore_signal(barrier, inc=1, device_id=device, device_id_type=MESH)
    pl.semaphore_wait(barrier, len(peers))


class Copies:
    def __init__(self, send, recv):
        self.send, self.recv, self.used = send, recv, 0

    def start(self, src, dst, device):
        k = self.used
        self.used += 1
        copy = pltpu.make_async_remote_copy(
            src_ref=src, dst_ref=dst, send_sem=self.send.at[k], recv_sem=self.recv.at[k],
            device_id=device, device_id_type=MESH,
        )
        copy.start()
        return copy

    def local(self, src, dst):
        k = self.used
        self.used += 1
        copy = pltpu.make_async_copy(src, dst, self.send.at[k])
        copy.start()
        return copy


def wait_all(copies):
    for copy in copies:
        copy.wait()


class CtxGather:
    COPIES = 10
    STAGES = 6

    def __init__(self, place, copies, shard, full, lo, n, big):
        self.p, self.c, self.shard, self.full = place, copies, shard, full
        self.lo, self.n, self.big, self.small = lo, n, big, ("z" if big == "x" else "x")
        self.live = []

    def block(self, o, i, y):
        x, z = (o, i) if self.big == "x" else (i, o)
        return self.full.at[x, z, y, pl.ds(self.lo, self.n)]

    def send(self, part, axis, by):
        dev = self.p.pair("y") if axis == "y" else self.p.step(axis, by)
        self.live.append(self.c.start(part, part, dev))

    def stage(self, s):
        p = self.p
        o, i, y = getattr(p, self.big), getattr(p, self.small), p.y
        wait_all(self.live)
        self.live = []
        every, both = pl.ds(0, 4), pl.ds(0, 2)
        if s == 0:
            own = self.shard.at[pl.ds(self.lo, self.n)]
            self.live.append(self.c.start(own, self.block(o, i, y), p.pair("y")))
            self.live.append(self.c.local(own, self.block(o, i, y)))
        elif s == 1:
            self.send(self.block(o, i, both), self.small, 1)
            self.send(self.block(o, i, both), self.small, 3)
        elif s == 2:
            self.send(self.block(o, (i + 3) % 4, 0), self.small, 1)
            self.send(self.block(o, (i + 1) % 4, 1), self.small, 3)
        elif s == 3:
            self.send(self.block(o, every, both), self.big, 1)
            self.send(self.block(o, every, both), self.big, 3)
        elif s == 4:
            self.send(self.block((o + 3) % 4, pl.ds(0, 2), both), self.big, 1)
            self.send(self.block((o + 1) % 4, pl.ds(2, 2), both), self.big, 3)


class CtxScatter:
    COPIES = 13
    STAGES = 6

    @staticmethod
    def scratch(n, width):
        return [
            pltpu.VMEM((2, 2, 2, n, width), BF16),
            pltpu.VMEM((4, 2, n, width), BF16),
            pltpu.VMEM((4, 2, n, width), BF16),
            pltpu.VMEM((2, n, width), BF16),
            pltpu.VMEM((2, n, width), BF16),
            pltpu.VMEM((2, n, width), BF16),
            pltpu.VMEM((n, width), BF16),
        ]

    def __init__(self, place, copies, src, out, bufs, lo, n, big):
        self.p, self.c, self.src, self.out = place, copies, src, out
        self.far, self.pos, self.neg, self.far2, self.pos2, self.neg2, self.last = bufs
        self.lo, self.n, self.big, self.small = lo, n, big, ("z" if big == "x" else "x")
        self.live = []

    def part(self, o, i):
        x, z = (o, i) if self.big == "x" else (i, o)
        return self.src.at[x, z, pl.ds(0, 2), pl.ds(self.lo, self.n)]

    def load(self, o, i, y):
        x, z = (o, i) if self.big == "x" else (i, o)
        return self.src[x, z, y, pl.ds(self.lo, self.n), :].astype(F32)

    def send(self, src, dst, axis, by):
        dev = self.p.pair("y") if axis == "y" else self.p.step(axis, by)
        self.live.append(self.c.start(src, dst, dev))

    def stage(self, s):
        p, big, small = self.p, self.big, self.small
        o, i, y = getattr(p, big), getattr(p, small), p.y
        up, down, across = (o + 1) % 4, (o + 3) % 4, (o + 2) % 4
        iup, idown, iacross = (i + 1) % 4, (i + 3) % 4, (i + 2) % 4
        low, high = pl.ds(0, 2), pl.ds(2, 2)
        if s == 1:
            wait_all(self.live[:2])
            self.live = self.live[2:]
        else:
            wait_all(self.live)
            self.live = []
        if s == 0:
            self.send(self.part(across, low), self.far.at[0], big, 1)
            self.send(self.part(across, high), self.far.at[1], big, 3)
            self.send(self.part(up, high), self.pos.at[high], big, 1)
            self.send(self.part(down, low), self.neg.at[low], big, 3)
        elif s == 1:

            def fold(k, _):
                b, q = k // 2, k % 2
                self.far[0, b, q] = (self.far[0, b, q].astype(F32) + self.load(up, b, q)).astype(BF16)
                self.far[1, b, q] = (self.far[1, b, q].astype(F32) + self.load(down, b + 2, q)).astype(BF16)
                return 0

            lax.fori_loop(0, 4, fold, 0)
            self.send(self.far.at[0], self.pos.at[low], big, 1)
            self.send(self.far.at[1], self.neg.at[high], big, 3)
        elif s == 2:

            def total(k, _):
                b, q = k // 2, k % 2
                here = self.load(o, b, q) + self.pos[b, q].astype(F32) + self.neg[b, q].astype(F32)
                self.pos[b, q] = here.astype(BF16)
                return 0

            lax.fori_loop(0, 8, total, 0)
            self.send(self.pos.at[iacross, 0], self.far2.at[0], small, 1)
            self.send(self.pos.at[iacross, 1], self.far2.at[1], small, 3)
            self.send(self.pos.at[iup, 1], self.pos2.at[1], small, 1)
            self.send(self.pos.at[idown, 0], self.neg2.at[0], small, 3)
        elif s == 3:
            self.far2[0] = (self.far2[0].astype(F32) + self.pos[iup, 0].astype(F32)).astype(BF16)
            self.far2[1] = (self.far2[1].astype(F32) + self.pos[idown, 1].astype(F32)).astype(BF16)
            self.send(self.far2.at[0], self.pos2.at[0], small, 1)
            self.send(self.far2.at[1], self.neg2.at[1], small, 3)
        elif s == 4:
            for q in range(2):
                here = self.pos[i, q].astype(F32) + self.pos2[q].astype(F32) + self.neg2[q].astype(F32)
                self.pos2[q] = here.astype(BF16)
            self.send(self.pos2.at[1 - y], self.last, "y", 0)
        elif s == 5:
            self.out[pl.ds(self.lo, self.n), :] = (self.pos2[y].astype(F32) + self.last[...].astype(F32)).astype(
                self.out.dtype
            )


class ShardGather:
    def __init__(self, place, copies, full, chunks):
        self.p, self.c, self.full, self.chunks = place, copies, full, chunks
        self.rows = full.shape[1] // chunks
        self.me, self.over = place.yl * 2 + place.co, (1 - place.yl) * 2 + place.co
        self.far, self.near = [], []

    COPIES = 3

    def part(self, who, k):
        return self.full.at[who, pl.ds(k * self.rows, self.rows)]

    def send(self, k, src=None):
        src = self.part(self.me, k) if src is None else src
        self.far.append(self.c.start(src, self.part(self.me, k), self.p.pair("yl")))
        self.near.append(self.c.start(src, self.part(self.me, k), self.p.pair("co")))

    def forward(self, k):
        self.far[k].wait()
        self.near.append(self.c.start(self.part(self.over, k), self.part(self.over, k), self.p.pair("co")))

    def finish(self):
        wait_all(self.near)


class ShardScatter:
    COPIES = 3

    @staticmethod
    def scratch(rows, width):
        return [pltpu.VMEM((rows, width), BF16)] * 3

    def __init__(self, place, copies, part, bufs, chunks):
        self.p, self.c, self.part, self.chunks = place, copies, part, chunks
        self.relay, self.near, self.over = bufs
        self.rows = part.shape[1] // chunks
        self.first, self.second, self.third = [], [], []

    def at(self, k):
        return pl.ds(k * self.rows, self.rows)

    def begin(self):
        p = self.p
        for k in range(self.chunks):
            src = self.part.at[(1 - p.yl) * 2 + 1 - p.co, self.at(k)]
            self.first.append(self.c.start(src, self.relay.at[self.at(k)], p.pair("co")))
        for k in range(self.chunks):
            src = self.part.at[p.yl * 2 + 1 - p.co, self.at(k)]
            self.second.append(self.c.start(src, self.near.at[self.at(k)], p.pair("co")))

    def relay_on(self, k):
        p = self.p
        self.first[k].wait()
        here = self.part[(1 - p.yl) * 2 + p.co, self.at(k), :].astype(F32)
        self.relay[self.at(k), :] = (self.relay[self.at(k), :].astype(F32) + here).astype(BF16)
        self.third.append(self.c.start(self.relay.at[self.at(k)], self.over.at[self.at(k)], p.pair("yl")))

    def total(self, k):
        p = self.p
        self.second[k].wait()
        self.third[k].wait()
        here = self.part[p.yl * 2 + p.co, self.at(k), :].astype(F32)
        return here + self.near[self.at(k), :].astype(F32) + self.over[self.at(k), :].astype(F32)


class GainScatter:
    COPIES = 9
    STAGES = 6

    @staticmethod
    def scratch():
        return [
            pltpu.VMEM((8, 2048), F32),
            pltpu.VMEM((3, 8, 512), F32),
            pltpu.VMEM((8, 512), F32),
            pltpu.VMEM((3, 8, 128), F32),
            pltpu.VMEM((3, 8, 128), F32),
            pltpu.VMEM((3, 8, 128), F32),
        ]

    def __init__(self, place, copies, out, bufs):
        self.p, self.c, self.out = place, copies, out
        self.vec, self.xs, self.mid, self.zs, self.own, self.rest = bufs
        self.live = []

    def stage(self, s):
        p = self.p
        wait_all(self.live)
        self.live = []
        if s == 0:
            for by in (1, 2, 3):
                cols = pl.ds(pl.multiple_of(((p.x + by) % 4) * 512, 512), 512)
                self.live.append(self.c.start(self.vec.at[:, cols], self.xs.at[by - 1], p.step("x", by)))
        elif s == 1:
            cols = pl.ds(pl.multiple_of(p.x * 512, 512), 512)
            self.mid[...] = self.vec[:, cols] + self.xs[0] + self.xs[1] + self.xs[2]
            for by in (1, 2, 3):
                cols = pl.ds(pl.multiple_of(((p.z + by) % 4) * 128, 128), 128)
                self.live.append(self.c.start(self.mid.at[:, cols], self.zs.at[by - 1], p.step("z", by)))
        elif s == 2:
            cols = pl.ds(pl.multiple_of(p.z * 128, 128), 128)
            self.own[0] = self.mid[:, cols] + self.zs[0] + self.zs[1] + self.zs[2]
            self.live.append(self.c.start(self.own.at[0], self.rest.at[0], p.pair("y")))
        elif s == 3:
            self.own[1] = self.own[0] + self.rest[0]
            self.live.append(self.c.start(self.own.at[1], self.rest.at[1], p.pair("co")))
        elif s == 4:
            self.own[2] = self.own[1] + self.rest[1]
            self.live.append(self.c.start(self.own.at[2], self.rest.at[2], p.pair("yl")))
        elif s == 5:
            self.out[...] = self.own[2] + self.rest[2]


def sems(n):
    return [pltpu.SemaphoreType.DMA((n,)), pltpu.SemaphoreType.DMA((n,))]


def params(cid):
    return pltpu.CompilerParams(collective_id=cid, has_side_effects=True, vmem_limit_bytes=VMEM_LIMIT)


def halves(rows):
    return ((0, rows // 2, "x"), (rows // 2, rows // 2, "z"))


def gather_kernel(n_ctx, n_shard, *refs):
    n = n_ctx + n_shard
    ins, outs, (send, recv) = refs[:n], refs[n : 2 * n], refs[2 * n :]
    place = Place()
    greet((place.ctx_peers() if n_ctx else []) + (place.shard_peers() if n_shard else []))
    copies = Copies(send, recv)
    shards = [ShardGather(place, copies, full, 1) for full in outs[n_ctx:]]
    own = []
    for src, g in zip(ins[n_ctx:], shards):
        g.send(0, src)
        own.append(copies.local(src, g.full.at[g.me]))
    gathers = [
        CtxGather(place, copies, src, full, lo, rows, big)
        for src, full in zip(ins[:n_ctx], outs[:n_ctx])
        for lo, rows, big in halves(src.shape[0])
    ]
    for s in range(CtxGather.STAGES):
        for g in gathers:
            g.stage(s)
        if s == 2:
            for g in shards:
                g.forward(0)
    for g in shards:
        g.finish()
    wait_all(own)


def gather(cid, name, ctx_arrays, shard_arrays):
    arrays = list(ctx_arrays) + list(shard_arrays)
    n_ctx, n_shard = len(ctx_arrays), len(shard_arrays)
    outs = [jax.ShapeDtypeStruct((4, 4, 2) + a.shape, a.dtype) for a in ctx_arrays]
    outs += [jax.ShapeDtypeStruct((4,) + a.shape, a.dtype) for a in shard_arrays]
    return pl.pallas_call(
        partial(gather_kernel, n_ctx, n_shard),
        out_shape=outs,
        in_specs=[ANY] * len(arrays),
        out_specs=[ANY] * len(arrays),
        scratch_shapes=sems(n_ctx * 2 * CtxGather.COPIES + n_shard * 4),
        compiler_params=params(cid),
        name=name,
    )(*arrays)


def scatter_kernel(n, *refs):
    ins, outs = refs[:n], refs[n : 2 * n]
    bufs, (send, recv) = refs[2 * n : -2], refs[-2:]
    place = Place()
    greet(place.ctx_peers())
    copies = Copies(send, recv)
    engines = []
    for k, (src, out) in enumerate(zip(ins, outs)):
        for h, (lo, rows, big) in enumerate(halves(src.shape[3])):
            mine = bufs[(2 * k + h) * 7 : (2 * k + h + 1) * 7]
            engines.append(CtxScatter(place, copies, src, out, mine, lo, rows, big))
    for s in range(CtxScatter.STAGES):
        for e in engines:
            e.stage(s)


def scatter(cid, name, arrays):
    n = len(arrays)
    scratch = []
    for a in arrays:
        scratch += CtxScatter.scratch(a.shape[3] // 2, a.shape[4]) * 2
    return pl.pallas_call(
        partial(scatter_kernel, n),
        out_shape=[jax.ShapeDtypeStruct(a.shape[3:], F32) for a in arrays],
        in_specs=[VMEM] * n,
        out_specs=[VMEM] * n,
        scratch_shapes=scratch + sems(n * 2 * CtxScatter.COPIES),
        compiler_params=params(cid),
        name=name,
    )(*arrays)


CHUNKS = 4


def norm_kernel(part, resid, gain, hidden, full, a, b, c, send, recv):
    place = Place()
    greet(place.shard_peers())
    copies = Copies(send, recv)
    scatter_, gather_ = ShardScatter(place, copies, part, (a, b, c), CHUNKS), ShardGather(place, copies, full, CHUNKS)
    scatter_.begin()
    for k in range(CHUNKS):
        scatter_.relay_on(k)
    for k in range(CHUNKS):
        rows = scatter_.at(k)
        here = resid[rows, :].astype(F32) + scatter_.total(k)
        hidden[rows, :] = here
        factor = lax.rsqrt(jnp.mean(here * here, -1, keepdims=True) + EPS)
        full[gather_.me, rows, :] = (here * factor * gain[...].astype(F32)).astype(BF16)
        gather_.send(k)
    for k in range(CHUNKS):
        gather_.forward(k)
    gather_.finish()


def out_and_norm(cid, part, resid, gain):
    tokens, width = resid.shape
    return pl.pallas_call(
        norm_kernel,
        out_shape=[jax.ShapeDtypeStruct((tokens, width), F32), jax.ShapeDtypeStruct((4, tokens, width), BF16)],
        in_specs=[VMEM] * 3,
        out_specs=[VMEM] * 2,
        scratch_shapes=ShardScatter.scratch(tokens, width) + sems(6 * CHUNKS),
        compiler_params=params(cid),
        name="out_and_norm",
    )(part, resid, gain.reshape(1, width))


def norm_back_rows(grad, resid, gain):
    factor = lax.rsqrt(jnp.mean(resid * resid, -1, keepdims=True) + EPS)
    weighted = grad * gain
    per_gain = grad * resid * factor
    back = factor * weighted - resid * (factor * factor * factor) * jnp.mean(weighted * resid, -1, keepdims=True)
    return back, per_gain


def eight(rows):
    return jnp.sum(rows.reshape(rows.shape[0] // 8, 8, rows.shape[1]), 0)


def norm_back_kernel(part, hidden, gain, cot, grad_hidden, full, grad_gain, a, b, c, send, recv):
    place = Place()
    greet(place.shard_peers())
    copies = Copies(send, recv)
    scatter_, gather_ = ShardScatter(place, copies, part, (a, b, c), CHUNKS), ShardGather(place, copies, full, CHUNKS)
    scatter_.begin()
    for k in range(CHUNKS):
        scatter_.relay_on(k)
    for k in range(CHUNKS):
        rows = scatter_.at(k)
        back, per_gain = norm_back_rows(scatter_.total(k), hidden[rows, :], gain[...].astype(F32))
        here = cot[rows, :].astype(F32) + back
        grad_hidden[rows, :] = here
        full[gather_.me, rows, :] = here.astype(BF16)
        gather_.send(k)
        grad_gain[...] = eight(per_gain) if k == 0 else grad_gain[...] + eight(per_gain)
    for k in range(CHUNKS):
        gather_.forward(k)
    gather_.finish()


def norm_back_and_spread(cid, part, hidden, gain, cot):
    tokens, width = hidden.shape
    return pl.pallas_call(
        norm_back_kernel,
        out_shape=[
            jax.ShapeDtypeStruct((tokens, width), F32),
            jax.ShapeDtypeStruct((4, tokens, width), BF16),
            jax.ShapeDtypeStruct((8, width), F32),
        ],
        in_specs=[VMEM] * 4,
        out_specs=[VMEM] * 3,
        scratch_shapes=ShardScatter.scratch(tokens, width) + sems(6 * CHUNKS),
        compiler_params=params(cid),
        name="norm_back",
    )(part, hidden, gain.reshape(1, width), cot)


def tail_kernel(n, *refs):
    grads, (part, x, gain, grad_hidden, gain_other) = refs[:n], refs[n : n + 5]
    refs = refs[n + 5 :]
    outs, (grad_in, gains), refs = refs[:n], refs[n : n + 2], refs[n + 2 :]
    bufs, (a, b, c), gain_bufs, (acc, send, recv) = refs[: 14 * n], refs[14 * n : 14 * n + 3], refs[14 * n + 3 : -3], refs[-3:]
    place = Place()
    greet(place.ctx_peers() + place.shard_peers() + place.far_peers())
    copies = Copies(send, recv)
    first = ShardScatter(place, copies, part, (a, b, c), CHUNKS)
    first.begin()
    engines = []
    for k, (src, out) in enumerate(zip(grads, outs)):
        for h, (lo, rows, big) in enumerate(halves(src.shape[3])):
            mine = bufs[(2 * k + h) * 7 : (2 * k + h + 1) * 7]
            engines.append(CtxScatter(place, copies, src, out, mine, lo, rows, big))
    for e in engines:
        e.stage(0)
    for k in range(CHUNKS):
        first.relay_on(k)
    for e in engines:
        e.stage(1)
    for k in range(CHUNKS):
        rows = first.at(k)
        back, per_gain = norm_back_rows(first.total(k), x[rows, :].astype(F32), gain[...].astype(F32))
        grad_in[rows, :] = (grad_hidden[rows, :] + back).astype(BF16)
        acc[...] = eight(per_gain) if k == 0 else acc[...] + eight(per_gain)
    gain_sum = GainScatter(place, copies, gains, gain_bufs)
    row = lax.broadcasted_iota(jnp.int32, acc.shape, 0)
    one = jnp.sum(acc[...], 0, keepdims=True)
    two = jnp.sum(gain_other[...], 0, keepdims=True)
    gain_sum.vec[...] = jnp.where(row == 0, one, jnp.where(row == 1, two, 0.0))
    gain_sum.stage(0)
    for s in range(2, CtxScatter.STAGES):
        for e in engines:
            e.stage(s)
        gain_sum.stage(s - 1)
    gain_sum.stage(5)


def tail(cid, grads, part, x, gain, grad_hidden, gain_other):
    tokens, width = x.shape
    n = len(grads)
    scratch = []
    for g in grads:
        scratch += CtxScatter.scratch(g.shape[3] // 2, g.shape[4]) * 2
    return pl.pallas_call(
        partial(tail_kernel, n),
        out_shape=[jax.ShapeDtypeStruct(g.shape[3:], F32) for g in grads]
        + [jax.ShapeDtypeStruct((tokens, width), BF16), jax.ShapeDtypeStruct((8, 128), F32)],
        in_specs=[VMEM] * (n + 5),
        out_specs=[VMEM] * (n + 2),
        scratch_shapes=scratch
        + ShardScatter.scratch(tokens, width)
        + GainScatter.scratch()
        + [pltpu.VMEM((8, width), F32)]
        + sems(n * 2 * CtxScatter.COPIES + 3 * CHUNKS + GainScatter.COPIES),
        compiler_params=params(cid),
        name="tail",
    )(*grads, part, x, gain.reshape(1, width), grad_hidden, gain_other)


def add_rows_kernel(part, hidden, out, a, b, c, send, recv):
    place = Place()
    greet(place.shard_peers())
    scatter_ = ShardScatter(place, Copies(send, recv), part, (a, b, c), CHUNKS)
    scatter_.begin()
    for k in range(CHUNKS):
        scatter_.relay_on(k)
    for k in range(CHUNKS):
        out[scatter_.at(k), :] = (hidden[scatter_.at(k), :] + scatter_.total(k)).astype(BF16)


def add_rows(cid, part, hidden):
    tokens, width = hidden.shape
    return pl.pallas_call(
        add_rows_kernel,
        out_shape=jax.ShapeDtypeStruct((tokens, width), BF16),
        in_specs=[VMEM] * 2,
        out_specs=VMEM,
        scratch_shapes=ShardScatter.scratch(tokens, width) + sems(3 * CHUNKS),
        compiler_params=params(cid),
        name="add_rows",
    )(part, hidden)


def rope_tables(positions, head_dim):
    freqs = 10000.0 ** (-jnp.arange(head_dim // 2, dtype=jnp.float32) * 2.0 / head_dim)
    angles = positions[:, None] * freqs[None]
    angles = jnp.concatenate([angles, angles], -1)
    return (jnp.cos(angles), jnp.sin(angles))


def rotate(values, cosine, sine_part):
    middle = values.shape[-1] // 2
    turned = jnp.concatenate([-values[..., middle:], values[..., :middle]], -1)
    return values * cosine[:, None] + turned * sine_part[:, None]


def unrotate(grads, cosine, sine_part):
    middle = grads.shape[-1] // 2
    shifted = grads * sine_part[:, None]
    return grads * cosine[:, None] + jnp.concatenate(
        [shifted[..., middle:], -shifted[..., :middle]], -1
    )


def to_order(gathered, ctx_count, half_len):
    seq_count = gathered.shape[0]
    width = gathered.shape[-1]
    blocks = gathered.reshape(seq_count, ctx_count, 2, half_len, width)
    first = blocks[:, :, 0].reshape(seq_count, -1, width)
    second = blocks[:, ::-1, 1].reshape(seq_count, -1, width)
    return jnp.concatenate([first, second], 1)


def from_order(ordered, ctx_count, half_len):
    seq_count = ordered.shape[0]
    width = ordered.shape[-1]
    middle = ordered.shape[1] // 2
    first = ordered[:, :middle].reshape(seq_count, ctx_count, half_len, width)
    second = ordered[:, middle:].reshape(seq_count, ctx_count, half_len, width)[:, ::-1]
    return jnp.stack([first, second], 2).reshape(seq_count, -1, width)


def masked_scores(query_pos, key_span, q_block, keys):
    scores = jnp.einsum(
        "tkgd,skd->ktgs", q_block, keys, preferred_element_type=jnp.float32
    ) * HD ** (-0.5)
    allowed = (
        query_pos[None, :, None, None]
        >= jnp.arange(key_span, dtype=jnp.float32)[None, None, None, :]
    )
    return jnp.where(allowed, scores, NEG)


def seq_forward(positions, length, operands):
    q_seq, kv_seq = operands
    half_len = q_seq.shape[0] // 2
    kv_local = q_seq.shape[1]
    kv_width = kv_local * HD
    mixed_parts = []
    lse_parts = []
    for block in range(2):
        key_span = length // 2 if block == 0 else length
        query_pos = positions[block * half_len : (block + 1) * half_len]
        q_block = q_seq[block * half_len : (block + 1) * half_len]
        keys = kv_seq[:key_span, :kv_width].reshape(key_span, kv_local, HD)
        values = kv_seq[:key_span, kv_width:].reshape(key_span, kv_local, HD)
        scores = masked_scores(query_pos, key_span, q_block, keys)
        top = jnp.max(scores, -1, keepdims=True)
        expd = jnp.exp(scores - top)
        total = jnp.sum(expd, -1, keepdims=True)
        probs = expd / total
        mixed = jnp.einsum(
            "ktgs,skd->tkgd", probs.astype(jnp.bfloat16), values, preferred_element_type=jnp.float32
        )
        mixed_parts.append(mixed)
        lse_parts.append((top + jnp.log(total))[..., 0])
    return (jnp.concatenate(mixed_parts, 0), jnp.stack(lse_parts, 0))


def seq_backward(positions, length, operands):
    q_seq, kv_seq, grad_seq, lse_seq = operands
    half_len = q_seq.shape[0] // 2
    kv_local = q_seq.shape[1]
    kv_width = kv_local * HD
    grad_q_parts = []
    grad_kv = jnp.zeros((length, 2 * kv_width), jnp.float32)
    for block in range(2):
        key_span = length // 2 if block == 0 else length
        query_pos = positions[block * half_len : (block + 1) * half_len]
        q_block = q_seq[block * half_len : (block + 1) * half_len]
        g_block = grad_seq[block * half_len : (block + 1) * half_len]
        keys = kv_seq[:key_span, :kv_width].reshape(key_span, kv_local, HD)
        values = kv_seq[:key_span, kv_width:].reshape(key_span, kv_local, HD)
        scores = masked_scores(query_pos, key_span, q_block, keys)
        probs = jnp.exp(scores - lse_seq[block][..., None])
        grad_probs = jnp.einsum(
            "tkgd,skd->ktgs", g_block, values, preferred_element_type=jnp.float32
        )
        grad_v = jnp.einsum(
            "ktgs,tkgd->skd",
            probs.astype(jnp.bfloat16),
            g_block,
            preferred_element_type=jnp.float32,
        )
        delta = jnp.sum(probs * grad_probs, -1, keepdims=True)
        grad_scores = (probs * (grad_probs - delta)).astype(jnp.bfloat16)
        grad_q = jnp.einsum(
            "ktgs,skd->tkgd", grad_scores, keys, preferred_element_type=jnp.float32
        ) * HD ** (-0.5)
        grad_k = jnp.einsum(
            "ktgs,tkgd->skd", grad_scores, q_block, preferred_element_type=jnp.float32
        ) * HD ** (-0.5)
        joined = jnp.concatenate(
            [grad_k.reshape(key_span, kv_width), grad_v.reshape(key_span, kv_width)], 1
        )
        grad_kv = grad_kv.at[:key_span].add(joined)
        grad_q_parts.append(grad_q)
    return (jnp.concatenate(grad_q_parts, 0), grad_kv)


def dot(a, b, dims):
    return lax.dot_general(a, b, (dims, ((), ())), preferred_element_type=F32)


def per_device(
    inputs, cotangent, norm_attn, w_query, w_key, w_value, w_out, norm_mlp, w_gate, w_up, w_down
):
    width = inputs.shape[-1]
    half_len = inputs.shape[2]
    tokens = 2 * half_len
    ctx_count = lax.axis_size("ctx")
    ctx_index = lax.axis_index("ctx")
    group = lax.axis_size("wshard")
    length = tokens * ctx_count
    heads = w_query.shape[1] // HD
    x = inputs.reshape(tokens, width)
    cot = cotangent.reshape(tokens, width)
    rows_local = jnp.arange(tokens)
    positions = jnp.where(
        rows_local < half_len,
        ctx_index * half_len + rows_local,
        length - (ctx_index + 1) * half_len + (rows_local - half_len),
    ).astype(F32)
    cosine, sine_part = rope_tables(positions, HD)
    cos_all = jnp.tile(cosine, (group, 1))
    sin_all = jnp.tile(sine_part, (group, 1))

    resid = x.astype(F32)
    factor1 = lax.rsqrt(jnp.mean(resid * resid, -1, keepdims=True) + EPS)
    normed1 = (resid * factor1 * norm_attn.astype(F32)).astype(BF16)
    w_qkv = jnp.concatenate([w_query, w_key, w_value], 1)
    w_qkv, w_out_t, w_gate, w_up, w_down_t, normed_all, cot_all = gather(
        0, "gather_weights", [w_qkv, w_out.T, w_gate, w_up, w_down.T], [normed1, cot]
    )
    w_qkv, w_out_t, w_gate, w_up, w_down_t = (
        a.reshape(width, a.shape[-1]) for a in (w_qkv, w_out_t, w_gate, w_up, w_down_t)
    )
    normed_all = normed_all.reshape(group * tokens, width)
    cot_all = cot_all.reshape(group * tokens, width)

    lin = dot(normed_all, w_qkv, ((1,), (0,)))
    q_width = heads * HD
    query = rotate(lin[:, :q_width].reshape(-1, heads, HD), cos_all, sin_all).astype(BF16)
    keys = rotate(lin[:, q_width : q_width + HD].reshape(-1, 1, HD), cos_all, sin_all).astype(BF16)
    packed = jnp.concatenate([keys.reshape(-1, HD), lin[:, q_width + HD :].astype(BF16)], 1)
    (kv_all,) = gather(1, "gather_kv", [packed], [])
    kv_all = kv_all.reshape(ctx_count, group, tokens, 2 * HD).swapaxes(0, 1).reshape(group, -1, 2 * HD)
    kv_ordered = to_order(kv_all, ctx_count, half_len)
    grouped = query.reshape(group, tokens, 1, heads, HD)
    mixed, lse_all = lax.map(partial(seq_forward, positions, length), (grouped, kv_ordered))
    attn = mixed.reshape(group * tokens, q_width).astype(BF16)

    part = dot(attn, w_out_t, ((1,), (1,))).astype(BF16).reshape(group, tokens, width)
    hidden1, normed2_all = out_and_norm(2, part, x, norm_mlp)
    normed2_all = normed2_all.reshape(group * tokens, width)
    gate_pre = dot(normed2_all, w_gate, ((1,), (0,)))
    up_pre = dot(normed2_all, w_up, ((1,), (0,)))
    sigmoid_gate = jax.nn.sigmoid(gate_pre)
    silu_gate = gate_pre * sigmoid_gate
    active = (silu_gate * up_pre).astype(BF16)
    result_part = dot(active, w_down_t, ((1,), (1,))).astype(BF16).reshape(group, tokens, width)
    grad_active = dot(cot_all, w_down_t, ((1,), (0,)))
    grad_gate_pre = (grad_active * up_pre * sigmoid_gate * (1.0 + gate_pre * (1.0 - sigmoid_gate))).astype(BF16)
    grad_up_pre = (grad_active * silu_gate).astype(BF16)
    part2 = (dot(grad_gate_pre, w_gate, ((1,), (1,))) + dot(grad_up_pre, w_up, ((1,), (1,)))).astype(BF16)
    grad_hidden1, branch_all, gain2_part = norm_back_and_spread(
        3, part2.reshape(group, tokens, width), hidden1, norm_mlp, cot
    )
    branch_all = branch_all.reshape(group * tokens, width)
    outputs = add_rows(4, result_part, hidden1)

    def blocks(a):
        return a.astype(BF16).reshape(4, 4, 2, -1, a.shape[-1])

    g_down_t = blocks(dot(cot_all, active, ((0,), (0,))))
    g_gate = blocks(dot(normed2_all, grad_gate_pre, ((0,), (0,))))
    g_up = blocks(dot(normed2_all, grad_up_pre, ((0,), (0,))))
    g_gate, g_up, g_down_t = scatter(5, "scatter_ffn", [g_gate, g_up, g_down_t])

    grad_mixed = dot(branch_all, w_out_t, ((1,), (0,)))
    grad_grouped = grad_mixed.astype(BF16).reshape(group, tokens, 1, heads, HD)
    grad_q, grad_kv = lax.map(
        partial(seq_backward, positions, length), (grouped, kv_ordered, grad_grouped, lse_all)
    )
    grad_kv = from_order(grad_kv, ctx_count, half_len).astype(BF16)
    grad_kv = grad_kv.reshape(group, ctx_count, tokens, 2 * HD).swapaxes(0, 1)
    (grad_kv,) = scatter(6, "scatter_kv", [grad_kv.reshape(4, 4, 2, group * tokens, 2 * HD)])
    grad_klin = unrotate(grad_kv[:, :HD].reshape(-1, 1, HD), cos_all, sin_all).reshape(-1, HD)
    grad_qlin = unrotate(grad_q.reshape(-1, heads, HD), cos_all, sin_all).reshape(-1, q_width)
    grad_lin = jnp.concatenate([grad_qlin, grad_klin, grad_kv[:, HD:]], 1).astype(BF16)
    g_qkv = blocks(dot(normed_all, grad_lin, ((0,), (0,))))
    g_out_t = blocks(dot(branch_all, attn, ((0,), (0,))))
    part3 = dot(grad_lin, w_qkv, ((1,), (1,))).astype(BF16).reshape(group, tokens, width)
    g_qkv, g_out_t, grad_inputs, gains = tail(
        7, [g_qkv, g_out_t], part3, x, norm_attn, grad_hidden1, gain2_part
    )
    start = (ctx_index % 2) * 64 + lax.axis_index("wshard") * 16
    gains = lax.dynamic_slice_in_dim(gains, start, 16, axis=1)
    return (
        outputs.reshape(inputs.shape),
        grad_inputs.reshape(inputs.shape),
        gains[0],
        g_qkv[:, :q_width],
        g_qkv[:, q_width : q_width + HD],
        g_qkv[:, q_width + HD :],
        g_out_t.T,
        gains[1],
        g_gate,
        g_up,
        g_down_t.T,
    )


def solution(mesh):
    return jax.shard_map(
        per_device,
        mesh=mesh,
        in_specs=(
            P("wshard", None, "ctx", None),
            P("wshard", None, "ctx", None),
            P(),
            P("ctx", "wshard"),
            P("ctx", "wshard"),
            P("ctx", "wshard"),
            P("wshard", "ctx"),
            P(),
            P("ctx", "wshard"),
            P("ctx", "wshard"),
            P("wshard", "ctx"),
        ),
        out_specs=(
            P("wshard", None, "ctx", None),
            P("wshard", None, "ctx", None),
            P(("ctx", "wshard")),
            P("ctx", "wshard"),
            P("ctx", "wshard"),
            P("ctx", "wshard"),
            P("wshard", "ctx"),
            P(("ctx", "wshard")),
            P("ctx", "wshard"),
            P("ctx", "wshard"),
            P("wshard", "ctx"),
        ),
        check_vma=False,
    )
```

```python
from functools import partial

import jax
import jax.numpy as jnp
from jax import lax
from jax.experimental import pallas as pl
from jax.experimental.pallas import tpu as pltpu
from jax.sharding import PartitionSpec as P

MESH = pl.DeviceIdType.MESH
HD = 64
EPS = 1e-05
NEG = -1e30
F32 = jnp.float32
BF16 = jnp.bfloat16
VMEM_LIMIT = 60 * 2**20
ANY = pl.BlockSpec(memory_space=pl.ANY)
VMEM = pl.BlockSpec(memory_space=pltpu.VMEM)


class Place:
    def __init__(self):
        ctx, shard = lax.axis_index("ctx"), lax.axis_index("wshard")
        self.x, self.z, self.y = ctx // 8, (ctx // 2) % 4, ctx % 2
        self.yl, self.co = shard // 2, shard % 2

    def at(self, x=None, z=None, y=None, yl=None, co=None):
        x, z, y = (self.x if x is None else x), (self.z if z is None else z), (self.y if y is None else y)
        yl, co = (self.yl if yl is None else yl), (self.co if co is None else co)
        return (x * 8 + z * 2 + y, yl * 2 + co)

    def step(self, axis, by):
        return self.at(**{axis: (getattr(self, axis) + by) % 4})

    def pair(self, axis):
        return self.at(**{axis: 1 - getattr(self, axis)})

    def ctx_peers(self):
        return [self.step("x", 1), self.step("x", 3), self.step("z", 1), self.step("z", 3), self.pair("y")]

    def shard_peers(self):
        return [self.pair("co"), self.pair("yl")]

    def far_peers(self):
        return [self.step("x", 2), self.step("z", 2)]


def greet(peers):
    barrier = pltpu.get_barrier_semaphore()
    for device in peers:
        pl.semaphore_signal(barrier, inc=1, device_id=device, device_id_type=MESH)
    pl.semaphore_wait(barrier, len(peers))


class Copies:
    def __init__(self, send, recv):
        self.send, self.recv, self.used = send, recv, 0

    def start(self, src, dst, device):
        k = self.used
        self.used += 1
        copy = pltpu.make_async_remote_copy(
            src_ref=src, dst_ref=dst, send_sem=self.send.at[k], recv_sem=self.recv.at[k],
            device_id=device, device_id_type=MESH,
        )
        copy.start()
        return copy

    def local(self, src, dst):
        k = self.used
        self.used += 1
        copy = pltpu.make_async_copy(src, dst, self.send.at[k])
        copy.start()
        return copy


def wait_all(copies):
    for copy in copies:
        copy.wait()


class CtxGather:
    COPIES = 10
    STAGES = 6

    def __init__(self, place, copies, shard, full, lo, n, big):
        self.p, self.c, self.shard, self.full = place, copies, shard, full
        self.lo, self.n, self.big, self.small = lo, n, big, ("z" if big == "x" else "x")
        self.live = []

    def block(self, o, i, y):
        x, z = (o, i) if self.big == "x" else (i, o)
        return self.full.at[x, z, y, pl.ds(self.lo, self.n)]

    def send(self, part, axis, by):
        dev = self.p.pair("y") if axis == "y" else self.p.step(axis, by)
        self.live.append(self.c.start(part, part, dev))

    def stage(self, s):
        p = self.p
        o, i, y = getattr(p, self.big), getattr(p, self.small), p.y
        wait_all(self.live)
        self.live = []
        every, both = pl.ds(0, 4), pl.ds(0, 2)
        if s == 0:
            own = self.shard.at[pl.ds(self.lo, self.n)]
            self.live.append(self.c.start(own, self.block(o, i, y), p.pair("y")))
            self.live.append(self.c.local(own, self.block(o, i, y)))
        elif s == 1:
            self.send(self.block(o, i, both), self.small, 1)
            self.send(self.block(o, i, both), self.small, 3)
        elif s == 2:
            self.send(self.block(o, (i + 3) % 4, 0), self.small, 1)
            self.send(self.block(o, (i + 1) % 4, 1), self.small, 3)
        elif s == 3:
            self.send(self.block(o, every, both), self.big, 1)
            self.send(self.block(o, every, both), self.big, 3)
        elif s == 4:
            self.send(self.block((o + 3) % 4, pl.ds(0, 2), both), self.big, 1)
            self.send(self.block((o + 1) % 4, pl.ds(2, 2), both), self.big, 3)


class CtxScatter:
    COPIES = 13
    STAGES = 6

    @staticmethod
    def scratch(n, width):
        return [
            pltpu.VMEM((2, 2, 2, n, width), BF16),
            pltpu.VMEM((4, 2, n, width), BF16),
            pltpu.VMEM((4, 2, n, width), BF16),
            pltpu.VMEM((2, n, width), BF16),
            pltpu.VMEM((2, n, width), BF16),
            pltpu.VMEM((2, n, width), BF16),
            pltpu.VMEM((n, width), BF16),
        ]

    def __init__(self, place, copies, src, out, bufs, lo, n, big):
        self.p, self.c, self.src, self.out = place, copies, src, out
        self.far, self.pos, self.neg, self.far2, self.pos2, self.neg2, self.last = bufs
        self.lo, self.n, self.big, self.small = lo, n, big, ("z" if big == "x" else "x")
        self.live = []

    def part(self, o, i):
        x, z = (o, i) if self.big == "x" else (i, o)
        return self.src.at[x, z, pl.ds(0, 2), pl.ds(self.lo, self.n)]

    def load(self, o, i, y):
        x, z = (o, i) if self.big == "x" else (i, o)
        return self.src[x, z, y, pl.ds(self.lo, self.n), :].astype(F32)

    def send(self, src, dst, axis, by):
        dev = self.p.pair("y") if axis == "y" else self.p.step(axis, by)
        self.live.append(self.c.start(src, dst, dev))

    def stage(self, s):
        p, big, small = self.p, self.big, self.small
        o, i, y = getattr(p, big), getattr(p, small), p.y
        up, down, across = (o + 1) % 4, (o + 3) % 4, (o + 2) % 4
        iup, idown, iacross = (i + 1) % 4, (i + 3) % 4, (i + 2) % 4
        low, high = pl.ds(0, 2), pl.ds(2, 2)
        if s == 1:
            wait_all(self.live[:2])
            self.live = self.live[2:]
        else:
            wait_all(self.live)
            self.live = []
        if s == 0:
            self.send(self.part(across, low), self.far.at[0], big, 1)
            self.send(self.part(across, high), self.far.at[1], big, 3)
            self.send(self.part(up, high), self.pos.at[high], big, 1)
            self.send(self.part(down, low), self.neg.at[low], big, 3)
        elif s == 1:

            def fold(k, _):
                b, q = k // 2, k % 2
                self.far[0, b, q] = (self.far[0, b, q].astype(F32) + self.load(up, b, q)).astype(BF16)
                self.far[1, b, q] = (self.far[1, b, q].astype(F32) + self.load(down, b + 2, q)).astype(BF16)
                return 0

            lax.fori_loop(0, 4, fold, 0)
            self.send(self.far.at[0], self.pos.at[low], big, 1)
            self.send(self.far.at[1], self.neg.at[high], big, 3)
        elif s == 2:

            def total(k, _):
                b, q = k // 2, k % 2
                here = self.load(o, b, q) + self.pos[b, q].astype(F32) + self.neg[b, q].astype(F32)
                self.pos[b, q] = here.astype(BF16)
                return 0

            lax.fori_loop(0, 8, total, 0)
            self.send(self.pos.at[iacross, 0], self.far2.at[0], small, 1)
            self.send(self.pos.at[iacross, 1], self.far2.at[1], small, 3)
            self.send(self.pos.at[iup, 1], self.pos2.at[1], small, 1)
            self.send(self.pos.at[idown, 0], self.neg2.at[0], small, 3)
        elif s == 3:
            self.far2[0] = (self.far2[0].astype(F32) + self.pos[iup, 0].astype(F32)).astype(BF16)
            self.far2[1] = (self.far2[1].astype(F32) + self.pos[idown, 1].astype(F32)).astype(BF16)
            self.send(self.far2.at[0], self.pos2.at[0], small, 1)
            self.send(self.far2.at[1], self.neg2.at[1], small, 3)
        elif s == 4:
            for q in range(2):
                here = self.pos[i, q].astype(F32) + self.pos2[q].astype(F32) + self.neg2[q].astype(F32)
                self.pos2[q] = here.astype(BF16)
            self.send(self.pos2.at[1 - y], self.last, "y", 0)
        elif s == 5:
            self.out[pl.ds(self.lo, self.n), :] = (self.pos2[y].astype(F32) + self.last[...].astype(F32)).astype(
                self.out.dtype
            )


class ShardGather:
    def __init__(self, place, copies, full, chunks):
        self.p, self.c, self.full, self.chunks = place, copies, full, chunks
        self.rows = full.shape[1] // chunks
        self.me, self.over = place.yl * 2 + place.co, (1 - place.yl) * 2 + place.co
        self.far, self.near = [], []

    COPIES = 3

    def part(self, who, k):
        return self.full.at[who, pl.ds(k * self.rows, self.rows)]

    def send(self, k, src=None):
        src = self.part(self.me, k) if src is None else src
        self.far.append(self.c.start(src, self.part(self.me, k), self.p.pair("yl")))
        self.near.append(self.c.start(src, self.part(self.me, k), self.p.pair("co")))

    def forward(self, k):
        self.far[k].wait()
        self.near.append(self.c.start(self.part(self.over, k), self.part(self.over, k), self.p.pair("co")))

    def finish(self):
        wait_all(self.near)


class ShardScatter:
    COPIES = 3

    @staticmethod
    def scratch(rows, width):
        return [pltpu.VMEM((rows, width), BF16)] * 3

    def __init__(self, place, copies, part, bufs, chunks):
        self.p, self.c, self.part, self.chunks = place, copies, part, chunks
        self.relay, self.near, self.over = bufs
        self.rows = part.shape[1] // chunks
        self.first, self.second, self.third = [], [], []

    def at(self, k):
        return pl.ds(k * self.rows, self.rows)

    def begin(self):
        p = self.p
        for k in range(self.chunks):
            src = self.part.at[(1 - p.yl) * 2 + 1 - p.co, self.at(k)]
            self.first.append(self.c.start(src, self.relay.at[self.at(k)], p.pair("co")))
        for k in range(self.chunks):
            src = self.part.at[p.yl * 2 + 1 - p.co, self.at(k)]
            self.second.append(self.c.start(src, self.near.at[self.at(k)], p.pair("co")))

    def relay_on(self, k):
        p = self.p
        self.first[k].wait()
        here = self.part[(1 - p.yl) * 2 + p.co, self.at(k), :].astype(F32)
        self.relay[self.at(k), :] = (self.relay[self.at(k), :].astype(F32) + here).astype(BF16)
        self.third.append(self.c.start(self.relay.at[self.at(k)], self.over.at[self.at(k)], p.pair("yl")))

    def total(self, k):
        p = self.p
        self.second[k].wait()
        self.third[k].wait()
        here = self.part[p.yl * 2 + p.co, self.at(k), :].astype(F32)
        return here + self.near[self.at(k), :].astype(F32) + self.over[self.at(k), :].astype(F32)


class GainScatter:
    COPIES = 9
    STAGES = 6

    @staticmethod
    def scratch():
        return [
            pltpu.VMEM((8, 2048), F32),
            pltpu.VMEM((3, 8, 512), F32),
            pltpu.VMEM((8, 512), F32),
            pltpu.VMEM((3, 8, 128), F32),
            pltpu.VMEM((3, 8, 128), F32),
            pltpu.VMEM((3, 8, 128), F32),
        ]

    def __init__(self, place, copies, out, bufs):
        self.p, self.c, self.out = place, copies, out
        self.vec, self.xs, self.mid, self.zs, self.own, self.rest = bufs
        self.live = []

    def stage(self, s):
        p = self.p
        wait_all(self.live)
        self.live = []
        if s == 0:
            for by in (1, 2, 3):
                cols = pl.ds(pl.multiple_of(((p.x + by) % 4) * 512, 512), 512)
                self.live.append(self.c.start(self.vec.at[:, cols], self.xs.at[by - 1], p.step("x", by)))
        elif s == 1:
            cols = pl.ds(pl.multiple_of(p.x * 512, 512), 512)
            self.mid[...] = self.vec[:, cols] + self.xs[0] + self.xs[1] + self.xs[2]
            for by in (1, 2, 3):
                cols = pl.ds(pl.multiple_of(((p.z + by) % 4) * 128, 128), 128)
                self.live.append(self.c.start(self.mid.at[:, cols], self.zs.at[by - 1], p.step("z", by)))
        elif s == 2:
            cols = pl.ds(pl.multiple_of(p.z * 128, 128), 128)
            self.own[0] = self.mid[:, cols] + self.zs[0] + self.zs[1] + self.zs[2]
            self.live.append(self.c.start(self.own.at[0], self.rest.at[0], p.pair("y")))
        elif s == 3:
            self.own[1] = self.own[0] + self.rest[0]
            self.live.append(self.c.start(self.own.at[1], self.rest.at[1], p.pair("co")))
        elif s == 4:
            self.own[2] = self.own[1] + self.rest[1]
            self.live.append(self.c.start(self.own.at[2], self.rest.at[2], p.pair("yl")))
        elif s == 5:
            self.out[...] = self.own[2] + self.rest[2]


def sems(n):
    return [pltpu.SemaphoreType.DMA((n,)), pltpu.SemaphoreType.DMA((n,))]


def params(cid):
    return pltpu.CompilerParams(collective_id=cid, has_side_effects=True, vmem_limit_bytes=VMEM_LIMIT)


def halves(rows):
    return ((0, rows // 2, "x"), (rows // 2, rows // 2, "z"))


def gather_kernel(n_ctx, n_shard, *refs):
    n = n_ctx + n_shard
    ins, outs, (send, recv) = refs[:n], refs[n : 2 * n], refs[2 * n :]
    place = Place()
    greet((place.ctx_peers() if n_ctx else []) + (place.shard_peers() if n_shard else []))
    copies = Copies(send, recv)
    shards = [ShardGather(place, copies, full, 1) for full in outs[n_ctx:]]
    own = []
    for src, g in zip(ins[n_ctx:], shards):
        g.send(0, src)
        own.append(copies.local(src, g.full.at[g.me]))
    gathers = [
        CtxGather(place, copies, src, full, lo, rows, big)
        for src, full in zip(ins[:n_ctx], outs[:n_ctx])
        for lo, rows, big in halves(src.shape[0])
    ]
    for s in range(CtxGather.STAGES):
        for g in gathers:
            g.stage(s)
        if s == 2:
            for g in shards:
                g.forward(0)
    for g in shards:
        g.finish()
    wait_all(own)


def gather(cid, name, ctx_arrays, shard_arrays):
    arrays = list(ctx_arrays) + list(shard_arrays)
    n_ctx, n_shard = len(ctx_arrays), len(shard_arrays)
    outs = [jax.ShapeDtypeStruct((4, 4, 2) + a.shape, a.dtype) for a in ctx_arrays]
    outs += [jax.ShapeDtypeStruct((4,) + a.shape, a.dtype) for a in shard_arrays]
    return pl.pallas_call(
        partial(gather_kernel, n_ctx, n_shard),
        out_shape=outs,
        in_specs=[ANY] * len(arrays),
        out_specs=[ANY] * len(arrays),
        scratch_shapes=sems(n_ctx * 2 * CtxGather.COPIES + n_shard * 4),
        compiler_params=params(cid),
        name=name,
    )(*arrays)


def scatter_kernel(n, *refs):
    ins, outs = refs[:n], refs[n : 2 * n]
    bufs, (send, recv) = refs[2 * n : -2], refs[-2:]
    place = Place()
    greet(place.ctx_peers())
    copies = Copies(send, recv)
    engines = []
    for k, (src, out) in enumerate(zip(ins, outs)):
        for h, (lo, rows, big) in enumerate(halves(src.shape[3])):
            mine = bufs[(2 * k + h) * 7 : (2 * k + h + 1) * 7]
            engines.append(CtxScatter(place, copies, src, out, mine, lo, rows, big))
    for s in range(CtxScatter.STAGES):
        for e in engines:
            e.stage(s)


def scatter(cid, name, arrays):
    n = len(arrays)
    scratch = []
    for a in arrays:
        scratch += CtxScatter.scratch(a.shape[3] // 2, a.shape[4]) * 2
    return pl.pallas_call(
        partial(scatter_kernel, n),
        out_shape=[jax.ShapeDtypeStruct(a.shape[3:], F32) for a in arrays],
        in_specs=[VMEM] * n,
        out_specs=[VMEM] * n,
        scratch_shapes=scratch + sems(n * 2 * CtxScatter.COPIES),
        compiler_params=params(cid),
        name=name,
    )(*arrays)


CHUNKS = 4


def norm_kernel(part, resid, gain, hidden, full, a, b, c, send, recv):
    place = Place()
    greet(place.shard_peers())
    copies = Copies(send, recv)
    scatter_, gather_ = ShardScatter(place, copies, part, (a, b, c), CHUNKS), ShardGather(place, copies, full, CHUNKS)
    scatter_.begin()
    for k in range(CHUNKS):
        scatter_.relay_on(k)
    for k in range(CHUNKS):
        rows = scatter_.at(k)
        here = resid[rows, :].astype(F32) + scatter_.total(k)
        hidden[rows, :] = here
        factor = lax.rsqrt(jnp.mean(here * here, -1, keepdims=True) + EPS)
        full[gather_.me, rows, :] = (here * factor * gain[...].astype(F32)).astype(BF16)
        gather_.send(k)
    for k in range(CHUNKS):
        gather_.forward(k)
    gather_.finish()


def out_and_norm(cid, part, resid, gain):
    tokens, width = resid.shape
    return pl.pallas_call(
        norm_kernel,
        out_shape=[jax.ShapeDtypeStruct((tokens, width), F32), jax.ShapeDtypeStruct((4, tokens, width), BF16)],
        in_specs=[VMEM] * 3,
        out_specs=[VMEM] * 2,
        scratch_shapes=ShardScatter.scratch(tokens, width) + sems(6 * CHUNKS),
        compiler_params=params(cid),
        name="out_and_norm",
    )(part, resid, gain.reshape(1, width))


def norm_back_rows(grad, resid, gain):
    factor = lax.rsqrt(jnp.mean(resid * resid, -1, keepdims=True) + EPS)
    weighted = grad * gain
    per_gain = grad * resid * factor
    back = factor * weighted - resid * (factor * factor * factor) * jnp.mean(weighted * resid, -1, keepdims=True)
    return back, per_gain


def eight(rows):
    return jnp.sum(rows.reshape(rows.shape[0] // 8, 8, rows.shape[1]), 0)


def norm_back_kernel(part, hidden, gain, cot, grad_hidden, full, grad_gain, a, b, c, send, recv):
    place = Place()
    greet(place.shard_peers())
    copies = Copies(send, recv)
    scatter_, gather_ = ShardScatter(place, copies, part, (a, b, c), CHUNKS), ShardGather(place, copies, full, CHUNKS)
    scatter_.begin()
    for k in range(CHUNKS):
        scatter_.relay_on(k)
    for k in range(CHUNKS):
        rows = scatter_.at(k)
        back, per_gain = norm_back_rows(scatter_.total(k), hidden[rows, :], gain[...].astype(F32))
        here = cot[rows, :].astype(F32) + back
        grad_hidden[rows, :] = here
        full[gather_.me, rows, :] = here.astype(BF16)
        gather_.send(k)
        grad_gain[...] = eight(per_gain) if k == 0 else grad_gain[...] + eight(per_gain)
    for k in range(CHUNKS):
        gather_.forward(k)
    gather_.finish()


def norm_back_and_spread(cid, part, hidden, gain, cot):
    tokens, width = hidden.shape
    return pl.pallas_call(
        norm_back_kernel,
        out_shape=[
            jax.ShapeDtypeStruct((tokens, width), F32),
            jax.ShapeDtypeStruct((4, tokens, width), BF16),
            jax.ShapeDtypeStruct((8, width), F32),
        ],
        in_specs=[VMEM] * 4,
        out_specs=[VMEM] * 3,
        scratch_shapes=ShardScatter.scratch(tokens, width) + sems(6 * CHUNKS),
        compiler_params=params(cid),
        name="norm_back",
    )(part, hidden, gain.reshape(1, width), cot)


def tail_kernel(n, *refs):
    grads, (part, x, gain, grad_hidden, gain_other) = refs[:n], refs[n : n + 5]
    refs = refs[n + 5 :]
    outs, (grad_in, gains), refs = refs[:n], refs[n : n + 2], refs[n + 2 :]
    bufs, (a, b, c), gain_bufs, (acc, send, recv) = refs[: 14 * n], refs[14 * n : 14 * n + 3], refs[14 * n + 3 : -3], refs[-3:]
    place = Place()
    greet(place.ctx_peers() + place.shard_peers() + place.far_peers())
    copies = Copies(send, recv)
    first = ShardScatter(place, copies, part, (a, b, c), CHUNKS)
    first.begin()
    engines = []
    for k, (src, out) in enumerate(zip(grads, outs)):
        for h, (lo, rows, big) in enumerate(halves(src.shape[3])):
            mine = bufs[(2 * k + h) * 7 : (2 * k + h + 1) * 7]
            engines.append(CtxScatter(place, copies, src, out, mine, lo, rows, big))
    for e in engines:
        e.stage(0)
    for k in range(CHUNKS):
        first.relay_on(k)
    for e in engines:
        e.stage(1)
    for k in range(CHUNKS):
        rows = first.at(k)
        back, per_gain = norm_back_rows(first.total(k), x[rows, :].astype(F32), gain[...].astype(F32))
        grad_in[rows, :] = (grad_hidden[rows, :] + back).astype(BF16)
        acc[...] = eight(per_gain) if k == 0 else acc[...] + eight(per_gain)
    gain_sum = GainScatter(place, copies, gains, gain_bufs)
    row = lax.broadcasted_iota(jnp.int32, acc.shape, 0)
    one = jnp.sum(acc[...], 0, keepdims=True)
    two = jnp.sum(gain_other[...], 0, keepdims=True)
    gain_sum.vec[...] = jnp.where(row == 0, one, jnp.where(row == 1, two, 0.0))
    gain_sum.stage(0)
    for s in range(2, CtxScatter.STAGES):
        for e in engines:
            e.stage(s)
        gain_sum.stage(s - 1)
    gain_sum.stage(5)


def tail(cid, grads, part, x, gain, grad_hidden, gain_other):
    tokens, width = x.shape
    n = len(grads)
    scratch = []
    for g in grads:
        scratch += CtxScatter.scratch(g.shape[3] // 2, g.shape[4]) * 2
    return pl.pallas_call(
        partial(tail_kernel, n),
        out_shape=[jax.ShapeDtypeStruct(g.shape[3:], F32) for g in grads]
        + [jax.ShapeDtypeStruct((tokens, width), BF16), jax.ShapeDtypeStruct((8, 128), F32)],
        in_specs=[VMEM] * (n + 5),
        out_specs=[VMEM] * (n + 2),
        scratch_shapes=scratch
        + ShardScatter.scratch(tokens, width)
        + GainScatter.scratch()
        + [pltpu.VMEM((8, width), F32)]
        + sems(n * 2 * CtxScatter.COPIES + 3 * CHUNKS + GainScatter.COPIES),
        compiler_params=params(cid),
        name="tail",
    )(*grads, part, x, gain.reshape(1, width), grad_hidden, gain_other)


KEYS = 256
KB = 4


def lane_iota(rows):
    return lax.broadcasted_iota(jnp.int32, (rows, 128), 1)


def rotate_tile(u, cosine, sine):
    low = lane_iota(u.shape[0]) % HD < HD // 2
    turned = jnp.where(low, -pltpu.roll(u, 128 - HD // 2, 1), pltpu.roll(u, HD // 2, 1))
    return u * cosine + turned * sine


def unrotate_tile(w, cosine, sine):
    low = lane_iota(w.shape[0]) % HD < HD // 2
    s = w * sine
    return w * cosine + jnp.where(low, pltpu.roll(s, 128 - HD // 2, 1), -pltpu.roll(s, HD // 2, 1))


def project_rows(rows, w_qkv, tables):
    lin = jnp.dot(rows, w_qkv, preferred_element_type=F32)
    tiles = []
    for hp in range(4):
        tile = lin[:, hp * 128 : (hp + 1) * 128]
        tiles.append((rotate_tile(tile, tables[0], tables[1])).astype(BF16) * jnp.asarray(HD**-0.5, BF16))
    kv = rotate_tile(lin[:, 512:640], tables[2], tables[3]).astype(BF16)
    return tiles, kv


def head_rows(ref, start, keep_low):
    low = lane_iota(64) < HD
    keep = low if keep_low else ~low
    pieces = []
    for hp in range(4):
        tile = ref[pl.ds(start, 64), hp * 128 : (hp + 1) * 128].astype(F32)
        turned = pltpu.roll(tile, HD, 1)
        even, odd = (tile, turned) if keep_low else (turned, tile)
        pieces += [jnp.where(keep, even, 0.0), jnp.where(keep, odd, 0.0)]
    return pieces


def key_chunk(kv, seq, chunk, half):
    start = pl.multiple_of(seq * 128 + half * 64, 64)
    return kv[pl.ds(chunk * KB, KB), pl.ds(start, 64), :].reshape(KEYS, 128)


def diagonal(block, here):
    key = lax.broadcasted_iota(jnp.int32, (KEYS, 512), 0)
    query = lax.broadcasted_iota(jnp.int32, (KEYS, 512), 1) % 64
    ahead = key // 64 - here
    return key % 64 - query <= (-ahead if block == 0 else ahead) * 64


def pick(u, own_chunk):
    late = u - 8
    block = jnp.where(u < 8, 1, jnp.where(late >= own_chunk, 1, 0))
    half = jnp.where(u < 8, 0, block)
    chunk = jnp.where(u < 8, u, late + half)
    return block, chunk, half


def nt(a, b):
    return lax.dot_general(a, b, (((1,), (1,)), ((), ())), preferred_element_type=F32)


def tn(a, b):
    return lax.dot_general(a, b, (((0,), (0,)), ((), ())), preferred_element_type=F32)


def attend_seq(seq, ctx, q, kv, attn, lse, scratch, hook):
    qe, top, acc = scratch
    low = lane_iota(64) < HD
    ones_low = lane_iota(KEYS) < HD
    own_chunk, here = ctx // KB, ctx % KB

    def with_ones(keys):
        return jnp.where(ones_low, jnp.ones_like(keys), keys)

    for b in range(2):
        for h, piece in enumerate(head_rows(q, seq * 128 + b * 64, True)):
            qe[b, h * 64 : (h + 1) * 64, :] = piece.astype(BF16)
    for b in range(2):
        keys = key_chunk(kv, seq, own_chunk, b)
        scores = jnp.where(diagonal(b, here), nt(keys, qe[b]), NEG)
        m = jnp.max(scores, 0, keepdims=True)
        p = jnp.exp(scores - m).astype(BF16)
        top[b] = m
        acc[b] = tn(with_ones(keys), p)

    def step(u, _):
        b, chunk, half = pick(u, own_chunk)
        keys = key_chunk(kv, seq, chunk, half)
        scores = nt(keys, qe[b])
        before = top[b]
        m = jnp.maximum(before, jnp.max(scores, 0, keepdims=True))
        p = jnp.exp(scores - m).astype(BF16)
        top[b] = m
        acc[b] = acc[b] * jnp.exp(before - m) + tn(with_ones(keys), p)
        return 0

    for k in range(3):
        lax.fori_loop(5 * k, 5 * k + 5, step, 0, unroll=True)
        hook()
    for b in range(2):
        here_acc = acc[b]
        total = here_acc[0:1, :]
        lse[pl.ds(seq * 2 + b, 1), :] = top[b] + jnp.log(total)
        out = (here_acc * (1.0 / total)).T
        for hp in range(4):
            even, odd = out[hp * 128 : hp * 128 + 64, :], out[hp * 128 + 64 : hp * 128 + 128, :]
            tile = jnp.where(low, pltpu.roll(even, HD, 1), odd)
            attn[pl.ds(seq * 128 + b * 64, 64), hp * 128 : (hp + 1) * 128] = tile.astype(BF16)


def attend_scratch():
    return [pltpu.VMEM((2, 512, 128), BF16), pltpu.VMEM((2, 1, 512), F32), pltpu.VMEM((2, 128, 512), F32)]


def attend_back_seq(seq, ctx, q, kv, grad, attn, lse, tables, grad_lin, grad_kv, scratch, hook):
    qd, delta, dq, dkv = scratch
    low = lane_iota(64) < HD
    own_chunk, here = ctx // KB, ctx % KB
    for b in range(2):
        start = seq * 128 + b * 64
        q_rows, g_rows, o_rows = (
            head_rows(q, start, True), head_rows(grad, start, False), head_rows(attn, start, False)
        )
        for h in range(8):
            qd[b, h * 64 : (h + 1) * 64, :] = q_rows[h].astype(BF16)
            qd[b, 512 + h * 64 : 512 + (h + 1) * 64, :] = g_rows[h].astype(BF16)
        products = jnp.concatenate([g * o for g, o in zip(g_rows, o_rows)], 0)
        delta[b] = jnp.sum(products.T, 0, keepdims=True)

    def grads(b, keys, allowed):
        both = nt(keys, qd[b])
        p = jnp.exp(both[:, :512] - lse[pl.ds(seq * 2 + b, 1), :])
        if allowed is not None:
            p = jnp.where(allowed, p, 0.0)
        ds = (p * (both[:, 512:] - delta[b])).astype(BF16)
        joined = jnp.concatenate([ds, p.astype(BF16)], 1)
        return tn(keys, ds), jnp.dot(joined, qd[b], preferred_element_type=F32)

    dkv[...] = jnp.zeros_like(dkv)

    def add_keys(chunk, half, value):
        start = pl.multiple_of(half * 64, 64)
        dkv[pl.ds(chunk * KB, KB), pl.ds(start, 64), :] += value.reshape(KB, 64, 128)

    for b in range(2):
        dq_part, dkv_part = grads(b, key_chunk(kv, seq, own_chunk, b), diagonal(b, here))
        dq[b] = dq_part
        add_keys(own_chunk, b, dkv_part)

    def step(u, _):
        b, chunk, half = pick(u, own_chunk)
        dq_part, dkv_part = grads(b, key_chunk(kv, seq, chunk, half), None)
        dq[b] += dq_part
        add_keys(chunk, half, dkv_part)
        return 0

    for k in range(3):
        lax.fori_loop(5 * k, 5 * k + 5, step, 0, unroll=True)
        hook()
    for b in range(2):
        out = (dq[b] * HD**-0.5).T
        cosine, sine = tables[0, b * 64 : (b + 1) * 64, :], tables[1, b * 64 : (b + 1) * 64, :]
        for hp in range(4):
            even, odd = out[hp * 128 : hp * 128 + 64, :], out[hp * 128 + 64 : hp * 128 + 128, :]
            tile = jnp.where(low, even, pltpu.roll(odd, HD, 1))
            tile = unrotate_tile(tile, cosine, sine)
            grad_lin[pl.ds(seq * 128 + b * 64, 64), hp * 128 : (hp + 1) * 128] = tile.astype(BF16)
    grad_kv[:, pl.ds(seq * 128, 128), :] = dkv[...].astype(BF16)


def attend_back_scratch():
    return [
        pltpu.VMEM((2, 1024, 128), BF16),
        pltpu.VMEM((2, 1, 512), F32),
        pltpu.VMEM((2, 128, 512), F32),
        pltpu.VMEM((32, 128, 128), F32),
    ]


def project_kernel(rows, w_qkv, tables, q, kv):
    def one(s, _):
        at = pl.ds(pl.multiple_of(s * 128, 128), 128)
        tiles, keys = project_rows(rows[at, :], w_qkv[...], tables)
        for hp, tile in enumerate(tiles):
            q[at, hp * 128 : (hp + 1) * 128] = tile
        kv[at, :] = keys
        return 0

    lax.fori_loop(0, 4, one, 0)


def project(rows, w_qkv, tables):
    return pl.pallas_call(
        project_kernel,
        out_shape=[jax.ShapeDtypeStruct((rows.shape[0], 512), BF16), jax.ShapeDtypeStruct((rows.shape[0], 128), BF16)],
        in_specs=[VMEM] * 3,
        out_specs=[VMEM] * 2,
        compiler_params=pltpu.CompilerParams(vmem_limit_bytes=VMEM_LIMIT),
        name="project",
    )(rows, w_qkv, tables)


class Stages:
    def __init__(self, engines):
        self.engines, self.done = engines, 0

    def step(self):
        if self.done < self.engines[0].STAGES:
            for e in self.engines:
                e.stage(self.done)
            self.done += 1

    def finish(self):
        while self.done < self.engines[0].STAGES:
            self.step()


def ctx_gathers(place, copies, shards, fulls):
    return [
        CtxGather(place, copies, src, full, lo, rows, big)
        for src, full in zip(shards, fulls)
        for lo, rows, big in halves(src.shape[0])
    ]


def ctx_scatters(place, copies, srcs, outs, bufs):
    engines = []
    for k, (src, out) in enumerate(zip(srcs, outs)):
        for h, (lo, rows, big) in enumerate(halves(src.shape[3])):
            mine = bufs[(2 * k + h) * 7 : (2 * k + h + 1) * 7]
            engines.append(CtxScatter(place, copies, src, out, mine, lo, rows, big))
    return engines


def attend_kernel(n, *refs):
    (q, kv), shards, (attn, lse), fulls = refs[:2], refs[2 : 2 + n], refs[2 + n : 4 + n], refs[4 + n : 4 + 2 * n]
    scratch, (send, recv) = refs[4 + 2 * n : 7 + 2 * n], refs[-2:]
    place = Place()
    greet(place.ctx_peers())
    copies = Copies(send, recv)
    stages = Stages(ctx_gathers(place, copies, shards, fulls))
    stages.step()
    ctx = lax.axis_index("ctx")
    for seq in range(4):
        attend_seq(seq, ctx, q, kv, attn, lse, scratch, stages.step)
    stages.finish()


def attend(cid, q, kv, shards):
    n = len(shards)
    return pl.pallas_call(
        partial(attend_kernel, n),
        out_shape=[jax.ShapeDtypeStruct((512, 512), BF16), jax.ShapeDtypeStruct((8, 512), F32)]
        + [jax.ShapeDtypeStruct((4, 4, 2) + a.shape, a.dtype) for a in shards],
        in_specs=[VMEM] * 2 + [ANY] * n,
        out_specs=[VMEM] * 2 + [ANY] * n,
        scratch_shapes=attend_scratch() + sems(n * 2 * CtxGather.COPIES),
        compiler_params=params(cid),
        name="attend",
    )(q, kv, *shards)


def attend_back_kernel(n, *refs):
    q, kv, grad, attn, lse, tables, part, hidden = refs[:8]
    srcs, (grad_lin, grad_kv, out), outs = refs[8 : 8 + n], refs[8 + n : 11 + n], refs[11 + n : 11 + 2 * n]
    refs = refs[11 + 2 * n :]
    scratch, relay, bufs, (send, recv) = refs[:4], refs[4:7], refs[7:-2], refs[-2:]
    place = Place()
    greet(place.ctx_peers() + place.shard_peers())
    copies = Copies(send, recv)
    stages = Stages(ctx_scatters(place, copies, srcs, outs, bufs))
    stages.step()
    rows = ShardScatter(place, copies, part, relay, 1)
    rows.begin()
    ctx = lax.axis_index("ctx")
    for seq in range(4):
        attend_back_seq(seq, ctx, q, kv, grad, attn, lse, tables, grad_lin, grad_kv, scratch, stages.step)
        if seq == 0:
            rows.relay_on(0)
    out[...] = (hidden[...] + rows.total(0)).astype(BF16)
    stages.finish()


def attend_back(cid, q, kv, grad, attn, lse, tables, part, hidden, srcs):
    n = len(srcs)
    scratch = []
    for a in srcs:
        scratch += CtxScatter.scratch(a.shape[3] // 2, a.shape[4]) * 2
    return pl.pallas_call(
        partial(attend_back_kernel, n),
        out_shape=[
            jax.ShapeDtypeStruct((512, 512), BF16),
            jax.ShapeDtypeStruct(kv.shape, BF16),
            jax.ShapeDtypeStruct(hidden.shape, BF16),
        ]
        + [jax.ShapeDtypeStruct(a.shape[3:], F32) for a in srcs],
        in_specs=[VMEM] * (8 + n),
        out_specs=[VMEM] * (3 + n),
        scratch_shapes=attend_back_scratch()
        + ShardScatter.scratch(*hidden.shape)
        + scratch
        + sems(n * 2 * CtxScatter.COPIES + 3),
        compiler_params=params(cid),
        name="attend_back",
    )(q, kv, grad, attn, lse, tables, part, hidden, *srcs)


def rope_tables(positions):
    freqs = 10000.0 ** (-jnp.arange(HD // 2, dtype=F32) * 2.0 / HD)
    angles = positions[:, None] * freqs[None]
    cosine, sine = jnp.cos(angles), jnp.sin(angles)
    one, zero = jnp.ones_like(cosine), jnp.zeros_like(cosine)
    return jnp.stack(
        [
            jnp.concatenate([cosine] * 4, -1),
            jnp.concatenate([sine] * 4, -1),
            jnp.concatenate([cosine, cosine, one, one], -1),
            jnp.concatenate([sine, sine, zero, zero], -1),
        ]
    )


def unrotate(grads, cosine, sine):
    middle = HD // 2
    shifted = grads * sine
    return grads * cosine + jnp.concatenate([shifted[:, middle:], -shifted[:, :middle]], -1)


def dot(a, b, dims):
    return lax.dot_general(a, b, (dims, ((), ())), preferred_element_type=F32)


def per_device(
    inputs, cotangent, norm_attn, w_query, w_key, w_value, w_out, norm_mlp, w_gate, w_up, w_down
):
    width = inputs.shape[-1]
    half_len = inputs.shape[2]
    tokens = 2 * half_len
    ctx_count = lax.axis_size("ctx")
    ctx_index = lax.axis_index("ctx")
    group = lax.axis_size("wshard")
    length = tokens * ctx_count
    q_width = w_query.shape[1]
    x = inputs.reshape(tokens, width)
    cot = cotangent.reshape(tokens, width)
    rows_local = jnp.arange(tokens)
    positions = jnp.where(
        rows_local < half_len,
        ctx_index * half_len + rows_local,
        length - (ctx_index + 1) * half_len + (rows_local - half_len),
    ).astype(F32)
    tables = rope_tables(positions)

    resid = x.astype(F32)
    factor1 = lax.rsqrt(jnp.mean(resid * resid, -1, keepdims=True) + EPS)
    normed1 = (resid * factor1 * norm_attn.astype(F32)).astype(BF16)
    w_qkv = jnp.concatenate([w_query, w_key, w_value], 1)
    w_qkv, normed_all, cot_all = gather(0, "gather_in", [w_qkv], [normed1, cot])
    w_qkv = w_qkv.reshape(width, -1)
    normed_all = normed_all.reshape(group * tokens, width)
    cot_all = cot_all.reshape(group * tokens, width)
    q, kv = project(normed_all, w_qkv, tables)
    (kv_all,) = gather(1, "gather_kv", [kv], [])
    kv_all = kv_all.reshape(ctx_count, group * tokens, 2 * HD)
    attn, lse, w_out_t, w_gate, w_up, w_down_t = attend(2, q, kv_all, [w_out.T, w_gate, w_up, w_down.T])
    w_out_t, w_gate, w_up, w_down_t = (a.reshape(width, a.shape[-1]) for a in (w_out_t, w_gate, w_up, w_down_t))

    part = dot(attn, w_out_t, ((1,), (1,))).astype(BF16).reshape(group, tokens, width)
    hidden1, normed2_all = out_and_norm(3, part, x, norm_mlp)
    normed2_all = normed2_all.reshape(group * tokens, width)
    gate_pre = dot(normed2_all, w_gate, ((1,), (0,)))
    up_pre = dot(normed2_all, w_up, ((1,), (0,)))
    sigmoid_gate = jax.nn.sigmoid(gate_pre)
    silu_gate = gate_pre * sigmoid_gate
    active = (silu_gate * up_pre).astype(BF16)
    result_part = dot(active, w_down_t, ((1,), (1,))).astype(BF16).reshape(group, tokens, width)
    grad_active = dot(cot_all, w_down_t, ((1,), (0,)))
    grad_gate_pre = (grad_active * up_pre * sigmoid_gate * (1.0 + gate_pre * (1.0 - sigmoid_gate))).astype(BF16)
    grad_up_pre = (grad_active * silu_gate).astype(BF16)
    part2 = (dot(grad_gate_pre, w_gate, ((1,), (1,))) + dot(grad_up_pre, w_up, ((1,), (1,)))).astype(BF16)
    grad_hidden1, branch_all, gain2_part = norm_back_and_spread(
        4, part2.reshape(group, tokens, width), hidden1, norm_mlp, cot
    )
    branch_all = branch_all.reshape(group * tokens, width)

    def blocks(a):
        return a.astype(BF16).reshape(4, 4, 2, -1, a.shape[-1])

    g_down_t = blocks(dot(cot_all, active, ((0,), (0,))))
    g_gate = blocks(dot(normed2_all, grad_gate_pre, ((0,), (0,))))
    g_up = blocks(dot(normed2_all, grad_up_pre, ((0,), (0,))))
    grad_mixed = dot(branch_all, w_out_t, ((1,), (0,))).astype(BF16)
    grad_qlin, grad_kv, outputs, g_gate, g_up, g_down_t = attend_back(
        5, q, kv_all, grad_mixed, attn, lse, tables, result_part, hidden1, [g_gate, g_up, g_down_t]
    )
    (grad_kv,) = scatter(6, "scatter_kv", [grad_kv.reshape(4, 4, 2, group * tokens, 2 * HD)])
    grad_klin = unrotate(
        grad_kv[:, :HD], jnp.tile(tables[0, :, :HD], (group, 1)), jnp.tile(tables[1, :, :HD], (group, 1))
    )
    grad_lin = jnp.concatenate([grad_qlin, grad_klin.astype(BF16), grad_kv[:, HD:].astype(BF16)], 1)
    g_qkv = blocks(dot(normed_all, grad_lin, ((0,), (0,))))
    g_out_t = blocks(dot(branch_all, attn, ((0,), (0,))))
    part3 = dot(grad_lin, w_qkv, ((1,), (1,))).astype(BF16).reshape(group, tokens, width)
    g_qkv, g_out_t, grad_inputs, gains = tail(
        7, [g_qkv, g_out_t], part3, x, norm_attn, grad_hidden1, gain2_part
    )
    start = (ctx_index % 2) * 64 + lax.axis_index("wshard") * 16
    gains = lax.dynamic_slice_in_dim(gains, start, 16, axis=1)
    return (
        outputs.reshape(inputs.shape),
        grad_inputs.reshape(inputs.shape),
        gains[0],
        g_qkv[:, :q_width],
        g_qkv[:, q_width : q_width + HD],
        g_qkv[:, q_width + HD :],
        g_out_t.T,
        gains[1],
        g_gate,
        g_up,
        g_down_t.T,
    )


def solution(mesh):
    return jax.shard_map(
        per_device,
        mesh=mesh,
        in_specs=(
            P("wshard", None, "ctx", None),
            P("wshard", None, "ctx", None),
            P(),
            P("ctx", "wshard"),
            P("ctx", "wshard"),
            P("ctx", "wshard"),
            P("wshard", "ctx"),
            P(),
            P("ctx", "wshard"),
            P("ctx", "wshard"),
            P("wshard", "ctx"),
        ),
        out_specs=(
            P("wshard", None, "ctx", None),
            P("wshard", None, "ctx", None),
            P(("ctx", "wshard")),
            P("ctx", "wshard"),
            P("ctx", "wshard"),
            P("ctx", "wshard"),
            P("wshard", "ctx"),
            P(("ctx", "wshard")),
            P("ctx", "wshard"),
            P("ctx", "wshard"),
            P("wshard", "ctx"),
        ),
        check_vma=False,
    )
```

```python
from functools import partial

import jax
import jax.numpy as jnp
from jax import lax
from jax.experimental import pallas as pl
from jax.experimental.pallas import tpu as pltpu
from jax.sharding import PartitionSpec as P

MESH = pl.DeviceIdType.MESH
HD = 64
EPS = 1e-05
NEG = -1e30
F32 = jnp.float32
BF16 = jnp.bfloat16
VMEM_LIMIT = 63 * 2**20
ANY = pl.BlockSpec(memory_space=pl.ANY)
VMEM = pl.BlockSpec(memory_space=pltpu.VMEM)


class Place:
    def __init__(self):
        ctx, shard = lax.axis_index("ctx"), lax.axis_index("wshard")
        self.x, self.z, self.y = ctx // 8, (ctx // 2) % 4, ctx % 2
        self.yl, self.co = shard // 2, shard % 2

    def at(self, x=None, z=None, y=None, yl=None, co=None):
        x, z, y = (self.x if x is None else x), (self.z if z is None else z), (self.y if y is None else y)
        yl, co = (self.yl if yl is None else yl), (self.co if co is None else co)
        return (x * 8 + z * 2 + y, yl * 2 + co)

    def step(self, axis, by):
        return self.at(**{axis: (getattr(self, axis) + by) % 4})

    def pair(self, axis):
        return self.at(**{axis: 1 - getattr(self, axis)})

    def ctx_peers(self):
        return [self.step("x", 1), self.step("x", 3), self.step("z", 1), self.step("z", 3), self.pair("y")]

    def shard_peers(self):
        return [self.pair("co"), self.pair("yl")]

    def far_peers(self):
        return [self.step("x", 2), self.step("z", 2)]


def greet(peers):
    barrier = pltpu.get_barrier_semaphore()
    for device in peers:
        pl.semaphore_signal(barrier, inc=1, device_id=device, device_id_type=MESH)
    pl.semaphore_wait(barrier, len(peers))


class Copies:
    def __init__(self, send, recv):
        self.send, self.recv, self.used = send, recv, 0

    def start(self, src, dst, device):
        k = self.used
        self.used += 1
        copy = pltpu.make_async_remote_copy(
            src_ref=src, dst_ref=dst, send_sem=self.send.at[k], recv_sem=self.recv.at[k],
            device_id=device, device_id_type=MESH,
        )
        copy.start()
        return copy

    def local(self, src, dst):
        k = self.used
        self.used += 1
        copy = pltpu.make_async_copy(src, dst, self.send.at[k])
        copy.start()
        return copy


def wait_all(copies):
    for copy in copies:
        copy.wait()


class CtxGather:
    COPIES = 10
    STAGES = 6

    def __init__(self, place, copies, shard, full, lo, n, big):
        self.p, self.c, self.shard, self.full = place, copies, shard, full
        self.lo, self.n, self.big, self.small = lo, n, big, ("z" if big == "x" else "x")
        self.live = []

    def block(self, o, i, y):
        x, z = (o, i) if self.big == "x" else (i, o)
        return self.full.at[x, z, y, pl.ds(self.lo, self.n)]

    def send(self, part, axis, by):
        dev = self.p.pair("y") if axis == "y" else self.p.step(axis, by)
        self.live.append(self.c.start(part, part, dev))

    def stage(self, s):
        p = self.p
        o, i, y = getattr(p, self.big), getattr(p, self.small), p.y
        wait_all(self.live)
        self.live = []
        every, both = pl.ds(0, 4), pl.ds(0, 2)
        if s == 0 and self.shard is None:
            self.send(self.block(o, i, y), "y", 0)
        elif s == 0:
            own = self.shard.at[pl.ds(self.lo, self.n)]
            self.live.append(self.c.start(own, self.block(o, i, y), p.pair("y")))
            self.live.append(self.c.local(own, self.block(o, i, y)))
        elif s == 1:
            self.send(self.block(o, i, both), self.small, 1)
            self.send(self.block(o, i, both), self.small, 3)
        elif s == 2:
            self.send(self.block(o, (i + 3) % 4, 0), self.small, 1)
            self.send(self.block(o, (i + 1) % 4, 1), self.small, 3)
        elif s == 3:
            self.send(self.block(o, every, both), self.big, 1)
            self.send(self.block(o, every, both), self.big, 3)
        elif s == 4:
            self.send(self.block((o + 3) % 4, pl.ds(0, 2), both), self.big, 1)
            self.send(self.block((o + 1) % 4, pl.ds(2, 2), both), self.big, 3)


class CtxScatter:
    COPIES = 16
    STAGES = 7

    @staticmethod
    def scratch(n, width, staged=False):
        shapes = [(2, 2, 2), (4, 2), (4, 2), (2,), (2,), (2,), ()]
        if staged:
            shapes += [(4, 2), (2, 2), (2, 2)]
        return [pltpu.VMEM(shape + (n, width), BF16) for shape in shapes]

    def __init__(self, place, copies, src, out, bufs, lo, n, big):
        self.p, self.c, self.src, self.out = place, copies, src, out
        self.far, self.pos, self.neg, self.far2, self.pos2, self.neg2, self.last = bufs[:7]
        self.staged = bufs[7:]
        self.lo, self.n, self.big, self.small = lo, n, big, ("z" if big == "x" else "x")
        self.first, self.live = [], []

    def part(self, o, i):
        x, z = (o, i) if self.big == "x" else (i, o)
        return self.src.at[x, z, pl.ds(0, 2), pl.ds(self.lo, self.n)]

    def load(self, o, i, y, which):
        if self.staged:
            return self.staged[which][i % 2 if which else i, y].astype(F32)
        x, z = (o, i) if self.big == "x" else (i, o)
        return self.src[x, z, y, pl.ds(self.lo, self.n), :].astype(F32)

    def send(self, src, dst, axis, by):
        dev = self.p.pair("y") if axis == "y" else self.p.step(axis, by)
        copy = self.c.start(src, dst, dev)
        self.live.append(copy)
        return copy

    def stage(self, s):
        p, big, small = self.p, self.big, self.small
        o, i, y = getattr(p, big), getattr(p, small), p.y
        up, down, across = (o + 1) % 4, (o + 3) % 4, (o + 2) % 4
        iup, idown, iacross = (i + 1) % 4, (i + 3) % 4, (i + 2) % 4
        low, high = pl.ds(0, 2), pl.ds(2, 2)
        if s == 2:
            wait_all(self.first)
        elif s > 2:
            wait_all(self.live)
            self.live = []
        if s == 0:
            for src, dst, by in (
                (self.part(across, low), self.far.at[0], 1), (self.part(across, high), self.far.at[1], 3)
            ):
                self.first.append(self.c.start(src, dst, p.step(big, by)))
            if self.staged:
                own, above, below = self.staged
                self.first.append(self.c.local(self.part(up, low), above))
                self.first.append(self.c.local(self.part(down, high), below))
        elif s == 1:
            self.send(self.part(up, high), self.pos.at[high], big, 1)
            self.send(self.part(down, low), self.neg.at[low], big, 3)
            if self.staged:
                self.live.append(self.c.local(self.part(o, pl.ds(0, 4)), self.staged[0]))
        elif s == 2:

            def fold(k, _):
                b, q = k // 2, k % 2
                self.far[0, b, q] = (self.far[0, b, q].astype(F32) + self.load(up, b, q, 1)).astype(BF16)
                self.far[1, b, q] = (self.far[1, b, q].astype(F32) + self.load(down, b + 2, q, 2)).astype(BF16)
                return 0

            lax.fori_loop(0, 4, fold, 0)
            self.send(self.far.at[0], self.pos.at[low], big, 1)
            self.send(self.far.at[1], self.neg.at[high], big, 3)
        elif s == 3:

            def total(k, _):
                b, q = k // 2, k % 2
                here = self.load(o, b, q, 0) + self.pos[b, q].astype(F32) + self.neg[b, q].astype(F32)
                self.pos[b, q] = here.astype(BF16)
                return 0

            lax.fori_loop(0, 8, total, 0)
            self.first = [
                self.c.start(self.pos.at[iacross, 0], self.far2.at[0], p.step(small, 1)),
                self.c.start(self.pos.at[iacross, 1], self.far2.at[1], p.step(small, 3)),
            ]
            self.send(self.pos.at[iup, 1], self.pos2.at[1], small, 1)
            self.send(self.pos.at[idown, 0], self.neg2.at[0], small, 3)
        elif s == 4:
            wait_all(self.first)
            self.far2[0] = (self.far2[0].astype(F32) + self.pos[iup, 0].astype(F32)).astype(BF16)
            self.far2[1] = (self.far2[1].astype(F32) + self.pos[idown, 1].astype(F32)).astype(BF16)
            self.send(self.far2.at[0], self.pos2.at[0], small, 1)
            self.send(self.far2.at[1], self.neg2.at[1], small, 3)
        elif s == 5:
            for q in range(2):
                here = self.pos[i, q].astype(F32) + self.pos2[q].astype(F32) + self.neg2[q].astype(F32)
                self.pos2[q] = here.astype(BF16)
            self.send(self.pos2.at[1 - y], self.last, "y", 0)
        elif s == 6:
            total = self.pos2[y].astype(F32) + self.last[...].astype(F32)
            self.out[pl.ds(self.lo, self.n), :] = total.astype(self.out.dtype)


class ShardGather:
    def __init__(self, place, copies, full, chunks):
        self.p, self.c, self.full, self.chunks = place, copies, full, chunks
        self.rows = full.shape[1] // chunks
        self.me, self.over = place.yl * 2 + place.co, (1 - place.yl) * 2 + place.co
        self.far, self.near = [], []

    COPIES = 3

    def part(self, who, k):
        return self.full.at[who, pl.ds(k * self.rows, self.rows)]

    def send(self, k, src=None):
        src = self.part(self.me, k) if src is None else src
        self.far.append(self.c.start(src, self.part(self.me, k), self.p.pair("yl")))
        self.near.append(self.c.start(src, self.part(self.me, k), self.p.pair("co")))

    def forward(self, k):
        self.far[k].wait()
        self.near.append(self.c.start(self.part(self.over, k), self.part(self.over, k), self.p.pair("co")))

    def finish(self):
        wait_all(self.near)


class ShardScatter:
    COPIES = 3

    @staticmethod
    def scratch(rows, width):
        return [pltpu.VMEM((rows, width), BF16)] * 3

    def __init__(self, place, copies, part, bufs, chunks):
        self.p, self.c, self.part, self.chunks = place, copies, part, chunks
        self.relay, self.near, self.over = bufs
        self.rows = part.shape[1] // chunks
        self.first, self.second, self.third = [], [], []

    def at(self, k):
        return pl.ds(k * self.rows, self.rows)

    def begin(self):
        self.begin_far()
        self.begin_near()

    def begin_far(self):
        p = self.p
        for k in range(self.chunks):
            src = self.part.at[(1 - p.yl) * 2 + 1 - p.co, self.at(k)]
            self.first.append(self.c.start(src, self.relay.at[self.at(k)], p.pair("co")))

    def begin_near(self):
        p = self.p
        for k in range(self.chunks):
            src = self.part.at[p.yl * 2 + 1 - p.co, self.at(k)]
            self.second.append(self.c.start(src, self.near.at[self.at(k)], p.pair("co")))

    def relay_on(self, k):
        p = self.p
        self.first[k].wait()
        here = self.part[(1 - p.yl) * 2 + p.co, self.at(k), :].astype(F32)
        self.relay[self.at(k), :] = (self.relay[self.at(k), :].astype(F32) + here).astype(BF16)
        self.third.append(self.c.start(self.relay.at[self.at(k)], self.over.at[self.at(k)], p.pair("yl")))

    def total(self, k):
        p = self.p
        self.second[k].wait()
        self.third[k].wait()
        here = self.part[p.yl * 2 + p.co, self.at(k), :].astype(F32)
        return here + self.near[self.at(k), :].astype(F32) + self.over[self.at(k), :].astype(F32)


class GainScatter:
    COPIES = 9
    STAGES = 6

    @staticmethod
    def scratch():
        return [
            pltpu.VMEM((8, 2048), F32),
            pltpu.VMEM((3, 8, 512), F32),
            pltpu.VMEM((8, 512), F32),
            pltpu.VMEM((3, 8, 128), F32),
            pltpu.VMEM((3, 8, 128), F32),
            pltpu.VMEM((3, 8, 128), F32),
        ]

    def __init__(self, place, copies, out, bufs):
        self.p, self.c, self.out = place, copies, out
        self.vec, self.xs, self.mid, self.zs, self.own, self.rest = bufs
        self.live = []

    def stage(self, s):
        p = self.p
        wait_all(self.live)
        self.live = []
        if s == 0:
            for by in (1, 2, 3):
                cols = pl.ds(pl.multiple_of(((p.x + by) % 4) * 512, 512), 512)
                self.live.append(self.c.start(self.vec.at[:, cols], self.xs.at[by - 1], p.step("x", by)))
        elif s == 1:
            cols = pl.ds(pl.multiple_of(p.x * 512, 512), 512)
            self.mid[...] = self.vec[:, cols] + self.xs[0] + self.xs[1] + self.xs[2]
            for by in (1, 2, 3):
                cols = pl.ds(pl.multiple_of(((p.z + by) % 4) * 128, 128), 128)
                self.live.append(self.c.start(self.mid.at[:, cols], self.zs.at[by - 1], p.step("z", by)))
        elif s == 2:
            cols = pl.ds(pl.multiple_of(p.z * 128, 128), 128)
            self.own[0] = self.mid[:, cols] + self.zs[0] + self.zs[1] + self.zs[2]
            self.live.append(self.c.start(self.own.at[0], self.rest.at[0], p.pair("y")))
        elif s == 3:
            self.own[1] = self.own[0] + self.rest[0]
            self.live.append(self.c.start(self.own.at[1], self.rest.at[1], p.pair("co")))
        elif s == 4:
            self.own[2] = self.own[1] + self.rest[1]
            self.live.append(self.c.start(self.own.at[2], self.rest.at[2], p.pair("yl")))
        elif s == 5:
            self.out[...] = self.own[2] + self.rest[2]


def sems(n):
    return [pltpu.SemaphoreType.DMA((n,)), pltpu.SemaphoreType.DMA((n,))]


def params(cid):
    return pltpu.CompilerParams(collective_id=cid, has_side_effects=True, vmem_limit_bytes=VMEM_LIMIT)


def halves(rows):
    return ((0, rows // 2, "x"), (rows // 2, rows // 2, "z"))


CHUNKS = 4


def norm_back_rows(grad, resid, gain):
    factor = lax.rsqrt(jnp.mean(resid * resid, -1, keepdims=True) + EPS)
    weighted = grad * gain
    per_gain = grad * resid * factor
    back = factor * weighted - resid * (factor * factor * factor) * jnp.mean(weighted * resid, -1, keepdims=True)
    return back, per_gain


def eight(rows):
    return jnp.sum(rows.reshape(rows.shape[0] // 8, 8, rows.shape[1]), 0)


def tail_kernel(n, *refs):
    grads, (part, x, gain, grad_hidden, gain_other) = refs[:n], refs[n : n + 5]
    refs = refs[n + 5 :]
    outs, (grad_in, gains), refs = refs[:n], refs[n : n + 2], refs[n + 2 :]
    bufs, (a, b, c), gain_bufs, (acc, send, recv) = refs[: 14 * n], refs[14 * n : 14 * n + 3], refs[14 * n + 3 : -3], refs[-3:]
    place = Place()
    greet(place.ctx_peers() + place.shard_peers() + place.far_peers())
    copies = Copies(send, recv)
    first = ShardScatter(place, copies, part, (a, b, c), CHUNKS)
    first.begin()
    engines = []
    for k, (src, out) in enumerate(zip(grads, outs)):
        for h, (lo, rows, big) in enumerate(halves(src.shape[3])):
            mine = bufs[(2 * k + h) * 7 : (2 * k + h + 1) * 7]
            engines.append(CtxScatter(place, copies, src, out, mine, lo, rows, big))
    for e in engines:
        e.stage(0)
        e.stage(1)
    for k in range(CHUNKS):
        first.relay_on(k)
    for e in engines:
        e.stage(2)
    for k in range(CHUNKS):
        rows = first.at(k)
        back, per_gain = norm_back_rows(first.total(k), x[rows, :].astype(F32), gain[...].astype(F32))
        grad_in[rows, :] = (grad_hidden[rows, :] + back).astype(BF16)
        acc[...] = eight(per_gain) if k == 0 else acc[...] + eight(per_gain)
    gain_sum = GainScatter(place, copies, gains, gain_bufs)
    row = lax.broadcasted_iota(jnp.int32, acc.shape, 0)
    one = jnp.sum(acc[...], 0, keepdims=True)
    two = jnp.sum(gain_other[...], 0, keepdims=True)
    gain_sum.vec[...] = jnp.where(row == 0, one, jnp.where(row == 1, two, 0.0))
    gain_sum.stage(0)
    for s in range(3, CtxScatter.STAGES):
        for e in engines:
            e.stage(s)
        gain_sum.stage(s - 2)
    gain_sum.stage(5)


def tail(cid, grads, part, x, gain, grad_hidden, gain_other):
    tokens, width = x.shape
    n = len(grads)
    scratch = []
    for g in grads:
        scratch += CtxScatter.scratch(g.shape[3] // 2, g.shape[4]) * 2
    return pl.pallas_call(
        partial(tail_kernel, n),
        out_shape=[jax.ShapeDtypeStruct(g.shape[3:], F32) for g in grads]
        + [jax.ShapeDtypeStruct((tokens, width), BF16), jax.ShapeDtypeStruct((8, 128), F32)],
        in_specs=[VMEM] * (n + 5),
        out_specs=[VMEM] * (n + 2),
        scratch_shapes=scratch
        + ShardScatter.scratch(tokens, width)
        + GainScatter.scratch()
        + [pltpu.VMEM((8, width), F32)]
        + sems(n * 2 * CtxScatter.COPIES + 3 * CHUNKS + GainScatter.COPIES),
        compiler_params=params(cid),
        name="tail",
    )(*grads, part, x, gain.reshape(1, width), grad_hidden, gain_other)


KEYS = 256
KB = 4


def lane_iota(rows):
    return lax.broadcasted_iota(jnp.int32, (rows, 128), 1)


def rotate_tile(u, cosine, sine):
    low = lane_iota(u.shape[0]) % HD < HD // 2
    turned = jnp.where(low, -pltpu.roll(u, 128 - HD // 2, 1), pltpu.roll(u, HD // 2, 1))
    return u * cosine + turned * sine


def unrotate_tile(w, cosine, sine):
    low = lane_iota(w.shape[0]) % HD < HD // 2
    s = w * sine
    return w * cosine + jnp.where(low, pltpu.roll(s, 128 - HD // 2, 1), -pltpu.roll(s, HD // 2, 1))


def project_rows(rows, w_qkv, tables):
    lin = jnp.dot(rows, w_qkv, preferred_element_type=F32)
    tiles = []
    for hp in range(4):
        tile = lin[:, hp * 128 : (hp + 1) * 128]
        tiles.append((rotate_tile(tile, tables[0], tables[1])).astype(BF16) * jnp.asarray(HD**-0.5, BF16))
    kv = rotate_tile(lin[:, 512:640], tables[2], tables[3]).astype(BF16)
    return tiles, kv


def head_rows(ref, start, keep_low):
    low = lane_iota(64) < HD
    keep = low if keep_low else ~low
    pieces = []
    for hp in range(4):
        tile = ref[pl.ds(start, 64), hp * 128 : (hp + 1) * 128].astype(F32)
        turned = pltpu.roll(tile, HD, 1)
        even, odd = (tile, turned) if keep_low else (turned, tile)
        pieces += [jnp.where(keep, even, 0.0), jnp.where(keep, odd, 0.0)]
    return pieces


def key_chunk(kv, seq, chunk, half):
    start = pl.multiple_of(seq * 128 + half * 64, 64)
    z = pl.ds((chunk % 2) * 2, 2)
    return kv[chunk // 2, z, :, pl.ds(start, 64), :].reshape(KEYS, 128)


def diagonal(block, here):
    key = lax.broadcasted_iota(jnp.int32, (KEYS, 512), 0)
    query = lax.broadcasted_iota(jnp.int32, (KEYS, 512), 1) % 64
    ahead = key // 64 - here
    return key % 64 - query <= (-ahead if block == 0 else ahead) * 64


def pick(u, own_chunk):
    late = u - 8
    block = jnp.where(u < 8, 1, jnp.where(late >= own_chunk, 1, 0))
    half = jnp.where(u < 8, 0, block)
    chunk = jnp.where(u < 8, u, late + half)
    return block, chunk, half


def nt(a, b):
    return lax.dot_general(a, b, (((1,), (1,)), ((), ())), preferred_element_type=F32)


def tn(a, b):
    return lax.dot_general(a, b, (((0,), (0,)), ((), ())), preferred_element_type=F32)


def attend_seq(seq, ctx, q, kv, attn, lse, scratch, hook):
    qe, top, acc = scratch
    low = lane_iota(64) < HD
    ones_low = lane_iota(KEYS) < HD
    own_chunk, here = ctx // KB, ctx % KB

    def with_ones(keys):
        return jnp.where(ones_low, jnp.ones_like(keys), keys)

    for b in range(2):
        for h, piece in enumerate(head_rows(q, seq * 128 + b * 64, True)):
            qe[b, h * 64 : (h + 1) * 64, :] = piece.astype(BF16)
    for b in range(2):
        keys = key_chunk(kv, seq, own_chunk, b)
        scores = jnp.where(diagonal(b, here), nt(keys, qe[b]), NEG)
        m = jnp.max(scores, 0, keepdims=True)
        p = jnp.exp(scores - m).astype(BF16)
        top[b] = m
        acc[b] = tn(with_ones(keys), p)

    def step(u, _):
        b, chunk, half = pick(u, own_chunk)
        keys = key_chunk(kv, seq, chunk, half)
        scores = nt(keys, qe[b])
        before = top[b]
        m = jnp.maximum(before, jnp.max(scores, 0, keepdims=True))
        p = jnp.exp(scores - m).astype(BF16)
        top[b] = m
        acc[b] = acc[b] * jnp.exp(before - m) + tn(with_ones(keys), p)
        return 0

    for k in range(3):
        lax.fori_loop(5 * k, 5 * k + 5, step, 0, unroll=True)
        hook()
    for b in range(2):
        here_acc = acc[b]
        total = here_acc[0:1, :]
        lse[pl.ds(seq * 2 + b, 1), :] = top[b] + jnp.log(total)
        out = (here_acc * (1.0 / total)).T
        for hp in range(4):
            even, odd = out[hp * 128 : hp * 128 + 64, :], out[hp * 128 + 64 : hp * 128 + 128, :]
            tile = jnp.where(low, pltpu.roll(even, HD, 1), odd)
            attn[pl.ds(seq * 128 + b * 64, 64), hp * 128 : (hp + 1) * 128] = tile.astype(BF16)


def attend_scratch():
    return [pltpu.VMEM((2, 512, 128), BF16), pltpu.VMEM((2, 1, 512), F32), pltpu.VMEM((2, 128, 512), F32)]


def attend_back_seq(seq, ctx, q, kv, grad, attn, lse, tables, grad_lin, grad_kv, scratch, hook):
    qd, delta, dq, dkv = scratch
    low = lane_iota(64) < HD
    own_chunk, here = ctx // KB, ctx % KB
    for b in range(2):
        start = seq * 128 + b * 64
        q_rows, g_rows, o_rows = (
            head_rows(q, start, True), head_rows(grad, start, False), head_rows(attn, start, False)
        )
        for h in range(8):
            qd[b, h * 64 : (h + 1) * 64, :] = q_rows[h].astype(BF16)
            qd[b, 512 + h * 64 : 512 + (h + 1) * 64, :] = g_rows[h].astype(BF16)
        products = jnp.concatenate([g * o for g, o in zip(g_rows, o_rows)], 0)
        delta[b] = jnp.sum(products.T, 0, keepdims=True)

    def grads(b, keys, allowed):
        both = nt(keys, qd[b])
        p = jnp.exp(both[:, :512] - lse[pl.ds(seq * 2 + b, 1), :])
        if allowed is not None:
            p = jnp.where(allowed, p, 0.0)
        ds = (p * (both[:, 512:] - delta[b])).astype(BF16)
        joined = jnp.concatenate([ds, p.astype(BF16)], 1)
        return tn(keys, ds), jnp.dot(joined, qd[b], preferred_element_type=F32)

    dkv[...] = jnp.zeros_like(dkv)

    def add_keys(chunk, half, value):
        start = pl.multiple_of(half * 64, 64)
        dkv[pl.ds(chunk * KB, KB), pl.ds(start, 64), :] += value.reshape(KB, 64, 128)

    for b in range(2):
        dq_part, dkv_part = grads(b, key_chunk(kv, seq, own_chunk, b), diagonal(b, here))
        dq[b] = dq_part
        add_keys(own_chunk, b, dkv_part)

    def step(u, _):
        b, chunk, half = pick(u, own_chunk)
        dq_part, dkv_part = grads(b, key_chunk(kv, seq, chunk, half), None)
        dq[b] += dq_part
        add_keys(chunk, half, dkv_part)
        return 0

    for k in range(3):
        lax.fori_loop(5 * k, 5 * k + 5, step, 0, unroll=True)
        hook()
    for b in range(2):
        out = (dq[b] * HD**-0.5).T
        cosine, sine = tables[0, b * 64 : (b + 1) * 64, :], tables[1, b * 64 : (b + 1) * 64, :]
        for hp in range(4):
            even, odd = out[hp * 128 : hp * 128 + 64, :], out[hp * 128 + 64 : hp * 128 + 128, :]
            tile = jnp.where(low, even, pltpu.roll(odd, HD, 1))
            tile = unrotate_tile(tile, cosine, sine)
            grad_lin[pl.ds(seq * 128 + b * 64, 64), hp * 128 : (hp + 1) * 128] = tile.astype(BF16)
    grad_kv[...] = dkv[...].reshape(4, 4, 2, 128, 128).astype(BF16)


def attend_back_scratch():
    return [
        pltpu.VMEM((2, 1024, 128), BF16),
        pltpu.VMEM((2, 1, 512), F32),
        pltpu.VMEM((2, 128, 512), F32),
        pltpu.VMEM((32, 128, 128), F32),
    ]


def ctx_gathers(place, copies, shards, fulls):
    return [
        CtxGather(place, copies, src, full, lo, rows, big)
        for src, full in zip(shards, fulls)
        for lo, rows, big in halves(src.shape[0])
    ]


def ctx_scatters(place, copies, srcs, outs, bufs):
    engines = []
    for k, (src, out) in enumerate(zip(srcs, outs)):
        for h, (lo, rows, big) in enumerate(halves(src.shape[3])):
            mine = bufs[(2 * k + h) * 7 : (2 * k + h + 1) * 7]
            engines.append(CtxScatter(place, copies, src, out, mine, lo, rows, big))
    return engines


def forward_kernel(
    x, cot, gain1, gain2, tables, w_qkv_shard, w_out_shard, w_gate_shard, w_up_shard, w_down_shard,
    normed1_out, cot_all, w_qkv_out, w_out_out, w_gate, w_up, w_down, q, kv_out, attn, lse, hidden, normed2_all,
    normed1_all, w_qkv, w_out, kv_all, part, relay, near, over, qe, top, acc, send, recv,
):
    place = Place()
    greet(place.ctx_peers() + place.shard_peers())
    copies = Copies(send, recv)
    ctx = lax.axis_index("ctx")
    order = [2 * (1 - place.yl) + 1 - place.co, 2 * (1 - place.yl) + place.co]
    order += [2 * place.yl + 1 - place.co, 2 * place.yl + place.co]
    weights = ctx_gathers(place, copies, [w_qkv_shard], [w_qkv])
    later = {
        name: ctx_gathers(place, copies, [shard], [full])
        for name, shard, full in (
            ("o", w_out_shard, w_out), ("g", w_gate_shard, w_gate), ("u", w_up_shard, w_up), ("d", w_down_shard, w_down)
        )
    }
    keys = [
        CtxGather(place, copies, None, kv_all, pl.multiple_of(order[k] * 128, 128), 128, "xz"[k % 2]) for k in range(4)
    ]
    outgoing = []

    def move(*names):
        for name in names:
            stage = int(name[-1])
            engines = {"w": weights, "k": keys}.get(name[0]) or later[name[0]]
            if name[0] == "k":
                engines = [engines[int(name[1])]]
            for e in engines:
                e.stage(stage)

    move("w0")
    normed = ShardGather(place, copies, normed1_all, 1)
    rows = x[...].astype(F32)
    factor = lax.rsqrt(jnp.mean(rows * rows, -1, keepdims=True) + EPS)
    normed1_all[normed.me] = (rows * factor * gain1[...].astype(F32)).astype(BF16)
    normed.send(0)
    move("w1", "w2", "w3", "o0", "g0")
    normed.forward(0)
    move("w4", "u0", "d0", "o1", "g1")
    normed.finish()
    outgoing.append(copies.local(normed1_all, normed1_out))
    move("w5")
    outgoing.append(copies.local(w_qkv, w_qkv_out))

    def project_seq(k):
        seq = order[k]
        at = pl.ds(pl.multiple_of(seq * 128, 128), 128)
        tiles, kv = project_rows(normed1_all[seq], w_qkv[...].reshape(2048, 640), tables)
        for hp, tile in enumerate(tiles):
            q[at, hp * 128 : (hp + 1) * 128] = tile
        kv_all[place.x, place.z, place.y, at, :] = kv

    project_seq(0)
    project_seq(1)
    move("k00", "k10")
    project_seq(2)
    project_seq(3)
    move("k01", "k11", "k20", "k30", "o2", "g2", "k02", "k12", "k21", "k31", "u1", "d1", "k03", "k13", "k22", "k32")
    move("o3", "k04", "k14", "k23", "k33", "u2", "d2", "k05", "k15")
    cots = ShardGather(place, copies, cot_all, 1)
    cots.send(0, cot)
    outgoing.append(copies.local(cot, cot_all.at[cots.me]))
    plan = iter([
        ("k24", "k34", "g3", "o4"), (), ("o5",),
        (), (), ("u3",),
        (), (), ("g4",),
        (), (), ("d3",),
    ])
    rows_out = ShardScatter(place, copies, part, (relay, near, over), CHUNKS)
    for k in range(4):
        seq = order[k]
        if k == 2:
            move("k25", "k35")
            outgoing.append(copies.local(kv_all, kv_out))
            cots.forward(0)
        attend_seq(seq, ctx, q, kv_all, attn, lse, (qe, top, acc), lambda: move(*next(plan)))
        mixed = attn[pl.ds(pl.multiple_of(seq * 128, 128), 128), :]
        part[seq] = nt(mixed, w_out[...].reshape(2048, 512)).astype(BF16)
        if k == 0:
            rows_out.begin_far()
            outgoing.append(copies.local(w_out, w_out_out))
        elif k == 1:
            for c in range(CHUNKS):
                rows_out.relay_on(c)
        elif k == 2:
            rows_out.begin_near()
    spread = ShardGather(place, copies, normed2_all, CHUNKS)
    for c in range(CHUNKS):
        at = rows_out.at(c)
        here = x[at, :].astype(F32) + rows_out.total(c)
        hidden[at, :] = here
        factor = lax.rsqrt(jnp.mean(here * here, -1, keepdims=True) + EPS)
        normed2_all[spread.me, at, :] = (here * factor * gain2[...].astype(F32)).astype(BF16)
        spread.send(c)
    move("u4")
    for c in range(CHUNKS):
        spread.forward(c)
    spread.finish()
    cots.finish()
    move("g5", "d4", "u5", "d5")
    wait_all(outgoing)


def forward(cid, x, cot, gain1, gain2, tables, shards):
    tokens, width = x.shape

    def full(a):
        return (4, 4, 2) + a.shape

    shapes = [
        ((4, tokens, width), BF16), ((4, tokens, width), BF16), *((full(a), BF16) for a in shards),
        ((512, 512), BF16), ((4, 4, 2, 512, 128), BF16), ((512, 512), BF16), ((8, 512), F32),
        ((tokens, width), F32), ((4, tokens, width), BF16),
    ]
    return pl.pallas_call(
        forward_kernel,
        out_shape=[jax.ShapeDtypeStruct(*s) for s in shapes],
        in_specs=[VMEM, ANY, VMEM, VMEM, VMEM] + [ANY] * 5,
        out_specs=[ANY] * 7 + [VMEM, ANY] + [VMEM] * 4,
        scratch_shapes=[
            pltpu.VMEM((4, tokens, width), BF16),
            pltpu.VMEM(full(shards[0]), BF16),
            pltpu.VMEM(full(shards[1]), BF16),
            pltpu.VMEM((4, 4, 2, 512, 128), BF16),
            pltpu.VMEM((4, tokens, width), BF16),
            *ShardScatter.scratch(tokens, width),
            *attend_scratch(),
            *sems(14 * CtxGather.COPIES + 6 * CHUNKS + 16),
        ],
        compiler_params=params(cid),
        name="forward",
    )(x, cot, gain1.reshape(1, width), gain2.reshape(1, width), tables, *shards)


def backward_kernel(*refs):
    part, hidden, gain, cot, w_out, q, kv, attn, lse, tables, result_part, g_gate, g_up, g_down = refs[:14]
    grad_hidden, grad_gain, grad_lin, grad_kv, outputs, out_o, out_gate, out_up, out_down = refs[14:23]
    branch, grad, g_out, dkv_send, relay, near, over = refs[23:30]
    scratch, bufs, (send, recv) = refs[30:34], refs[34:-2], refs[-2:]
    place = Place()
    greet(place.ctx_peers() + place.shard_peers())
    copies = Copies(send, recv)
    ctx = lax.axis_index("ctx")
    order = [2 * place.yl + place.co, 2 * place.yl + 1 - place.co]
    order += [2 * (1 - place.yl) + place.co, 2 * (1 - place.yl) + 1 - place.co]
    taken = 0

    def take(n):
        nonlocal taken
        taken += n
        return bufs[taken - n : taken]

    engines = {}
    for name, src, out, count in (
        ("d", g_down, out_down, 10), ("g", g_gate, out_gate, 10), ("u", g_up, out_up, 10), ("o", g_out, out_o, 7)
    ):
        engines[name] = [
            CtxScatter(place, copies, src, out, take(count), lo, rows, big) for lo, rows, big in halves(64)
        ]
    for k in range(4):
        rows = pl.ds(pl.multiple_of(order[k] * 128, 128), 128)
        engines[f"k{k}"] = [
            CtxScatter(place, copies, dkv_send.at[k], grad_kv.at[rows], take(7), 0, 128, "xz"[k % 2])
        ]

    def move(*names):
        for name in names:
            for e in engines[name[:-1]]:
                e.stage(int(name[-1]))

    move("d0", "g0", "u0")
    scatter_ = ShardScatter(place, copies, part, (relay, near, over), CHUNKS)
    spread = ShardGather(place, copies, branch, CHUNKS)
    scatter_.begin()
    for c in range(CHUNKS):
        scatter_.relay_on(c)
    for c in range(CHUNKS):
        rows = scatter_.at(c)
        back, per_gain = norm_back_rows(scatter_.total(c), hidden[rows, :], gain[...].astype(F32))
        here = cot[rows, :].astype(F32) + back
        grad_hidden[rows, :] = here
        branch[spread.me, rows, :] = here.astype(BF16)
        spread.send(c)
        grad_gain[...] = eight(per_gain) if c == 0 else grad_gain[...] + eight(per_gain)
    move("d1", "g1", "u1")
    result = ShardScatter(place, copies, result_part, (relay, near, over), 1)
    plan = iter([
        (), (), ("d2",),
        ("g2",), ("u2",), ("k02",),
        ("o2",), ("k03",), ("k12",),
        ("d3",), ("k13",), ("k22", "k04"),
    ])
    for k in range(4):
        seq = order[k]
        at = pl.ds(pl.multiple_of(seq * 128, 128), 128)
        grad[at, :] = jnp.dot(branch[seq], w_out[...], preferred_element_type=F32).astype(BF16)
        attend_back_seq(
            seq, ctx, q, kv, grad, attn, lse, tables, grad_lin, dkv_send.at[k], scratch, lambda: move(*next(plan))
        )
        move(f"k{k}0", f"k{k}1")
        if k == 0:
            for c in range(CHUNKS):
                spread.forward(c)
            spread.finish()
            rows = branch[...].reshape(512, 2048)
            for j in range(8):
                block = tn(rows[:, j * 256 : (j + 1) * 256], attn[...]).astype(BF16)
                g_out[j // 2, pl.ds((j % 2) * 2, 2)] = block.reshape(2, 2, 64, 512)
            move("o0", "o1")
            result.begin()
        elif k == 1:
            result.relay_on(0)
    outputs[...] = (hidden[...] + result.total(0)).astype(BF16)
    move("g3", "k32", "k14", "k23", "u3", "d4", "k05", "o3", "g4", "k33", "k24", "k15", "d5", "u4", "k06", "o4")
    move("k34", "k25", "g5", "k16", "u5", "o5", "k35", "k26", "d6", "g6", "k36", "u6", "o6")


def backward(cid, part, hidden, gain, cot, w_out, q, kv, attn, lse, tables, result_part, ffn):
    tokens, width = hidden.shape
    ffn_width = ffn[0].shape[4]
    f32_outs = [(64, 512)] + [(64, ffn_width)] * 3
    scratch = []
    for _ in range(6):
        scratch += CtxScatter.scratch(32, ffn_width, True)
    for _ in range(2):
        scratch += CtxScatter.scratch(32, 512)
    for _ in range(4):
        scratch += CtxScatter.scratch(128, 128)
    return pl.pallas_call(
        backward_kernel,
        out_shape=[
            jax.ShapeDtypeStruct((tokens, width), F32),
            jax.ShapeDtypeStruct((8, width), F32),
            jax.ShapeDtypeStruct((512, 512), BF16),
            jax.ShapeDtypeStruct((512, 128), F32),
            jax.ShapeDtypeStruct((tokens, width), BF16),
        ]
        + [jax.ShapeDtypeStruct(shape, F32) for shape in f32_outs],
        in_specs=[VMEM] * 11 + [ANY] * 3,
        out_specs=[VMEM] * 9,
        scratch_shapes=[
            pltpu.VMEM((4, tokens, width), BF16),
            pltpu.VMEM((512, 512), BF16),
            pltpu.VMEM((4, 4, 2, 64, 512), BF16),
            pltpu.VMEM((4, 4, 4, 2, 128, 128), BF16),
            *ShardScatter.scratch(tokens, width),
            *attend_back_scratch(),
            *scratch,
            *sems(12 * CtxScatter.COPIES + 6 * CHUNKS + 3),
        ],
        compiler_params=params(cid),
        name="backward",
    )(part, hidden, gain.reshape(1, width), cot, w_out, q, kv, attn, lse, tables, result_part, *ffn)


def rope_tables(positions):
    freqs = 10000.0 ** (-jnp.arange(HD // 2, dtype=F32) * 2.0 / HD)
    angles = positions[:, None] * freqs[None]
    cosine, sine = jnp.cos(angles), jnp.sin(angles)
    one, zero = jnp.ones_like(cosine), jnp.zeros_like(cosine)
    return jnp.stack(
        [
            jnp.concatenate([cosine] * 4, -1),
            jnp.concatenate([sine] * 4, -1),
            jnp.concatenate([cosine, cosine, one, one], -1),
            jnp.concatenate([sine, sine, zero, zero], -1),
        ]
    )


def unrotate(grads, cosine, sine):
    middle = HD // 2
    shifted = grads * sine
    return grads * cosine + jnp.concatenate([shifted[:, middle:], -shifted[:, :middle]], -1)


def dot(a, b, dims):
    return lax.dot_general(a, b, (dims, ((), ())), preferred_element_type=F32)


def per_device(
    inputs, cotangent, norm_attn, w_query, w_key, w_value, w_out, norm_mlp, w_gate, w_up, w_down
):
    width = inputs.shape[-1]
    half_len = inputs.shape[2]
    tokens = 2 * half_len
    ctx_count = lax.axis_size("ctx")
    ctx_index = lax.axis_index("ctx")
    group = lax.axis_size("wshard")
    length = tokens * ctx_count
    q_width = w_query.shape[1]
    x = inputs.reshape(tokens, width)
    cot = cotangent.reshape(tokens, width)
    rows_local = jnp.arange(tokens)
    positions = jnp.where(
        rows_local < half_len,
        ctx_index * half_len + rows_local,
        length - (ctx_index + 1) * half_len + (rows_local - half_len),
    ).astype(F32)
    tables = rope_tables(positions)

    w_qkv = jnp.concatenate([w_query, w_key, w_value], 1)
    forward_results = forward(0, x, cot, norm_attn, norm_mlp, tables, [w_qkv, w_out.T, w_gate, w_up, w_down.T])
    normed_all, cot_all, w_qkv, w_out_t, w_gate, w_up, w_down_t, q, kv_all, attn, lse, hidden1, normed2_all = (
        forward_results
    )
    w_qkv, w_out_t, w_gate, w_up, w_down_t = (
        a.reshape(width, a.shape[-1]) for a in (w_qkv, w_out_t, w_gate, w_up, w_down_t)
    )
    normed_all, cot_all, normed2_all = (a.reshape(group * tokens, width) for a in (normed_all, cot_all, normed2_all))
    gate_pre = dot(normed2_all, w_gate, ((1,), (0,)))
    up_pre = dot(normed2_all, w_up, ((1,), (0,)))
    sigmoid_gate = jax.nn.sigmoid(gate_pre)
    silu_gate = gate_pre * sigmoid_gate
    active = (silu_gate * up_pre).astype(BF16)
    result_part = dot(active, w_down_t, ((1,), (1,))).astype(BF16).reshape(group, tokens, width)
    grad_active = dot(cot_all, w_down_t, ((1,), (0,)))
    grad_gate_pre = (grad_active * up_pre * sigmoid_gate * (1.0 + gate_pre * (1.0 - sigmoid_gate))).astype(BF16)
    grad_up_pre = (grad_active * silu_gate).astype(BF16)
    part2 = (dot(grad_gate_pre, w_gate, ((1,), (1,))) + dot(grad_up_pre, w_up, ((1,), (1,)))).astype(BF16)

    def blocks(a):
        return a.astype(BF16).reshape(4, 4, 2, -1, a.shape[-1])

    g_down_t = blocks(dot(cot_all, active, ((0,), (0,))))
    g_gate = blocks(dot(normed2_all, grad_gate_pre, ((0,), (0,))))
    g_up = blocks(dot(normed2_all, grad_up_pre, ((0,), (0,))))
    grad_hidden1, gain2_part, grad_qlin, grad_kv, outputs, g_out_t, g_gate, g_up, g_down_t = backward(
        1, part2.reshape(group, tokens, width), hidden1, norm_mlp, cot, w_out_t, q, kv_all, attn, lse, tables,
        result_part, [g_gate, g_up, g_down_t],
    )
    grad_klin = unrotate(
        grad_kv[:, :HD], jnp.tile(tables[0, :, :HD], (group, 1)), jnp.tile(tables[1, :, :HD], (group, 1))
    )
    grad_lin = jnp.concatenate([grad_qlin, grad_klin.astype(BF16), grad_kv[:, HD:].astype(BF16)], 1)
    g_qkv = blocks(dot(normed_all, grad_lin, ((0,), (0,))))
    part3 = dot(grad_lin, w_qkv, ((1,), (1,))).astype(BF16).reshape(group, tokens, width)
    g_qkv, grad_inputs, gains = tail(2, [g_qkv], part3, x, norm_attn, grad_hidden1, gain2_part)
    start = (ctx_index % 2) * 64 + lax.axis_index("wshard") * 16
    gains = lax.dynamic_slice_in_dim(gains, start, 16, axis=1)
    return (
        outputs.reshape(inputs.shape),
        grad_inputs.reshape(inputs.shape),
        gains[0],
        g_qkv[:, :q_width],
        g_qkv[:, q_width : q_width + HD],
        g_qkv[:, q_width + HD :],
        g_out_t.T,
        gains[1],
        g_gate,
        g_up,
        g_down_t.T,
    )


def solution(mesh):
    return jax.shard_map(
        per_device,
        mesh=mesh,
        in_specs=(
            P("wshard", None, "ctx", None),
            P("wshard", None, "ctx", None),
            P(),
            P("ctx", "wshard"),
            P("ctx", "wshard"),
            P("ctx", "wshard"),
            P("wshard", "ctx"),
            P(),
            P("ctx", "wshard"),
            P("ctx", "wshard"),
            P("wshard", "ctx"),
        ),
        out_specs=(
            P("wshard", None, "ctx", None),
            P("wshard", None, "ctx", None),
            P(("ctx", "wshard")),
            P("ctx", "wshard"),
            P("ctx", "wshard"),
            P("ctx", "wshard"),
            P("wshard", "ctx"),
            P(("ctx", "wshard")),
            P("ctx", "wshard"),
            P("ctx", "wshard"),
            P("wshard", "ctx"),
        ),
        check_vma=False,
    )
```

```python
from functools import partial

import jax
import jax.numpy as jnp
from jax import lax
from jax.experimental import pallas as pl
from jax.experimental.pallas import tpu as pltpu
from jax.sharding import PartitionSpec as P

MESH = pl.DeviceIdType.MESH
HD = 64
EPS = 1e-05
NEG = -1e30
F32 = jnp.float32
BF16 = jnp.bfloat16
VMEM_LIMIT = 63 * 2**20
ANY = pl.BlockSpec(memory_space=pl.ANY)
VMEM = pl.BlockSpec(memory_space=pltpu.VMEM)


class Place:
    def __init__(self):
        ctx, shard = lax.axis_index("ctx"), lax.axis_index("wshard")
        self.x, self.z, self.y = ctx // 8, (ctx // 2) % 4, ctx % 2
        self.yl, self.co = shard // 2, shard % 2

    def at(self, x=None, z=None, y=None, yl=None, co=None):
        x, z, y = (self.x if x is None else x), (self.z if z is None else z), (self.y if y is None else y)
        yl, co = (self.yl if yl is None else yl), (self.co if co is None else co)
        return (x * 8 + z * 2 + y, yl * 2 + co)

    def step(self, axis, by):
        return self.at(**{axis: (getattr(self, axis) + by) % 4})

    def pair(self, axis):
        return self.at(**{axis: 1 - getattr(self, axis)})

    def ctx_peers(self):
        return [self.step("x", 1), self.step("x", 3), self.step("z", 1), self.step("z", 3), self.pair("y")]

    def shard_peers(self):
        return [self.pair("co"), self.pair("yl")]

    def far_peers(self):
        return [self.step("x", 2), self.step("z", 2)]


def greet(peers):
    barrier = pltpu.get_barrier_semaphore()
    for device in peers:
        pl.semaphore_signal(barrier, inc=1, device_id=device, device_id_type=MESH)
    pl.semaphore_wait(barrier, len(peers))


class Copies:
    def __init__(self, send, recv):
        self.send, self.recv, self.used = send, recv, 0

    def start(self, src, dst, device):
        k = self.used
        self.used += 1
        copy = pltpu.make_async_remote_copy(
            src_ref=src, dst_ref=dst, send_sem=self.send.at[k], recv_sem=self.recv.at[k],
            device_id=device, device_id_type=MESH,
        )
        copy.start()
        return copy

    def local(self, src, dst):
        k = self.used
        self.used += 1
        copy = pltpu.make_async_copy(src, dst, self.send.at[k])
        copy.start()
        return copy


def wait_all(copies):
    for copy in copies:
        copy.wait()


class CtxGather:
    COPIES = 10
    STAGES = 6

    def __init__(self, place, copies, shard, full, lo, n, big):
        self.p, self.c, self.shard, self.full = place, copies, shard, full
        self.lo, self.n, self.big, self.small = lo, n, big, ("z" if big == "x" else "x")
        self.live = []

    def block(self, o, i, y):
        x, z = (o, i) if self.big == "x" else (i, o)
        return self.full.at[x, z, y, pl.ds(self.lo, self.n)]

    def send(self, part, axis, by):
        dev = self.p.pair("y") if axis == "y" else self.p.step(axis, by)
        self.live.append(self.c.start(part, part, dev))

    def stage(self, s):
        p = self.p
        o, i, y = getattr(p, self.big), getattr(p, self.small), p.y
        wait_all(self.live)
        self.live = []
        every, both = pl.ds(0, 4), pl.ds(0, 2)
        if s == 0 and self.shard is None:
            self.send(self.block(o, i, y), "y", 0)
        elif s == 0:
            own = self.shard.at[pl.ds(self.lo, self.n)]
            self.live.append(self.c.start(own, self.block(o, i, y), p.pair("y")))
            self.live.append(self.c.local(own, self.block(o, i, y)))
        elif s == 1:
            self.send(self.block(o, i, both), self.small, 1)
            self.send(self.block(o, i, both), self.small, 3)
        elif s == 2:
            self.send(self.block(o, (i + 3) % 4, 0), self.small, 1)
            self.send(self.block(o, (i + 1) % 4, 1), self.small, 3)
        elif s == 3:
            self.send(self.block(o, every, both), self.big, 1)
            self.send(self.block(o, every, both), self.big, 3)
        elif s == 4:
            self.send(self.block((o + 3) % 4, pl.ds(0, 2), both), self.big, 1)
            self.send(self.block((o + 1) % 4, pl.ds(2, 2), both), self.big, 3)


class CtxGatherLate(CtxGather):
    def block(self, o, i, y, lo=None, n=None):
        x, z = (o, i) if self.big == "x" else (i, o)
        return self.full.at[x, z, y, pl.ds(self.lo if lo is None else lo, self.n if n is None else n)]

    def stage(self, s):
        p = self.p
        o, i, y = getattr(p, self.big), getattr(p, self.small), p.y
        wait_all(self.live)
        self.live = []
        every, half = pl.ds(0, 4), self.n // 2
        if s == 0:
            own = self.shard.at[pl.ds(self.lo, self.n)]
            for by in (1, 3):
                self.live.append(self.c.start(own, self.block(o, i, y), p.step(self.big, by)))
            self.live.append(self.c.local(own, self.block(o, i, y)))
        elif s == 1:
            self.send(self.block((o + 3) % 4, i, y, self.lo, half), self.big, 1)
            self.send(self.block((o + 1) % 4, i, y, self.lo + half, half), self.big, 3)
        elif s == 2:
            self.send(self.block(every, i, y), self.small, 1)
            self.send(self.block(every, i, y), self.small, 3)
        elif s == 3:
            self.send(self.block(pl.ds(0, 2), (i + 3) % 4, y), self.small, 1)
            self.send(self.block(pl.ds(2, 2), (i + 1) % 4, y), self.small, 3)
        elif s == 4:
            self.send(self.block(every, every, y), "y", 0)


class CtxScatter:
    COPIES = 17
    STAGES = 7

    @staticmethod
    def scratch(n, width, staged=False):
        shapes = [(2, 2, 2), (4, 2), (4, 2), (2,), (2,), (2,), ()]
        if staged:
            shapes += [(2, 2), (2, 2)]
        return [pltpu.VMEM(shape + (n, width), BF16) for shape in shapes]

    def __init__(self, place, copies, src, out, bufs, lo, n, big):
        self.p, self.c, self.src, self.out = place, copies, src, out
        self.far, self.pos, self.neg, self.far2, self.pos2, self.neg2, self.last = bufs[:7]
        self.staged = bufs[7:]
        self.lo, self.n, self.big, self.small = lo, n, big, ("z" if big == "x" else "x")
        self.first, self.live = [], []

    def part(self, o, i):
        x, z = (o, i) if self.big == "x" else (i, o)
        return self.src.at[x, z, pl.ds(0, 2), pl.ds(self.lo, self.n)]

    def load(self, o, i, y, which):
        if self.staged:
            return self.staged[which][i % 2, y].astype(F32)
        x, z = (o, i) if self.big == "x" else (i, o)
        return self.src[x, z, y, pl.ds(self.lo, self.n), :].astype(F32)

    def send(self, src, dst, axis, by):
        dev = self.p.pair("y") if axis == "y" else self.p.step(axis, by)
        copy = self.c.start(src, dst, dev)
        self.live.append(copy)
        return copy

    def stage(self, s):
        p, big, small = self.p, self.big, self.small
        o, i, y = getattr(p, big), getattr(p, small), p.y
        up, down, across = (o + 1) % 4, (o + 3) % 4, (o + 2) % 4
        iup, idown, iacross = (i + 1) % 4, (i + 3) % 4, (i + 2) % 4
        low, high = pl.ds(0, 2), pl.ds(2, 2)
        if s == 2:
            wait_all(self.first)
        elif s > 2:
            wait_all(self.live)
            self.live = []
        if s == 0:
            for src, dst, by in (
                (self.part(across, low), self.far.at[0], 1), (self.part(across, high), self.far.at[1], 3)
            ):
                self.first.append(self.c.start(src, dst, p.step(big, by)))
            if self.staged:
                self.first.append(self.c.local(self.part(up, low), self.staged[0]))
                self.first.append(self.c.local(self.part(down, high), self.staged[1]))
        elif s == 1:
            self.send(self.part(up, high), self.pos.at[high], big, 1)
            self.send(self.part(down, low), self.neg.at[low], big, 3)
        elif s == 2:

            def fold(k, _):
                b, q = k // 2, k % 2
                self.far[0, b, q] = (self.far[0, b, q].astype(F32) + self.load(up, b, q, 0)).astype(BF16)
                self.far[1, b, q] = (self.far[1, b, q].astype(F32) + self.load(down, b + 2, q, 1)).astype(BF16)
                return 0

            lax.fori_loop(0, 4, fold, 0)
            self.send(self.far.at[0], self.pos.at[low], big, 1)
            self.send(self.far.at[1], self.neg.at[high], big, 3)
            if self.staged:
                self.live.append(self.c.local(self.part(o, low), self.staged[0]))
                self.live.append(self.c.local(self.part(o, high), self.staged[1]))
        elif s == 3:

            def total(k, _):
                b, q = k // 2, k % 2
                for which in range(2):
                    at = b + 2 * which
                    here = self.load(o, at, q, which) + self.pos[at, q].astype(F32) + self.neg[at, q].astype(F32)
                    self.pos[at, q] = here.astype(BF16)
                return 0

            lax.fori_loop(0, 4, total, 0)
            self.first = [
                self.c.start(self.pos.at[iacross, 0], self.far2.at[0], p.step(small, 1)),
                self.c.start(self.pos.at[iacross, 1], self.far2.at[1], p.step(small, 3)),
            ]
            self.send(self.pos.at[iup, 1], self.pos2.at[1], small, 1)
            self.send(self.pos.at[idown, 0], self.neg2.at[0], small, 3)
        elif s == 4:
            wait_all(self.first)
            self.far2[0] = (self.far2[0].astype(F32) + self.pos[iup, 0].astype(F32)).astype(BF16)
            self.far2[1] = (self.far2[1].astype(F32) + self.pos[idown, 1].astype(F32)).astype(BF16)
            self.send(self.far2.at[0], self.pos2.at[0], small, 1)
            self.send(self.far2.at[1], self.neg2.at[1], small, 3)
        elif s == 5:
            for q in range(2):
                here = self.pos[i, q].astype(F32) + self.pos2[q].astype(F32) + self.neg2[q].astype(F32)
                self.pos2[q] = here.astype(BF16)
            self.send(self.pos2.at[1 - y], self.last, "y", 0)
        elif s == 6:
            total = self.pos2[y].astype(F32) + self.last[...].astype(F32)
            self.out[pl.ds(self.lo, self.n), :] = total.astype(self.out.dtype)


class ShardGather:
    def __init__(self, place, copies, full, chunks):
        self.p, self.c, self.full, self.chunks = place, copies, full, chunks
        self.rows = full.shape[1] // chunks
        self.me, self.over = place.yl * 2 + place.co, (1 - place.yl) * 2 + place.co
        self.far, self.near = [], []

    COPIES = 3

    def part(self, who, k):
        return self.full.at[who, pl.ds(k * self.rows, self.rows)]

    def send(self, k, src=None):
        src = self.part(self.me, k) if src is None else src
        self.far.append(self.c.start(src, self.part(self.me, k), self.p.pair("yl")))
        self.near.append(self.c.start(src, self.part(self.me, k), self.p.pair("co")))

    def forward(self, k):
        self.far[k].wait()
        self.near.append(self.c.start(self.part(self.over, k), self.part(self.over, k), self.p.pair("co")))

    def finish(self):
        wait_all(self.near)


class ShardScatter:
    COPIES = 3

    @staticmethod
    def scratch(rows, width):
        return [pltpu.VMEM((rows, width), BF16)] * 3

    def __init__(self, place, copies, part, bufs, chunks):
        self.p, self.c, self.part, self.chunks = place, copies, part, chunks
        self.relay, self.near, self.over = bufs
        self.rows = part.shape[1] // chunks
        self.first, self.second, self.third = [], [], []

    def at(self, k):
        return pl.ds(k * self.rows, self.rows)

    def begin(self):
        self.begin_far()
        self.begin_near()

    def begin_far(self):
        p = self.p
        for k in range(self.chunks):
            src = self.part.at[(1 - p.yl) * 2 + 1 - p.co, self.at(k)]
            self.first.append(self.c.start(src, self.relay.at[self.at(k)], p.pair("co")))

    def begin_near(self):
        p = self.p
        for k in range(self.chunks):
            src = self.part.at[p.yl * 2 + 1 - p.co, self.at(k)]
            self.second.append(self.c.start(src, self.near.at[self.at(k)], p.pair("co")))

    def relay_on(self, k):
        p = self.p
        self.first[k].wait()
        here = self.part[(1 - p.yl) * 2 + p.co, self.at(k), :].astype(F32)
        self.relay[self.at(k), :] = (self.relay[self.at(k), :].astype(F32) + here).astype(BF16)
        self.third.append(self.c.start(self.relay.at[self.at(k)], self.over.at[self.at(k)], p.pair("yl")))

    def total(self, k):
        p = self.p
        self.second[k].wait()
        self.third[k].wait()
        here = self.part[p.yl * 2 + p.co, self.at(k), :].astype(F32)
        return here + self.near[self.at(k), :].astype(F32) + self.over[self.at(k), :].astype(F32)


class GainScatter:
    COPIES = 9
    STAGES = 6

    @staticmethod
    def scratch():
        return [
            pltpu.VMEM((8, 2048), F32),
            pltpu.VMEM((3, 8, 512), F32),
            pltpu.VMEM((8, 512), F32),
            pltpu.VMEM((3, 8, 128), F32),
            pltpu.VMEM((3, 8, 128), F32),
            pltpu.VMEM((3, 8, 128), F32),
        ]

    def __init__(self, place, copies, out, bufs):
        self.p, self.c, self.out = place, copies, out
        self.vec, self.xs, self.mid, self.zs, self.own, self.rest = bufs
        self.live = []

    def stage(self, s):
        p = self.p
        wait_all(self.live)
        self.live = []
        if s == 0:
            for by in (1, 2, 3):
                cols = pl.ds(pl.multiple_of(((p.x + by) % 4) * 512, 512), 512)
                self.live.append(self.c.start(self.vec.at[:, cols], self.xs.at[by - 1], p.step("x", by)))
        elif s == 1:
            cols = pl.ds(pl.multiple_of(p.x * 512, 512), 512)
            self.mid[...] = self.vec[:, cols] + self.xs[0] + self.xs[1] + self.xs[2]
            for by in (1, 2, 3):
                cols = pl.ds(pl.multiple_of(((p.z + by) % 4) * 128, 128), 128)
                self.live.append(self.c.start(self.mid.at[:, cols], self.zs.at[by - 1], p.step("z", by)))
        elif s == 2:
            cols = pl.ds(pl.multiple_of(p.z * 128, 128), 128)
            self.own[0] = self.mid[:, cols] + self.zs[0] + self.zs[1] + self.zs[2]
            self.live.append(self.c.start(self.own.at[0], self.rest.at[0], p.pair("y")))
        elif s == 3:
            self.own[1] = self.own[0] + self.rest[0]
            self.live.append(self.c.start(self.own.at[1], self.rest.at[1], p.pair("co")))
        elif s == 4:
            self.own[2] = self.own[1] + self.rest[1]
            self.live.append(self.c.start(self.own.at[2], self.rest.at[2], p.pair("yl")))
        elif s == 5:
            self.out[...] = self.own[2] + self.rest[2]


def sems(n):
    return [pltpu.SemaphoreType.DMA((n,)), pltpu.SemaphoreType.DMA((n,))]


def params(cid):
    return pltpu.CompilerParams(collective_id=cid, has_side_effects=True, vmem_limit_bytes=VMEM_LIMIT)


def halves(rows):
    return ((0, rows // 2, "x"), (rows // 2, rows // 2, "z"))


CHUNKS = 4


def norm_back_rows(grad, resid, gain):
    factor = lax.rsqrt(jnp.mean(resid * resid, -1, keepdims=True) + EPS)
    weighted = grad * gain
    per_gain = grad * resid * factor
    back = factor * weighted - resid * (factor * factor * factor) * jnp.mean(weighted * resid, -1, keepdims=True)
    return back, per_gain


def eight(rows):
    return jnp.sum(rows.reshape(rows.shape[0] // 8, 8, rows.shape[1]), 0)


KEYS = 256
KB = 4


def lane_iota(rows):
    return lax.broadcasted_iota(jnp.int32, (rows, 128), 1)


def rotate_tile(u, cosine, sine):
    low = lane_iota(u.shape[0]) % HD < HD // 2
    turned = jnp.where(low, -pltpu.roll(u, 128 - HD // 2, 1), pltpu.roll(u, HD // 2, 1))
    return u * cosine + turned * sine


def unrotate_tile(w, cosine, sine):
    low = lane_iota(w.shape[0]) % HD < HD // 2
    s = w * sine
    return w * cosine + jnp.where(low, pltpu.roll(s, 128 - HD // 2, 1), -pltpu.roll(s, HD // 2, 1))


def project_rows(rows, w_qkv, tables):
    lin = jnp.dot(rows, w_qkv, preferred_element_type=F32)
    tiles = []
    for hp in range(4):
        tile = lin[:, hp * 128 : (hp + 1) * 128]
        tiles.append((rotate_tile(tile, tables[0], tables[1])).astype(BF16) * jnp.asarray(HD**-0.5, BF16))
    kv = rotate_tile(lin[:, 512:640], tables[2], tables[3]).astype(BF16)
    return tiles, kv


def head_rows(ref, start, keep_low):
    low = lane_iota(64) < HD
    keep = low if keep_low else ~low
    pieces = []
    for hp in range(4):
        tile = ref[pl.ds(start, 64), hp * 128 : (hp + 1) * 128].astype(F32)
        turned = pltpu.roll(tile, HD, 1)
        even, odd = (tile, turned) if keep_low else (turned, tile)
        pieces += [jnp.where(keep, even, 0.0), jnp.where(keep, odd, 0.0)]
    return pieces


def key_chunk(kv, seq, chunk, half):
    start = pl.multiple_of(seq * 128 + half * 64, 64)
    z = pl.ds((chunk % 2) * 2, 2)
    return kv[chunk // 2, z, :, pl.ds(start, 64), :].reshape(KEYS, 128)


def diagonal(block, here):
    key = lax.broadcasted_iota(jnp.int32, (KEYS, 512), 0)
    query = lax.broadcasted_iota(jnp.int32, (KEYS, 512), 1) % 64
    ahead = key // 64 - here
    return key % 64 - query <= (-ahead if block == 0 else ahead) * 64


def pick(u, own_chunk):
    late = u - 8
    block = jnp.where(u < 8, 1, jnp.where(late >= own_chunk, 1, 0))
    half = jnp.where(u < 8, 0, block)
    chunk = jnp.where(u < 8, u, late + half)
    return block, chunk, half


def nt(a, b):
    return lax.dot_general(a, b, (((1,), (1,)), ((), ())), preferred_element_type=F32)


def tn(a, b):
    return lax.dot_general(a, b, (((0,), (0,)), ((), ())), preferred_element_type=F32)


def attend_seq(seq, ctx, q, kv, attn, lse, scratch):
    qe, top, acc = scratch
    low = lane_iota(64) < HD
    ones_low = lane_iota(KEYS) < HD
    own_chunk, here = ctx // KB, ctx % KB

    def with_ones(keys):
        return jnp.where(ones_low, jnp.ones_like(keys), keys)

    for b in range(2):
        for h, piece in enumerate(head_rows(q, seq * 128 + b * 64, True)):
            qe[b, h * 64 : (h + 1) * 64, :] = piece.astype(BF16)
    for b in range(2):
        keys = key_chunk(kv, seq, own_chunk, b)
        scores = jnp.where(diagonal(b, here), nt(keys, qe[b]), NEG)
        m = jnp.max(scores, 0, keepdims=True)
        p = jnp.exp(scores - m).astype(BF16)
        top[b] = m
        acc[b] = tn(with_ones(keys), p)

    def step(u, _):
        b, chunk, half = pick(u, own_chunk)
        keys = key_chunk(kv, seq, chunk, half)
        scores = nt(keys, qe[b])
        before = top[b]
        m = jnp.maximum(before, jnp.max(scores, 0, keepdims=True))
        p = jnp.exp(scores - m).astype(BF16)
        top[b] = m
        acc[b] = acc[b] * jnp.exp(before - m) + tn(with_ones(keys), p)
        return 0

    for k in range(3):
        lax.fori_loop(5 * k, 5 * k + 5, step, 0, unroll=True)
        if k < 2:
            yield
    for b in range(2):
        here_acc = acc[b]
        total = here_acc[0:1, :]
        lse[pl.ds(seq * 2 + b, 1), :] = top[b] + jnp.log(total)
        out = (here_acc * (1.0 / total)).T
        for hp in range(4):
            even, odd = out[hp * 128 : hp * 128 + 64, :], out[hp * 128 + 64 : hp * 128 + 128, :]
            tile = jnp.where(low, pltpu.roll(even, HD, 1), odd)
            attn[pl.ds(seq * 128 + b * 64, 64), hp * 128 : (hp + 1) * 128] = tile.astype(BF16)


def attend_scratch():
    return [pltpu.VMEM((2, 512, 128), BF16), pltpu.VMEM((2, 1, 512), F32), pltpu.VMEM((2, 128, 512), F32)]


def attend_back_seq(seq, ctx, q, kv, grad, attn, lse, tables, grad_lin, grad_kv, scratch):
    qd, delta, dq, dkv = scratch
    low = lane_iota(64) < HD
    own_chunk, here = ctx // KB, ctx % KB
    for b in range(2):
        start = seq * 128 + b * 64
        q_rows, g_rows, o_rows = (
            head_rows(q, start, True), head_rows(grad, start, False), head_rows(attn, start, False)
        )
        for h in range(8):
            qd[b, h * 64 : (h + 1) * 64, :] = q_rows[h].astype(BF16)
            qd[b, 512 + h * 64 : 512 + (h + 1) * 64, :] = g_rows[h].astype(BF16)
        products = jnp.concatenate([g * o for g, o in zip(g_rows, o_rows)], 0)
        delta[b] = jnp.sum(products.T, 0, keepdims=True)

    def grads(b, keys, allowed):
        both = nt(keys, qd[b])
        p = jnp.exp(both[:, :512] - lse[pl.ds(seq * 2 + b, 1), :])
        if allowed is not None:
            p = jnp.where(allowed, p, 0.0)
        ds = (p * (both[:, 512:] - delta[b])).astype(BF16)
        joined = jnp.concatenate([ds, p.astype(BF16)], 1)
        return tn(keys, ds), jnp.dot(joined, qd[b], preferred_element_type=F32)

    dkv[...] = jnp.zeros_like(dkv)

    def add_keys(chunk, half, value):
        start = pl.multiple_of(half * 64, 64)
        dkv[pl.ds(chunk * KB, KB), pl.ds(start, 64), :] += value.reshape(KB, 64, 128)

    for b in range(2):
        dq_part, dkv_part = grads(b, key_chunk(kv, seq, own_chunk, b), diagonal(b, here))
        dq[b] = dq_part
        add_keys(own_chunk, b, dkv_part)

    def step(u, _):
        b, chunk, half = pick(u, own_chunk)
        dq_part, dkv_part = grads(b, key_chunk(kv, seq, chunk, half), None)
        dq[b] += dq_part
        add_keys(chunk, half, dkv_part)
        return 0

    for k in range(3):
        lax.fori_loop(5 * k, 5 * k + 5, step, 0, unroll=True)
        if k < 2:
            yield
    for b in range(2):
        out = (dq[b] * HD**-0.5).T
        cosine, sine = tables[0, b * 64 : (b + 1) * 64, :], tables[1, b * 64 : (b + 1) * 64, :]
        for hp in range(4):
            even, odd = out[hp * 128 : hp * 128 + 64, :], out[hp * 128 + 64 : hp * 128 + 128, :]
            tile = jnp.where(low, even, pltpu.roll(odd, HD, 1))
            tile = unrotate_tile(tile, cosine, sine)
            grad_lin[pl.ds(seq * 128 + b * 64, 64), hp * 128 : (hp + 1) * 128] = tile.astype(BF16)
    grad_kv[...] = dkv[...].reshape(4, 4, 2, 128, 128).astype(BF16)


def attend_back_scratch():
    return [
        pltpu.VMEM((2, 1024, 128), BF16),
        pltpu.VMEM((2, 1, 512), F32),
        pltpu.VMEM((2, 128, 512), F32),
        pltpu.VMEM((32, 128, 128), F32),
    ]


def ctx_gathers(place, copies, src, full, kind=CtxGather):
    return [kind(place, copies, src, full, lo, rows, big) for lo, rows, big in halves(src.shape[0])]


FORWARD = [
    "w0", "N1", "g0", "w1", "w2", "d0", "w3", "CB", "NF", "d1", "w4", "NW", "d2", "w5", "P1", "P0", "o0", "k10",
    "P3", "k00", "P2", "k20", "u0", "o1", "k30", "d3", "k11", "k21", "k31", "o2", "d4", "k01", "g1", "k12", "k02",
    "k32", "u1", "k13", "k22", "CF", "k03", "k33", "o3", "k04", "k23", "CW", "k05", "g2", "A00", "u2", "k14", "o4",
    "A01", "k24", "A02", "k34", "k15", "A10", "o5", "g3", "A11", "OP0", "u3", "k25", "A12", "A20", "A21", "A22",
    "k35", "RF", "OP1", "OP2", "g4", "RR", "RN", "A30", "A31", "A32", "OP3", "NT", "d5", "u4", "SF", "SW", "u5",
    "g5",
]

BACKWARD = [
    "d0", "g0", "g1", "RSB", "u0", "u1", "RSR", "RST", "A00", "d1", "A01", "FWD", "A02", "DO", "A10", "d2", "A11",
    "A12", "RESB", "k00", "A20", "u2", "GO", "A21", "k10", "A22", "g2", "A30", "RESR", "A31", "A32", "k30", "k20",
    "k11", "k01", "k02", "k31", "k21", "k22", "k32", "k12", "k33", "k03", "o0", "k13", "k23", "k34", "k04", "g3",
    "d3", "k24", "k14", "k35", "u3", "k05", "RES", "k15", "g4", "o1", "k25", "o2", "k16", "I1", "k26", "k06", "I0",
    "k36", "I3", "I2", "d4", "QG", "q0", "q1", "d5", "q2", "o3", "TOT", "n0", "u4", "g5", "n1", "o4", "q3", "n2",
    "u5", "o5", "g6", "d6", "q4", "n3", "n4", "q5", "u6", "o6", "q6", "n5",
]


def run_steps(steps, engines, actions):
    for step in steps:
        if step in actions:
            actions[step]()
        else:
            for e in engines[step[:-1]]:
                e.stage(int(step[-1]))


def forward_kernel(
    x, cot, gain1, gain2, tables, w_qkv_shard, w_out_shard, w_gate_shard, w_up_shard, w_down_shard,
    normed1_out, cot_all, w_qkv_out, w_out_out, w_gate, w_up, w_down, q, kv_out, attn, lse, hidden, normed2_all,
    normed1_all, w_qkv, w_out, kv_all, part, relay, near, over, qe, top, acc, send, recv,
):
    place = Place()
    greet(place.ctx_peers() + place.shard_peers())
    copies = Copies(send, recv)
    ctx = lax.axis_index("ctx")
    order = [2 * (1 - place.yl) + 1 - place.co, 2 * (1 - place.yl) + place.co]
    order += [2 * place.yl + 1 - place.co, 2 * place.yl + place.co]
    starts = [pl.multiple_of(seq * 128, 128) for seq in order]
    engines = {
        "w": ctx_gathers(place, copies, w_qkv_shard, w_qkv),
        "o": ctx_gathers(place, copies, w_out_shard, w_out),
        "g": ctx_gathers(place, copies, w_gate_shard, w_gate),
        "u": ctx_gathers(place, copies, w_up_shard, w_up),
        "d": ctx_gathers(place, copies, w_down_shard, w_down, CtxGatherLate),
    }
    for k in range(4):
        engines[f"k{k}"] = [CtxGather(place, copies, None, kv_all, starts[k], 128, "xz"[k % 2])]
    normed = ShardGather(place, copies, normed1_all, 1)
    cots = ShardGather(place, copies, cot_all, 1)
    rows_out = ShardScatter(place, copies, part, (relay, near, over), CHUNKS)
    spread = ShardGather(place, copies, normed2_all, CHUNKS)
    thirds = [attend_seq(seq, ctx, q, kv_all, attn, lse, (qe, top, acc)) for seq in order]
    outgoing = []

    def first_norm():
        rows = x[...].astype(F32)
        factor = lax.rsqrt(jnp.mean(rows * rows, -1, keepdims=True) + EPS)
        normed1_all[normed.me] = (rows * factor * gain1[...].astype(F32)).astype(BF16)
        normed.send(0)

    def normed_here():
        normed.finish()
        outgoing.append(copies.local(normed1_all, normed1_out))

    def project_seq(k):
        at = pl.ds(starts[k], 128)
        tiles, kv = project_rows(normed1_all[order[k]], w_qkv[...].reshape(2048, 640), tables)
        for hp, tile in enumerate(tiles):
            q[at, hp * 128 : (hp + 1) * 128] = tile
        kv_all[place.x, place.z, place.y, at, :] = kv

    def send_cot():
        cots.send(0, cot)
        outgoing.append(copies.local(cot, cot_all.at[cots.me]))

    def project_out(k):
        part[order[k]] = nt(attn[pl.ds(starts[k], 128), :], w_out[...].reshape(2048, 512)).astype(BF16)

    def relay_rows():
        for c in range(CHUNKS):
            rows_out.relay_on(c)

    def second_norm():
        for c in range(CHUNKS):
            at = rows_out.at(c)
            here = x[at, :].astype(F32) + rows_out.total(c)
            hidden[at, :] = here
            factor = lax.rsqrt(jnp.mean(here * here, -1, keepdims=True) + EPS)
            normed2_all[spread.me, at, :] = (here * factor * gain2[...].astype(F32)).astype(BF16)
            spread.send(c)

    def spread_on():
        for c in range(CHUNKS):
            spread.forward(c)

    actions = {
        "N1": first_norm, "NF": lambda: normed.forward(0), "NW": normed_here,
        "CB": send_cot, "CF": lambda: cots.forward(0), "CW": cots.finish,
        "RF": rows_out.begin_far, "RR": relay_rows, "RN": rows_out.begin_near,
        "NT": second_norm, "SF": spread_on, "SW": spread.finish,
    }
    for k in range(4):
        actions[f"P{k}"] = partial(project_seq, k)
        actions[f"OP{k}"] = partial(project_out, k)
        for third in range(3):
            actions[f"A{k}{third}"] = partial(next, thirds[k], None)
    run_steps(FORWARD, engines, actions)
    outgoing += [copies.local(w_qkv, w_qkv_out), copies.local(w_out, w_out_out), copies.local(kv_all, kv_out)]
    wait_all(outgoing)


def forward(cid, x, cot, gain1, gain2, tables, shards):
    tokens, width = x.shape

    def full(a):
        return (4, 4, 2) + a.shape

    shapes = [
        ((4, tokens, width), BF16), ((4, tokens, width), BF16), *((full(a), BF16) for a in shards),
        ((512, 512), BF16), ((4, 4, 2, 512, 128), BF16), ((512, 512), BF16), ((8, 512), F32),
        ((tokens, width), F32), ((4, tokens, width), BF16),
    ]
    return pl.pallas_call(
        forward_kernel,
        out_shape=[jax.ShapeDtypeStruct(*s) for s in shapes],
        in_specs=[VMEM, ANY, VMEM, VMEM, VMEM] + [ANY] * 5,
        out_specs=[ANY] * 7 + [VMEM, ANY] + [VMEM] * 4,
        scratch_shapes=[
            pltpu.VMEM((4, tokens, width), BF16),
            pltpu.VMEM(full(shards[0]), BF16),
            pltpu.VMEM(full(shards[1]), BF16),
            pltpu.VMEM((4, 4, 2, 512, 128), BF16),
            pltpu.VMEM((4, tokens, width), BF16),
            *ShardScatter.scratch(tokens, width),
            *attend_scratch(),
            *sems(14 * CtxGather.COPIES + 6 * CHUNKS + 16),
        ],
        compiler_params=params(cid),
        name="forward",
    )(x, cot, gain1.reshape(1, width), gain2.reshape(1, width), tables, *shards)


def backward_kernel(*refs):
    (
        part_in, result_in, w_out_in, w_qkv_in, normed_in, g_gate, g_up, g_down,
        hidden, gain2, cot, q, kv, attn, lse, tables, x, gain1,
    ) = refs[:18]
    grad_inputs, gains, outputs, out_q, out_kv, out_o, out_gate, out_up, out_down = refs[18:27]
    part, result_part, w_out, w_qkv, branch, dkv_send, relay, near, over = refs[27:36]
    grad_hidden, grad_gain, grad_lin, grad_kv, out_qkv = refs[36:41]
    scratch, gain_bufs, bufs, (free, send, recv) = refs[41:45], refs[45:51], refs[51:-3], refs[-3:]
    place = Place()
    greet(place.ctx_peers() + place.shard_peers() + place.far_peers())
    copies = Copies(send, recv)
    ctx = lax.axis_index("ctx")
    me, co = 2 * place.yl + place.co, 2 * place.yl + 1 - place.co
    far, far_co = 2 * (1 - place.yl) + place.co, 2 * (1 - place.yl) + 1 - place.co
    order = [me, far_co, far, co]
    taken = 0

    def take(n):
        nonlocal taken
        taken += n
        return bufs[taken - n : taken]

    def rows_of(seq):
        return pl.ds(pl.multiple_of(seq * 128, 128), 128)

    engines = {}
    for name, src, out, count in (
        ("d", g_down, out_down, 9), ("g", g_gate, out_gate, 9), ("u", g_up, out_up, 9),
        ("o", w_out, out_o, 7), ("q", w_qkv, out_qkv, 7),
    ):
        engines[name] = [
            CtxScatter(place, copies, src, out, take(count), lo, rows, big) for lo, rows, big in halves(64)
        ]
    for k in range(4):
        engines[f"k{k}"] = [
            CtxScatter(place, copies, dkv_send.at[k], grad_kv.at[rows_of(order[k])], take(7), 0, 128, "xz"[k % 2])
        ]
    gain_sum = GainScatter(place, copies, gains, gain_bufs)
    engines["n"] = [gain_sum]
    loads = [copies.local(a, b) for a, b in (
        (part_in, part), (w_out_in, w_out), (result_in, result_part), (w_qkv_in, w_qkv)
    )]
    scatter_ = ShardScatter(place, copies, part, (relay, near, over), CHUNKS)
    spread = ShardGather(place, copies, branch, CHUNKS)
    result = ShardScatter(place, copies, result_part, (relay, near, over), 1)
    last = ShardScatter(place, copies, branch, (relay, near, over), CHUNKS)
    thirds = [
        attend_back_seq(
            order[k], ctx, q, kv, grad_lin, attn, lse, tables, grad_lin, dkv_send.at[k], scratch
        )
        for k in range(4)
    ]

    def begin():
        loads[0].wait()
        scatter_.begin()

    def relay_rows(rows_scatter):
        for c in range(CHUNKS):
            rows_scatter.relay_on(c)

    def grad_rows(seq):
        w = w_out[...].reshape(2048, 512)
        grad_lin[rows_of(seq), :512] = jnp.dot(branch[seq], w, preferred_element_type=F32).astype(BF16)

    def second_norm_back():
        for c in range(CHUNKS):
            rows = scatter_.at(c)
            back, per_gain = norm_back_rows(scatter_.total(c), hidden[rows, :], gain2[...].astype(F32))
            here = cot[rows, :].astype(F32) + back
            grad_hidden[rows, :] = here
            branch[spread.me, rows, :] = here.astype(BF16)
            spread.send(c)
            grad_gain[...] = eight(per_gain) if c == 0 else grad_gain[...] + eight(per_gain)
        wait_all(loads[1:])
        loads.append(copies.local(normed_in, part))
        grad_rows(me)

    def spread_on():
        for c in range(CHUNKS):
            spread.forward(c)

    def grad_mixed():
        spread.finish()
        for seq in order[1:]:
            grad_rows(seq)

    def grad_of_out():
        rows = branch[...].reshape(512, 2048)
        for j in range(8):
            block = tn(rows[:, j * 256 : (j + 1) * 256], attn[...]).astype(BF16)
            w_out[j // 2, pl.ds((j % 2) * 2, 2)] = block.reshape(2, 2, 64, 512)

    def result_rows():
        outputs[...] = (hidden[...] + result.total(0)).astype(BF16)
        for device in place.shard_peers():
            pl.semaphore_signal(free, inc=1, device_id=device, device_id_type=MESH)

    def input_rows(k):
        at = rows_of(order[k])
        grad_lin[at, 512:640] = unrotate_tile(grad_kv[at, :], tables[2], tables[3]).astype(BF16)
        branch[order[k]] = nt(grad_lin[at, :], w_qkv[...].reshape(2048, 640)).astype(BF16)
        if k == 1:
            pl.semaphore_wait(free, 2)
            last.begin_far()
        elif k == 2:
            relay_rows(last)
        elif k == 3:
            last.begin_near()

    def grad_of_qkv():
        loads[-1].wait()
        rows = part[...].reshape(512, 2048)
        for j in range(8):
            block = tn(rows[:, j * 256 : (j + 1) * 256], grad_lin[...]).astype(BF16)
            w_qkv[j // 2, pl.ds((j % 2) * 2, 2)] = block.reshape(2, 2, 64, 640)

    def first_norm_back():
        for c in range(CHUNKS):
            rows = last.at(c)
            back, per_gain = norm_back_rows(last.total(c), x[rows, :].astype(F32), gain1[...].astype(F32))
            grad_inputs[rows, :] = (grad_hidden[rows, :] + back).astype(BF16)
            total = eight(per_gain) if c == 0 else total + eight(per_gain)
        row = lax.broadcasted_iota(jnp.int32, total.shape, 0)
        one, two = jnp.sum(total, 0, keepdims=True), jnp.sum(grad_gain[...], 0, keepdims=True)
        gain_sum.vec[...] = jnp.where(row == 0, one, jnp.where(row == 1, two, 0.0))

    actions = {
        "RSB": begin, "RSR": lambda: relay_rows(scatter_), "RST": second_norm_back, "FWD": spread_on,
        "DO": grad_mixed, "GO": grad_of_out, "RESB": result.begin, "RESR": lambda: result.relay_on(0),
        "RES": result_rows, "QG": grad_of_qkv, "TOT": first_norm_back,
    }
    for k in range(4):
        actions[f"I{k}"] = partial(input_rows, k)
        for third in range(3):
            actions[f"A{k}{third}"] = partial(next, thirds[k], None)
    run_steps(BACKWARD, engines, actions)
    out_q[...] = out_qkv[:, :512]
    out_kv[...] = out_qkv[:, 512:]


def backward(cid, in_hbm, in_vmem):
    hidden, gain2 = in_vmem[0], in_vmem[1]
    tokens, width = hidden.shape
    ffn_width = in_hbm[5].shape[4]
    in_vmem = [a.reshape(1, width) if a.ndim == 1 else a for a in in_vmem]
    scratch = []
    for _ in range(6):
        scratch += CtxScatter.scratch(32, ffn_width, True)
    for _ in range(2):
        scratch += CtxScatter.scratch(32, 512)
    for _ in range(2):
        scratch += CtxScatter.scratch(32, 640)
    for _ in range(4):
        scratch += CtxScatter.scratch(128, 128)
    shapes = [
        ((tokens, width), BF16), ((8, 128), F32), ((tokens, width), BF16), ((64, 512), F32), ((64, 128), F32),
        ((64, 512), F32), ((64, ffn_width), F32), ((64, ffn_width), F32), ((64, ffn_width), F32),
    ]
    return pl.pallas_call(
        backward_kernel,
        out_shape=[jax.ShapeDtypeStruct(*shape) for shape in shapes],
        in_specs=[ANY] * len(in_hbm) + [VMEM] * len(in_vmem),
        out_specs=[VMEM] * len(shapes),
        scratch_shapes=[
            pltpu.VMEM((4, tokens, width), BF16),
            pltpu.VMEM((4, tokens, width), BF16),
            pltpu.VMEM((4, 4, 2, 64, 512), BF16),
            pltpu.VMEM((4, 4, 2, 64, 640), BF16),
            pltpu.VMEM((4, tokens, width), BF16),
            pltpu.VMEM((4, 4, 4, 2, 128, 128), BF16),
            *ShardScatter.scratch(tokens, width),
            pltpu.VMEM((tokens, width), F32),
            pltpu.VMEM((8, width), F32),
            pltpu.VMEM((512, 640), BF16),
            pltpu.VMEM((512, 128), F32),
            pltpu.VMEM((64, 640), F32),
            *attend_back_scratch(),
            *GainScatter.scratch(),
            *scratch,
            pltpu.SemaphoreType.REGULAR,
            *sems(14 * CtxScatter.COPIES + 9 * CHUNKS + GainScatter.COPIES + 8),
        ],
        compiler_params=params(cid),
        name="backward",
    )(*in_hbm, *in_vmem)


def rope_tables(positions):
    freqs = 10000.0 ** (-jnp.arange(HD // 2, dtype=F32) * 2.0 / HD)
    angles = positions[:, None] * freqs[None]
    cosine, sine = jnp.cos(angles), jnp.sin(angles)
    one, zero = jnp.ones_like(cosine), jnp.zeros_like(cosine)
    return jnp.stack(
        [
            jnp.concatenate([cosine] * 4, -1),
            jnp.concatenate([sine] * 4, -1),
            jnp.concatenate([cosine, cosine, one, one], -1),
            jnp.concatenate([sine, sine, zero, zero], -1),
        ]
    )


def dot(a, b, dims):
    return lax.dot_general(a, b, (dims, ((), ())), preferred_element_type=F32)


def per_device(
    inputs, cotangent, norm_attn, w_query, w_key, w_value, w_out, norm_mlp, w_gate, w_up, w_down
):
    width = inputs.shape[-1]
    half_len = inputs.shape[2]
    tokens = 2 * half_len
    ctx_count = lax.axis_size("ctx")
    ctx_index = lax.axis_index("ctx")
    group = lax.axis_size("wshard")
    length = tokens * ctx_count
    x = inputs.reshape(tokens, width)
    cot = cotangent.reshape(tokens, width)
    rows_local = jnp.arange(tokens)
    positions = jnp.where(
        rows_local < half_len,
        ctx_index * half_len + rows_local,
        length - (ctx_index + 1) * half_len + (rows_local - half_len),
    ).astype(F32)
    tables = rope_tables(positions)

    w_qkv = jnp.concatenate([w_query, w_key, w_value], 1)
    forward_results = forward(0, x, cot, norm_attn, norm_mlp, tables, [w_qkv, w_out.T, w_gate, w_up, w_down.T])
    normed_all, cot_all, w_qkv, w_out_t, w_gate, w_up, w_down_t, q, kv_all, attn, lse, hidden1, normed2_all = (
        forward_results
    )
    w_gate, w_up, w_down_t = (a.reshape(width, a.shape[-1]) for a in (w_gate, w_up, w_down_t))
    cot_all, normed2_all = (a.reshape(group * tokens, width) for a in (cot_all, normed2_all))
    gate_pre = dot(normed2_all, w_gate, ((1,), (0,)))
    up_pre = dot(normed2_all, w_up, ((1,), (0,)))
    sigmoid_gate = jax.nn.sigmoid(gate_pre)
    silu_gate = gate_pre * sigmoid_gate
    active = (silu_gate * up_pre).astype(BF16)
    result_part = dot(active, w_down_t, ((1,), (1,))).astype(BF16).reshape(group, tokens, width)
    grad_active = dot(cot_all, w_down_t, ((1,), (0,)))
    grad_gate_pre = (grad_active * up_pre * sigmoid_gate * (1.0 + gate_pre * (1.0 - sigmoid_gate))).astype(BF16)
    grad_up_pre = (grad_active * silu_gate).astype(BF16)
    part2 = (dot(grad_gate_pre, w_gate, ((1,), (1,))) + dot(grad_up_pre, w_up, ((1,), (1,)))).astype(BF16)

    def blocks(a):
        return a.astype(BF16).reshape(4, 4, 2, -1, a.shape[-1])

    g_down_t = blocks(dot(cot_all, active, ((0,), (0,))))
    g_gate = blocks(dot(normed2_all, grad_gate_pre, ((0,), (0,))))
    g_up = blocks(dot(normed2_all, grad_up_pre, ((0,), (0,))))
    grad_inputs, gains, outputs, g_query, g_kv, g_out, g_gate, g_up, g_down = backward(
        1,
        [a.reshape(group, tokens, width) for a in (part2, result_part)]
        + [w_out_t, w_qkv, normed_all, g_gate, g_up, g_down_t],
        [hidden1, norm_mlp, cot, q, kv_all, attn, lse, tables, x, norm_attn],
    )
    start = (ctx_index % 2) * 64 + lax.axis_index("wshard") * 16
    gains = lax.dynamic_slice_in_dim(gains, start, 16, axis=1)
    return (
        outputs.reshape(inputs.shape),
        grad_inputs.reshape(inputs.shape),
        gains[0],
        g_query,
        g_kv[:, :HD],
        g_kv[:, HD:],
        g_out.T,
        gains[1],
        g_gate,
        g_up,
        g_down.T,
    )


def solution(mesh):
    return jax.shard_map(
        per_device,
        mesh=mesh,
        in_specs=(
            P("wshard", None, "ctx", None),
            P("wshard", None, "ctx", None),
            P(),
            P("ctx", "wshard"),
            P("ctx", "wshard"),
            P("ctx", "wshard"),
            P("wshard", "ctx"),
            P(),
            P("ctx", "wshard"),
            P("ctx", "wshard"),
            P("wshard", "ctx"),
        ),
        out_specs=(
            P("wshard", None, "ctx", None),
            P("wshard", None, "ctx", None),
            P(("ctx", "wshard")),
            P("ctx", "wshard"),
            P("ctx", "wshard"),
            P("ctx", "wshard"),
            P("wshard", "ctx"),
            P(("ctx", "wshard")),
            P("ctx", "wshard"),
            P("ctx", "wshard"),
            P("wshard", "ctx"),
        ),
        check_vma=False,
    )
```

```python
from functools import partial

import jax
import jax.numpy as jnp
from jax import lax
from jax.experimental import pallas as pl
from jax.experimental.pallas import tpu as pltpu
from jax.sharding import PartitionSpec as P

MESH = pl.DeviceIdType.MESH
HD = 64
EPS = 1e-05
NEG = -1e30
F32 = jnp.float32
BF16 = jnp.bfloat16
VMEM_LIMIT = 63 * 2**20
ANY = pl.BlockSpec(memory_space=pl.ANY)
VMEM = pl.BlockSpec(memory_space=pltpu.VMEM)


class Place:
    def __init__(self):
        ctx, shard = lax.axis_index("ctx"), lax.axis_index("wshard")
        self.x, self.z, self.y = ctx // 8, (ctx // 2) % 4, ctx % 2
        self.yl, self.co = shard // 2, shard % 2

    def at(self, x=None, z=None, y=None, yl=None, co=None):
        x, z, y = (self.x if x is None else x), (self.z if z is None else z), (self.y if y is None else y)
        yl, co = (self.yl if yl is None else yl), (self.co if co is None else co)
        return (x * 8 + z * 2 + y, yl * 2 + co)

    def step(self, axis, by):
        return self.at(**{axis: (getattr(self, axis) + by) % 4})

    def pair(self, axis):
        return self.at(**{axis: 1 - getattr(self, axis)})

    def ctx_peers(self):
        return [self.step("x", 1), self.step("x", 3), self.step("z", 1), self.step("z", 3), self.pair("y")]

    def shard_peers(self):
        return [self.pair("co"), self.pair("yl")]

    def far_peers(self):
        return [self.step("x", 2), self.step("z", 2)]


def greet(peers):
    barrier = pltpu.get_barrier_semaphore()
    for device in peers:
        pl.semaphore_signal(barrier, inc=1, device_id=device, device_id_type=MESH)
    pl.semaphore_wait(barrier, len(peers))


class Copies:
    def __init__(self, send, recv):
        self.send, self.recv, self.used = send, recv, 0

    def start(self, src, dst, device):
        k = self.used
        self.used += 1
        copy = pltpu.make_async_remote_copy(
            src_ref=src, dst_ref=dst, send_sem=self.send.at[k], recv_sem=self.recv.at[k],
            device_id=device, device_id_type=MESH,
        )
        copy.start()
        return copy

    def local(self, src, dst):
        k = self.used
        self.used += 1
        copy = pltpu.make_async_copy(src, dst, self.send.at[k])
        copy.start()
        return copy


def wait_all(copies):
    for copy in copies:
        copy.wait()


class CtxGather:
    COPIES = 10
    STAGES = 6

    def __init__(self, place, copies, shard, full, lo, n, big):
        self.p, self.c, self.shard, self.full = place, copies, shard, full
        self.lo, self.n, self.big, self.small = lo, n, big, ("z" if big == "x" else "x")
        self.live = []

    def block(self, o, i, y):
        x, z = (o, i) if self.big == "x" else (i, o)
        return self.full.at[x, z, y, pl.ds(self.lo, self.n)]

    def send(self, part, axis, by):
        dev = self.p.pair("y") if axis == "y" else self.p.step(axis, by)
        self.live.append(self.c.start(part, part, dev))

    def stage(self, s):
        p = self.p
        o, i, y = getattr(p, self.big), getattr(p, self.small), p.y
        wait_all(self.live)
        self.live = []
        every, both = pl.ds(0, 4), pl.ds(0, 2)
        if s == 0 and self.shard is None:
            self.send(self.block(o, i, y), "y", 0)
        elif s == 0:
            own = self.shard.at[pl.ds(self.lo, self.n)]
            self.live.append(self.c.start(own, self.block(o, i, y), p.pair("y")))
            self.live.append(self.c.local(own, self.block(o, i, y)))
        elif s == 1:
            self.send(self.block(o, i, both), self.small, 1)
            self.send(self.block(o, i, both), self.small, 3)
        elif s == 2:
            self.send(self.block(o, (i + 3) % 4, 0), self.small, 1)
            self.send(self.block(o, (i + 1) % 4, 1), self.small, 3)
        elif s == 3:
            self.send(self.block(o, every, both), self.big, 1)
            self.send(self.block(o, every, both), self.big, 3)
        elif s == 4:
            self.send(self.block((o + 3) % 4, pl.ds(0, 2), both), self.big, 1)
            self.send(self.block((o + 1) % 4, pl.ds(2, 2), both), self.big, 3)


class CtxGatherLate(CtxGather):
    def block(self, o, i, y, lo=None, n=None):
        x, z = (o, i) if self.big == "x" else (i, o)
        return self.full.at[x, z, y, pl.ds(self.lo if lo is None else lo, self.n if n is None else n)]

    def stage(self, s):
        p = self.p
        o, i, y = getattr(p, self.big), getattr(p, self.small), p.y
        wait_all(self.live)
        self.live = []
        every, half = pl.ds(0, 4), self.n // 2
        if s == 0:
            own = self.shard.at[pl.ds(self.lo, self.n)]
            for by in (1, 3):
                self.live.append(self.c.start(own, self.block(o, i, y), p.step(self.big, by)))
            self.live.append(self.c.local(own, self.block(o, i, y)))
        elif s == 1:
            self.send(self.block((o + 3) % 4, i, y, self.lo, half), self.big, 1)
            self.send(self.block((o + 1) % 4, i, y, self.lo + half, half), self.big, 3)
        elif s == 2:
            self.send(self.block(every, i, y), self.small, 1)
            self.send(self.block(every, i, y), self.small, 3)
        elif s == 3:
            self.send(self.block(pl.ds(0, 2), (i + 3) % 4, y), self.small, 1)
            self.send(self.block(pl.ds(2, 2), (i + 1) % 4, y), self.small, 3)
        elif s == 4:
            self.send(self.block(every, every, y), "y", 0)


class CtxScatter:
    COPIES = 17
    STAGES = 7

    @staticmethod
    def scratch(n, width, staged=False):
        shapes = [(2, 2, 2), (4, 2), (4, 2), (2,), (2,), (2,), ()]
        if staged:
            shapes += [(2, 2), (2, 2)]
        return [pltpu.VMEM(shape + (n, width), BF16) for shape in shapes]

    def __init__(self, place, copies, src, out, bufs, lo, n, big, stop=False, resumed=None):
        self.p, self.c, self.src, self.out = place, copies, src, out
        self.far, self.pos, self.neg, self.far2, self.pos2, self.neg2, self.last = bufs[:7]
        self.staged = bufs[7:]
        self.lo, self.n, self.big, self.small = lo, n, big, ("z" if big == "x" else "x")
        self.first, self.live = [], []
        self.stop, self.resumed = stop, resumed
        if resumed is not None:
            self.live = [resumed]

    def part(self, o, i):
        x, z = (o, i) if self.big == "x" else (i, o)
        return self.src.at[x, z, pl.ds(0, 2), pl.ds(self.lo, self.n)]

    def load(self, o, i, y, which):
        if self.staged:
            return self.staged[which][i % 2, y].astype(F32)
        x, z = (o, i) if self.big == "x" else (i, o)
        return self.src[x, z, y, pl.ds(self.lo, self.n), :].astype(F32)

    def send(self, src, dst, axis, by):
        dev = self.p.pair("y") if axis == "y" else self.p.step(axis, by)
        copy = self.c.start(src, dst, dev)
        self.live.append(copy)
        return copy

    def stage(self, s):
        p, big, small = self.p, self.big, self.small
        o, i, y = getattr(p, big), getattr(p, small), p.y
        up, down, across = (o + 1) % 4, (o + 3) % 4, (o + 2) % 4
        iup, idown, iacross = (i + 1) % 4, (i + 3) % 4, (i + 2) % 4
        low, high = pl.ds(0, 2), pl.ds(2, 2)
        if s == 2:
            wait_all(self.first)
        elif s > 2:
            wait_all(self.live)
            self.live = []
        if s == 0:
            for src, dst, by in (
                (self.part(across, low), self.far.at[0], 1), (self.part(across, high), self.far.at[1], 3)
            ):
                self.first.append(self.c.start(src, dst, p.step(big, by)))
            if self.staged:
                self.first.append(self.c.local(self.part(up, low), self.staged[0]))
                self.first.append(self.c.local(self.part(down, high), self.staged[1]))
        elif s == 1:
            self.send(self.part(up, high), self.pos.at[high], big, 1)
            self.send(self.part(down, low), self.neg.at[low], big, 3)
        elif s == 2:

            def fold(k, _):
                b, q = k // 2, k % 2
                self.far[0, b, q] = (self.far[0, b, q].astype(F32) + self.load(up, b, q, 0)).astype(BF16)
                self.far[1, b, q] = (self.far[1, b, q].astype(F32) + self.load(down, b + 2, q, 1)).astype(BF16)
                return 0

            lax.fori_loop(0, 4, fold, 0)
            self.send(self.far.at[0], self.pos.at[low], big, 1)
            self.send(self.far.at[1], self.neg.at[high], big, 3)
            if self.staged:
                self.live.append(self.c.local(self.part(o, low), self.staged[0]))
                self.live.append(self.c.local(self.part(o, high), self.staged[1]))
        elif s == 3:

            def total(k, _):
                b, q = k // 2, k % 2
                for which in range(2):
                    at = b + 2 * which
                    here = self.load(o, at, q, which) + self.pos[at, q].astype(F32) + self.neg[at, q].astype(F32)
                    self.pos[at, q] = here.astype(BF16)
                return 0

            if self.resumed is None:
                lax.fori_loop(0, 4, total, 0)
            if self.stop:
                self.live = [self.c.local(self.pos, self.out)]
                return
            self.first = [
                self.c.start(self.pos.at[iacross, 0], self.far2.at[0], p.step(small, 1)),
                self.c.start(self.pos.at[iacross, 1], self.far2.at[1], p.step(small, 3)),
            ]
            self.send(self.pos.at[iup, 1], self.pos2.at[1], small, 1)
            self.send(self.pos.at[idown, 0], self.neg2.at[0], small, 3)
        elif s == 4:
            wait_all(self.first)
            self.far2[0] = (self.far2[0].astype(F32) + self.pos[iup, 0].astype(F32)).astype(BF16)
            self.far2[1] = (self.far2[1].astype(F32) + self.pos[idown, 1].astype(F32)).astype(BF16)
            self.send(self.far2.at[0], self.pos2.at[0], small, 1)
            self.send(self.far2.at[1], self.neg2.at[1], small, 3)
        elif s == 5:
            for q in range(2):
                here = self.pos[i, q].astype(F32) + self.pos2[q].astype(F32) + self.neg2[q].astype(F32)
                self.pos2[q] = here.astype(BF16)
            self.send(self.pos2.at[1 - y], self.last, "y", 0)
        elif s == 6:
            total = self.pos2[y].astype(F32) + self.last[...].astype(F32)
            self.out[pl.ds(self.lo, self.n), :] = total.astype(self.out.dtype)


class ShardGather:
    def __init__(self, place, copies, full, chunks):
        self.p, self.c, self.full, self.chunks = place, copies, full, chunks
        self.rows = full.shape[1] // chunks
        self.me, self.over = place.yl * 2 + place.co, (1 - place.yl) * 2 + place.co
        self.far, self.near = [], []

    COPIES = 3

    def part(self, who, k):
        return self.full.at[who, pl.ds(k * self.rows, self.rows)]

    def send(self, k, src=None):
        src = self.part(self.me, k) if src is None else src
        self.far.append(self.c.start(src, self.part(self.me, k), self.p.pair("yl")))
        self.near.append(self.c.start(src, self.part(self.me, k), self.p.pair("co")))

    def forward(self, k):
        self.far[k].wait()
        self.near.append(self.c.start(self.part(self.over, k), self.part(self.over, k), self.p.pair("co")))

    def finish(self):
        wait_all(self.near)


class ShardScatter:
    COPIES = 3

    @staticmethod
    def scratch(rows, width):
        return [pltpu.VMEM((rows, width), BF16)] * 3

    def __init__(self, place, copies, part, bufs, chunks):
        self.p, self.c, self.part, self.chunks = place, copies, part, chunks
        self.relay, self.near, self.over = bufs
        self.rows = part.shape[1] // chunks
        self.first, self.second, self.third = [], [], []

    def at(self, k):
        return pl.ds(k * self.rows, self.rows)

    def begin(self):
        self.begin_far()
        self.begin_near()

    def begin_far(self):
        p = self.p
        for k in range(self.chunks):
            src = self.part.at[(1 - p.yl) * 2 + 1 - p.co, self.at(k)]
            self.first.append(self.c.start(src, self.relay.at[self.at(k)], p.pair("co")))

    def begin_near(self):
        p = self.p
        for k in range(self.chunks):
            src = self.part.at[p.yl * 2 + 1 - p.co, self.at(k)]
            self.second.append(self.c.start(src, self.near.at[self.at(k)], p.pair("co")))

    def relay_on(self, k):
        p = self.p
        self.first[k].wait()
        here = self.part[(1 - p.yl) * 2 + p.co, self.at(k), :].astype(F32)
        self.relay[self.at(k), :] = (self.relay[self.at(k), :].astype(F32) + here).astype(BF16)
        self.third.append(self.c.start(self.relay.at[self.at(k)], self.over.at[self.at(k)], p.pair("yl")))

    def total(self, k):
        p = self.p
        self.second[k].wait()
        self.third[k].wait()
        here = self.part[p.yl * 2 + p.co, self.at(k), :].astype(F32)
        return here + self.near[self.at(k), :].astype(F32) + self.over[self.at(k), :].astype(F32)


class GainScatter:
    COPIES = 9
    STAGES = 6

    @staticmethod
    def scratch():
        return [
            pltpu.VMEM((8, 2048), F32),
            pltpu.VMEM((3, 8, 512), F32),
            pltpu.VMEM((8, 512), F32),
            pltpu.VMEM((3, 8, 128), F32),
            pltpu.VMEM((3, 8, 128), F32),
            pltpu.VMEM((3, 8, 128), F32),
        ]

    def __init__(self, place, copies, out, bufs):
        self.p, self.c, self.out = place, copies, out
        self.vec, self.xs, self.mid, self.zs, self.own, self.rest = bufs
        self.live = []

    def stage(self, s):
        p = self.p
        wait_all(self.live)
        self.live = []
        if s == 0:
            for by in (1, 2, 3):
                cols = pl.ds(pl.multiple_of(((p.x + by) % 4) * 512, 512), 512)
                self.live.append(self.c.start(self.vec.at[:, cols], self.xs.at[by - 1], p.step("x", by)))
        elif s == 1:
            cols = pl.ds(pl.multiple_of(p.x * 512, 512), 512)
            self.mid[...] = self.vec[:, cols] + self.xs[0] + self.xs[1] + self.xs[2]
            for by in (1, 2, 3):
                cols = pl.ds(pl.multiple_of(((p.z + by) % 4) * 128, 128), 128)
                self.live.append(self.c.start(self.mid.at[:, cols], self.zs.at[by - 1], p.step("z", by)))
        elif s == 2:
            cols = pl.ds(pl.multiple_of(p.z * 128, 128), 128)
            self.own[0] = self.mid[:, cols] + self.zs[0] + self.zs[1] + self.zs[2]
            self.live.append(self.c.start(self.own.at[0], self.rest.at[0], p.pair("y")))
        elif s == 3:
            self.own[1] = self.own[0] + self.rest[0]
            self.live.append(self.c.start(self.own.at[1], self.rest.at[1], p.pair("co")))
        elif s == 4:
            self.own[2] = self.own[1] + self.rest[1]
            self.live.append(self.c.start(self.own.at[2], self.rest.at[2], p.pair("yl")))
        elif s == 5:
            self.out[...] = self.own[2] + self.rest[2]


def sems(n):
    return [pltpu.SemaphoreType.DMA((n,)), pltpu.SemaphoreType.DMA((n,))]


def params(cid):
    return pltpu.CompilerParams(collective_id=cid, has_side_effects=True, vmem_limit_bytes=VMEM_LIMIT)


def halves(rows):
    return ((0, rows // 2, "x"), (rows // 2, rows // 2, "z"))


CHUNKS = 4


def norm_back_rows(grad, resid, gain):
    factor = lax.rsqrt(jnp.mean(resid * resid, -1, keepdims=True) + EPS)
    weighted = grad * gain
    per_gain = grad * resid * factor
    back = factor * weighted - resid * (factor * factor * factor) * jnp.mean(weighted * resid, -1, keepdims=True)
    return back, per_gain


def eight(rows):
    return jnp.sum(rows.reshape(rows.shape[0] // 8, 8, rows.shape[1]), 0)


KEYS = 256
KB = 4


def lane_iota(rows):
    return lax.broadcasted_iota(jnp.int32, (rows, 128), 1)


def rotate_tile(u, cosine, sine):
    low = lane_iota(u.shape[0]) % HD < HD // 2
    turned = jnp.where(low, -pltpu.roll(u, 128 - HD // 2, 1), pltpu.roll(u, HD // 2, 1))
    return u * cosine + turned * sine


def unrotate_tile(w, cosine, sine):
    low = lane_iota(w.shape[0]) % HD < HD // 2
    s = w * sine
    return w * cosine + jnp.where(low, pltpu.roll(s, 128 - HD // 2, 1), -pltpu.roll(s, HD // 2, 1))


def project_rows(rows, w_qkv, tables):
    lin = jnp.dot(rows, w_qkv, preferred_element_type=F32)
    tiles = []
    for hp in range(4):
        tile = lin[:, hp * 128 : (hp + 1) * 128]
        tiles.append((rotate_tile(tile, tables[0], tables[1])).astype(BF16) * jnp.asarray(HD**-0.5, BF16))
    kv = rotate_tile(lin[:, 512:640], tables[2], tables[3]).astype(BF16)
    return tiles, kv


def head_rows(ref, start, keep_low):
    low = lane_iota(64) < HD
    keep = low if keep_low else ~low
    pieces = []
    for hp in range(4):
        tile = ref[pl.ds(start, 64), hp * 128 : (hp + 1) * 128].astype(F32)
        turned = pltpu.roll(tile, HD, 1)
        even, odd = (tile, turned) if keep_low else (turned, tile)
        pieces += [jnp.where(keep, even, 0.0), jnp.where(keep, odd, 0.0)]
    return pieces


def key_chunk(kv, seq, chunk, half):
    start = pl.multiple_of(seq * 128 + half * 64, 64)
    z = pl.ds((chunk % 2) * 2, 2)
    return kv[chunk // 2, z, :, pl.ds(start, 64), :].reshape(KEYS, 128)


def diagonal(block, here):
    key = lax.broadcasted_iota(jnp.int32, (KEYS, 512), 0)
    query = lax.broadcasted_iota(jnp.int32, (KEYS, 512), 1) % 64
    ahead = key // 64 - here
    return key % 64 - query <= (-ahead if block == 0 else ahead) * 64


def pick(u, own_chunk):
    late = u - 8
    block = jnp.where(u < 8, 1, jnp.where(late >= own_chunk, 1, 0))
    half = jnp.where(u < 8, 0, block)
    chunk = jnp.where(u < 8, u, late + half)
    return block, chunk, half


def nt(a, b):
    return lax.dot_general(a, b, (((1,), (1,)), ((), ())), preferred_element_type=F32)


def tn(a, b):
    return lax.dot_general(a, b, (((0,), (0,)), ((), ())), preferred_element_type=F32)


def attend_seq(seq, ctx, q, kv, attn, lse, scratch):
    qe, top, acc = scratch
    low = lane_iota(64) < HD
    ones_low = lane_iota(KEYS) < HD
    own_chunk, here = ctx // KB, ctx % KB

    def with_ones(keys):
        return jnp.where(ones_low, jnp.ones_like(keys), keys)

    for b in range(2):
        for h, piece in enumerate(head_rows(q, seq * 128 + b * 64, True)):
            qe[b, h * 64 : (h + 1) * 64, :] = piece.astype(BF16)
    for b in range(2):
        keys = key_chunk(kv, seq, own_chunk, b)
        scores = jnp.where(diagonal(b, here), nt(keys, qe[b]), NEG)
        m = jnp.max(scores, 0, keepdims=True)
        p = jnp.exp(scores - m).astype(BF16)
        top[b] = m
        acc[b] = tn(with_ones(keys), p)

    def step(u, _):
        b, chunk, half = pick(u, own_chunk)
        keys = key_chunk(kv, seq, chunk, half)
        scores = nt(keys, qe[b])
        before = top[b]
        m = jnp.maximum(before, jnp.max(scores, 0, keepdims=True))
        p = jnp.exp(scores - m).astype(BF16)
        top[b] = m
        acc[b] = acc[b] * jnp.exp(before - m) + tn(with_ones(keys), p)
        return 0

    for k in range(3):
        lax.fori_loop(5 * k, 5 * k + 5, step, 0, unroll=True)
        if k < 2:
            yield
    for b in range(2):
        here_acc = acc[b]
        total = here_acc[0:1, :]
        lse[pl.ds(seq * 2 + b, 1), :] = top[b] + jnp.log(total)
        out = (here_acc * (1.0 / total)).T
        for hp in range(4):
            even, odd = out[hp * 128 : hp * 128 + 64, :], out[hp * 128 + 64 : hp * 128 + 128, :]
            tile = jnp.where(low, pltpu.roll(even, HD, 1), odd)
            attn[pl.ds(seq * 128 + b * 64, 64), hp * 128 : (hp + 1) * 128] = tile.astype(BF16)


def attend_scratch():
    return [pltpu.VMEM((2, 512, 128), BF16), pltpu.VMEM((2, 1, 512), F32), pltpu.VMEM((2, 128, 512), F32)]


def attend_back_seq(seq, ctx, q, kv, grad, attn, lse, tables, grad_lin, grad_kv, scratch):
    qd, delta, dq, dkv = scratch
    low = lane_iota(64) < HD
    own_chunk, here = ctx // KB, ctx % KB
    for b in range(2):
        start = seq * 128 + b * 64
        q_rows, g_rows, o_rows = (
            head_rows(q, start, True), head_rows(grad, start, False), head_rows(attn, start, False)
        )
        for h in range(8):
            qd[b, h * 64 : (h + 1) * 64, :] = q_rows[h].astype(BF16)
            qd[b, 512 + h * 64 : 512 + (h + 1) * 64, :] = g_rows[h].astype(BF16)
        products = jnp.concatenate([g * o for g, o in zip(g_rows, o_rows)], 0)
        delta[b] = jnp.sum(products.T, 0, keepdims=True)

    def grads(b, keys, allowed):
        both = nt(keys, qd[b])
        p = jnp.exp(both[:, :512] - lse[pl.ds(seq * 2 + b, 1), :])
        if allowed is not None:
            p = jnp.where(allowed, p, 0.0)
        ds = (p * (both[:, 512:] - delta[b])).astype(BF16)
        joined = jnp.concatenate([ds, p.astype(BF16)], 1)
        return tn(keys, ds), jnp.dot(joined, qd[b], preferred_element_type=F32)

    dkv[...] = jnp.zeros_like(dkv)

    def add_keys(chunk, half, value):
        start = pl.multiple_of(half * 64, 64)
        dkv[pl.ds(chunk * KB, KB), pl.ds(start, 64), :] += value.reshape(KB, 64, 128)

    for b in range(2):
        dq_part, dkv_part = grads(b, key_chunk(kv, seq, own_chunk, b), diagonal(b, here))
        dq[b] = dq_part
        add_keys(own_chunk, b, dkv_part)

    def step(u, _):
        b, chunk, half = pick(u, own_chunk)
        dq_part, dkv_part = grads(b, key_chunk(kv, seq, chunk, half), None)
        dq[b] += dq_part
        add_keys(chunk, half, dkv_part)
        return 0

    for k in range(3):
        lax.fori_loop(5 * k, 5 * k + 5, step, 0, unroll=True)
        if k < 2:
            yield
    for b in range(2):
        out = (dq[b] * HD**-0.5).T
        cosine, sine = tables[0, b * 64 : (b + 1) * 64, :], tables[1, b * 64 : (b + 1) * 64, :]
        for hp in range(4):
            even, odd = out[hp * 128 : hp * 128 + 64, :], out[hp * 128 + 64 : hp * 128 + 128, :]
            tile = jnp.where(low, even, pltpu.roll(odd, HD, 1))
            tile = unrotate_tile(tile, cosine, sine)
            grad_lin[pl.ds(seq * 128 + b * 64, 64), hp * 128 : (hp + 1) * 128] = tile.astype(BF16)
    grad_kv[...] = dkv[...].reshape(4, 4, 2, 128, 128).astype(BF16)


def attend_back_scratch():
    return [
        pltpu.VMEM((2, 1024, 128), BF16),
        pltpu.VMEM((2, 1, 512), F32),
        pltpu.VMEM((2, 128, 512), F32),
        pltpu.VMEM((32, 128, 128), F32),
    ]


def ctx_gathers(place, copies, src, full, kind=CtxGather):
    return [kind(place, copies, src, full, lo, rows, big) for lo, rows, big in halves(src.shape[0])]


FORWARD = [
    "w0", "o0", "u0", "d0", "w1", "N1", "CB", "o1", "w2", "d1", "o2", "w3", "g0", "d2", "w4", "NF", "d3", "o3",
    "w5", "NW", "J2", "J3", "k30", "J1", "k10", "k20", "J0", "k00", "d4", "k31", "k01", "k11", "k02", "o4", "k21",
    "u1", "k22", "k32", "k12", "g1", "k03", "k23", "o5", "k13", "g2", "k04", "k33", "u2", "k34", "k14", "k24", "g3",
    "k05", "A00", "A01", "A02", "OP0", "k15", "RF", "k25", "A10", "k35", "A11", "u3", "A12", "OP1", "A20", "CF",
    "RR", "A21", "A22", "A30", "A31", "OP2", "RN", "A32", "OP3", "g4", "NT", "u4", "d5", "CW", "DA", "SF", "SW",
    "g5", "u5", "FU", "P2", "XB", "RP", "GD", "e0", "e1", "XN", "XR", "e2", "XT", "GU", "GG", "XF", "e3", "XW",
]

BACKWARD = [
    "u0", "DO", "g0", "RESB", "d3", "DP", "A00", "A01", "A02", "g1", "k00", "A10", "A11", "A12", "k01", "A20",
    "k10", "k11", "g2", "A21", "k02", "A22", "A30", "k12", "k20", "u1", "A31", "A32", "k03", "RESR", "k13", "d4",
    "k21", "k30", "k31", "GO", "k32", "k04", "k22", "RES", "k14", "o0", "k23", "k33", "k15", "u2", "k05", "k16",
    "I1", "k34", "k24", "g3", "k35", "k06", "o1", "k25", "I0", "u3", "k26", "I2", "g4", "k36", "I3", "QG", "o2",
    "d5", "q0", "q1", "g5", "TOT", "n0", "q2", "d6", "n1", "u4", "o3", "n2", "q3", "u5", "n3", "o4", "n4", "q4",
    "o5", "q5", "o6", "g6", "u6", "n5", "q6",
]


def run_steps(steps, engines, actions):
    for step in steps:
        if step in actions:
            actions[step]()
        else:
            for e in engines[step[:-1]]:
                e.stage(int(step[-1]))


def gain_row(ref):
    gain = ref[...].astype(F32)
    return jnp.concatenate([gain[k : k + 1, :] for k in range(16)], 1)


def over_hidden_units(tile):
    for start, width in ((0, 512), (512, 512), (1024, 384)):
        tile(pl.ds(start, width), width)


def over_width(step):
    def one(j, _):
        step(j, pl.ds(pl.multiple_of(j * 512, 512), 512))
        return 0

    lax.fori_loop(0, 4, one, 0)


def forward_kernel(
    x, cot, gain1, gain2, tables, wq, wk, wv, w_out_shard, w_gate_shard, w_up_shard, w_down_shard,
    normed1_out, w_qkv_out, w_out_out, q, kv_out, attn, lse, hidden, branch_out, grad_hidden, grad_gain,
    result_out, g_gate_out, g_up_out, g_down_x, g_down_z,
    normed1_all, w_qkv_shard, w_qkv, w_out, kv_all, part, relay, near, over, qe, top, acc,
    w_gate, w_up, w_down, cot_all, normed2_all, gate_pre, up_pre, grad_active, active, grad_gate, grad_up, result_part, branch,
    *rest,
):
    bufs, (send, recv) = rest[:14], rest[14:]
    place = Place()
    greet(place.ctx_peers() + place.shard_peers())
    copies = Copies(send, recv)
    ctx = lax.axis_index("ctx")
    order = [2 * (1 - place.yl) + 1 - place.co, 2 * (1 - place.yl) + place.co]
    order += [2 * place.yl + 1 - place.co, 2 * place.yl + place.co]
    starts = [pl.multiple_of(seq * 128, 128) for seq in order]
    engines = {
        "w": ctx_gathers(place, copies, w_qkv_shard, w_qkv),
        "o": ctx_gathers(place, copies, w_out_shard, w_out),
        "g": ctx_gathers(place, copies, w_gate_shard, w_gate),
        "u": ctx_gathers(place, copies, w_up_shard, w_up),
        "d": ctx_gathers(place, copies, w_down_shard, w_down, CtxGatherLate),
    }
    for k in range(4):
        engines[f"k{k}"] = [CtxGather(place, copies, None, kv_all, starts[k], 128, "xz"[k % 2])]
    normed = ShardGather(place, copies, normed1_all, 1)
    cots = ShardGather(place, copies, cot_all, 1)
    rows_out = ShardScatter(place, copies, part, (relay, near, over), CHUNKS)
    spread = ShardGather(place, copies, normed2_all, CHUNKS)
    thirds = [attend_seq(seq, ctx, q, kv_all, attn, lse, (qe, top, acc)) for seq in order]
    back = ShardScatter(place, copies, part, (relay, near, over), CHUNKS)
    branches = ShardGather(place, copies, branch, CHUNKS)
    engines["e"] = [
        CtxScatter(place, copies, w_down, out, bufs[7 * h : 7 * h + 7], lo, rows, big, stop=True)
        for h, (out, (lo, rows, big)) in enumerate(zip((g_down_x, g_down_z), halves(64)))
    ]
    outgoing = []
    w_qkv_shard[:, :512] = wq[...]
    w_qkv_shard[:, 512:640] = jnp.concatenate([wk[...], wv[...]], 1)

    def first_norm():
        rows = x[...].astype(F32)
        factor = lax.rsqrt(jnp.mean(rows * rows, -1, keepdims=True) + EPS)
        normed1_all[normed.me] = (rows * factor * gain_row(gain1)).astype(BF16)
        normed.send(0)

    def normed_here():
        normed.finish()
        outgoing.append(copies.local(normed1_all, normed1_out))

    def project_seq(k):
        at = pl.ds(starts[k], 128)
        tiles, kv = project_rows(normed1_all[order[k]], w_qkv[...].reshape(2048, 640), tables)
        for hp, tile in enumerate(tiles):
            q[at, hp * 128 : (hp + 1) * 128] = tile
        kv_all[place.x, place.z, place.y, at, :] = kv

    own_cot = []

    def send_cot():
        cots.send(0, cot)
        own_cot.append(copies.local(cot, cot_all.at[cots.me]))

    def cot_here():
        cots.finish()
        wait_all(own_cot)

    def project_out(k):
        part[order[k]] = nt(attn[pl.ds(starts[k], 128), :], w_out[...].reshape(2048, 512)).astype(BF16)

    def relay_rows():
        for c in range(CHUNKS):
            rows_out.relay_on(c)

    def second_norm():
        outgoing.extend(copies.local(*pair) for pair in ((w_qkv, w_qkv_out), (w_out, w_out_out), (kv_all, kv_out)))
        gain = gain_row(gain2)
        for c in range(CHUNKS):
            at = rows_out.at(c)
            here = x[at, :].astype(F32) + rows_out.total(c)
            hidden[at, :] = here
            factor = lax.rsqrt(jnp.mean(here * here, -1, keepdims=True) + EPS)
            normed2_all[spread.me, at, :] = (here * factor * gain).astype(BF16)
            spread.send(c)

    def spread_on():
        for c in range(CHUNKS):
            spread.forward(c)

    def columns_of(w, cols, width):
        return w[:, :, :, :, cols].reshape(2048, width)

    def grad_active_tiles():
        def tile(cols, width):
            rows = cot_all[...].reshape(512, 2048)
            grad_active[:, cols] = jnp.dot(rows, columns_of(w_down, cols, width), preferred_element_type=F32)

        over_hidden_units(tile)

    def hidden_units():
        def tile(cols, width):
            rows = normed2_all[...].reshape(512, 2048)
            here = pl.ds(0, width)
            gate_pre[:, here] = jnp.dot(rows, columns_of(w_gate, cols, width), preferred_element_type=F32)
            up_pre[:, here] = jnp.dot(rows, columns_of(w_up, cols, width), preferred_element_type=F32)

            def some(r, _):
                at = pl.ds(pl.multiple_of(r * 64, 64), 64)
                gate, up, grad = gate_pre[at, here], up_pre[at, here], grad_active[at, cols]
                sigmoid = 1.0 / (1.0 + jnp.exp(-gate))
                silu = gate * sigmoid
                active[at, cols] = (silu * up).astype(BF16)
                grad_gate[at, cols] = (grad * up * sigmoid * (1.0 + gate * (1.0 - sigmoid))).astype(BF16)
                grad_up[at, cols] = (grad * silu).astype(BF16)
                return 0

            lax.fori_loop(0, 8, some, 0)

        over_hidden_units(tile)

    def result_tiles():
        def step(j, cols):
            rows = nt(active[...], w_down[j].reshape(512, 1408))
            result_part[:, :, cols] = rows.astype(BF16).reshape(4, 128, 512)

        over_width(step)
        outgoing.append(copies.local(result_part, result_out))

    def grad_normed_tiles():
        def step(j, cols):
            rows = nt(grad_gate[...], w_gate[j].reshape(512, 1408)) + nt(grad_up[...], w_up[j].reshape(512, 1408))
            part[:, :, cols] = rows.astype(BF16).reshape(4, 128, 512)

        over_width(step)

    def weight_grad(left, right, w):
        def step(j, cols):
            block = tn(left[:, :, cols].reshape(512, 512), right[...])
            w[j] = block.astype(BF16).reshape(4, 2, 64, 1408)

        over_width(step)

    def gate_grad():
        weight_grad(normed2_all, grad_gate, w_gate)
        outgoing.append(copies.local(w_gate, g_gate_out))

    def up_grad():
        weight_grad(normed2_all, grad_up, w_up)
        outgoing.append(copies.local(w_up, g_up_out))

    def relay_back():
        for c in range(CHUNKS):
            back.relay_on(c)

    def second_norm_back():
        gain = gain_row(gain2)
        for c in range(CHUNKS):
            at = back.at(c)
            grad, per_gain = norm_back_rows(back.total(c), hidden[at, :], gain)
            here = cot_all[branches.me, at, :].astype(F32) + grad
            grad_hidden[at, :] = here
            branch[branches.me, at, :] = here.astype(BF16)
            branches.send(c)
            grad_gain[...] = eight(per_gain) if c == 0 else grad_gain[...] + eight(per_gain)

    def branch_on():
        for c in range(CHUNKS):
            branches.forward(c)

    def branch_here():
        branches.finish()
        outgoing.append(copies.local(branch, branch_out))

    actions = {
        "N1": first_norm, "NF": lambda: normed.forward(0), "NW": normed_here,
        "CB": send_cot, "CF": lambda: cots.forward(0), "CW": cot_here,
        "RF": rows_out.begin_far, "RR": relay_rows, "RN": rows_out.begin_near,
        "NT": second_norm, "SF": spread_on, "SW": spread.finish,
        "DA": grad_active_tiles, "FU": hidden_units, "RP": result_tiles, "P2": grad_normed_tiles,
        "GD": lambda: weight_grad(cot_all, active, w_down), "GG": gate_grad, "GU": up_grad,
        "XB": back.begin_far, "XN": back.begin_near, "XR": relay_back, "XT": second_norm_back,
        "XF": branch_on, "XW": branch_here,
    }
    for k in range(4):
        actions[f"J{k}"] = partial(project_seq, k)
        actions[f"OP{k}"] = partial(project_out, k)
        for third in range(3):
            actions[f"A{k}{third}"] = partial(next, thirds[k], None)
    run_steps(FORWARD, engines, actions)
    wait_all(outgoing + [copy for e in engines["e"] for copy in e.live])


def forward(cid, x, cot, gain1, gain2, tables, w_qkv, shards):
    tokens, width = x.shape
    every = (4, tokens, width)
    ffn_width = shards[1].shape[1]

    def full(n):
        return (4, 4, 2, 64, n)

    kv_all, totals = (4, 4, 2, 512, 128), (4, 2, 32, ffn_width)
    outs = [
        (ANY, every, BF16), (ANY, full(640), BF16), (ANY, full(512), BF16), (VMEM, (512, 512), BF16),
        (ANY, kv_all, BF16), (VMEM, (512, 512), BF16), (VMEM, (8, 512), F32), (VMEM, (tokens, width), F32),
        (ANY, every, BF16), (VMEM, (tokens, width), F32), (VMEM, (8, width), F32), (ANY, every, BF16),
        (ANY, full(ffn_width), BF16), (ANY, full(ffn_width), BF16), (ANY, totals, BF16), (ANY, totals, BF16),
    ]
    return pl.pallas_call(
        forward_kernel,
        out_shape=[jax.ShapeDtypeStruct(shape, dtype) for _, shape, dtype in outs],
        in_specs=[VMEM, ANY, VMEM, VMEM, VMEM, VMEM, VMEM, VMEM] + [ANY] * 4,
        out_specs=[space for space, _, _ in outs],
        scratch_shapes=[
            pltpu.VMEM(every, BF16),
            pltpu.VMEM((64, 640), BF16),
            pltpu.VMEM(full(640), BF16),
            pltpu.VMEM(full(512), BF16),
            pltpu.VMEM(kv_all, BF16),
            pltpu.VMEM(every, BF16),
            *ShardScatter.scratch(tokens, width),
            *attend_scratch(),
            *[pltpu.VMEM(full(ffn_width), BF16)] * 3,
            pltpu.VMEM(every, BF16),
            pltpu.VMEM(every, BF16),
            *[pltpu.VMEM((512, 512), F32)] * 2,
            pltpu.VMEM((512, ffn_width), F32),
            *[pltpu.VMEM((512, ffn_width), BF16)] * 3,
            pltpu.VMEM(every, BF16),
            pltpu.VMEM(every, BF16),
            *CtxScatter.scratch(32, ffn_width),
            *CtxScatter.scratch(32, ffn_width),
            *sems(14 * CtxGather.COPIES + 2 * CtxScatter.COPIES + 12 * CHUNKS + 24),
        ],
        compiler_params=params(cid),
        name="forward",
    )(x, cot, gain1.reshape(16, 128), gain2.reshape(16, 128), tables, *w_qkv, *shards)


def backward_kernel(*refs):
    (
        branch_in, result_in, w_out_in, w_qkv_in, normed_in, g_gate, g_up, g_down_x, g_down_z,
        hidden, grad_hidden, grad_gain, q, kv, attn, lse, tables, x, gain1,
    ) = refs[:19]
    grad_inputs, gains, outputs, out_q, out_kv, out_o, out_gate, out_up, out_down = refs[19:28]
    normed, result_part, w_out, w_qkv, branch, dkv_send, relay, near, over = refs[28:37]
    grad_lin, grad_kv, out_qkv = refs[37:40]
    scratch, gain_bufs, bufs, (free, send, recv) = refs[40:44], refs[44:50], refs[50:-3], refs[-3:]
    place = Place()
    greet(place.ctx_peers() + place.shard_peers() + place.far_peers())
    copies = Copies(send, recv)
    ctx = lax.axis_index("ctx")
    me, co = 2 * place.yl + place.co, 2 * place.yl + 1 - place.co
    far, far_co = 2 * (1 - place.yl) + place.co, 2 * (1 - place.yl) + 1 - place.co
    order = [me, far_co, far, co]
    taken = 0

    def take(n):
        nonlocal taken
        taken += n
        return bufs[taken - n : taken]

    def rows_of(seq):
        return pl.ds(pl.multiple_of(seq * 128, 128), 128)

    engines = {}
    for name, src, out, count in (
        ("g", g_gate, out_gate, 9), ("u", g_up, out_up, 9),
        ("o", w_out, out_o, 7), ("q", w_qkv, out_qkv, 7),
    ):
        engines[name] = [
            CtxScatter(place, copies, src, out, take(count), lo, rows, big) for lo, rows, big in halves(64)
        ]
    for k in range(4):
        engines[f"k{k}"] = [
            CtxScatter(place, copies, dkv_send.at[k], grad_kv.at[rows_of(order[k])], take(7), 0, 128, "xz"[k % 2])
        ]
    engines["d"] = []
    for (lo, rows, big), totals in zip(halves(64), (g_down_x, g_down_z)):
        pos, far2, pos2, neg2, last = take(5)
        load = copies.local(totals, pos)
        engines["d"].append(
            CtxScatter(
                place, copies, None, out_down, (None, pos, None, far2, pos2, neg2, last), lo, rows, big, resumed=load
            )
        )
    gain_sum = GainScatter(place, copies, gains, gain_bufs)
    engines["n"] = [gain_sum]
    loads = [copies.local(a, b) for a, b in (
        (branch_in, branch), (w_out_in, w_out), (result_in, result_part), (w_qkv_in, w_qkv), (normed_in, normed)
    )]
    result = ShardScatter(place, copies, result_part, (relay, near, over), 1)
    last = ShardScatter(place, copies, branch, (relay, near, over), CHUNKS)
    thirds = [
        attend_back_seq(
            order[k], ctx, q, kv, grad_lin, attn, lse, tables, grad_lin, dkv_send.at[k], scratch
        )
        for k in range(4)
    ]

    def relay_rows(rows_scatter):
        for c in range(CHUNKS):
            rows_scatter.relay_on(c)

    def grad_rows(seq):
        w = w_out[...].reshape(2048, 512)
        grad_lin[rows_of(seq), :512] = jnp.dot(branch[seq], w, preferred_element_type=F32).astype(BF16)

    def grad_mixed_own():
        wait_all(loads[:2])
        grad_rows(me)

    def grad_mixed():
        for seq in order[1:]:
            grad_rows(seq)

    def begin_result():
        loads[2].wait()
        result.begin()

    def grad_of_out():
        rows = branch[...].reshape(512, 2048)
        for j in range(8):
            block = tn(rows[:, j * 256 : (j + 1) * 256], attn[...]).astype(BF16)
            w_out[j // 2, pl.ds((j % 2) * 2, 2)] = block.reshape(2, 2, 64, 512)

    def result_rows():
        outputs[...] = (hidden[...] + result.total(0)).astype(BF16)
        for device in place.shard_peers():
            pl.semaphore_signal(free, inc=1, device_id=device, device_id_type=MESH)

    def input_rows(k):
        if k == FIRST_INPUT_ROWS:
            loads[3].wait()
        at = rows_of(order[k])
        grad_lin[at, 512:640] = unrotate_tile(grad_kv[at, :], tables[2], tables[3]).astype(BF16)
        branch[order[k]] = nt(grad_lin[at, :], w_qkv[...].reshape(2048, 640)).astype(BF16)
        if k == 1:
            pl.semaphore_wait(free, 2)
            last.begin_far()
        elif k == 2:
            relay_rows(last)
        elif k == 3:
            last.begin_near()

    def grad_of_qkv():
        loads[4].wait()
        rows = normed[...].reshape(512, 2048)
        for j in range(8):
            block = tn(rows[:, j * 256 : (j + 1) * 256], grad_lin[...]).astype(BF16)
            w_qkv[j // 2, pl.ds((j % 2) * 2, 2)] = block.reshape(2, 2, 64, 640)

    def first_norm_back():
        gain = gain_row(gain1)
        for c in range(CHUNKS):
            rows = last.at(c)
            back, per_gain = norm_back_rows(last.total(c), x[rows, :].astype(F32), gain)
            grad_inputs[rows, :] = (grad_hidden[rows, :] + back).astype(BF16)
            total = eight(per_gain) if c == 0 else total + eight(per_gain)
        row = lax.broadcasted_iota(jnp.int32, total.shape, 0)
        one, two = jnp.sum(total, 0, keepdims=True), jnp.sum(grad_gain[...], 0, keepdims=True)
        gain_sum.vec[...] = jnp.where(row == 0, one, jnp.where(row == 1, two, 0.0))

    actions = {
        "DO": grad_mixed_own, "DP": grad_mixed, "GO": grad_of_out, "RESB": begin_result,
        "RESR": lambda: result.relay_on(0), "RES": result_rows, "QG": grad_of_qkv, "TOT": first_norm_back,
    }
    for k in range(4):
        actions[f"I{k}"] = partial(input_rows, k)
        for third in range(3):
            actions[f"A{k}{third}"] = partial(next, thirds[k], None)
    run_steps(BACKWARD, engines, actions)
    out_q[...] = out_qkv[:, :512]
    out_kv[...] = out_qkv[:, 512:]


def backward(cid, in_hbm, in_vmem):
    hidden = in_vmem[0]
    tokens, width = hidden.shape
    ffn_width = in_hbm[5].shape[4]
    in_vmem = [a.reshape(16, 128) if a.ndim == 1 else a for a in in_vmem]
    scratch = []
    for _ in range(4):
        scratch += CtxScatter.scratch(32, ffn_width, True)
    for _ in range(2):
        scratch += CtxScatter.scratch(32, 512)
    for _ in range(2):
        scratch += CtxScatter.scratch(32, 640)
    for _ in range(4):
        scratch += CtxScatter.scratch(128, 128)
    for _ in range(2):
        whole = CtxScatter.scratch(32, ffn_width)
        scratch += whole[1:2] + whole[3:]
    shapes = [
        ((tokens, width), BF16), ((8, 128), F32), ((tokens, width), BF16), ((64, 512), F32), ((64, 128), F32),
        ((64, 512), F32), ((64, ffn_width), F32), ((64, ffn_width), F32), ((64, ffn_width), F32),
    ]
    return pl.pallas_call(
        backward_kernel,
        out_shape=[jax.ShapeDtypeStruct(*shape) for shape in shapes],
        in_specs=[ANY] * len(in_hbm) + [VMEM] * len(in_vmem),
        out_specs=[VMEM] * len(shapes),
        scratch_shapes=[
            pltpu.VMEM((4, tokens, width), BF16),
            pltpu.VMEM((4, tokens, width), BF16),
            pltpu.VMEM((4, 4, 2, 64, 512), BF16),
            pltpu.VMEM((4, 4, 2, 64, 640), BF16),
            pltpu.VMEM((4, tokens, width), BF16),
            pltpu.VMEM((4, 4, 4, 2, 128, 128), BF16),
            *ShardScatter.scratch(tokens, width),
            pltpu.VMEM((512, 640), BF16),
            pltpu.VMEM((512, 128), F32),
            pltpu.VMEM((64, 640), F32),
            *attend_back_scratch(),
            *GainScatter.scratch(),
            *scratch,
            pltpu.SemaphoreType.REGULAR,
            *sems(14 * CtxScatter.COPIES + 6 * CHUNKS + GainScatter.COPIES + 12),
        ],
        compiler_params=params(cid),
        name="backward",
    )(*in_hbm, *in_vmem)


FIRST_INPUT_ROWS = int([step for step in BACKWARD if step[0] == "I"][0][1])


def finish_kernel(grad_in, out_in, g_query, g_kv, g_out, g_gate, g_up, g_down, *outs):
    grad_inputs, outputs, query, key, value, out, gate, up, down = outs
    grad_inputs[...] = grad_in[...]
    outputs[...] = out_in[...]
    query[...] = g_query[...]
    key[...] = g_kv[:, :HD]
    value[...] = g_kv[:, HD:]
    out[...] = g_out[...].T
    gate[...] = g_gate[...]
    up[...] = g_up[...]
    down[...] = g_down[...].T


def finish(*arrays):
    ffn_width = arrays[5].shape[1]
    shapes = [(a.shape, a.dtype) for a in arrays[:3]]
    shapes += [((64, HD), F32)] * 2 + [((512, 64), F32), ((64, ffn_width), F32), ((64, ffn_width), F32)]
    shapes += [((ffn_width, 64), F32)]
    return pl.pallas_call(
        finish_kernel,
        out_shape=[jax.ShapeDtypeStruct(*shape) for shape in shapes],
        in_specs=[VMEM] * len(arrays),
        out_specs=[VMEM] * len(shapes),
        compiler_params=pltpu.CompilerParams(vmem_limit_bytes=VMEM_LIMIT),
        name="finish",
    )(*arrays)


def rope_tables(positions):
    freqs = 10000.0 ** (-jnp.arange(HD // 2, dtype=F32) * 2.0 / HD)
    angles = positions[:, None] * freqs[None]
    cosine, sine = jnp.cos(angles), jnp.sin(angles)
    one, zero = jnp.ones_like(cosine), jnp.zeros_like(cosine)
    return jnp.stack(
        [
            jnp.concatenate([cosine] * 4, -1),
            jnp.concatenate([sine] * 4, -1),
            jnp.concatenate([cosine, cosine, one, one], -1),
            jnp.concatenate([sine, sine, zero, zero], -1),
        ]
    )


def per_device(
    inputs, cotangent, norm_attn, w_query, w_key, w_value, w_out, norm_mlp, w_gate, w_up, w_down
):
    width = inputs.shape[-1]
    half_len = inputs.shape[2]
    tokens = 2 * half_len
    ctx_count = lax.axis_size("ctx")
    ctx_index = lax.axis_index("ctx")
    length = tokens * ctx_count
    x = inputs.reshape(tokens, width)
    cot = cotangent.reshape(tokens, width)
    rows_local = jnp.arange(tokens)
    positions = jnp.where(
        rows_local < half_len,
        ctx_index * half_len + rows_local,
        length - (ctx_index + 1) * half_len + (rows_local - half_len),
    ).astype(F32)
    tables = rope_tables(positions)

    (
        normed_all, w_qkv, w_out_t, q, kv_all, attn, lse, hidden, branch_all, grad_hidden, gain2_part, result_part,
        g_gate, g_up, g_down_x, g_down_z,
    ) = forward(
        0, x, cot, norm_attn, norm_mlp, tables, [w_query, w_key, w_value], [w_out.T, w_gate, w_up, w_down.T]
    )
    grad_inputs, gains, outputs, g_query, g_kv, g_out, g_gate, g_up, g_down = backward(
        1,
        [branch_all, result_part, w_out_t, w_qkv, normed_all, g_gate, g_up, g_down_x, g_down_z],
        [hidden, grad_hidden, gain2_part, q, kv_all, attn, lse, tables, x, norm_attn],
    )
    grad_inputs, outputs, g_query, g_key, g_value, g_out, g_gate, g_up, g_down = finish(
        grad_inputs, outputs, g_query, g_kv, g_out, g_gate, g_up, g_down
    )
    start = (ctx_index % 2) * 64 + lax.axis_index("wshard") * 16
    gains = lax.dynamic_slice_in_dim(gains, start, 16, axis=1)
    return (
        outputs.reshape(inputs.shape),
        grad_inputs.reshape(inputs.shape),
        gains[0],
        g_query,
        g_key,
        g_value,
        g_out,
        gains[1],
        g_gate,
        g_up,
        g_down,
    )


def solution(mesh):
    return jax.shard_map(
        per_device,
        mesh=mesh,
        in_specs=(
            P("wshard", None, "ctx", None),
            P("wshard", None, "ctx", None),
            P(),
            P("ctx", "wshard"),
            P("ctx", "wshard"),
            P("ctx", "wshard"),
            P("wshard", "ctx"),
            P(),
            P("ctx", "wshard"),
            P("ctx", "wshard"),
            P("wshard", "ctx"),
        ),
        out_specs=(
            P("wshard", None, "ctx", None),
            P("wshard", None, "ctx", None),
            P(("ctx", "wshard")),
            P("ctx", "wshard"),
            P("ctx", "wshard"),
            P("ctx", "wshard"),
            P("wshard", "ctx"),
            P(("ctx", "wshard")),
            P("ctx", "wshard"),
            P("ctx", "wshard"),
            P("wshard", "ctx"),
        ),
        check_vma=False,
    )
```

```python
from functools import partial

import jax
import jax.numpy as jnp
from jax import lax
from jax.experimental import pallas as pl
from jax.experimental.pallas import tpu as pltpu
from jax.sharding import PartitionSpec as P

MESH = pl.DeviceIdType.MESH
HD = 64
EPS = 1e-05
NEG = -1e30
F32 = jnp.float32
BF16 = jnp.bfloat16
VMEM_LIMIT = 63 * 2**20
ANY = pl.BlockSpec(memory_space=pl.ANY)
VMEM = pl.BlockSpec(memory_space=pltpu.VMEM)


class Place:
    def __init__(self):
        ctx, shard = lax.axis_index("ctx"), lax.axis_index("wshard")
        self.x, self.z, self.y = ctx // 8, (ctx // 2) % 4, ctx % 2
        self.yl, self.co = shard // 2, shard % 2

    def at(self, x=None, z=None, y=None, yl=None, co=None):
        x, z, y = (self.x if x is None else x), (self.z if z is None else z), (self.y if y is None else y)
        yl, co = (self.yl if yl is None else yl), (self.co if co is None else co)
        return (x * 8 + z * 2 + y, yl * 2 + co)

    def step(self, axis, by):
        return self.at(**{axis: (getattr(self, axis) + by) % 4})

    def pair(self, axis):
        return self.at(**{axis: 1 - getattr(self, axis)})

    def ctx_peers(self):
        return [self.step("x", 1), self.step("x", 3), self.step("z", 1), self.step("z", 3), self.pair("y")]

    def shard_peers(self):
        return [self.pair("co"), self.pair("yl")]

    def far_peers(self):
        return [self.step("x", 2), self.step("z", 2)]


def greet(peers):
    barrier = pltpu.get_barrier_semaphore()
    for device in peers:
        pl.semaphore_signal(barrier, inc=1, device_id=device, device_id_type=MESH)
    pl.semaphore_wait(barrier, len(peers))


class Copies:
    def __init__(self, send, recv):
        self.send, self.recv, self.used = send, recv, 0

    def start(self, src, dst, device):
        k = self.used
        self.used += 1
        copy = pltpu.make_async_remote_copy(
            src_ref=src, dst_ref=dst, send_sem=self.send.at[k], recv_sem=self.recv.at[k],
            device_id=device, device_id_type=MESH,
        )
        copy.start()
        return copy

    def local(self, src, dst):
        k = self.used
        self.used += 1
        copy = pltpu.make_async_copy(src, dst, self.send.at[k])
        copy.start()
        return copy


def wait_all(copies):
    for copy in copies:
        copy.wait()


class CtxGather:
    COPIES = 10
    STAGES = 6

    def __init__(self, place, copies, shard, full, lo, n, big):
        self.p, self.c, self.shard, self.full = place, copies, shard, full
        self.lo, self.n, self.big, self.small = lo, n, big, ("z" if big == "x" else "x")
        self.live = []

    def block(self, o, i, y):
        x, z = (o, i) if self.big == "x" else (i, o)
        return self.full.at[x, z, y, pl.ds(self.lo, self.n)]

    def send(self, part, axis, by):
        dev = self.p.pair("y") if axis == "y" else self.p.step(axis, by)
        self.live.append(self.c.start(part, part, dev))

    def stage(self, s):
        p = self.p
        o, i, y = getattr(p, self.big), getattr(p, self.small), p.y
        wait_all(self.live)
        self.live = []
        every, both = pl.ds(0, 4), pl.ds(0, 2)
        if s == 0 and self.shard is None:
            self.send(self.block(o, i, y), "y", 0)
        elif s == 0:
            own = self.shard.at[pl.ds(self.lo, self.n)]
            self.live.append(self.c.start(own, self.block(o, i, y), p.pair("y")))
            self.live.append(self.c.local(own, self.block(o, i, y)))
        elif s == 1:
            self.send(self.block(o, i, both), self.small, 1)
            self.send(self.block(o, i, both), self.small, 3)
        elif s == 2:
            self.send(self.block(o, (i + 3) % 4, 0), self.small, 1)
            self.send(self.block(o, (i + 1) % 4, 1), self.small, 3)
        elif s == 3:
            self.send(self.block(o, every, both), self.big, 1)
            self.send(self.block(o, every, both), self.big, 3)
        elif s == 4:
            self.send(self.block((o + 3) % 4, pl.ds(0, 2), both), self.big, 1)
            self.send(self.block((o + 1) % 4, pl.ds(2, 2), both), self.big, 3)


class CtxGatherLate(CtxGather):
    def block(self, o, i, y, lo=None, n=None):
        x, z = (o, i) if self.big == "x" else (i, o)
        return self.full.at[x, z, y, pl.ds(self.lo if lo is None else lo, self.n if n is None else n)]

    def stage(self, s):
        p = self.p
        o, i, y = getattr(p, self.big), getattr(p, self.small), p.y
        wait_all(self.live)
        self.live = []
        every, half = pl.ds(0, 4), self.n // 2
        if s == 0:
            own = self.shard.at[pl.ds(self.lo, self.n)]
            for by in (1, 3):
                self.live.append(self.c.start(own, self.block(o, i, y), p.step(self.big, by)))
            self.live.append(self.c.local(own, self.block(o, i, y)))
        elif s == 1:
            self.send(self.block((o + 3) % 4, i, y, self.lo, half), self.big, 1)
            self.send(self.block((o + 1) % 4, i, y, self.lo + half, half), self.big, 3)
        elif s == 2:
            self.send(self.block(every, i, y), self.small, 1)
            self.send(self.block(every, i, y), self.small, 3)
        elif s == 3:
            self.send(self.block(pl.ds(0, 2), (i + 3) % 4, y), self.small, 1)
            self.send(self.block(pl.ds(2, 2), (i + 1) % 4, y), self.small, 3)
        elif s == 4:
            self.send(self.block(every, every, y), "y", 0)


class CtxScatter:
    COPIES = 17
    STAGES = 7

    @staticmethod
    def scratch(n, width, staged=False):
        shapes = [(2, 2, 2), (4, 2), (4, 2), (2,), (2,), (2,), ()]
        if staged:
            shapes += [(2, 2), (2, 2)]
        return [pltpu.VMEM(shape + (n, width), BF16) for shape in shapes]

    def __init__(self, place, copies, src, out, bufs, lo, n, big, stop=False, resumed=None):
        self.p, self.c, self.src, self.out = place, copies, src, out
        self.far, self.pos, self.neg, self.far2, self.pos2, self.neg2, self.last = bufs[:7]
        self.staged = bufs[7:]
        self.lo, self.n, self.big, self.small = lo, n, big, ("z" if big == "x" else "x")
        self.first, self.live = [], []
        self.stop, self.resumed = stop, resumed
        if resumed is not None:
            self.live = [resumed]

    def part(self, o, i):
        x, z = (o, i) if self.big == "x" else (i, o)
        return self.src.at[x, z, pl.ds(0, 2), pl.ds(self.lo, self.n)]

    def load(self, o, i, y, which):
        if self.staged:
            return self.staged[which][i % 2, y].astype(F32)
        x, z = (o, i) if self.big == "x" else (i, o)
        return self.src[x, z, y, pl.ds(self.lo, self.n), :].astype(F32)

    def send(self, src, dst, axis, by):
        dev = self.p.pair("y") if axis == "y" else self.p.step(axis, by)
        copy = self.c.start(src, dst, dev)
        self.live.append(copy)
        return copy

    def stage(self, s):
        p, big, small = self.p, self.big, self.small
        o, i, y = getattr(p, big), getattr(p, small), p.y
        up, down, across = (o + 1) % 4, (o + 3) % 4, (o + 2) % 4
        iup, idown, iacross = (i + 1) % 4, (i + 3) % 4, (i + 2) % 4
        low, high = pl.ds(0, 2), pl.ds(2, 2)
        if s == 2:
            wait_all(self.first)
        elif s > 2:
            wait_all(self.live)
            self.live = []
        if s == 0:
            for src, dst, by in (
                (self.part(across, low), self.far.at[0], 1), (self.part(across, high), self.far.at[1], 3)
            ):
                self.first.append(self.c.start(src, dst, p.step(big, by)))
            if self.staged:
                self.first.append(self.c.local(self.part(up, low), self.staged[0]))
                self.first.append(self.c.local(self.part(down, high), self.staged[1]))
        elif s == 1:
            self.send(self.part(up, high), self.pos.at[high], big, 1)
            self.send(self.part(down, low), self.neg.at[low], big, 3)
        elif s == 2:

            def fold(k, _):
                b, q = k // 2, k % 2
                self.far[0, b, q] = (self.far[0, b, q].astype(F32) + self.load(up, b, q, 0)).astype(BF16)
                self.far[1, b, q] = (self.far[1, b, q].astype(F32) + self.load(down, b + 2, q, 1)).astype(BF16)
                return 0

            lax.fori_loop(0, 4, fold, 0)
            self.send(self.far.at[0], self.pos.at[low], big, 1)
            self.send(self.far.at[1], self.neg.at[high], big, 3)
            if self.staged:
                self.live.append(self.c.local(self.part(o, low), self.staged[0]))
                self.live.append(self.c.local(self.part(o, high), self.staged[1]))
        elif s == 3:

            def total(k, _):
                b, q = k // 2, k % 2
                for which in range(2):
                    at = b + 2 * which
                    here = self.load(o, at, q, which) + self.pos[at, q].astype(F32) + self.neg[at, q].astype(F32)
                    self.pos[at, q] = here.astype(BF16)
                return 0

            if self.resumed is None:
                lax.fori_loop(0, 4, total, 0)
            if self.stop:
                self.live = [self.c.local(self.pos, self.out)]
                return
            self.first = [
                self.c.start(self.pos.at[iacross, 0], self.far2.at[0], p.step(small, 1)),
                self.c.start(self.pos.at[iacross, 1], self.far2.at[1], p.step(small, 3)),
            ]
            self.send(self.pos.at[iup, 1], self.pos2.at[1], small, 1)
            self.send(self.pos.at[idown, 0], self.neg2.at[0], small, 3)
        elif s == 4:
            wait_all(self.first)
            self.far2[0] = (self.far2[0].astype(F32) + self.pos[iup, 0].astype(F32)).astype(BF16)
            self.far2[1] = (self.far2[1].astype(F32) + self.pos[idown, 1].astype(F32)).astype(BF16)
            self.send(self.far2.at[0], self.pos2.at[0], small, 1)
            self.send(self.far2.at[1], self.neg2.at[1], small, 3)
        elif s == 5:
            for q in range(2):
                here = self.pos[i, q].astype(F32) + self.pos2[q].astype(F32) + self.neg2[q].astype(F32)
                self.pos2[q] = here.astype(BF16)
            self.send(self.pos2.at[1 - y], self.last, "y", 0)
        elif s == 6:
            total = self.pos2[y].astype(F32) + self.last[...].astype(F32)
            self.out[pl.ds(self.lo, self.n), :] = total.astype(self.out.dtype)


class CtxScatterLate:
    COPIES = 19
    STAGES = 6

    @staticmethod
    def scratch(n, width):
        shapes = [(4, 4, n), (2, 4, n), (2, 2, n), (4, n), (4, n), (2, n // 2), (2, n // 2), (2, n // 2)]
        return [pltpu.VMEM(shape + (width,), BF16) for shape in shapes]

    def __init__(self, place, copies, src, out, bufs, lo, n, big):
        self.p, self.c, self.src, self.out = place, copies, src, out
        self.all, self.staged, self.far, self.pos, self.neg, self.far2, self.pos2, self.neg2 = bufs
        self.lo, self.n, self.big, self.small = lo, n, big, ("z" if big == "x" else "x")
        self.first, self.live, self.loads = [], [], []

    def part(self, o, i):
        x, z = (o, i) if self.big == "x" else (i, o)
        return self.all.at[x, z]

    def load(self, o, i):
        x, z = (o, i) if self.big == "x" else (i, o)
        return self.all[x, z].astype(F32)

    def start(self, src, dst, axis, by):
        return self.c.start(src, dst, self.p.pair("y") if axis == "y" else self.p.step(axis, by))

    def stage_own(self, o):
        every, rows = pl.ds(0, 4), pl.ds(self.lo, self.n)
        x, z = (o, every) if self.big == "x" else (every, o)
        self.loads.append(self.c.local(self.src.at[x, z, self.p.y, rows], self.staged.at[o % 2]))

    def stage(self, s):
        p, big, small, n = self.p, self.big, self.small, self.n
        o, i = getattr(p, big), getattr(p, small)
        up, down, across = (o + 1) % 4, (o + 3) % 4, (o + 2) % 4
        iup, idown, iacross = (i + 1) % 4, (i + 3) % 4, (i + 2) % 4
        low, high, every = pl.ds(0, 2), pl.ds(2, 2), pl.ds(0, 4)
        rows = [pl.ds(0, n // 2), pl.ds(n // 2, n // 2)]
        if s in (2, 4):
            wait_all(self.first)
        else:
            wait_all(self.live)
            self.live = []
        if s == 0:
            theirs = self.src.at[every, every, 1 - p.y, pl.ds(self.lo, n)]
            self.live = [self.start(theirs, self.all, "y", 0)]
            self.stage_own(0)
            self.stage_own(1)
        elif s == 1:
            for slab in range(4):
                self.loads[slab].wait()

                def add(k, _):
                    x, z = (slab, k) if big == "x" else (k, slab)
                    here = self.all[x, z].astype(F32) + self.staged[slab % 2, k].astype(F32)
                    self.all[x, z] = here.astype(BF16)
                    return 0

                lax.fori_loop(0, 4, add, 0)
                if slab < 2:
                    self.stage_own(slab + 2)
            self.first = [
                self.start(self.part(across, low), self.far.at[0], big, 1),
                self.start(self.part(across, high), self.far.at[1], big, 3),
            ]
            self.live = [
                self.start(self.part(up, high), self.pos.at[high], big, 1),
                self.start(self.part(down, low), self.neg.at[low], big, 3),
            ]
        elif s == 2:
            for b in range(2):
                self.far[0, b] = (self.far[0, b].astype(F32) + self.load(up, b)).astype(BF16)
                self.far[1, b] = (self.far[1, b].astype(F32) + self.load(down, b + 2)).astype(BF16)
            self.live += [
                self.start(self.far.at[0], self.pos.at[low], big, 1),
                self.start(self.far.at[1], self.neg.at[high], big, 3),
            ]
        elif s == 3:
            for b in range(4):
                here = self.load(o, b) + self.pos[b].astype(F32) + self.neg[b].astype(F32)
                self.pos[b] = here.astype(BF16)
            self.first = [
                self.start(self.pos.at[iacross, rows[0]], self.far2.at[0], small, 1),
                self.start(self.pos.at[iacross, rows[1]], self.far2.at[1], small, 3),
            ]
            self.live = [
                self.start(self.pos.at[iup, rows[1]], self.pos2.at[1], small, 1),
                self.start(self.pos.at[idown, rows[0]], self.neg2.at[0], small, 3),
            ]
        elif s == 4:
            self.far2[0] = (self.far2[0].astype(F32) + self.pos[iup, rows[0], :].astype(F32)).astype(BF16)
            self.far2[1] = (self.far2[1].astype(F32) + self.pos[idown, rows[1], :].astype(F32)).astype(BF16)
            self.live += [
                self.start(self.far2.at[0], self.pos2.at[0], small, 1),
                self.start(self.far2.at[1], self.neg2.at[1], small, 3),
            ]
        elif s == 5:
            for h in range(2):
                here = self.pos[i, rows[h], :].astype(F32) + self.pos2[h].astype(F32) + self.neg2[h].astype(F32)
                self.out[pl.ds(self.lo + h * (n // 2), n // 2), :] = here


class ShardGather:
    def __init__(self, place, copies, full, chunks):
        self.p, self.c, self.full, self.chunks = place, copies, full, chunks
        self.rows = full.shape[1] // chunks
        self.me, self.over = place.yl * 2 + place.co, (1 - place.yl) * 2 + place.co
        self.far, self.near = [], []

    COPIES = 3

    def part(self, who, k):
        return self.full.at[who, pl.ds(k * self.rows, self.rows)]

    def send(self, k, src=None):
        src = self.part(self.me, k) if src is None else src
        self.far.append(self.c.start(src, self.part(self.me, k), self.p.pair("yl")))
        self.near.append(self.c.start(src, self.part(self.me, k), self.p.pair("co")))

    def forward(self, k):
        self.far[k].wait()
        self.near.append(self.c.start(self.part(self.over, k), self.part(self.over, k), self.p.pair("co")))

    def finish(self):
        wait_all(self.near)


class ShardScatter:
    COPIES = 3

    @staticmethod
    def scratch(rows, width):
        return [pltpu.VMEM((rows, width), BF16)] * 3

    def __init__(self, place, copies, part, bufs, chunks):
        self.p, self.c, self.part, self.chunks = place, copies, part, chunks
        self.relay, self.near, self.over = bufs
        self.rows = part.shape[1] // chunks
        self.first, self.second, self.third = [], [], []

    def at(self, k):
        return pl.ds(k * self.rows, self.rows)

    def begin(self):
        self.begin_far()
        self.begin_near()

    def begin_far(self):
        p = self.p
        for k in range(self.chunks):
            src = self.part.at[(1 - p.yl) * 2 + 1 - p.co, self.at(k)]
            self.first.append(self.c.start(src, self.relay.at[self.at(k)], p.pair("co")))

    def begin_near(self):
        p = self.p
        for k in range(self.chunks):
            src = self.part.at[p.yl * 2 + 1 - p.co, self.at(k)]
            self.second.append(self.c.start(src, self.near.at[self.at(k)], p.pair("co")))

    def relay_on(self, k):
        p = self.p
        self.first[k].wait()
        here = self.part[(1 - p.yl) * 2 + p.co, self.at(k), :].astype(F32)
        self.relay[self.at(k), :] = (self.relay[self.at(k), :].astype(F32) + here).astype(BF16)
        self.third.append(self.c.start(self.relay.at[self.at(k)], self.over.at[self.at(k)], p.pair("yl")))

    def total(self, k):
        p = self.p
        self.second[k].wait()
        self.third[k].wait()
        here = self.part[p.yl * 2 + p.co, self.at(k), :].astype(F32)
        return here + self.near[self.at(k), :].astype(F32) + self.over[self.at(k), :].astype(F32)


class GainScatter:
    COPIES = 9
    STAGES = 6

    @staticmethod
    def scratch():
        return [
            pltpu.VMEM((8, 2048), F32),
            pltpu.VMEM((3, 8, 512), F32),
            pltpu.VMEM((8, 512), F32),
            pltpu.VMEM((3, 8, 128), F32),
            pltpu.VMEM((3, 8, 128), F32),
            pltpu.VMEM((3, 8, 128), F32),
        ]

    def __init__(self, place, copies, out, bufs):
        self.p, self.c, self.out = place, copies, out
        self.vec, self.xs, self.mid, self.zs, self.own, self.rest = bufs
        self.live = []

    def stage(self, s):
        p = self.p
        wait_all(self.live)
        self.live = []
        if s == 0:
            for by in (1, 2, 3):
                cols = pl.ds(pl.multiple_of(((p.x + by) % 4) * 512, 512), 512)
                self.live.append(self.c.start(self.vec.at[:, cols], self.xs.at[by - 1], p.step("x", by)))
        elif s == 1:
            cols = pl.ds(pl.multiple_of(p.x * 512, 512), 512)
            self.mid[...] = self.vec[:, cols] + self.xs[0] + self.xs[1] + self.xs[2]
            for by in (1, 2, 3):
                cols = pl.ds(pl.multiple_of(((p.z + by) % 4) * 128, 128), 128)
                self.live.append(self.c.start(self.mid.at[:, cols], self.zs.at[by - 1], p.step("z", by)))
        elif s == 2:
            cols = pl.ds(pl.multiple_of(p.z * 128, 128), 128)
            self.own[0] = self.mid[:, cols] + self.zs[0] + self.zs[1] + self.zs[2]
            self.live.append(self.c.start(self.own.at[0], self.rest.at[0], p.pair("y")))
        elif s == 3:
            self.own[1] = self.own[0] + self.rest[0]
            self.live.append(self.c.start(self.own.at[1], self.rest.at[1], p.pair("co")))
        elif s == 4:
            self.own[2] = self.own[1] + self.rest[1]
            self.live.append(self.c.start(self.own.at[2], self.rest.at[2], p.pair("yl")))
        elif s == 5:
            self.out[...] = self.own[2] + self.rest[2]


def sems(n):
    return [pltpu.SemaphoreType.DMA((n,)), pltpu.SemaphoreType.DMA((n,))]


def params(cid):
    return pltpu.CompilerParams(collective_id=cid, has_side_effects=True, vmem_limit_bytes=VMEM_LIMIT)


def halves(rows):
    return ((0, rows // 2, "x"), (rows // 2, rows // 2, "z"))


CHUNKS = 4


def norm_back_rows(grad, resid, gain):
    factor = lax.rsqrt(jnp.mean(resid * resid, -1, keepdims=True) + EPS)
    weighted = grad * gain
    per_gain = grad * resid * factor
    back = factor * weighted - resid * (factor * factor * factor) * jnp.mean(weighted * resid, -1, keepdims=True)
    return back, per_gain


def eight(rows):
    return jnp.sum(rows.reshape(rows.shape[0] // 8, 8, rows.shape[1]), 0)


KEYS = 256
KB = 4


def lane_iota(rows):
    return lax.broadcasted_iota(jnp.int32, (rows, 128), 1)


def rotate_tile(u, cosine, sine):
    low = lane_iota(u.shape[0]) % HD < HD // 2
    turned = jnp.where(low, -pltpu.roll(u, 128 - HD // 2, 1), pltpu.roll(u, HD // 2, 1))
    return u * cosine + turned * sine


def unrotate_tile(w, cosine, sine):
    low = lane_iota(w.shape[0]) % HD < HD // 2
    s = w * sine
    return w * cosine + jnp.where(low, pltpu.roll(s, 128 - HD // 2, 1), -pltpu.roll(s, HD // 2, 1))


def project_rows(rows, w_qkv, tables):
    lin = jnp.dot(rows, w_qkv, preferred_element_type=F32)
    tiles = []
    for hp in range(4):
        tile = lin[:, hp * 128 : (hp + 1) * 128]
        tiles.append((rotate_tile(tile, tables[0], tables[1])).astype(BF16) * jnp.asarray(HD**-0.5, BF16))
    kv = rotate_tile(lin[:, 512:640], tables[2], tables[3]).astype(BF16)
    return tiles, kv


def head_rows(ref, start, keep_low):
    low = lane_iota(64) < HD
    keep = low if keep_low else ~low
    pieces = []
    for hp in range(4):
        tile = ref[pl.ds(start, 64), hp * 128 : (hp + 1) * 128].astype(F32)
        turned = pltpu.roll(tile, HD, 1)
        even, odd = (tile, turned) if keep_low else (turned, tile)
        pieces += [jnp.where(keep, even, 0.0), jnp.where(keep, odd, 0.0)]
    return pieces


def key_chunk(kv, seq, chunk, half):
    start = pl.multiple_of(seq * 128 + half * 64, 64)
    z = pl.ds((chunk % 2) * 2, 2)
    return kv[chunk // 2, z, :, pl.ds(start, 64), :].reshape(KEYS, 128)


def diagonal(block, here):
    key = lax.broadcasted_iota(jnp.int32, (KEYS, 512), 0)
    query = lax.broadcasted_iota(jnp.int32, (KEYS, 512), 1) % 64
    ahead = key // 64 - here
    return key % 64 - query <= (-ahead if block == 0 else ahead) * 64


def pick(u, own_chunk):
    late = u - 8
    block = jnp.where(u < 8, 1, jnp.where(late >= own_chunk, 1, 0))
    half = jnp.where(u < 8, 0, block)
    chunk = jnp.where(u < 8, u, late + half)
    return block, chunk, half


def nt(a, b):
    return lax.dot_general(a, b, (((1,), (1,)), ((), ())), preferred_element_type=F32)


def tn(a, b):
    return lax.dot_general(a, b, (((0,), (0,)), ((), ())), preferred_element_type=F32)


def attend_seq(seq, ctx, q, kv, attn, lse, scratch):
    qe, top, acc = scratch
    low = lane_iota(64) < HD
    ones_low = lane_iota(KEYS) < HD
    own_chunk, here = ctx // KB, ctx % KB

    def with_ones(keys):
        return jnp.where(ones_low, jnp.ones_like(keys), keys)

    for b in range(2):
        for h, piece in enumerate(head_rows(q, seq * 128 + b * 64, True)):
            qe[b, h * 64 : (h + 1) * 64, :] = piece.astype(BF16)
    for b in range(2):
        keys = key_chunk(kv, seq, own_chunk, b)
        scores = jnp.where(diagonal(b, here), nt(keys, qe[b]), NEG)
        m = jnp.max(scores, 0, keepdims=True)
        p = jnp.exp(scores - m).astype(BF16)
        top[b] = m
        acc[b] = tn(with_ones(keys), p)

    def step(u, _):
        b, chunk, half = pick(u, own_chunk)
        keys = key_chunk(kv, seq, chunk, half)
        scores = nt(keys, qe[b])
        before = top[b]
        m = jnp.maximum(before, jnp.max(scores, 0, keepdims=True))
        p = jnp.exp(scores - m).astype(BF16)
        top[b] = m
        acc[b] = acc[b] * jnp.exp(before - m) + tn(with_ones(keys), p)
        return 0

    for k in range(3):
        lax.fori_loop(5 * k, 5 * k + 5, step, 0, unroll=True)
        if k < 2:
            yield
    for b in range(2):
        here_acc = acc[b]
        total = here_acc[0:1, :]
        lse[pl.ds(seq * 2 + b, 1), :] = top[b] + jnp.log(total)
        out = (here_acc * (1.0 / total)).T
        for hp in range(4):
            even, odd = out[hp * 128 : hp * 128 + 64, :], out[hp * 128 + 64 : hp * 128 + 128, :]
            tile = jnp.where(low, pltpu.roll(even, HD, 1), odd)
            attn[pl.ds(seq * 128 + b * 64, 64), hp * 128 : (hp + 1) * 128] = tile.astype(BF16)


def attend_scratch():
    return [pltpu.VMEM((2, 512, 128), BF16), pltpu.VMEM((2, 1, 512), F32), pltpu.VMEM((2, 128, 512), F32)]


def attend_back_seq(seq, ctx, q, kv, grad, attn, lse, tables, grad_lin, grad_kv, scratch):
    qd, delta, dq, dkv = scratch
    low = lane_iota(64) < HD
    own_chunk, here = ctx // KB, ctx % KB
    for b in range(2):
        start = seq * 128 + b * 64
        q_rows, g_rows, o_rows = (
            head_rows(q, start, True), head_rows(grad, start, False), head_rows(attn, start, False)
        )
        for h in range(8):
            qd[b, h * 64 : (h + 1) * 64, :] = q_rows[h].astype(BF16)
            qd[b, 512 + h * 64 : 512 + (h + 1) * 64, :] = g_rows[h].astype(BF16)
        products = jnp.concatenate([g * o for g, o in zip(g_rows, o_rows)], 0)
        delta[b] = jnp.sum(products.T, 0, keepdims=True)

    def grads(b, keys, allowed):
        both = nt(keys, qd[b])
        p = jnp.exp(both[:, :512] - lse[pl.ds(seq * 2 + b, 1), :])
        if allowed is not None:
            p = jnp.where(allowed, p, 0.0)
        ds = (p * (both[:, 512:] - delta[b])).astype(BF16)
        joined = jnp.concatenate([ds, p.astype(BF16)], 1)
        return tn(keys, ds), jnp.dot(joined, qd[b], preferred_element_type=F32)

    dkv[...] = jnp.zeros_like(dkv)

    def add_keys(chunk, half, value):
        start = pl.multiple_of(half * 64, 64)
        dkv[pl.ds(chunk * KB, KB), pl.ds(start, 64), :] += value.reshape(KB, 64, 128)

    for b in range(2):
        dq_part, dkv_part = grads(b, key_chunk(kv, seq, own_chunk, b), diagonal(b, here))
        dq[b] = dq_part
        add_keys(own_chunk, b, dkv_part)

    def step(u, _):
        b, chunk, half = pick(u, own_chunk)
        dq_part, dkv_part = grads(b, key_chunk(kv, seq, chunk, half), None)
        dq[b] += dq_part
        add_keys(chunk, half, dkv_part)
        return 0

    for k in range(3):
        lax.fori_loop(5 * k, 5 * k + 5, step, 0, unroll=True)
        if k < 2:
            yield
    for b in range(2):
        out = (dq[b] * HD**-0.5).T
        cosine, sine = tables[0, b * 64 : (b + 1) * 64, :], tables[1, b * 64 : (b + 1) * 64, :]
        for hp in range(4):
            even, odd = out[hp * 128 : hp * 128 + 64, :], out[hp * 128 + 64 : hp * 128 + 128, :]
            tile = jnp.where(low, even, pltpu.roll(odd, HD, 1))
            tile = unrotate_tile(tile, cosine, sine)
            grad_lin[pl.ds(seq * 128 + b * 64, 64), hp * 128 : (hp + 1) * 128] = tile.astype(BF16)
    grad_kv[...] = dkv[...].reshape(4, 4, 2, 128, 128).astype(BF16)


def attend_back_scratch():
    return [
        pltpu.VMEM((2, 1024, 128), BF16),
        pltpu.VMEM((2, 1, 512), F32),
        pltpu.VMEM((2, 128, 512), F32),
        pltpu.VMEM((32, 128, 128), F32),
    ]


def ctx_gathers(place, copies, src, full, kind=CtxGather):
    return [kind(place, copies, src, full, lo, rows, big) for lo, rows, big in halves(src.shape[0])]


FORWARD = [
    "w0", "o0", "u0", "d0", "w1", "N1", "CB", "o1", "w2", "d1", "o2", "w3", "g0", "d2", "w4", "NF", "d3", "o3",
    "w5", "NW", "J2", "J3", "k30", "J1", "k10", "k20", "J0", "k00", "d4", "k31", "k01", "k11", "k02", "o4", "k21",
    "u1", "k22", "k32", "k12", "g1", "k03", "k23", "o5", "k13", "g2", "k04", "k33", "u2", "k34", "k14", "k24", "g3",
    "k05", "A00", "A01", "A02", "OP0", "k15", "RF", "k25", "A10", "k35", "A11", "u3", "A12", "OP1", "A20", "CF",
    "RR", "A21", "A22", "A30", "A31", "OP2", "RN", "A32", "OP3", "g4", "NT", "u4", "d5", "CW", "DA", "SF", "SW",
    "g5", "u5", "FU", "P2", "XB", "RP", "GD", "e0", "e1", "XN", "XR", "e2", "XT", "GU", "GG", "XF", "e3", "XW",
]

BACKWARD = [
    "u0", "g0", "DO", "DP", "GO", "g1", "o0", "A00", "A01", "o1", "A02", "k00", "A10", "A11", "o2", "g2", "d3",
    "k01", "A12", "k02", "RESB", "A20", "A21", "k10", "k11", "A22", "k20", "A30", "k12", "g3", "k21", "A31", "d4",
    "A32", "k30", "QG", "k31", "k22", "k03", "k13", "RESR", "k32", "k04", "g4", "k33", "k23", "k14", "q0", "k34",
    "k24", "q1", "k15", "u1", "q2", "k25", "RES", "k16", "I1", "k26", "k35", "k05", "I2", "d5", "o3", "k06", "k36",
    "I3", "I0", "VG", "v0", "v1", "g5", "q3", "u2", "v2", "TOT", "n0", "q4", "o4", "v3", "n1", "u3", "n2", "v4",
    "q5", "o5", "u4", "n3", "v5", "q6", "n4", "v6", "u5", "o6", "g6", "d6", "n5",
]


def run_steps(steps, engines, actions):
    for step in steps:
        if step in actions:
            actions[step]()
        else:
            for e in engines[step[:-1]]:
                e.stage(int(step[-1]))


def gain_row(ref):
    gain = ref[...].astype(F32)
    return jnp.concatenate([gain[k : k + 1, :] for k in range(16)], 1)


def over_hidden_units(tile):
    for start, width in ((0, 512), (512, 512), (1024, 384)):
        tile(pl.ds(start, width), width)


def over_width(step):
    def one(j, _):
        step(j, pl.ds(pl.multiple_of(j * 512, 512), 512))
        return 0

    lax.fori_loop(0, 4, one, 0)


def forward_kernel(
    x, cot, gain1, gain2, tables, wq, wk, wv, w_out_shard, w_gate_shard, w_up_shard, w_down_shard,
    normed1_out, w_qkv_out, w_out_out, q, kv_out, attn, lse, hidden, branch_out, grad_hidden, grad_gain,
    result_out, g_gate_out, g_up_out, g_down_x, g_down_z,
    normed1_all, w_qkv_shard, w_qkv, w_out, kv_all, part, relay, near, over, qe, top, acc,
    w_gate, w_up, w_down, cot_all, normed2_all, gate_pre, up_pre, grad_active, active, grad_gate, grad_up, result_part, branch,
    *rest,
):
    bufs, (send, recv) = rest[:14], rest[14:]
    place = Place()
    greet(place.ctx_peers() + place.shard_peers())
    copies = Copies(send, recv)
    ctx = lax.axis_index("ctx")
    order = [2 * (1 - place.yl) + 1 - place.co, 2 * (1 - place.yl) + place.co]
    order += [2 * place.yl + 1 - place.co, 2 * place.yl + place.co]
    starts = [pl.multiple_of(seq * 128, 128) for seq in order]
    engines = {
        "w": ctx_gathers(place, copies, w_qkv_shard, w_qkv),
        "o": ctx_gathers(place, copies, w_out_shard, w_out),
        "g": ctx_gathers(place, copies, w_gate_shard, w_gate),
        "u": ctx_gathers(place, copies, w_up_shard, w_up),
        "d": ctx_gathers(place, copies, w_down_shard, w_down, CtxGatherLate),
    }
    for k in range(4):
        engines[f"k{k}"] = [CtxGather(place, copies, None, kv_all, starts[k], 128, "xz"[k % 2])]
    normed = ShardGather(place, copies, normed1_all, 1)
    cots = ShardGather(place, copies, cot_all, 1)
    rows_out = ShardScatter(place, copies, part, (relay, near, over), CHUNKS)
    spread = ShardGather(place, copies, normed2_all, CHUNKS)
    thirds = [attend_seq(seq, ctx, q, kv_all, attn, lse, (qe, top, acc)) for seq in order]
    back = ShardScatter(place, copies, part, (relay, near, over), CHUNKS)
    branches = ShardGather(place, copies, branch, CHUNKS)
    engines["e"] = [
        CtxScatter(place, copies, w_down, out, bufs[7 * h : 7 * h + 7], lo, rows, big, stop=True)
        for h, (out, (lo, rows, big)) in enumerate(zip((g_down_x, g_down_z), halves(64)))
    ]
    outgoing = []
    w_qkv_shard[:, :512] = wq[...]
    w_qkv_shard[:, 512:640] = jnp.concatenate([wk[...], wv[...]], 1)

    def first_norm():
        rows = x[...].astype(F32)
        factor = lax.rsqrt(jnp.mean(rows * rows, -1, keepdims=True) + EPS)
        normed1_all[normed.me] = (rows * factor * gain_row(gain1)).astype(BF16)
        normed.send(0)

    def normed_here():
        normed.finish()
        outgoing.append(copies.local(normed1_all, normed1_out))

    def project_seq(k):
        at = pl.ds(starts[k], 128)
        tiles, kv = project_rows(normed1_all[order[k]], w_qkv[...].reshape(2048, 640), tables)
        for hp, tile in enumerate(tiles):
            q[at, hp * 128 : (hp + 1) * 128] = tile
        kv_all[place.x, place.z, place.y, at, :] = kv

    own_cot = []

    def send_cot():
        cots.send(0, cot)
        own_cot.append(copies.local(cot, cot_all.at[cots.me]))

    def cot_here():
        cots.finish()
        wait_all(own_cot)

    def project_out(k):
        part[order[k]] = nt(attn[pl.ds(starts[k], 128), :], w_out[...].reshape(2048, 512)).astype(BF16)

    def relay_rows():
        for c in range(CHUNKS):
            rows_out.relay_on(c)

    def second_norm():
        outgoing.extend(copies.local(*pair) for pair in ((w_qkv, w_qkv_out), (w_out, w_out_out), (kv_all, kv_out)))
        gain = gain_row(gain2)
        for c in range(CHUNKS):
            at = rows_out.at(c)
            here = x[at, :].astype(F32) + rows_out.total(c)
            hidden[at, :] = here
            factor = lax.rsqrt(jnp.mean(here * here, -1, keepdims=True) + EPS)
            normed2_all[spread.me, at, :] = (here * factor * gain).astype(BF16)
            spread.send(c)

    def spread_on():
        for c in range(CHUNKS):
            spread.forward(c)

    def columns_of(w, cols, width):
        return w[:, :, :, :, cols].reshape(2048, width)

    def grad_active_tiles():
        def tile(cols, width):
            rows = cot_all[...].reshape(512, 2048)
            grad_active[:, cols] = jnp.dot(rows, columns_of(w_down, cols, width), preferred_element_type=F32)

        over_hidden_units(tile)

    def hidden_units():
        def tile(cols, width):
            rows = normed2_all[...].reshape(512, 2048)
            here = pl.ds(0, width)
            gate_pre[:, here] = jnp.dot(rows, columns_of(w_gate, cols, width), preferred_element_type=F32)
            up_pre[:, here] = jnp.dot(rows, columns_of(w_up, cols, width), preferred_element_type=F32)

            def some(r, _):
                at = pl.ds(pl.multiple_of(r * 64, 64), 64)
                gate, up, grad = gate_pre[at, here], up_pre[at, here], grad_active[at, cols]
                sigmoid = 1.0 / (1.0 + jnp.exp(-gate))
                silu = gate * sigmoid
                active[at, cols] = (silu * up).astype(BF16)
                grad_gate[at, cols] = (grad * up * sigmoid * (1.0 + gate * (1.0 - sigmoid))).astype(BF16)
                grad_up[at, cols] = (grad * silu).astype(BF16)
                return 0

            lax.fori_loop(0, 8, some, 0)

        over_hidden_units(tile)

    def result_tiles():
        def step(j, cols):
            rows = nt(active[...], w_down[j].reshape(512, 1408))
            result_part[:, :, cols] = rows.astype(BF16).reshape(4, 128, 512)

        over_width(step)
        outgoing.append(copies.local(result_part, result_out))

    def grad_normed_tiles():
        def step(j, cols):
            rows = nt(grad_gate[...], w_gate[j].reshape(512, 1408)) + nt(grad_up[...], w_up[j].reshape(512, 1408))
            part[:, :, cols] = rows.astype(BF16).reshape(4, 128, 512)

        over_width(step)

    def weight_grad(left, right, w):
        def step(j, cols):
            block = tn(left[:, :, cols].reshape(512, 512), right[...])
            w[j] = block.astype(BF16).reshape(4, 2, 64, 1408)

        over_width(step)

    def gate_grad():
        weight_grad(normed2_all, grad_gate, w_gate)
        outgoing.append(copies.local(w_gate, g_gate_out))

    def up_grad():
        weight_grad(normed2_all, grad_up, w_up)
        outgoing.append(copies.local(w_up, g_up_out))

    def relay_back():
        for c in range(CHUNKS):
            back.relay_on(c)

    def second_norm_back():
        gain = gain_row(gain2)
        for c in range(CHUNKS):
            at = back.at(c)
            grad, per_gain = norm_back_rows(back.total(c), hidden[at, :], gain)
            here = cot_all[branches.me, at, :].astype(F32) + grad
            grad_hidden[at, :] = here
            branch[branches.me, at, :] = here.astype(BF16)
            branches.send(c)
            grad_gain[...] = eight(per_gain) if c == 0 else grad_gain[...] + eight(per_gain)

    def branch_on():
        for c in range(CHUNKS):
            branches.forward(c)

    def branch_here():
        branches.finish()
        outgoing.append(copies.local(branch, branch_out))

    actions = {
        "N1": first_norm, "NF": lambda: normed.forward(0), "NW": normed_here,
        "CB": send_cot, "CF": lambda: cots.forward(0), "CW": cot_here,
        "RF": rows_out.begin_far, "RR": relay_rows, "RN": rows_out.begin_near,
        "NT": second_norm, "SF": spread_on, "SW": spread.finish,
        "DA": grad_active_tiles, "FU": hidden_units, "RP": result_tiles, "P2": grad_normed_tiles,
        "GD": lambda: weight_grad(cot_all, active, w_down), "GG": gate_grad, "GU": up_grad,
        "XB": back.begin_far, "XN": back.begin_near, "XR": relay_back, "XT": second_norm_back,
        "XF": branch_on, "XW": branch_here,
    }
    for k in range(4):
        actions[f"J{k}"] = partial(project_seq, k)
        actions[f"OP{k}"] = partial(project_out, k)
        for third in range(3):
            actions[f"A{k}{third}"] = partial(next, thirds[k], None)
    run_steps(FORWARD, engines, actions)
    wait_all(outgoing + [copy for e in engines["e"] for copy in e.live])


def forward(cid, x, cot, gain1, gain2, tables, w_qkv, shards):
    tokens, width = x.shape
    every = (4, tokens, width)
    ffn_width = shards[1].shape[1]

    def full(n):
        return (4, 4, 2, 64, n)

    kv_all, totals = (4, 4, 2, 512, 128), (4, 2, 32, ffn_width)
    outs = [
        (ANY, every, BF16), (ANY, full(640), BF16), (ANY, full(512), BF16), (VMEM, (512, 512), BF16),
        (ANY, kv_all, BF16), (VMEM, (512, 512), BF16), (VMEM, (8, 512), F32), (VMEM, (tokens, width), F32),
        (ANY, every, BF16), (VMEM, (tokens, width), F32), (VMEM, (8, width), F32), (ANY, every, BF16),
        (ANY, full(ffn_width), BF16), (ANY, full(ffn_width), BF16), (ANY, totals, BF16), (ANY, totals, BF16),
    ]
    return pl.pallas_call(
        forward_kernel,
        out_shape=[jax.ShapeDtypeStruct(shape, dtype) for _, shape, dtype in outs],
        in_specs=[VMEM, ANY, VMEM, VMEM, VMEM, VMEM, VMEM, VMEM] + [ANY] * 4,
        out_specs=[space for space, _, _ in outs],
        scratch_shapes=[
            pltpu.VMEM(every, BF16),
            pltpu.VMEM((64, 640), BF16),
            pltpu.VMEM(full(640), BF16),
            pltpu.VMEM(full(512), BF16),
            pltpu.VMEM(kv_all, BF16),
            pltpu.VMEM(every, BF16),
            *ShardScatter.scratch(tokens, width),
            *attend_scratch(),
            *[pltpu.VMEM(full(ffn_width), BF16)] * 3,
            pltpu.VMEM(every, BF16),
            pltpu.VMEM(every, BF16),
            *[pltpu.VMEM((512, 512), F32)] * 2,
            pltpu.VMEM((512, ffn_width), F32),
            *[pltpu.VMEM((512, ffn_width), BF16)] * 3,
            pltpu.VMEM(every, BF16),
            pltpu.VMEM(every, BF16),
            *CtxScatter.scratch(32, ffn_width),
            *CtxScatter.scratch(32, ffn_width),
            *sems(14 * CtxGather.COPIES + 2 * CtxScatter.COPIES + 12 * CHUNKS + 24),
        ],
        compiler_params=params(cid),
        name="forward",
    )(x, cot, gain1.reshape(16, 128), gain2.reshape(16, 128), tables, *w_qkv, *shards)


def backward_kernel(*refs):
    (
        branch_in, result_in, w_out_in, w_qkv_in, normed_in, g_gate, g_up, g_down_x, g_down_z,
        hidden, grad_hidden, grad_gain, q, kv, attn, lse, tables, x, gain1,
    ) = refs[:19]
    grad_inputs, gains, outputs, out_q, out_kv, out_o, out_gate, out_up, out_down = refs[19:28]
    normed, result_part, w_out, w_qkv, branch, dkv_send, relay, near, over = refs[28:37]
    grad_lin, grad_kv, g_query, g_kv = refs[37:41]
    scratch, gain_bufs, bufs, (free, send, recv) = refs[41:45], refs[45:51], refs[51:-3], refs[-3:]
    place = Place()
    greet(place.ctx_peers() + place.shard_peers() + place.far_peers())
    copies = Copies(send, recv)
    ctx = lax.axis_index("ctx")
    me, co = 2 * place.yl + place.co, 2 * place.yl + 1 - place.co
    far, far_co = 2 * (1 - place.yl) + place.co, 2 * (1 - place.yl) + 1 - place.co
    order = [me, far_co, far, co]
    taken = 0

    def take(n):
        nonlocal taken
        taken += n
        return bufs[taken - n : taken]

    def rows_of(seq):
        return pl.ds(pl.multiple_of(seq * 128, 128), 128)

    engines = {}
    for name, src, out, count in (
        ("g", g_gate, out_gate, 9), ("o", w_out, out_o, 7), ("q", g_query, out_q, 7), ("v", g_kv, out_kv, 7),
    ):
        engines[name] = [
            CtxScatter(place, copies, src, out, take(count), lo, rows, big) for lo, rows, big in halves(64)
        ]
    for k in range(4):
        engines[f"k{k}"] = [
            CtxScatter(place, copies, dkv_send.at[k], grad_kv.at[rows_of(order[k])], take(7), 0, 128, "xz"[k % 2])
        ]
    engines["u"] = [
        CtxScatterLate(place, copies, g_up, out_up, take(8), lo, rows, big) for lo, rows, big in halves(64)
    ]
    engines["d"] = []
    for (lo, rows, big), totals in zip(halves(64), (g_down_x, g_down_z)):
        pos, far2, pos2, neg2, last = take(5)
        load = copies.local(totals, pos)
        engines["d"].append(
            CtxScatter(
                place, copies, None, out_down, (None, pos, None, far2, pos2, neg2, last), lo, rows, big, resumed=load
            )
        )
    gain_sum = GainScatter(place, copies, gains, gain_bufs)
    engines["n"] = [gain_sum]
    loads = [copies.local(a, b) for a, b in (
        (branch_in, branch), (w_out_in, w_out), (result_in, result_part), (w_qkv_in, w_qkv), (normed_in, normed)
    )]
    result = ShardScatter(place, copies, result_part, (relay, near, over), 1)
    last = ShardScatter(place, copies, branch, (relay, near, over), CHUNKS)
    thirds = [
        attend_back_seq(
            order[k], ctx, q, kv, grad_lin, attn, lse, tables, grad_lin, dkv_send.at[k], scratch
        )
        for k in range(4)
    ]

    def relay_rows(rows_scatter):
        for c in range(CHUNKS):
            rows_scatter.relay_on(c)

    def grad_rows(seq):
        w = w_out[...].reshape(2048, 512)
        grad_lin[rows_of(seq), :512] = jnp.dot(branch[seq], w, preferred_element_type=F32).astype(BF16)

    def grad_mixed_own():
        wait_all(loads[:2])
        grad_rows(me)

    def grad_mixed():
        for seq in order[1:]:
            grad_rows(seq)

    def begin_result():
        loads[2].wait()
        result.begin()

    def grad_of_out():
        rows = branch[...].reshape(512, 2048)
        for j in range(8):
            block = tn(rows[:, j * 256 : (j + 1) * 256], attn[...]).astype(BF16)
            w_out[j // 2, pl.ds((j % 2) * 2, 2)] = block.reshape(2, 2, 64, 512)

    def result_rows():
        outputs[...] = (hidden[...] + result.total(0)).astype(BF16)
        for device in place.shard_peers():
            pl.semaphore_signal(free, inc=1, device_id=device, device_id_type=MESH)

    def input_rows(k):
        if k == FIRST_INPUT_ROWS:
            loads[3].wait()
        at = rows_of(order[k])
        grad_lin[at, 512:640] = unrotate_tile(grad_kv[at, :], tables[2], tables[3]).astype(BF16)
        branch[order[k]] = nt(grad_lin[at, :], w_qkv[...].reshape(2048, 640)).astype(BF16)
        if k == 1:
            pl.semaphore_wait(free, 2)
            last.begin_far()
        elif k == 2:
            relay_rows(last)
        elif k == 3:
            last.begin_near()

    def weight_grad(w, start, width):
        def step(j, cols):
            block = tn(normed[:, :, cols].reshape(512, 512), grad_lin[:, start : start + width])
            w[j] = block.astype(BF16).reshape(4, 2, 64, width)

        over_width(step)

    def grad_of_query():
        loads[4].wait()
        weight_grad(g_query, 0, 512)

    def first_norm_back():
        gain = gain_row(gain1)
        for c in range(CHUNKS):
            rows = last.at(c)
            back, per_gain = norm_back_rows(last.total(c), x[rows, :].astype(F32), gain)
            grad_inputs[rows, :] = (grad_hidden[rows, :] + back).astype(BF16)
            total = eight(per_gain) if c == 0 else total + eight(per_gain)
        row = lax.broadcasted_iota(jnp.int32, total.shape, 0)
        one, two = jnp.sum(total, 0, keepdims=True), jnp.sum(grad_gain[...], 0, keepdims=True)
        gain_sum.vec[...] = jnp.where(row == 0, one, jnp.where(row == 1, two, 0.0))

    actions = {
        "DO": grad_mixed_own, "DP": grad_mixed, "GO": grad_of_out, "RESB": begin_result,
        "RESR": lambda: result.relay_on(0), "RES": result_rows, "QG": grad_of_query,
        "VG": lambda: weight_grad(g_kv, 512, 128), "TOT": first_norm_back,
    }
    for k in range(4):
        actions[f"I{k}"] = partial(input_rows, k)
        for third in range(3):
            actions[f"A{k}{third}"] = partial(next, thirds[k], None)
    run_steps(BACKWARD, engines, actions)


def backward(cid, in_hbm, in_vmem):
    hidden = in_vmem[0]
    tokens, width = hidden.shape
    ffn_width = in_hbm[5].shape[4]
    in_vmem = [a.reshape(16, 128) if a.ndim == 1 else a for a in in_vmem]
    scratch = []
    for _ in range(2):
        scratch += CtxScatter.scratch(32, ffn_width, True)
    for _ in range(4):
        scratch += CtxScatter.scratch(32, 512)
    for _ in range(2):
        scratch += CtxScatter.scratch(32, 128)
    for _ in range(4):
        scratch += CtxScatter.scratch(128, 128)
    for _ in range(2):
        scratch += CtxScatterLate.scratch(32, ffn_width)
    for _ in range(2):
        whole = CtxScatter.scratch(32, ffn_width)
        scratch += whole[1:2] + whole[3:]
    shapes = [
        ((tokens, width), BF16), ((8, 128), F32), ((tokens, width), BF16), ((64, 512), F32), ((64, 128), F32),
        ((64, 512), F32), ((64, ffn_width), F32), ((64, ffn_width), F32), ((64, ffn_width), F32),
    ]
    return pl.pallas_call(
        backward_kernel,
        out_shape=[jax.ShapeDtypeStruct(*shape) for shape in shapes],
        in_specs=[ANY] * len(in_hbm) + [VMEM] * len(in_vmem),
        out_specs=[VMEM] * len(shapes),
        scratch_shapes=[
            pltpu.VMEM((4, tokens, width), BF16),
            pltpu.VMEM((4, tokens, width), BF16),
            pltpu.VMEM((4, 4, 2, 64, 512), BF16),
            pltpu.VMEM((4, 4, 2, 64, 640), BF16),
            pltpu.VMEM((4, tokens, width), BF16),
            pltpu.VMEM((4, 4, 4, 2, 128, 128), BF16),
            *ShardScatter.scratch(tokens, width),
            pltpu.VMEM((512, 640), BF16),
            pltpu.VMEM((512, 128), F32),
            pltpu.VMEM((4, 4, 2, 64, 512), BF16),
            pltpu.VMEM((4, 4, 2, 64, 128), BF16),
            *attend_back_scratch(),
            *GainScatter.scratch(),
            *scratch,
            pltpu.SemaphoreType.REGULAR,
            *sems(16 * CtxScatter.COPIES + 2 * CtxScatterLate.COPIES + 6 * CHUNKS + GainScatter.COPIES + 12),
        ],
        compiler_params=params(cid),
        name="backward",
    )(*in_hbm, *in_vmem)


FIRST_INPUT_ROWS = int([step for step in BACKWARD if step[0] == "I"][0][1])


def finish_kernel(gains, grad_in, out_in, g_query, g_kv, g_out, g_gate, g_up, g_down, *outs):
    first, second, grad_inputs, outputs, query, key, value, out, gate, up, down = outs
    start = (lax.axis_index("ctx") % 2) * 64 + lax.axis_index("wshard") * 16
    own = pltpu.roll(gains[...], 128 - start, 1)
    first[...] = own[0:1, :16]
    second[...] = own[1:2, :16]
    grad_inputs[...] = grad_in[...]
    outputs[...] = out_in[...]
    query[...] = g_query[...]
    key[...] = g_kv[:, :HD]
    value[...] = g_kv[:, HD:]
    out[...] = g_out[...]
    gate[...] = g_gate[...]
    up[...] = g_up[...]
    down[...] = g_down[...]


def finish(*arrays):
    shapes = [((1, 16), F32)] * 2 + [(a.shape, a.dtype) for a in arrays[1:4]] + [((64, HD), F32)] * 2
    shapes += [(a.shape, a.dtype) for a in arrays[5:]]
    return pl.pallas_call(
        finish_kernel,
        out_shape=[jax.ShapeDtypeStruct(*shape) for shape in shapes],
        in_specs=[VMEM] * len(arrays),
        out_specs=[VMEM] * len(shapes),
        compiler_params=pltpu.CompilerParams(vmem_limit_bytes=VMEM_LIMIT),
        name="finish",
    )(*arrays)


def rope_tables(positions):
    freqs = 10000.0 ** (-jnp.arange(HD // 2, dtype=F32) * 2.0 / HD)
    angles = positions[:, None] * freqs[None]
    cosine, sine = jnp.cos(angles), jnp.sin(angles)
    one, zero = jnp.ones_like(cosine), jnp.zeros_like(cosine)
    return jnp.stack(
        [
            jnp.concatenate([cosine] * 4, -1),
            jnp.concatenate([sine] * 4, -1),
            jnp.concatenate([cosine, cosine, one, one], -1),
            jnp.concatenate([sine, sine, zero, zero], -1),
        ]
    )


def per_device(
    inputs, cotangent, norm_attn, w_query, w_key, w_value, w_out, norm_mlp, w_gate, w_up, w_down
):
    width = inputs.shape[-1]
    half_len = inputs.shape[2]
    tokens = 2 * half_len
    ctx_count = lax.axis_size("ctx")
    ctx_index = lax.axis_index("ctx")
    length = tokens * ctx_count
    x = inputs.reshape(tokens, width)
    cot = cotangent.reshape(tokens, width)
    rows_local = jnp.arange(tokens)
    positions = jnp.where(
        rows_local < half_len,
        ctx_index * half_len + rows_local,
        length - (ctx_index + 1) * half_len + (rows_local - half_len),
    ).astype(F32)
    tables = rope_tables(positions)

    (
        normed_all, w_qkv, w_out_t, q, kv_all, attn, lse, hidden, branch_all, grad_hidden, gain2_part, result_part,
        g_gate, g_up, g_down_x, g_down_z,
    ) = forward(
        0, x, cot, norm_attn, norm_mlp, tables, [w_query, w_key, w_value], [w_out.T, w_gate, w_up, w_down.T]
    )
    grad_inputs, gains, outputs, g_query, g_kv, g_out, g_gate, g_up, g_down = backward(
        1,
        [branch_all, result_part, w_out_t, w_qkv, normed_all, g_gate, g_up, g_down_x, g_down_z],
        [hidden, grad_hidden, gain2_part, q, kv_all, attn, lse, tables, x, norm_attn],
    )
    gain1, gain2, grad_inputs, outputs, g_query, g_key, g_value, g_out, g_gate, g_up, g_down = finish(
        gains, grad_inputs, outputs, g_query, g_kv, g_out, g_gate, g_up, g_down
    )
    return (
        outputs.reshape(inputs.shape),
        grad_inputs.reshape(inputs.shape),
        gain1.reshape(16),
        g_query,
        g_key,
        g_value,
        g_out.T,
        gain2.reshape(16),
        g_gate,
        g_up,
        g_down.T,
    )


def solution(mesh):
    return jax.shard_map(
        per_device,
        mesh=mesh,
        in_specs=(
            P("wshard", None, "ctx", None),
            P("wshard", None, "ctx", None),
            P(),
            P("ctx", "wshard"),
            P("ctx", "wshard"),
            P("ctx", "wshard"),
            P("wshard", "ctx"),
            P(),
            P("ctx", "wshard"),
            P("ctx", "wshard"),
            P("wshard", "ctx"),
        ),
        out_specs=(
            P("wshard", None, "ctx", None),
            P("wshard", None, "ctx", None),
            P(("ctx", "wshard")),
            P("ctx", "wshard"),
            P("ctx", "wshard"),
            P("ctx", "wshard"),
            P("wshard", "ctx"),
            P(("ctx", "wshard")),
            P("ctx", "wshard"),
            P("ctx", "wshard"),
            P("wshard", "ctx"),
        ),
        check_vma=False,
    )
```

```python
from functools import partial

import jax
import jax.numpy as jnp
from jax import lax
from jax.experimental import pallas as pl
from jax.experimental.pallas import tpu as pltpu
from jax.sharding import PartitionSpec as P

MESH = pl.DeviceIdType.MESH
HD = 64
EPS = 1e-05
NEG = -1e30
F32 = jnp.float32
BF16 = jnp.bfloat16
VMEM_LIMIT = 63 * 2**20
ANY = pl.BlockSpec(memory_space=pl.ANY)
VMEM = pl.BlockSpec(memory_space=pltpu.VMEM)


class Place:
    def __init__(self):
        ctx, shard = lax.axis_index("ctx"), lax.axis_index("wshard")
        self.x, self.z, self.y = ctx // 8, (ctx // 2) % 4, ctx % 2
        self.yl, self.co = shard // 2, shard % 2

    def at(self, x=None, z=None, y=None, yl=None, co=None):
        x, z, y = (self.x if x is None else x), (self.z if z is None else z), (self.y if y is None else y)
        yl, co = (self.yl if yl is None else yl), (self.co if co is None else co)
        return (x * 8 + z * 2 + y, yl * 2 + co)

    def step(self, axis, by):
        return self.at(**{axis: (getattr(self, axis) + by) % 4})

    def pair(self, axis):
        return self.at(**{axis: 1 - getattr(self, axis)})

    def ctx_peers(self):
        return [self.step("x", 1), self.step("x", 3), self.step("z", 1), self.step("z", 3), self.pair("y")]

    def shard_peers(self):
        return [self.pair("co"), self.pair("yl")]

    def far_peers(self):
        return [self.step("x", 2), self.step("z", 2)]


def greet(peers):
    barrier = pltpu.get_barrier_semaphore()
    for device in peers:
        pl.semaphore_signal(barrier, inc=1, device_id=device, device_id_type=MESH)
    pl.semaphore_wait(barrier, len(peers))


class Copies:
    def __init__(self, send, recv):
        self.send, self.recv, self.used = send, recv, 0

    def start(self, src, dst, device):
        k = self.used
        self.used += 1
        copy = pltpu.make_async_remote_copy(
            src_ref=src, dst_ref=dst, send_sem=self.send.at[k], recv_sem=self.recv.at[k],
            device_id=device, device_id_type=MESH,
        )
        copy.start()
        return copy

    def local(self, src, dst):
        k = self.used
        self.used += 1
        copy = pltpu.make_async_copy(src, dst, self.send.at[k])
        copy.start()
        return copy


def wait_all(copies):
    for copy in copies:
        copy.wait()


class CtxGather:
    COPIES = 10
    STAGES = 6

    def __init__(self, place, copies, shard, full, lo, n, big):
        self.p, self.c, self.shard, self.full = place, copies, shard, full
        self.lo, self.n, self.big, self.small = lo, n, big, ("z" if big == "x" else "x")
        self.live = []

    def block(self, o, i, y):
        x, z = (o, i) if self.big == "x" else (i, o)
        return self.full.at[x, z, y, pl.ds(self.lo, self.n)]

    def send(self, part, axis, by):
        dev = self.p.pair("y") if axis == "y" else self.p.step(axis, by)
        self.live.append(self.c.start(part, part, dev))

    def stage(self, s):
        p = self.p
        o, i, y = getattr(p, self.big), getattr(p, self.small), p.y
        wait_all(self.live)
        self.live = []
        every, both = pl.ds(0, 4), pl.ds(0, 2)
        if s == 0 and self.shard is None:
            self.send(self.block(o, i, y), "y", 0)
        elif s == 0:
            own = self.shard.at[pl.ds(self.lo, self.n)]
            self.live.append(self.c.start(own, self.block(o, i, y), p.pair("y")))
            self.live.append(self.c.local(own, self.block(o, i, y)))
        elif s == 1:
            self.send(self.block(o, i, both), self.small, 1)
            self.send(self.block(o, i, both), self.small, 3)
        elif s == 2:
            self.send(self.block(o, (i + 3) % 4, 0), self.small, 1)
            self.send(self.block(o, (i + 1) % 4, 1), self.small, 3)
        elif s == 3:
            self.send(self.block(o, every, both), self.big, 1)
            self.send(self.block(o, every, both), self.big, 3)
        elif s == 4:
            self.send(self.block((o + 3) % 4, pl.ds(0, 2), both), self.big, 1)
            self.send(self.block((o + 1) % 4, pl.ds(2, 2), both), self.big, 3)


class CtxGatherLate(CtxGather):
    def block(self, o, i, y, lo=None, n=None):
        x, z = (o, i) if self.big == "x" else (i, o)
        return self.full.at[x, z, y, pl.ds(self.lo if lo is None else lo, self.n if n is None else n)]

    def stage(self, s):
        p = self.p
        o, i, y = getattr(p, self.big), getattr(p, self.small), p.y
        wait_all(self.live)
        self.live = []
        every, half = pl.ds(0, 4), self.n // 2
        if s == 0:
            own = self.shard.at[pl.ds(self.lo, self.n)]
            for by in (1, 3):
                self.live.append(self.c.start(own, self.block(o, i, y), p.step(self.big, by)))
            self.live.append(self.c.local(own, self.block(o, i, y)))
        elif s == 1:
            self.send(self.block((o + 3) % 4, i, y, self.lo, half), self.big, 1)
            self.send(self.block((o + 1) % 4, i, y, self.lo + half, half), self.big, 3)
        elif s == 2:
            self.send(self.block(every, i, y), self.small, 1)
            self.send(self.block(every, i, y), self.small, 3)
        elif s == 3:
            self.send(self.block(pl.ds(0, 2), (i + 3) % 4, y), self.small, 1)
            self.send(self.block(pl.ds(2, 2), (i + 1) % 4, y), self.small, 3)
        elif s == 4:
            self.send(self.block(every, every, y), "y", 0)


class CtxScatter:
    COPIES = 17
    STAGES = 7

    @staticmethod
    def scratch(n, width, staged=False):
        shapes = [(2, 2, 2), (4, 2), (4, 2), (2,), (2,), (2,), ()]
        if staged:
            shapes += [(2, 2), (2, 2)]
        return [pltpu.VMEM(shape + (n, width), BF16) for shape in shapes]

    def __init__(self, place, copies, src, out, bufs, lo, n, big, stop=False, resumed=None):
        self.p, self.c, self.src, self.out = place, copies, src, out
        self.far, self.pos, self.neg, self.far2, self.pos2, self.neg2, self.last = bufs[:7]
        self.staged = bufs[7:]
        self.lo, self.n, self.big, self.small = lo, n, big, ("z" if big == "x" else "x")
        self.first, self.live = [], []
        self.stop, self.resumed = stop, resumed
        if resumed is not None:
            self.live = [resumed]

    def part(self, o, i):
        x, z = (o, i) if self.big == "x" else (i, o)
        return self.src.at[x, z, pl.ds(0, 2), pl.ds(self.lo, self.n)]

    def load(self, o, i, y, which):
        if self.staged:
            return self.staged[which][i % 2, y].astype(F32)
        x, z = (o, i) if self.big == "x" else (i, o)
        return self.src[x, z, y, pl.ds(self.lo, self.n), :].astype(F32)

    def send(self, src, dst, axis, by):
        dev = self.p.pair("y") if axis == "y" else self.p.step(axis, by)
        copy = self.c.start(src, dst, dev)
        self.live.append(copy)
        return copy

    def stage(self, s):
        p, big, small = self.p, self.big, self.small
        o, i, y = getattr(p, big), getattr(p, small), p.y
        up, down, across = (o + 1) % 4, (o + 3) % 4, (o + 2) % 4
        iup, idown, iacross = (i + 1) % 4, (i + 3) % 4, (i + 2) % 4
        low, high = pl.ds(0, 2), pl.ds(2, 2)
        if s == 2:
            wait_all(self.first)
        elif s > 2:
            wait_all(self.live)
            self.live = []
        if s == 0:
            for src, dst, by in (
                (self.part(across, low), self.far.at[0], 1), (self.part(across, high), self.far.at[1], 3)
            ):
                self.first.append(self.c.start(src, dst, p.step(big, by)))
            if self.staged:
                self.first.append(self.c.local(self.part(up, low), self.staged[0]))
                self.first.append(self.c.local(self.part(down, high), self.staged[1]))
        elif s == 1:
            self.send(self.part(up, high), self.pos.at[high], big, 1)
            self.send(self.part(down, low), self.neg.at[low], big, 3)
        elif s == 2:

            def fold(k, _):
                b, q = k // 2, k % 2
                self.far[0, b, q] = (self.far[0, b, q].astype(F32) + self.load(up, b, q, 0)).astype(BF16)
                self.far[1, b, q] = (self.far[1, b, q].astype(F32) + self.load(down, b + 2, q, 1)).astype(BF16)
                return 0

            lax.fori_loop(0, 4, fold, 0)
            self.send(self.far.at[0], self.pos.at[low], big, 1)
            self.send(self.far.at[1], self.neg.at[high], big, 3)
            if self.staged:
                self.live.append(self.c.local(self.part(o, low), self.staged[0]))
                self.live.append(self.c.local(self.part(o, high), self.staged[1]))
        elif s == 3:

            def total(k, _):
                b, q = k // 2, k % 2
                for which in range(2):
                    at = b + 2 * which
                    here = self.load(o, at, q, which) + self.pos[at, q].astype(F32) + self.neg[at, q].astype(F32)
                    self.pos[at, q] = here.astype(BF16)
                return 0

            if self.resumed is None:
                lax.fori_loop(0, 4, total, 0)
            if self.stop:
                self.live = [self.c.local(self.pos, self.out)]
                return
            self.first = [
                self.c.start(self.pos.at[iacross, 0], self.far2.at[0], p.step(small, 1)),
                self.c.start(self.pos.at[iacross, 1], self.far2.at[1], p.step(small, 3)),
            ]
            self.send(self.pos.at[iup, 1], self.pos2.at[1], small, 1)
            self.send(self.pos.at[idown, 0], self.neg2.at[0], small, 3)
        elif s == 4:
            wait_all(self.first)
            self.far2[0] = (self.far2[0].astype(F32) + self.pos[iup, 0].astype(F32)).astype(BF16)
            self.far2[1] = (self.far2[1].astype(F32) + self.pos[idown, 1].astype(F32)).astype(BF16)
            self.send(self.far2.at[0], self.pos2.at[0], small, 1)
            self.send(self.far2.at[1], self.neg2.at[1], small, 3)
        elif s == 5:
            for q in range(2):
                here = self.pos[i, q].astype(F32) + self.pos2[q].astype(F32) + self.neg2[q].astype(F32)
                self.pos2[q] = here.astype(BF16)
            self.send(self.pos2.at[1 - y], self.last, "y", 0)
        elif s == 6:
            total = self.pos2[y].astype(F32) + self.last[...].astype(F32)
            self.out[pl.ds(self.lo, self.n), :] = total.astype(self.out.dtype)


class CtxScatterLate:
    COPIES = 19
    STAGES = 6

    @staticmethod
    def scratch(n, width):
        shapes = [(4, 4, n), (4, 4, n), (2, 2, n), (4, n), (4, n), (2, n // 2), (2, n // 2), (2, n // 2)]
        return [pltpu.VMEM(shape + (width,), BF16) for shape in shapes]

    def __init__(self, place, copies, src, out, bufs, lo, n, big):
        self.p, self.c, self.src, self.out = place, copies, src, out
        self.all, self.staged, self.far, self.pos, self.neg, self.far2, self.pos2, self.neg2 = bufs
        self.lo, self.n, self.big, self.small = lo, n, big, ("z" if big == "x" else "x")
        self.first, self.live, self.loads = [], [], []

    def part(self, o, i):
        x, z = (o, i) if self.big == "x" else (i, o)
        return self.all.at[x, z]

    def load(self, o, i):
        x, z = (o, i) if self.big == "x" else (i, o)
        return self.all[x, z].astype(F32)

    def start(self, src, dst, axis, by):
        return self.c.start(src, dst, self.p.pair("y") if axis == "y" else self.p.step(axis, by))

    def stage_own(self, o):
        every, rows = pl.ds(0, 4), pl.ds(self.lo, self.n)
        x, z = (o, every) if self.big == "x" else (every, o)
        self.loads.append(self.c.local(self.src.at[x, z, self.p.y, rows], self.staged.at[o]))

    def stage(self, s):
        p, big, small, n = self.p, self.big, self.small, self.n
        o, i = getattr(p, big), getattr(p, small)
        up, down, across = (o + 1) % 4, (o + 3) % 4, (o + 2) % 4
        iup, idown, iacross = (i + 1) % 4, (i + 3) % 4, (i + 2) % 4
        low, high, every = pl.ds(0, 2), pl.ds(2, 2), pl.ds(0, 4)
        rows = [pl.ds(0, n // 2), pl.ds(n // 2, n // 2)]
        if s in (2, 4):
            wait_all(self.first)
        else:
            wait_all(self.live)
            self.live = []
        if s == 0:
            theirs = self.src.at[every, every, 1 - p.y, pl.ds(self.lo, n)]
            self.live = [self.start(theirs, self.all, "y", 0)]
            for slab in range(4):
                self.stage_own(slab)
        elif s == 1:
            for slab in range(4):
                self.loads[slab].wait()

                def add(k, _):
                    x, z = (slab, k) if big == "x" else (k, slab)
                    here = self.all[x, z].astype(F32) + self.staged[slab, k].astype(F32)
                    self.all[x, z] = here.astype(BF16)
                    return 0

                lax.fori_loop(0, 4, add, 0)
            self.first = [
                self.start(self.part(across, low), self.far.at[0], big, 1),
                self.start(self.part(across, high), self.far.at[1], big, 3),
            ]
            self.live = [
                self.start(self.part(up, high), self.pos.at[high], big, 1),
                self.start(self.part(down, low), self.neg.at[low], big, 3),
            ]
        elif s == 2:
            for b in range(2):
                self.far[0, b] = (self.far[0, b].astype(F32) + self.load(up, b)).astype(BF16)
                self.far[1, b] = (self.far[1, b].astype(F32) + self.load(down, b + 2)).astype(BF16)
            self.live += [
                self.start(self.far.at[0], self.pos.at[low], big, 1),
                self.start(self.far.at[1], self.neg.at[high], big, 3),
            ]
        elif s == 3:
            for b in range(4):
                here = self.load(o, b) + self.pos[b].astype(F32) + self.neg[b].astype(F32)
                self.pos[b] = here.astype(BF16)
            self.first = [
                self.start(self.pos.at[iacross, rows[0]], self.far2.at[0], small, 1),
                self.start(self.pos.at[iacross, rows[1]], self.far2.at[1], small, 3),
            ]
            self.live = [
                self.start(self.pos.at[iup, rows[1]], self.pos2.at[1], small, 1),
                self.start(self.pos.at[idown, rows[0]], self.neg2.at[0], small, 3),
            ]
        elif s == 4:
            self.far2[0] = (self.far2[0].astype(F32) + self.pos[iup, rows[0], :].astype(F32)).astype(BF16)
            self.far2[1] = (self.far2[1].astype(F32) + self.pos[idown, rows[1], :].astype(F32)).astype(BF16)
            self.live += [
                self.start(self.far2.at[0], self.pos2.at[0], small, 1),
                self.start(self.far2.at[1], self.neg2.at[1], small, 3),
            ]
        elif s == 5:
            for h in range(2):
                here = self.pos[i, rows[h], :].astype(F32) + self.pos2[h].astype(F32) + self.neg2[h].astype(F32)
                self.out[pl.ds(self.lo + h * (n // 2), n // 2), :] = here


class ShardGather:
    def __init__(self, place, copies, full, chunks):
        self.p, self.c, self.full, self.chunks = place, copies, full, chunks
        self.rows = full.shape[1] // chunks
        self.me, self.over = place.yl * 2 + place.co, (1 - place.yl) * 2 + place.co
        self.far, self.near = [], []

    COPIES = 3

    def part(self, who, k):
        return self.full.at[who, pl.ds(k * self.rows, self.rows)]

    def send(self, k, src=None):
        src = self.part(self.me, k) if src is None else src
        self.far.append(self.c.start(src, self.part(self.me, k), self.p.pair("yl")))
        self.near.append(self.c.start(src, self.part(self.me, k), self.p.pair("co")))

    def forward(self, k):
        self.far[k].wait()
        self.near.append(self.c.start(self.part(self.over, k), self.part(self.over, k), self.p.pair("co")))

    def finish(self):
        wait_all(self.near)


class ShardScatter:
    COPIES = 3

    @staticmethod
    def scratch(rows, width):
        return [pltpu.VMEM((rows, width), BF16)] * 3

    def __init__(self, place, copies, part, bufs, chunks):
        self.p, self.c, self.part, self.chunks = place, copies, part, chunks
        self.relay, self.near, self.over = bufs
        self.rows = part.shape[1] // chunks
        self.first, self.second, self.third = [], [], []

    def at(self, k):
        return pl.ds(k * self.rows, self.rows)

    def begin(self):
        self.begin_far()
        self.begin_near()

    def begin_far(self):
        p = self.p
        for k in range(self.chunks):
            src = self.part.at[(1 - p.yl) * 2 + 1 - p.co, self.at(k)]
            self.first.append(self.c.start(src, self.relay.at[self.at(k)], p.pair("co")))

    def begin_near(self):
        p = self.p
        for k in range(self.chunks):
            src = self.part.at[p.yl * 2 + 1 - p.co, self.at(k)]
            self.second.append(self.c.start(src, self.near.at[self.at(k)], p.pair("co")))

    def relay_on(self, k):
        p = self.p
        self.first[k].wait()
        here = self.part[(1 - p.yl) * 2 + p.co, self.at(k), :].astype(F32)
        self.relay[self.at(k), :] = (self.relay[self.at(k), :].astype(F32) + here).astype(BF16)
        self.third.append(self.c.start(self.relay.at[self.at(k)], self.over.at[self.at(k)], p.pair("yl")))

    def total(self, k):
        p = self.p
        self.second[k].wait()
        self.third[k].wait()
        here = self.part[p.yl * 2 + p.co, self.at(k), :].astype(F32)
        return here + self.near[self.at(k), :].astype(F32) + self.over[self.at(k), :].astype(F32)


class ShardScatterColumns(ShardScatter):
    def __init__(self, place, copies, part, bufs, chunks):
        super().__init__(place, copies, part, bufs, chunks)
        self.columns = part.shape[2] // chunks

    def begin(self, k):
        p, cols = self.p, pl.ds(k * self.columns, self.columns)
        far, near = (1 - p.yl) * 2 + 1 - p.co, p.yl * 2 + 1 - p.co
        self.first.append(self.c.start(self.part.at[far, :, cols], self.relay.at[:, cols], p.pair("co")))
        self.second.append(self.c.start(self.part.at[near, :, cols], self.near.at[:, cols], p.pair("co")))

    def relay_on(self, k):
        p, cols = self.p, pl.ds(k * self.columns, self.columns)
        self.first[k].wait()
        here = self.part[(1 - p.yl) * 2 + p.co, :, cols].astype(F32)
        self.relay[:, cols] = (self.relay[:, cols].astype(F32) + here).astype(BF16)
        self.third.append(self.c.start(self.relay.at[:, cols], self.over.at[:, cols], p.pair("yl")))

    def total(self, k):
        if k == 0:
            wait_all(self.second + self.third)
        here = self.part[self.p.yl * 2 + self.p.co, self.at(k), :].astype(F32)
        return here + self.near[self.at(k), :].astype(F32) + self.over[self.at(k), :].astype(F32)


class GainScatter:
    COPIES = 9
    STAGES = 6

    @staticmethod
    def scratch():
        return [
            pltpu.VMEM((8, 2048), F32),
            pltpu.VMEM((3, 8, 512), F32),
            pltpu.VMEM((8, 512), F32),
            pltpu.VMEM((3, 8, 128), F32),
            pltpu.VMEM((3, 8, 128), F32),
            pltpu.VMEM((3, 8, 128), F32),
        ]

    def __init__(self, place, copies, out, bufs):
        self.p, self.c, self.out = place, copies, out
        self.vec, self.xs, self.mid, self.zs, self.own, self.rest = bufs
        self.live = []

    def stage(self, s):
        p = self.p
        wait_all(self.live)
        self.live = []
        if s == 0:
            for by in (1, 2, 3):
                cols = pl.ds(pl.multiple_of(((p.x + by) % 4) * 512, 512), 512)
                self.live.append(self.c.start(self.vec.at[:, cols], self.xs.at[by - 1], p.step("x", by)))
        elif s == 1:
            cols = pl.ds(pl.multiple_of(p.x * 512, 512), 512)
            self.mid[...] = self.vec[:, cols] + self.xs[0] + self.xs[1] + self.xs[2]
            for by in (1, 2, 3):
                cols = pl.ds(pl.multiple_of(((p.z + by) % 4) * 128, 128), 128)
                self.live.append(self.c.start(self.mid.at[:, cols], self.zs.at[by - 1], p.step("z", by)))
        elif s == 2:
            cols = pl.ds(pl.multiple_of(p.z * 128, 128), 128)
            self.own[0] = self.mid[:, cols] + self.zs[0] + self.zs[1] + self.zs[2]
            self.live.append(self.c.start(self.own.at[0], self.rest.at[0], p.pair("y")))
        elif s == 3:
            self.own[1] = self.own[0] + self.rest[0]
            self.live.append(self.c.start(self.own.at[1], self.rest.at[1], p.pair("co")))
        elif s == 4:
            self.own[2] = self.own[1] + self.rest[1]
            self.live.append(self.c.start(self.own.at[2], self.rest.at[2], p.pair("yl")))
        elif s == 5:
            self.out[...] = self.own[2] + self.rest[2]


def sems(n):
    return [pltpu.SemaphoreType.DMA((n,)), pltpu.SemaphoreType.DMA((n,))]


def params(cid):
    return pltpu.CompilerParams(collective_id=cid, has_side_effects=True, vmem_limit_bytes=VMEM_LIMIT)


def halves(rows):
    return ((0, rows // 2, "x"), (rows // 2, rows // 2, "z"))


CHUNKS = 4


def norm_back_rows(grad, resid, gain):
    factor = lax.rsqrt(jnp.mean(resid * resid, -1, keepdims=True) + EPS)
    weighted = grad * gain
    per_gain = grad * resid * factor
    back = factor * weighted - resid * (factor * factor * factor) * jnp.mean(weighted * resid, -1, keepdims=True)
    return back, per_gain


def eight(rows):
    return jnp.sum(rows.reshape(rows.shape[0] // 8, 8, rows.shape[1]), 0)


KEYS = 256
KB = 4


def lane_iota(rows):
    return lax.broadcasted_iota(jnp.int32, (rows, 128), 1)


def rotate_tile(u, cosine, sine):
    low = lane_iota(u.shape[0]) % HD < HD // 2
    turned = jnp.where(low, -pltpu.roll(u, 128 - HD // 2, 1), pltpu.roll(u, HD // 2, 1))
    return u * cosine + turned * sine


def unrotate_tile(w, cosine, sine):
    low = lane_iota(w.shape[0]) % HD < HD // 2
    s = w * sine
    return w * cosine + jnp.where(low, pltpu.roll(s, 128 - HD // 2, 1), -pltpu.roll(s, HD // 2, 1))


def project_rows(rows, w_qkv, tables):
    lin = jnp.dot(rows, w_qkv, preferred_element_type=F32)
    tiles = []
    for hp in range(4):
        tile = lin[:, hp * 128 : (hp + 1) * 128]
        tiles.append((rotate_tile(tile, tables[0], tables[1])).astype(BF16) * jnp.asarray(HD**-0.5, BF16))
    kv = rotate_tile(lin[:, 512:640], tables[2], tables[3]).astype(BF16)
    return tiles, kv


def head_rows(ref, start, keep_low):
    low = lane_iota(64) < HD
    keep = low if keep_low else ~low
    pieces = []
    for hp in range(4):
        tile = ref[pl.ds(start, 64), hp * 128 : (hp + 1) * 128].astype(F32)
        turned = pltpu.roll(tile, HD, 1)
        even, odd = (tile, turned) if keep_low else (turned, tile)
        pieces += [jnp.where(keep, even, 0.0), jnp.where(keep, odd, 0.0)]
    return pieces


def key_chunk(kv, seq, chunk, half):
    start = pl.multiple_of(seq * 128 + half * 64, 64)
    z = pl.ds((chunk % 2) * 2, 2)
    return kv[chunk // 2, z, :, pl.ds(start, 64), :].reshape(KEYS, 128)


def diagonal(block, here):
    key = lax.broadcasted_iota(jnp.int32, (KEYS, 512), 0)
    query = lax.broadcasted_iota(jnp.int32, (KEYS, 512), 1) % 64
    ahead = key // 64 - here
    return key % 64 - query <= (-ahead if block == 0 else ahead) * 64


def pick(u, own_chunk):
    late = u - 8
    block = jnp.where(u < 8, 1, jnp.where(late >= own_chunk, 1, 0))
    half = jnp.where(u < 8, 0, block)
    chunk = jnp.where(u < 8, u, late + half)
    return block, chunk, half


def nt(a, b):
    return lax.dot_general(a, b, (((1,), (1,)), ((), ())), preferred_element_type=F32)


def tn(a, b):
    return lax.dot_general(a, b, (((0,), (0,)), ((), ())), preferred_element_type=F32)


def attend_seq(seq, ctx, q, kv, attn, lse, scratch):
    qe, top, acc = scratch
    low = lane_iota(64) < HD
    ones_low = lane_iota(KEYS) < HD
    own_chunk, here = ctx // KB, ctx % KB

    def with_ones(keys):
        return jnp.where(ones_low, jnp.ones_like(keys), keys)

    for b in range(2):
        for h, piece in enumerate(head_rows(q, seq * 128 + b * 64, True)):
            qe[b, h * 64 : (h + 1) * 64, :] = piece.astype(BF16)
    for b in range(2):
        keys = key_chunk(kv, seq, own_chunk, b)
        scores = jnp.where(diagonal(b, here), nt(keys, qe[b]), NEG)
        m = jnp.max(scores, 0, keepdims=True)
        p = jnp.exp(scores - m).astype(BF16)
        top[b] = m
        acc[b] = tn(with_ones(keys), p)

    def step(u, _):
        b, chunk, half = pick(u, own_chunk)
        keys = key_chunk(kv, seq, chunk, half)
        scores = nt(keys, qe[b])
        before = top[b]
        m = jnp.maximum(before, jnp.max(scores, 0, keepdims=True))
        p = jnp.exp(scores - m).astype(BF16)
        top[b] = m
        acc[b] = acc[b] * jnp.exp(before - m) + tn(with_ones(keys), p)
        return 0

    for k in range(3):
        lax.fori_loop(5 * k, 5 * k + 5, step, 0, unroll=True)
        if k < 2:
            yield
    for b in range(2):
        here_acc = acc[b]
        total = here_acc[0:1, :]
        lse[pl.ds(seq * 2 + b, 1), :] = top[b] + jnp.log(total)
        out = (here_acc * (1.0 / total)).T
        for hp in range(4):
            even, odd = out[hp * 128 : hp * 128 + 64, :], out[hp * 128 + 64 : hp * 128 + 128, :]
            tile = jnp.where(low, pltpu.roll(even, HD, 1), odd)
            attn[pl.ds(seq * 128 + b * 64, 64), hp * 128 : (hp + 1) * 128] = tile.astype(BF16)


def attend_scratch():
    return [pltpu.VMEM((2, 512, 128), BF16), pltpu.VMEM((2, 1, 512), F32), pltpu.VMEM((2, 128, 512), F32)]


def attend_back_seq(seq, ctx, q, kv, grad, attn, lse, tables, grad_lin, grad_kv, scratch):
    qd, delta, dq, dkv = scratch
    low = lane_iota(64) < HD
    own_chunk, here = ctx // KB, ctx % KB
    for b in range(2):
        start = seq * 128 + b * 64
        q_rows, g_rows, o_rows = (
            head_rows(q, start, True), head_rows(grad, start, False), head_rows(attn, start, False)
        )
        for h in range(8):
            qd[b, h * 64 : (h + 1) * 64, :] = q_rows[h].astype(BF16)
            qd[b, 512 + h * 64 : 512 + (h + 1) * 64, :] = g_rows[h].astype(BF16)
        products = jnp.concatenate([g * o for g, o in zip(g_rows, o_rows)], 0)
        delta[b] = jnp.sum(products.T, 0, keepdims=True)

    def grads(b, keys, allowed):
        both = nt(keys, qd[b])
        p = jnp.exp(both[:, :512] - lse[pl.ds(seq * 2 + b, 1), :])
        if allowed is not None:
            p = jnp.where(allowed, p, 0.0)
        ds = (p * (both[:, 512:] - delta[b])).astype(BF16)
        joined = jnp.concatenate([ds, p.astype(BF16)], 1)
        return tn(keys, ds), jnp.dot(joined, qd[b], preferred_element_type=F32)

    dkv[...] = jnp.zeros_like(dkv)

    def add_keys(chunk, half, value):
        start = pl.multiple_of(half * 64, 64)
        dkv[pl.ds(chunk * KB, KB), pl.ds(start, 64), :] += value.reshape(KB, 64, 128)

    for b in range(2):
        dq_part, dkv_part = grads(b, key_chunk(kv, seq, own_chunk, b), diagonal(b, here))
        dq[b] = dq_part
        add_keys(own_chunk, b, dkv_part)

    def step(u, _):
        b, chunk, half = pick(u, own_chunk)
        dq_part, dkv_part = grads(b, key_chunk(kv, seq, chunk, half), None)
        dq[b] += dq_part
        add_keys(chunk, half, dkv_part)
        return 0

    for k in range(3):
        lax.fori_loop(5 * k, 5 * k + 5, step, 0, unroll=True)
        if k < 2:
            yield
    for b in range(2):
        out = (dq[b] * HD**-0.5).T
        cosine, sine = tables[0, b * 64 : (b + 1) * 64, :], tables[1, b * 64 : (b + 1) * 64, :]
        for hp in range(4):
            even, odd = out[hp * 128 : hp * 128 + 64, :], out[hp * 128 + 64 : hp * 128 + 128, :]
            tile = jnp.where(low, even, pltpu.roll(odd, HD, 1))
            tile = unrotate_tile(tile, cosine, sine)
            grad_lin[pl.ds(seq * 128 + b * 64, 64), hp * 128 : (hp + 1) * 128] = tile.astype(BF16)
    grad_kv[...] = dkv[...].reshape(4, 4, 2, 128, 128).astype(BF16)


def attend_back_scratch():
    return [
        pltpu.VMEM((2, 1024, 128), BF16),
        pltpu.VMEM((2, 1, 512), F32),
        pltpu.VMEM((2, 128, 512), F32),
        pltpu.VMEM((32, 128, 128), F32),
    ]


def ctx_gathers(place, copies, src, full, kind=CtxGather):
    return [kind(place, copies, src, full, lo, rows, big) for lo, rows, big in halves(src.shape[0])]


FORWARD = [
    "w0", "N1", "o0", "d0", "w1", "d1", "w2", "w3", "u0", "d2", "CB", "w4", "NF", "g0", "o1", "d3", "u1", "w5",
    "NW", "J0", "k00", "J3", "k30", "J1", "k10", "J2", "k20", "d4", "CF", "g1", "k31", "k01", "o2", "k11", "g2",
    "k21", "k02", "k12", "k32", "o3", "CW", "k22", "k33", "k13", "k03", "k04", "o4", "k23", "k05", "k34", "k14",
    "A00", "A01", "u2", "k24", "A02", "k15", "o5", "g3", "A10", "k25", "OP0", "A11", "u3", "A12", "k35", "A20",
    "A21", "OP1", "A22", "g4", "RF", "A30", "RR", "OP2", "RN", "A31", "A32", "d5", "DA", "OP3", "NT", "u4", "SF",
    "SW", "u5", "g5", "FU", "T0", "T1", "XR0", "GD", "e0", "XR1", "T2", "T3", "XR2", "XR3", "e1", "RP", "e2", "XT",
    "GU", "GG", "XF", "e3", "XW",
]

BACKWARD = [
    "u0", "g0", "DO", "DP", "GO", "g1", "o0", "A00", "A01", "o1", "A02", "k00", "A10", "A11", "o2", "g2", "d3",
    "k01", "A12", "k02", "RESB", "A20", "A21", "k10", "k11", "A22", "k20", "A30", "k12", "g3", "k21", "A31", "d4",
    "A32", "k30", "QG", "k31", "k22", "k03", "k13", "RESR", "k32", "k04", "g4", "k33", "k23", "k14", "q0", "k34",
    "k24", "q1", "k15", "u1", "q2", "k25", "RES", "k16", "I1", "k26", "k35", "k05", "I2", "d5", "o3", "k06", "k36",
    "I3", "I0", "VG", "v0", "v1", "g5", "q3", "u2", "v2", "TOT", "n0", "q4", "o4", "v3", "n1", "u3", "n2", "v4",
    "q5", "o5", "u4", "n3", "v5", "q6", "n4", "v6", "u5", "o6", "g6", "d6", "n5",
]


def run_steps(steps, engines, actions):
    for step in steps:
        if step in actions:
            actions[step]()
        else:
            for e in engines[step[:-1]]:
                e.stage(int(step[-1]))


def gain_row(ref):
    gain = ref[...].astype(F32)
    return jnp.concatenate([gain[k : k + 1, :] for k in range(16)], 1)


def over_hidden_units(tile):
    def one(j, _):
        tile(pl.ds(pl.multiple_of(j * 512, 512), 512), 512)
        return 0

    lax.fori_loop(0, 2, one, 0)
    tile(pl.ds(1024, 384), 384)


def over_width(step):
    def one(j, _):
        step(j, pl.ds(pl.multiple_of(j * 512, 512), 512))
        return 0

    lax.fori_loop(0, 4, one, 0)


def forward_kernel(
    x, cot, gain1, gain2, tables, wq, wk, wv, w_out_shard, w_gate_shard, w_up_shard, w_down_shard,
    normed1_out, w_qkv_out, w_out_out, q, kv_out, attn, lse, hidden, branch_out, grad_hidden, grad_gain,
    result_out, g_gate_out, g_up_out, g_down_x, g_down_z,
    normed1_all, w_qkv_shard, w_qkv, w_out, kv_all, part, relay, near, over, qe, top, acc,
    w_gate, w_up, w_down, g_down, cot_all, normed2_all, gate_pre, up_pre, active, grad_gate, grad_up, branch,
    *rest,
):
    bufs, (send, recv) = rest[:14], rest[14:]
    place = Place()
    greet(place.ctx_peers() + place.shard_peers())
    copies = Copies(send, recv)
    ctx = lax.axis_index("ctx")
    order = [2 * (1 - place.yl) + 1 - place.co, 2 * (1 - place.yl) + place.co]
    order += [2 * place.yl + 1 - place.co, 2 * place.yl + place.co]
    starts = [pl.multiple_of(seq * 128, 128) for seq in order]
    engines = {
        "w": ctx_gathers(place, copies, w_qkv_shard, w_qkv),
        "o": ctx_gathers(place, copies, w_out_shard, w_out),
        "g": ctx_gathers(place, copies, w_gate_shard, w_gate),
        "u": ctx_gathers(place, copies, w_up_shard, w_up),
        "d": ctx_gathers(place, copies, w_down_shard, w_down, CtxGatherLate),
    }
    for k in range(4):
        engines[f"k{k}"] = [CtxGather(place, copies, None, kv_all, starts[k], 128, "xz"[k % 2])]
    normed = ShardGather(place, copies, normed1_all, 1)
    cots = ShardGather(place, copies, cot_all, 1)
    rows_out = ShardScatter(place, copies, part, (relay, near, over), CHUNKS)
    spread = ShardGather(place, copies, normed2_all, CHUNKS)
    thirds = [attend_seq(seq, ctx, q, kv_all, attn, lse, (qe, top, acc)) for seq in order]
    back = ShardScatterColumns(place, copies, part, (relay, near, over), CHUNKS)
    branches = ShardGather(place, copies, branch, CHUNKS)
    engines["e"] = [
        CtxScatter(place, copies, g_down, out, bufs[7 * h : 7 * h + 7], lo, rows, big, stop=True)
        for h, (out, (lo, rows, big)) in enumerate(zip((g_down_x, g_down_z), halves(64)))
    ]
    outgoing, normed_copy = [], []
    w_qkv_shard[:, :512] = wq[...]
    w_qkv_shard[:, 512:640] = jnp.concatenate([wk[...], wv[...]], 1)

    def first_norm():
        rows = x[...].astype(F32)
        factor = lax.rsqrt(jnp.mean(rows * rows, -1, keepdims=True) + EPS)
        normed1_all[normed.me] = (rows * factor * gain_row(gain1)).astype(BF16)
        normed.send(0)

    def normed_here():
        normed.finish()
        normed_copy.append(copies.local(normed1_all, normed1_out))

    def project_seq(k):
        at = pl.ds(starts[k], 128)
        tiles, kv = project_rows(normed1_all[order[k]], w_qkv[...].reshape(2048, 640), tables)
        for hp, tile in enumerate(tiles):
            q[at, hp * 128 : (hp + 1) * 128] = tile
        kv_all[place.x, place.z, place.y, at, :] = kv

    own_cot = []

    def send_cot():
        cots.send(0, cot)
        own_cot.append(copies.local(cot, cot_all.at[cots.me]))

    def cot_here():
        cots.finish()
        wait_all(own_cot)

    def project_out(k):
        part[order[k]] = nt(attn[pl.ds(starts[k], 128), :], w_out[...].reshape(2048, 512)).astype(BF16)

    def relay_rows():
        for c in range(CHUNKS):
            rows_out.relay_on(c)

    def second_norm():
        outgoing.extend(copies.local(*pair) for pair in ((w_qkv, w_qkv_out), (w_out, w_out_out), (kv_all, kv_out)))
        gain = gain_row(gain2)
        for c in range(CHUNKS):
            at = rows_out.at(c)
            here = x[at, :].astype(F32) + rows_out.total(c)
            hidden[at, :] = here
            factor = lax.rsqrt(jnp.mean(here * here, -1, keepdims=True) + EPS)
            normed2_all[spread.me, at, :] = (here * factor * gain).astype(BF16)
            spread.send(c)

    def spread_on():
        for c in range(CHUNKS):
            spread.forward(c)

    def columns_of(w, cols, width):
        return w[:, :, :, :, cols].reshape(2048, width)

    def grad_active_tiles():
        def tile(cols, width):
            rows = cot_all[...].reshape(512, 2048)
            here = jnp.dot(rows, columns_of(w_down, cols, width), preferred_element_type=F32)
            grad_up[:, cols] = here.astype(BF16)

        over_hidden_units(tile)

    def hidden_units():
        def tile(cols, width):
            rows = normed2_all[...].reshape(512, 2048)
            here = pl.ds(0, width)
            gate_pre[:, here] = jnp.dot(rows, columns_of(w_gate, cols, width), preferred_element_type=F32)
            up_pre[:, here] = jnp.dot(rows, columns_of(w_up, cols, width), preferred_element_type=F32)

            def some(r, _):
                at = pl.ds(pl.multiple_of(r * 64, 64), 64)
                gate, up, grad = gate_pre[at, here], up_pre[at, here], grad_up[at, cols].astype(F32)
                sigmoid = 1.0 / (1.0 + jnp.exp(-gate))
                silu = gate * sigmoid
                active[at, cols] = (silu * up).astype(BF16)
                grad_gate[at, cols] = (grad * up * sigmoid * (1.0 + gate * (1.0 - sigmoid))).astype(BF16)
                grad_up[at, cols] = (grad * silu).astype(BF16)
                return 0

            lax.fori_loop(0, 8, some, 0)

        over_hidden_units(tile)

    def result_tiles():
        wait_all(normed_copy)
        result_part = normed1_all

        def step(j, cols):
            rows = nt(active[...], w_down[j].reshape(512, 1408))
            result_part[:, :, cols] = rows.astype(BF16).reshape(4, 128, 512)

        over_width(step)
        outgoing.append(copies.local(result_part, result_out))

    def grad_normed_tile(j):
        rows = nt(grad_gate[...], w_gate[j].reshape(512, 1408)) + nt(grad_up[...], w_up[j].reshape(512, 1408))
        part[:, :, j * 512 : (j + 1) * 512] = rows.astype(BF16).reshape(4, 128, 512)
        back.begin(j)

    def weight_grad(left, right, w):
        def step(j, cols):
            block = tn(left[:, :, cols].reshape(512, 512), right[...])
            w[j] = block.astype(BF16).reshape(4, 2, 64, 1408)

        over_width(step)

    def gate_grad():
        weight_grad(normed2_all, grad_gate, w_gate)
        outgoing.append(copies.local(w_gate, g_gate_out))

    def up_grad():
        weight_grad(normed2_all, grad_up, w_up)
        outgoing.append(copies.local(w_up, g_up_out))

    def second_norm_back():
        gain = gain_row(gain2)
        for c in range(CHUNKS):
            at = back.at(c)
            grad, per_gain = norm_back_rows(back.total(c), hidden[at, :], gain)
            here = cot_all[branches.me, at, :].astype(F32) + grad
            grad_hidden[at, :] = here
            branch[branches.me, at, :] = here.astype(BF16)
            branches.send(c)
            grad_gain[...] = eight(per_gain) if c == 0 else grad_gain[...] + eight(per_gain)

    def branch_on():
        for c in range(CHUNKS):
            branches.forward(c)

    def branch_here():
        branches.finish()
        outgoing.append(copies.local(branch, branch_out))

    actions = {
        "N1": first_norm, "NF": lambda: normed.forward(0), "NW": normed_here,
        "CB": send_cot, "CF": lambda: cots.forward(0), "CW": cot_here,
        "RF": rows_out.begin_far, "RR": relay_rows, "RN": rows_out.begin_near,
        "NT": second_norm, "SF": spread_on, "SW": spread.finish,
        "DA": grad_active_tiles, "FU": hidden_units, "RP": result_tiles,
        "GD": lambda: weight_grad(cot_all, active, g_down), "GG": gate_grad, "GU": up_grad, "XT": second_norm_back,
        "XF": branch_on, "XW": branch_here,
    }
    for k in range(4):
        actions[f"T{k}"] = partial(grad_normed_tile, k)
        actions[f"XR{k}"] = partial(back.relay_on, k)
        actions[f"J{k}"] = partial(project_seq, k)
        actions[f"OP{k}"] = partial(project_out, k)
        for third in range(3):
            actions[f"A{k}{third}"] = partial(next, thirds[k], None)
    run_steps(FORWARD, engines, actions)
    wait_all(outgoing + [copy for e in engines["e"] for copy in e.live])


def forward(cid, x, cot, gain1, gain2, tables, w_qkv, shards):
    tokens, width = x.shape
    every = (4, tokens, width)
    ffn_width = shards[1].shape[1]

    def full(n):
        return (4, 4, 2, 64, n)

    kv_all, totals = (4, 4, 2, 512, 128), (4, 2, 32, ffn_width)
    outs = [
        (ANY, every, BF16), (ANY, full(640), BF16), (ANY, full(512), BF16), (VMEM, (512, 512), BF16),
        (ANY, kv_all, BF16), (VMEM, (512, 512), BF16), (VMEM, (8, 512), F32), (VMEM, (tokens, width), F32),
        (ANY, every, BF16), (VMEM, (tokens, width), F32), (VMEM, (8, width), F32), (ANY, every, BF16),
        (ANY, full(ffn_width), BF16), (ANY, full(ffn_width), BF16), (ANY, totals, BF16), (ANY, totals, BF16),
    ]
    return pl.pallas_call(
        forward_kernel,
        out_shape=[jax.ShapeDtypeStruct(shape, dtype) for _, shape, dtype in outs],
        in_specs=[VMEM, ANY, VMEM, VMEM, VMEM, VMEM, VMEM, VMEM] + [ANY] * 4,
        out_specs=[space for space, _, _ in outs],
        scratch_shapes=[
            pltpu.VMEM(every, BF16),
            pltpu.VMEM((64, 640), BF16),
            pltpu.VMEM(full(640), BF16),
            pltpu.VMEM(full(512), BF16),
            pltpu.VMEM(kv_all, BF16),
            pltpu.VMEM(every, BF16),
            *ShardScatter.scratch(tokens, width),
            *attend_scratch(),
            *[pltpu.VMEM(full(ffn_width), BF16)] * 4,
            pltpu.VMEM(every, BF16),
            pltpu.VMEM(every, BF16),
            *[pltpu.VMEM((512, 512), F32)] * 2,
            *[pltpu.VMEM((512, ffn_width), BF16)] * 3,
            pltpu.VMEM(every, BF16),
            *CtxScatter.scratch(32, ffn_width),
            *CtxScatter.scratch(32, ffn_width),
            *sems(14 * CtxGather.COPIES + 2 * CtxScatter.COPIES + 12 * CHUNKS + 24),
        ],
        compiler_params=params(cid),
        name="forward",
    )(x, cot, gain1.reshape(16, 128), gain2.reshape(16, 128), tables, *w_qkv, *shards)


def backward_kernel(*refs):
    (
        branch_in, result_in, w_out_in, w_qkv_in, normed_in, g_gate, g_up, g_down_x, g_down_z,
        q_in, kv_in, attn_in, hidden_in, grad_hidden_in, x_in, grad_gain, lse, tables, gain1,
    ) = refs[:19]
    grad_inputs, gains, outputs, out_q, out_kv, out_o, out_gate, out_up, out_down = refs[19:28]
    normed, result_part, w_out, w_qkv, branch, dkv_send, relay, near, over = refs[28:37]
    grad_lin, grad_kv, g_query, g_kv, q, kv, attn, hidden, grad_hidden, x = refs[37:47]
    scratch, gain_bufs, bufs, (free, send, recv) = refs[47:51], refs[51:57], refs[57:-3], refs[-3:]
    place = Place()
    copies = Copies(send, recv)
    loads = [copies.local(a, b) for a, b in (
        (branch_in, branch), (w_out_in, w_out), (q_in, q), (kv_in, kv), (attn_in, attn), (result_in, result_part),
        (w_qkv_in, w_qkv), (normed_in, normed), (hidden_in, hidden), (grad_hidden_in, grad_hidden), (x_in, x),
    )]
    greet(place.ctx_peers() + place.shard_peers() + place.far_peers())
    ctx = lax.axis_index("ctx")
    me, co = 2 * place.yl + place.co, 2 * place.yl + 1 - place.co
    far, far_co = 2 * (1 - place.yl) + place.co, 2 * (1 - place.yl) + 1 - place.co
    order = [me, far_co, far, co]
    taken = 0

    def take(n):
        nonlocal taken
        taken += n
        return bufs[taken - n : taken]

    def rows_of(seq):
        return pl.ds(pl.multiple_of(seq * 128, 128), 128)

    engines = {}
    for name, src, out, count in (
        ("g", g_gate, out_gate, 9), ("o", w_out, out_o, 7), ("q", g_query, out_q, 7), ("v", g_kv, out_kv, 7),
    ):
        engines[name] = [
            CtxScatter(place, copies, src, out, take(count), lo, rows, big) for lo, rows, big in halves(64)
        ]
    for k in range(4):
        engines[f"k{k}"] = [
            CtxScatter(place, copies, dkv_send.at[k], grad_kv.at[rows_of(order[k])], take(7), 0, 128, "xz"[k % 2])
        ]
    engines["u"] = [
        CtxScatterLate(place, copies, g_up, out_up, take(8), lo, rows, big) for lo, rows, big in halves(64)
    ]
    engines["d"] = []
    for (lo, rows, big), totals in zip(halves(64), (g_down_x, g_down_z)):
        pos, far2, pos2, neg2, last = take(5)
        load = copies.local(totals, pos)
        engines["d"].append(
            CtxScatter(
                place, copies, None, out_down, (None, pos, None, far2, pos2, neg2, last), lo, rows, big, resumed=load
            )
        )
    gain_sum = GainScatter(place, copies, gains, gain_bufs)
    engines["n"] = [gain_sum]
    result = ShardScatter(place, copies, result_part, (relay, near, over), 1)
    last = ShardScatter(place, copies, branch, (relay, near, over), CHUNKS)
    thirds = [
        attend_back_seq(
            order[k], ctx, q, kv, grad_lin, attn, lse, tables, grad_lin, dkv_send.at[k], scratch
        )
        for k in range(4)
    ]

    def relay_rows(rows_scatter):
        for c in range(CHUNKS):
            rows_scatter.relay_on(c)

    def grad_rows(seq):
        w = w_out[...].reshape(2048, 512)
        grad_lin[rows_of(seq), :512] = jnp.dot(branch[seq], w, preferred_element_type=F32).astype(BF16)

    def grad_mixed_own():
        wait_all(loads[:5])
        grad_rows(me)

    def grad_mixed():
        for seq in order[1:]:
            grad_rows(seq)

    def begin_result():
        loads[5].wait()
        result.begin()

    def grad_of_out():
        rows = branch[...].reshape(512, 2048)
        for j in range(8):
            block = tn(rows[:, j * 256 : (j + 1) * 256], attn[...]).astype(BF16)
            w_out[j // 2, pl.ds((j % 2) * 2, 2)] = block.reshape(2, 2, 64, 512)

    def result_rows():
        loads[8].wait()
        outputs[...] = (hidden[...] + result.total(0)).astype(BF16)
        for device in place.shard_peers():
            pl.semaphore_signal(free, inc=1, device_id=device, device_id_type=MESH)

    def input_rows(k):
        if k == FIRST_INPUT_ROWS:
            loads[6].wait()
        at = rows_of(order[k])
        grad_lin[at, 512:640] = unrotate_tile(grad_kv[at, :], tables[2], tables[3]).astype(BF16)
        branch[order[k]] = nt(grad_lin[at, :], w_qkv[...].reshape(2048, 640)).astype(BF16)
        if k == 1:
            pl.semaphore_wait(free, 2)
            last.begin_far()
        elif k == 2:
            relay_rows(last)
        elif k == 3:
            last.begin_near()

    def weight_grad(w, start, width):
        def step(j, cols):
            block = tn(normed[:, :, cols].reshape(512, 512), grad_lin[:, start : start + width])
            w[j] = block.astype(BF16).reshape(4, 2, 64, width)

        over_width(step)

    def grad_of_query():
        loads[7].wait()
        weight_grad(g_query, 0, 512)

    def first_norm_back():
        wait_all(loads[9:])
        gain = gain_row(gain1)
        for c in range(CHUNKS):
            rows = last.at(c)
            back, per_gain = norm_back_rows(last.total(c), x[rows, :].astype(F32), gain)
            grad_inputs[rows, :] = (grad_hidden[rows, :] + back).astype(BF16)
            total = eight(per_gain) if c == 0 else total + eight(per_gain)
        row = lax.broadcasted_iota(jnp.int32, total.shape, 0)
        one, two = jnp.sum(total, 0, keepdims=True), jnp.sum(grad_gain[...], 0, keepdims=True)
        gain_sum.vec[...] = jnp.where(row == 0, one, jnp.where(row == 1, two, 0.0))

    actions = {
        "DO": grad_mixed_own, "DP": grad_mixed, "GO": grad_of_out, "RESB": begin_result,
        "RESR": lambda: result.relay_on(0), "RES": result_rows, "QG": grad_of_query,
        "VG": lambda: weight_grad(g_kv, 512, 128), "TOT": first_norm_back,
    }
    for k in range(4):
        actions[f"I{k}"] = partial(input_rows, k)
        for third in range(3):
            actions[f"A{k}{third}"] = partial(next, thirds[k], None)
    run_steps(BACKWARD, engines, actions)


def backward(cid, in_hbm, in_vmem):
    tokens, width = in_hbm[-1].shape
    ffn_width = in_hbm[5].shape[4]
    in_vmem = [a.reshape(16, 128) if a.ndim == 1 else a for a in in_vmem]
    scratch = []
    for _ in range(2):
        scratch += CtxScatter.scratch(32, ffn_width, True)
    for _ in range(4):
        scratch += CtxScatter.scratch(32, 512)
    for _ in range(2):
        scratch += CtxScatter.scratch(32, 128)
    for _ in range(4):
        scratch += CtxScatter.scratch(128, 128)
    for _ in range(2):
        scratch += CtxScatterLate.scratch(32, ffn_width)
    for _ in range(2):
        whole = CtxScatter.scratch(32, ffn_width)
        scratch += whole[1:2] + whole[3:]
    shapes = [
        ((tokens, width), BF16), ((8, 128), F32), ((tokens, width), BF16), ((64, 512), F32), ((64, 128), F32),
        ((64, 512), F32), ((64, ffn_width), F32), ((64, ffn_width), F32), ((64, ffn_width), F32),
    ]
    return pl.pallas_call(
        backward_kernel,
        out_shape=[jax.ShapeDtypeStruct(*shape) for shape in shapes],
        in_specs=[ANY] * len(in_hbm) + [VMEM] * len(in_vmem),
        out_specs=[VMEM] * len(shapes),
        scratch_shapes=[
            pltpu.VMEM((4, tokens, width), BF16),
            pltpu.VMEM((4, tokens, width), BF16),
            pltpu.VMEM((4, 4, 2, 64, 512), BF16),
            pltpu.VMEM((4, 4, 2, 64, 640), BF16),
            pltpu.VMEM((4, tokens, width), BF16),
            pltpu.VMEM((4, 4, 4, 2, 128, 128), BF16),
            *ShardScatter.scratch(tokens, width),
            pltpu.VMEM((512, 640), BF16),
            pltpu.VMEM((512, 128), F32),
            pltpu.VMEM((4, 4, 2, 64, 512), BF16),
            pltpu.VMEM((4, 4, 2, 64, 128), BF16),
            *[pltpu.VMEM(a.shape, a.dtype) for a in in_hbm[9:]],
            *attend_back_scratch(),
            *GainScatter.scratch(),
            *scratch,
            pltpu.SemaphoreType.REGULAR,
            *sems(16 * CtxScatter.COPIES + 2 * CtxScatterLate.COPIES + 6 * CHUNKS + GainScatter.COPIES + 20),
        ],
        compiler_params=params(cid),
        name="backward",
    )(*in_hbm, *in_vmem)


FIRST_INPUT_ROWS = int([step for step in BACKWARD if step[0] == "I"][0][1])


def finish_kernel(gains, grad_in, out_in, g_query, g_kv, g_out, g_gate, g_up, g_down, *outs):
    first, second, grad_inputs, outputs, query, key, value, out, gate, up, down = outs
    start = (lax.axis_index("ctx") % 2) * 64 + lax.axis_index("wshard") * 16
    own = pltpu.roll(gains[...], 128 - start, 1)
    first[...] = own[0:1, :16]
    second[...] = own[1:2, :16]
    grad_inputs[...] = grad_in[...]
    outputs[...] = out_in[...]
    query[...] = g_query[...]
    key[...] = g_kv[:, :HD]
    value[...] = g_kv[:, HD:]
    out[...] = g_out[...]
    gate[...] = g_gate[...]
    up[...] = g_up[...]
    down[...] = g_down[...]


def finish(*arrays):
    shapes = [((1, 16), F32)] * 2 + [(a.shape, a.dtype) for a in arrays[1:4]] + [((64, HD), F32)] * 2
    shapes += [(a.shape, a.dtype) for a in arrays[5:]]
    return pl.pallas_call(
        finish_kernel,
        out_shape=[jax.ShapeDtypeStruct(*shape) for shape in shapes],
        in_specs=[VMEM] * len(arrays),
        out_specs=[VMEM] * len(shapes),
        compiler_params=pltpu.CompilerParams(vmem_limit_bytes=VMEM_LIMIT),
        name="finish",
    )(*arrays)


def rope_tables(positions):
    freqs = 10000.0 ** (-jnp.arange(HD // 2, dtype=F32) * 2.0 / HD)
    angles = positions[:, None] * freqs[None]
    cosine, sine = jnp.cos(angles), jnp.sin(angles)
    one, zero = jnp.ones_like(cosine), jnp.zeros_like(cosine)
    return jnp.stack(
        [
            jnp.concatenate([cosine] * 4, -1),
            jnp.concatenate([sine] * 4, -1),
            jnp.concatenate([cosine, cosine, one, one], -1),
            jnp.concatenate([sine, sine, zero, zero], -1),
        ]
    )


def per_device(
    inputs, cotangent, norm_attn, w_query, w_key, w_value, w_out, norm_mlp, w_gate, w_up, w_down
):
    width = inputs.shape[-1]
    half_len = inputs.shape[2]
    tokens = 2 * half_len
    ctx_count = lax.axis_size("ctx")
    ctx_index = lax.axis_index("ctx")
    length = tokens * ctx_count
    x = inputs.reshape(tokens, width)
    cot = cotangent.reshape(tokens, width)
    rows_local = jnp.arange(tokens)
    positions = jnp.where(
        rows_local < half_len,
        ctx_index * half_len + rows_local,
        length - (ctx_index + 1) * half_len + (rows_local - half_len),
    ).astype(F32)
    tables = rope_tables(positions)

    (
        normed_all, w_qkv, w_out_t, q, kv_all, attn, lse, hidden, branch_all, grad_hidden, gain2_part, result_part,
        g_gate, g_up, g_down_x, g_down_z,
    ) = forward(
        0, x, cot, norm_attn, norm_mlp, tables, [w_query, w_key, w_value], [w_out.T, w_gate, w_up, w_down.T]
    )
    grad_inputs, gains, outputs, g_query, g_kv, g_out, g_gate, g_up, g_down = backward(
        1,
        [branch_all, result_part, w_out_t, w_qkv, normed_all, g_gate, g_up, g_down_x, g_down_z]
        + [q, kv_all, attn, hidden, grad_hidden, x],
        [gain2_part, lse, tables, norm_attn],
    )
    gain1, gain2, grad_inputs, outputs, g_query, g_key, g_value, g_out, g_gate, g_up, g_down = finish(
        gains, grad_inputs, outputs, g_query, g_kv, g_out, g_gate, g_up, g_down
    )
    return (
        outputs.reshape(inputs.shape),
        grad_inputs.reshape(inputs.shape),
        gain1.reshape(16),
        g_query,
        g_key,
        g_value,
        g_out.T,
        gain2.reshape(16),
        g_gate,
        g_up,
        g_down.T,
    )


def solution(mesh):
    return jax.shard_map(
        per_device,
        mesh=mesh,
        in_specs=(
            P("wshard", None, "ctx", None),
            P("wshard", None, "ctx", None),
            P(),
            P("ctx", "wshard"),
            P("ctx", "wshard"),
            P("ctx", "wshard"),
            P("wshard", "ctx"),
            P(),
            P("ctx", "wshard"),
            P("ctx", "wshard"),
            P("wshard", "ctx"),
        ),
        out_specs=(
            P("wshard", None, "ctx", None),
            P("wshard", None, "ctx", None),
            P(("ctx", "wshard")),
            P("ctx", "wshard"),
            P("ctx", "wshard"),
            P("ctx", "wshard"),
            P("wshard", "ctx"),
            P(("ctx", "wshard")),
            P("ctx", "wshard"),
            P("ctx", "wshard"),
            P("wshard", "ctx"),
        ),
        check_vma=False,
    )
```

```python
from functools import partial

import jax
import jax.numpy as jnp
from jax import lax
from jax.experimental import pallas as pl
from jax.experimental.pallas import tpu as pltpu
from jax.sharding import PartitionSpec as P

MESH = pl.DeviceIdType.MESH
HD = 64
EPS = 1e-05
NEG = -1e30
F32 = jnp.float32
BF16 = jnp.bfloat16
VMEM_LIMIT = 63 * 2**20
ANY = pl.BlockSpec(memory_space=pl.ANY)
VMEM = pl.BlockSpec(memory_space=pltpu.VMEM)


class Place:
    def __init__(self):
        ctx, shard = lax.axis_index("ctx"), lax.axis_index("wshard")
        self.x, self.z, self.y = ctx // 8, (ctx // 2) % 4, ctx % 2
        self.yl, self.co = shard // 2, shard % 2

    def at(self, x=None, z=None, y=None, yl=None, co=None):
        x, z, y = (self.x if x is None else x), (self.z if z is None else z), (self.y if y is None else y)
        yl, co = (self.yl if yl is None else yl), (self.co if co is None else co)
        return (x * 8 + z * 2 + y, yl * 2 + co)

    def step(self, axis, by):
        return self.at(**{axis: (getattr(self, axis) + by) % 4})

    def pair(self, axis):
        return self.at(**{axis: 1 - getattr(self, axis)})

    def ctx_peers(self):
        return [self.step("x", 1), self.step("x", 3), self.step("z", 1), self.step("z", 3), self.pair("y")]

    def shard_peers(self):
        return [self.pair("co"), self.pair("yl")]

    def far_peers(self):
        return [self.step("x", 2), self.step("z", 2)]


def greet(peers, meanwhile=None):
    barrier = pltpu.get_barrier_semaphore()
    for device in peers:
        pl.semaphore_signal(barrier, inc=1, device_id=device, device_id_type=MESH)
    if meanwhile is not None:
        meanwhile()
    pl.semaphore_wait(barrier, len(peers))


class Copies:
    def __init__(self, send, recv):
        self.send, self.recv, self.used = send, recv, 0

    def start(self, src, dst, device):
        k = self.used
        self.used += 1
        copy = pltpu.make_async_remote_copy(
            src_ref=src, dst_ref=dst, send_sem=self.send.at[k], recv_sem=self.recv.at[k],
            device_id=device, device_id_type=MESH,
        )
        copy.start()
        return copy

    def local(self, src, dst):
        k = self.used
        self.used += 1
        copy = pltpu.make_async_copy(src, dst, self.send.at[k])
        copy.start()
        return copy


def wait_all(copies):
    for copy in copies:
        copy.wait()


class CtxGather:
    COPIES = 10
    STAGES = 6

    def __init__(self, place, copies, shard, full, lo, n, big):
        self.p, self.c, self.shard, self.full = place, copies, shard, full
        self.lo, self.n, self.big, self.small = lo, n, big, ("z" if big == "x" else "x")
        self.live = []

    def block(self, o, i, y):
        x, z = (o, i) if self.big == "x" else (i, o)
        return self.full.at[x, z, y, pl.ds(self.lo, self.n)]

    def send(self, part, axis, by):
        dev = self.p.pair("y") if axis == "y" else self.p.step(axis, by)
        self.live.append(self.c.start(part, part, dev))

    def stage(self, s):
        p = self.p
        o, i, y = getattr(p, self.big), getattr(p, self.small), p.y
        wait_all(self.live)
        self.live = []
        every, both = pl.ds(0, 4), pl.ds(0, 2)
        if s == 0 and self.shard is None:
            self.send(self.block(o, i, y), "y", 0)
        elif s == 0:
            own = self.shard.at[pl.ds(self.lo, self.n)]
            self.live.append(self.c.start(own, self.block(o, i, y), p.pair("y")))
            self.live.append(self.c.local(own, self.block(o, i, y)))
        elif s == 1:
            self.send(self.block(o, i, both), self.small, 1)
            self.send(self.block(o, i, both), self.small, 3)
        elif s == 2:
            self.send(self.block(o, (i + 3) % 4, 0), self.small, 1)
            self.send(self.block(o, (i + 1) % 4, 1), self.small, 3)
        elif s == 3:
            self.send(self.block(o, every, both), self.big, 1)
            self.send(self.block(o, every, both), self.big, 3)
        elif s == 4:
            self.send(self.block((o + 3) % 4, pl.ds(0, 2), both), self.big, 1)
            self.send(self.block((o + 1) % 4, pl.ds(2, 2), both), self.big, 3)


class CtxGatherLate(CtxGather):
    def block(self, o, i, y, lo=None, n=None):
        x, z = (o, i) if self.big == "x" else (i, o)
        return self.full.at[x, z, y, pl.ds(self.lo if lo is None else lo, self.n if n is None else n)]

    def stage(self, s):
        p = self.p
        o, i, y = getattr(p, self.big), getattr(p, self.small), p.y
        wait_all(self.live)
        self.live = []
        every, half = pl.ds(0, 4), self.n // 2
        if s == 0:
            own = self.shard.at[pl.ds(self.lo, self.n)]
            for by in (1, 3):
                self.live.append(self.c.start(own, self.block(o, i, y), p.step(self.big, by)))
            self.live.append(self.c.local(own, self.block(o, i, y)))
        elif s == 1:
            self.send(self.block((o + 3) % 4, i, y, self.lo, half), self.big, 1)
            self.send(self.block((o + 1) % 4, i, y, self.lo + half, half), self.big, 3)
        elif s == 2:
            self.send(self.block(every, i, y), self.small, 1)
            self.send(self.block(every, i, y), self.small, 3)
        elif s == 3:
            self.send(self.block(pl.ds(0, 2), (i + 3) % 4, y), self.small, 1)
            self.send(self.block(pl.ds(2, 2), (i + 1) % 4, y), self.small, 3)
        elif s == 4:
            self.send(self.block(every, every, y), "y", 0)


class CtxScatter:
    COPIES = 17
    STAGES = 7

    @staticmethod
    def scratch(n, width, staged=False):
        shapes = [(2, 2, 2), (4, 2), (4, 2), (2,), (2,), (2,), ()]
        if staged:
            shapes += [(2, 2), (2, 2)]
        return [pltpu.VMEM(shape + (n, width), BF16) for shape in shapes]

    def __init__(self, place, copies, src, out, bufs, lo, n, big, stop=False, resumed=None):
        self.p, self.c, self.src, self.out = place, copies, src, out
        self.far, self.pos, self.neg, self.far2, self.pos2, self.neg2, self.last = bufs[:7]
        self.staged = bufs[7:]
        self.lo, self.n, self.big, self.small = lo, n, big, ("z" if big == "x" else "x")
        self.first, self.live = [], []
        self.stop, self.resumed = stop, resumed
        if resumed is not None:
            self.live = [resumed]

    def part(self, o, i):
        x, z = (o, i) if self.big == "x" else (i, o)
        return self.src.at[x, z, pl.ds(0, 2), pl.ds(self.lo, self.n)]

    def load(self, o, i, y, which):
        if self.staged:
            return self.staged[which][i % 2, y].astype(F32)
        x, z = (o, i) if self.big == "x" else (i, o)
        return self.src[x, z, y, pl.ds(self.lo, self.n), :].astype(F32)

    def send(self, src, dst, axis, by):
        dev = self.p.pair("y") if axis == "y" else self.p.step(axis, by)
        copy = self.c.start(src, dst, dev)
        self.live.append(copy)
        return copy

    def stage(self, s):
        p, big, small = self.p, self.big, self.small
        o, i, y = getattr(p, big), getattr(p, small), p.y
        up, down, across = (o + 1) % 4, (o + 3) % 4, (o + 2) % 4
        iup, idown, iacross = (i + 1) % 4, (i + 3) % 4, (i + 2) % 4
        low, high = pl.ds(0, 2), pl.ds(2, 2)
        if s == 2:
            wait_all(self.first)
        elif s > 2:
            wait_all(self.live)
            self.live = []
        if s == 0:
            for src, dst, by in (
                (self.part(across, low), self.far.at[0], 1), (self.part(across, high), self.far.at[1], 3)
            ):
                self.first.append(self.c.start(src, dst, p.step(big, by)))
            if self.staged:
                self.first.append(self.c.local(self.part(up, low), self.staged[0]))
                self.first.append(self.c.local(self.part(down, high), self.staged[1]))
        elif s == 1:
            self.send(self.part(up, high), self.pos.at[high], big, 1)
            self.send(self.part(down, low), self.neg.at[low], big, 3)
        elif s == 2:

            def fold(k, _):
                b, q = k // 2, k % 2
                self.far[0, b, q] = (self.far[0, b, q].astype(F32) + self.load(up, b, q, 0)).astype(BF16)
                self.far[1, b, q] = (self.far[1, b, q].astype(F32) + self.load(down, b + 2, q, 1)).astype(BF16)
                return 0

            lax.fori_loop(0, 4, fold, 0)
            self.send(self.far.at[0], self.pos.at[low], big, 1)
            self.send(self.far.at[1], self.neg.at[high], big, 3)
            if self.staged:
                self.live.append(self.c.local(self.part(o, low), self.staged[0]))
                self.live.append(self.c.local(self.part(o, high), self.staged[1]))
        elif s == 3:

            def total(k, _):
                b, q = k // 2, k % 2
                for which in range(2):
                    at = b + 2 * which
                    here = self.load(o, at, q, which) + self.pos[at, q].astype(F32) + self.neg[at, q].astype(F32)
                    self.pos[at, q] = here.astype(BF16)
                return 0

            if self.resumed is None:
                lax.fori_loop(0, 4, total, 0)
            if self.stop:
                self.live = [self.c.local(self.pos, self.out)]
                return
            self.first = [
                self.c.start(self.pos.at[iacross, 0], self.far2.at[0], p.step(small, 1)),
                self.c.start(self.pos.at[iacross, 1], self.far2.at[1], p.step(small, 3)),
            ]
            self.send(self.pos.at[iup, 1], self.pos2.at[1], small, 1)
            self.send(self.pos.at[idown, 0], self.neg2.at[0], small, 3)
        elif s == 4:
            wait_all(self.first)
            self.far2[0] = (self.far2[0].astype(F32) + self.pos[iup, 0].astype(F32)).astype(BF16)
            self.far2[1] = (self.far2[1].astype(F32) + self.pos[idown, 1].astype(F32)).astype(BF16)
            self.send(self.far2.at[0], self.pos2.at[0], small, 1)
            self.send(self.far2.at[1], self.neg2.at[1], small, 3)
        elif s == 5:
            for q in range(2):
                here = self.pos[i, q].astype(F32) + self.pos2[q].astype(F32) + self.neg2[q].astype(F32)
                self.pos2[q] = here.astype(BF16)
            self.send(self.pos2.at[1 - y], self.last, "y", 0)
        elif s == 6:
            total = self.pos2[y].astype(F32) + self.last[...].astype(F32)
            self.out[pl.ds(self.lo, self.n), :] = total.astype(self.out.dtype)


class CtxScatterLate:
    COPIES = 19
    STAGES = 6

    @staticmethod
    def scratch(n, width):
        shapes = [(4, 4, n), (4, 4, n), (2, 2, n), (4, n), (4, n), (2, n // 2), (2, n // 2), (2, n // 2)]
        return [pltpu.VMEM(shape + (width,), BF16) for shape in shapes]

    def __init__(self, place, copies, src, out, bufs, lo, n, big):
        self.p, self.c, self.src, self.out = place, copies, src, out
        self.all, self.staged, self.far, self.pos, self.neg, self.far2, self.pos2, self.neg2 = bufs
        self.lo, self.n, self.big, self.small = lo, n, big, ("z" if big == "x" else "x")
        self.first, self.live, self.loads = [], [], []

    def part(self, o, i):
        x, z = (o, i) if self.big == "x" else (i, o)
        return self.all.at[x, z]

    def load(self, o, i):
        x, z = (o, i) if self.big == "x" else (i, o)
        return self.all[x, z].astype(F32)

    def start(self, src, dst, axis, by):
        return self.c.start(src, dst, self.p.pair("y") if axis == "y" else self.p.step(axis, by))

    def stage_own(self, o):
        every, rows = pl.ds(0, 4), pl.ds(self.lo, self.n)
        x, z = (o, every) if self.big == "x" else (every, o)
        self.loads.append(self.c.local(self.src.at[x, z, self.p.y, rows], self.staged.at[o]))

    def stage(self, s):
        p, big, small, n = self.p, self.big, self.small, self.n
        o, i = getattr(p, big), getattr(p, small)
        up, down, across = (o + 1) % 4, (o + 3) % 4, (o + 2) % 4
        iup, idown, iacross = (i + 1) % 4, (i + 3) % 4, (i + 2) % 4
        low, high, every = pl.ds(0, 2), pl.ds(2, 2), pl.ds(0, 4)
        rows = [pl.ds(0, n // 2), pl.ds(n // 2, n // 2)]
        if s in (2, 4):
            wait_all(self.first)
        else:
            wait_all(self.live)
            self.live = []
        if s == 0:
            theirs = self.src.at[every, every, 1 - p.y, pl.ds(self.lo, n)]
            self.live = [self.start(theirs, self.all, "y", 0)]
            for slab in range(4):
                self.stage_own(slab)
        elif s == 1:
            for slab in range(4):
                self.loads[slab].wait()

                def add(k, _):
                    x, z = (slab, k) if big == "x" else (k, slab)
                    here = self.all[x, z].astype(F32) + self.staged[slab, k].astype(F32)
                    self.all[x, z] = here.astype(BF16)
                    return 0

                lax.fori_loop(0, 4, add, 0)
            self.first = [
                self.start(self.part(across, low), self.far.at[0], big, 1),
                self.start(self.part(across, high), self.far.at[1], big, 3),
            ]
            self.live = [
                self.start(self.part(up, high), self.pos.at[high], big, 1),
                self.start(self.part(down, low), self.neg.at[low], big, 3),
            ]
        elif s == 2:
            for b in range(2):
                self.far[0, b] = (self.far[0, b].astype(F32) + self.load(up, b)).astype(BF16)
                self.far[1, b] = (self.far[1, b].astype(F32) + self.load(down, b + 2)).astype(BF16)
            self.live += [
                self.start(self.far.at[0], self.pos.at[low], big, 1),
                self.start(self.far.at[1], self.neg.at[high], big, 3),
            ]
        elif s == 3:
            for b in range(4):
                here = self.load(o, b) + self.pos[b].astype(F32) + self.neg[b].astype(F32)
                self.pos[b] = here.astype(BF16)
            self.first = [
                self.start(self.pos.at[iacross, rows[0]], self.far2.at[0], small, 1),
                self.start(self.pos.at[iacross, rows[1]], self.far2.at[1], small, 3),
            ]
            self.live = [
                self.start(self.pos.at[iup, rows[1]], self.pos2.at[1], small, 1),
                self.start(self.pos.at[idown, rows[0]], self.neg2.at[0], small, 3),
            ]
        elif s == 4:
            self.far2[0] = (self.far2[0].astype(F32) + self.pos[iup, rows[0], :].astype(F32)).astype(BF16)
            self.far2[1] = (self.far2[1].astype(F32) + self.pos[idown, rows[1], :].astype(F32)).astype(BF16)
            self.live += [
                self.start(self.far2.at[0], self.pos2.at[0], small, 1),
                self.start(self.far2.at[1], self.neg2.at[1], small, 3),
            ]
        elif s == 5:
            for h in range(2):
                here = self.pos[i, rows[h], :].astype(F32) + self.pos2[h].astype(F32) + self.neg2[h].astype(F32)
                self.out[pl.ds(self.lo + h * (n // 2), n // 2), :] = here


class ShardGather:
    def __init__(self, place, copies, full, chunks):
        self.p, self.c, self.full, self.chunks = place, copies, full, chunks
        self.rows = full.shape[1] // chunks
        self.me, self.over = place.yl * 2 + place.co, (1 - place.yl) * 2 + place.co
        self.far, self.near = [], []

    COPIES = 3

    def part(self, who, k):
        return self.full.at[who, pl.ds(k * self.rows, self.rows)]

    def send(self, k, src=None):
        src = self.part(self.me, k) if src is None else src
        self.far.append(self.c.start(src, self.part(self.me, k), self.p.pair("yl")))
        self.near.append(self.c.start(src, self.part(self.me, k), self.p.pair("co")))

    def forward(self, k):
        self.far[k].wait()
        self.near.append(self.c.start(self.part(self.over, k), self.part(self.over, k), self.p.pair("co")))

    def finish(self):
        wait_all(self.near)


class ShardScatter:
    COPIES = 3

    @staticmethod
    def scratch(rows, width):
        return [pltpu.VMEM((rows, width), BF16)] * 3

    def __init__(self, place, copies, part, bufs, chunks):
        self.p, self.c, self.part, self.chunks = place, copies, part, chunks
        self.relay, self.near, self.over = bufs
        self.rows = part.shape[1] // chunks
        self.first, self.second, self.third = [], [], []

    def at(self, k):
        return pl.ds(k * self.rows, self.rows)

    def begin(self):
        self.begin_far()
        self.begin_near()

    def begin_far(self):
        p = self.p
        for k in range(self.chunks):
            src = self.part.at[(1 - p.yl) * 2 + 1 - p.co, self.at(k)]
            self.first.append(self.c.start(src, self.relay.at[self.at(k)], p.pair("co")))

    def begin_near(self):
        p = self.p
        for k in range(self.chunks):
            src = self.part.at[p.yl * 2 + 1 - p.co, self.at(k)]
            self.second.append(self.c.start(src, self.near.at[self.at(k)], p.pair("co")))

    def relay_on(self, k):
        p = self.p
        self.first[k].wait()
        here = self.part[(1 - p.yl) * 2 + p.co, self.at(k), :].astype(F32)
        self.relay[self.at(k), :] = (self.relay[self.at(k), :].astype(F32) + here).astype(BF16)
        self.third.append(self.c.start(self.relay.at[self.at(k)], self.over.at[self.at(k)], p.pair("yl")))

    def total(self, k):
        p = self.p
        self.second[k].wait()
        self.third[k].wait()
        here = self.part[p.yl * 2 + p.co, self.at(k), :].astype(F32)
        return here + self.near[self.at(k), :].astype(F32) + self.over[self.at(k), :].astype(F32)


class ShardScatterColumns(ShardScatter):
    def __init__(self, place, copies, part, bufs, chunks):
        super().__init__(place, copies, part, bufs, chunks)
        self.columns = part.shape[2] // chunks

    def begin(self, k):
        p, cols = self.p, pl.ds(k * self.columns, self.columns)
        far, near = (1 - p.yl) * 2 + 1 - p.co, p.yl * 2 + 1 - p.co
        self.first.append(self.c.start(self.part.at[far, :, cols], self.relay.at[:, cols], p.pair("co")))
        self.second.append(self.c.start(self.part.at[near, :, cols], self.near.at[:, cols], p.pair("co")))

    def relay_on(self, k):
        p, cols = self.p, pl.ds(k * self.columns, self.columns)
        self.first[k].wait()
        here = self.part[(1 - p.yl) * 2 + p.co, :, cols].astype(F32)
        self.relay[:, cols] = (self.relay[:, cols].astype(F32) + here).astype(BF16)
        self.third.append(self.c.start(self.relay.at[:, cols], self.over.at[:, cols], p.pair("yl")))

    def total(self, k):
        if k == 0:
            wait_all(self.second + self.third)
        here = self.part[self.p.yl * 2 + self.p.co, self.at(k), :].astype(F32)
        return here + self.near[self.at(k), :].astype(F32) + self.over[self.at(k), :].astype(F32)


class GainScatter:
    COPIES = 9
    STAGES = 6

    @staticmethod
    def scratch():
        return [
            pltpu.VMEM((8, 2048), F32),
            pltpu.VMEM((3, 8, 512), F32),
            pltpu.VMEM((8, 512), F32),
            pltpu.VMEM((3, 8, 128), F32),
            pltpu.VMEM((3, 8, 128), F32),
            pltpu.VMEM((3, 8, 128), F32),
        ]

    def __init__(self, place, copies, out, bufs):
        self.p, self.c, self.out = place, copies, out
        self.vec, self.xs, self.mid, self.zs, self.own, self.rest = bufs
        self.live = []

    def stage(self, s):
        p = self.p
        wait_all(self.live)
        self.live = []
        if s == 0:
            for by in (1, 2, 3):
                cols = pl.ds(pl.multiple_of(((p.x + by) % 4) * 512, 512), 512)
                self.live.append(self.c.start(self.vec.at[:, cols], self.xs.at[by - 1], p.step("x", by)))
        elif s == 1:
            cols = pl.ds(pl.multiple_of(p.x * 512, 512), 512)
            self.mid[...] = self.vec[:, cols] + self.xs[0] + self.xs[1] + self.xs[2]
            for by in (1, 2, 3):
                cols = pl.ds(pl.multiple_of(((p.z + by) % 4) * 128, 128), 128)
                self.live.append(self.c.start(self.mid.at[:, cols], self.zs.at[by - 1], p.step("z", by)))
        elif s == 2:
            cols = pl.ds(pl.multiple_of(p.z * 128, 128), 128)
            self.own[0] = self.mid[:, cols] + self.zs[0] + self.zs[1] + self.zs[2]
            self.live.append(self.c.start(self.own.at[0], self.rest.at[0], p.pair("y")))
        elif s == 3:
            self.own[1] = self.own[0] + self.rest[0]
            self.live.append(self.c.start(self.own.at[1], self.rest.at[1], p.pair("co")))
        elif s == 4:
            self.own[2] = self.own[1] + self.rest[1]
            self.live.append(self.c.start(self.own.at[2], self.rest.at[2], p.pair("yl")))
        elif s == 5:
            self.out[...] = self.own[2] + self.rest[2]


def sems(n):
    return [pltpu.SemaphoreType.DMA((n,)), pltpu.SemaphoreType.DMA((n,))]


def params(cid):
    return pltpu.CompilerParams(collective_id=cid, has_side_effects=True, vmem_limit_bytes=VMEM_LIMIT)


def halves(rows):
    return ((0, rows // 2, "x"), (rows // 2, rows // 2, "z"))


CHUNKS = 4
LATE = 1280


def norm_back_rows(grad, resid, gain):
    factor = lax.rsqrt(jnp.mean(resid * resid, -1, keepdims=True) + EPS)
    weighted = grad * gain
    per_gain = grad * resid * factor
    back = factor * weighted - resid * (factor * factor * factor) * jnp.mean(weighted * resid, -1, keepdims=True)
    return back, per_gain


def eight(rows):
    return jnp.sum(rows.reshape(rows.shape[0] // 8, 8, rows.shape[1]), 0)


KEYS = 256
KB = 4


def lane_iota(rows):
    return lax.broadcasted_iota(jnp.int32, (rows, 128), 1)


def rotate_tile(u, cosine, sine):
    low = lane_iota(u.shape[0]) % HD < HD // 2
    turned = jnp.where(low, -pltpu.roll(u, 128 - HD // 2, 1), pltpu.roll(u, HD // 2, 1))
    return u * cosine + turned * sine


def unrotate_tile(w, cosine, sine):
    low = lane_iota(w.shape[0]) % HD < HD // 2
    s = w * sine
    return w * cosine + jnp.where(low, pltpu.roll(s, 128 - HD // 2, 1), -pltpu.roll(s, HD // 2, 1))


def project_rows(rows, w_qkv, tables):
    lin = jnp.dot(rows, w_qkv, preferred_element_type=F32)
    tiles = []
    for hp in range(4):
        tile = lin[:, hp * 128 : (hp + 1) * 128]
        tiles.append((rotate_tile(tile, tables[0], tables[1])).astype(BF16) * jnp.asarray(HD**-0.5, BF16))
    kv = rotate_tile(lin[:, 512:640], tables[2], tables[3]).astype(BF16)
    return tiles, kv


def head_rows(ref, start, keep_low):
    low = lane_iota(64) < HD
    keep = low if keep_low else ~low
    pieces = []
    for hp in range(4):
        tile = ref[pl.ds(start, 64), hp * 128 : (hp + 1) * 128].astype(F32)
        turned = pltpu.roll(tile, HD, 1)
        even, odd = (tile, turned) if keep_low else (turned, tile)
        pieces += [jnp.where(keep, even, 0.0), jnp.where(keep, odd, 0.0)]
    return pieces


def key_chunk(kv, seq, chunk, half):
    start = pl.multiple_of(seq * 128 + half * 64, 64)
    z = pl.ds((chunk % 2) * 2, 2)
    return kv[chunk // 2, z, :, pl.ds(start, 64), :].reshape(KEYS, 128)


def diagonal(block, here):
    key = lax.broadcasted_iota(jnp.int32, (KEYS, 512), 0)
    query = lax.broadcasted_iota(jnp.int32, (KEYS, 512), 1) % 64
    ahead = key // 64 - here
    return key % 64 - query <= (-ahead if block == 0 else ahead) * 64


def pick(u, own_chunk):
    late = u - 8
    block = jnp.where(u < 8, 1, jnp.where(late >= own_chunk, 1, 0))
    half = jnp.where(u < 8, 0, block)
    chunk = jnp.where(u < 8, u, late + half)
    return block, chunk, half


def nt(a, b):
    return lax.dot_general(a, b, (((1,), (1,)), ((), ())), preferred_element_type=F32)


def tn(a, b):
    return lax.dot_general(a, b, (((0,), (0,)), ((), ())), preferred_element_type=F32)


def attend_seq(seq, ctx, q, kv, attn, lse, scratch):
    qe, top, acc = scratch
    low = lane_iota(64) < HD
    ones_low = lane_iota(KEYS) < HD
    own_chunk, here = ctx // KB, ctx % KB

    def with_ones(keys):
        return jnp.where(ones_low, jnp.ones_like(keys), keys)

    for b in range(2):
        for h, piece in enumerate(head_rows(q, seq * 128 + b * 64, True)):
            qe[b, h * 64 : (h + 1) * 64, :] = piece.astype(BF16)
    for b in range(2):
        keys = key_chunk(kv, seq, own_chunk, b)
        scores = jnp.where(diagonal(b, here), nt(keys, qe[b]), NEG)
        m = jnp.max(scores, 0, keepdims=True)
        p = jnp.exp(scores - m).astype(BF16)
        top[b] = m
        acc[b] = tn(with_ones(keys), p)

    def step(u, _):
        b, chunk, half = pick(u, own_chunk)
        keys = key_chunk(kv, seq, chunk, half)
        scores = nt(keys, qe[b])
        before = top[b]
        m = jnp.maximum(before, jnp.max(scores, 0, keepdims=True))
        p = jnp.exp(scores - m).astype(BF16)
        top[b] = m
        acc[b] = acc[b] * jnp.exp(before - m) + tn(with_ones(keys), p)
        return 0

    for k in range(3):
        lax.fori_loop(5 * k, 5 * k + 5, step, 0, unroll=True)
        if k < 2:
            yield
    for b in range(2):
        here_acc = acc[b]
        total = here_acc[0:1, :]
        lse[pl.ds(seq * 2 + b, 1), :] = top[b] + jnp.log(total)
        out = (here_acc * (1.0 / total)).T
        for hp in range(4):
            even, odd = out[hp * 128 : hp * 128 + 64, :], out[hp * 128 + 64 : hp * 128 + 128, :]
            tile = jnp.where(low, pltpu.roll(even, HD, 1), odd)
            attn[pl.ds(seq * 128 + b * 64, 64), hp * 128 : (hp + 1) * 128] = tile.astype(BF16)


def attend_scratch():
    return [pltpu.VMEM((2, 512, 128), BF16), pltpu.VMEM((2, 1, 512), F32), pltpu.VMEM((2, 128, 512), F32)]


def attend_back_seq(seq, ctx, q, kv, grad, attn, lse, tables, grad_lin, grad_kv, scratch):
    qd, delta, dq, dkv = scratch
    low = lane_iota(64) < HD
    own_chunk, here = ctx // KB, ctx % KB
    for b in range(2):
        start = seq * 128 + b * 64
        q_rows, g_rows, o_rows = (
            head_rows(q, start, True), head_rows(grad, start, False), head_rows(attn, start, False)
        )
        for h in range(8):
            qd[b, h * 64 : (h + 1) * 64, :] = q_rows[h].astype(BF16)
            qd[b, 512 + h * 64 : 512 + (h + 1) * 64, :] = g_rows[h].astype(BF16)
        products = jnp.concatenate([g * o for g, o in zip(g_rows, o_rows)], 0)
        delta[b] = jnp.sum(products.T, 0, keepdims=True)

    def grads(b, keys, allowed):
        both = nt(keys, qd[b])
        p = jnp.exp(both[:, :512] - lse[pl.ds(seq * 2 + b, 1), :])
        if allowed is not None:
            p = jnp.where(allowed, p, 0.0)
        ds = (p * (both[:, 512:] - delta[b])).astype(BF16)
        joined = jnp.concatenate([ds, p.astype(BF16)], 1)
        return tn(keys, ds), jnp.dot(joined, qd[b], preferred_element_type=F32)

    dkv[...] = jnp.zeros_like(dkv)

    def add_keys(chunk, half, value):
        start = pl.multiple_of(half * 64, 64)
        dkv[pl.ds(chunk * KB, KB), pl.ds(start, 64), :] += value.reshape(KB, 64, 128)

    for b in range(2):
        dq_part, dkv_part = grads(b, key_chunk(kv, seq, own_chunk, b), diagonal(b, here))
        dq[b] = dq_part
        add_keys(own_chunk, b, dkv_part)

    def step(u, _):
        b, chunk, half = pick(u, own_chunk)
        dq_part, dkv_part = grads(b, key_chunk(kv, seq, chunk, half), None)
        dq[b] += dq_part
        add_keys(chunk, half, dkv_part)
        return 0

    for k in range(3):
        lax.fori_loop(5 * k, 5 * k + 5, step, 0, unroll=True)
        if k < 2:
            yield
    for b in range(2):
        out = (dq[b] * HD**-0.5).T
        cosine, sine = tables[0, b * 64 : (b + 1) * 64, :], tables[1, b * 64 : (b + 1) * 64, :]
        for hp in range(4):
            even, odd = out[hp * 128 : hp * 128 + 64, :], out[hp * 128 + 64 : hp * 128 + 128, :]
            tile = jnp.where(low, even, pltpu.roll(odd, HD, 1))
            tile = unrotate_tile(tile, cosine, sine)
            grad_lin[pl.ds(seq * 128 + b * 64, 64), hp * 128 : (hp + 1) * 128] = tile.astype(BF16)
    grad_kv[...] = dkv[...].reshape(4, 4, 2, 128, 128).astype(BF16)


def attend_back_scratch():
    return [
        pltpu.VMEM((2, 1024, 128), BF16),
        pltpu.VMEM((2, 1, 512), F32),
        pltpu.VMEM((2, 128, 512), F32),
        pltpu.VMEM((32, 128, 128), F32),
    ]


def ctx_gathers(place, copies, src, full, kind=CtxGather):
    return [kind(place, copies, src, full, lo, rows, big) for lo, rows, big in halves(src.shape[0])]


FORWARD = [
    "w0", "o0", "h0", "u0", "d0", "w1", "d1", "g0", "o1", "N1", "w2", "d2", "w3", "o2", "u1", "NF", "w4", "d3",
    "CB", "o3", "NW", "w5", "J1", "J2", "k20", "k10", "J0", "k00", "J3", "k30", "d4", "g1", "k01", "k11", "k21",
    "k31", "o4", "k02", "h1", "k32", "k22", "k12", "u2", "k03", "g2", "k23", "k13", "k33", "h2", "k04", "k14",
    "k24", "h3", "g3", "k05", "k15", "CF", "A00", "A01", "A02", "h4", "k25", "A10", "o5", "OP0", "A11", "A12",
    "k34", "CW", "u3", "A20", "A21", "RF", "A22", "g4", "OP2", "OP1", "k35", "RR", "A30", "A31", "RN", "A32", "OP3",
    "NT", "u4", "d5", "h5", "DA", "SF", "u5", "SW", "g5", "FU", "T0", "T1", "XR0", "GD", "e0", "XR1", "T2", "T3",
    "e1", "XR2", "XR3", "GU", "e2", "XT", "GG", "RP", "XF", "e3", "XW",
]

BACKWARD = [
    "u0", "g0", "DO", "DP", "GO", "g1", "o0", "A00", "A01", "o1", "A02", "k00", "A10", "A11", "o2", "g2", "d3",
    "k01", "A12", "k02", "RESB", "A20", "A21", "k10", "k11", "A22", "k20", "A30", "k12", "g3", "k21", "A31", "d4",
    "A32", "k30", "QG", "k31", "k22", "k03", "k13", "RESR", "k32", "k04", "g4", "k33", "k23", "k14", "q0", "k34",
    "k24", "q1", "k15", "u1", "q2", "k25", "RES", "k16", "I1", "k26", "k35", "k05", "I2", "d5", "o3", "k06", "k36",
    "I3", "I0", "VG", "v0", "v1", "g5", "q3", "u2", "v2", "TOT", "n0", "q4", "o4", "v3", "n1", "u3", "n2", "v4",
    "q5", "o5", "u4", "n3", "v5", "q6", "n4", "v6", "u5", "o6", "g6", "d6", "n5",
]


def run_steps(steps, engines, actions):
    for step in steps:
        if step in actions:
            actions[step]()
        else:
            for e in engines[step[:-1]]:
                e.stage(int(step[-1]))


def gain_row(ref):
    gain = ref[...].astype(F32)
    return jnp.concatenate([gain[k : k + 1, :] for k in range(16)], 1)


def over_hidden_units(tile):
    def one(j, _):
        tile(pl.ds(pl.multiple_of(j * 512, 512), 512), 512)
        return 0

    lax.fori_loop(0, 2, one, 0)
    tile(pl.ds(1024, 384), 384)


def over_width(step):
    def one(j, _):
        step(j, pl.ds(pl.multiple_of(j * 512, 512), 512))
        return 0

    lax.fori_loop(0, 4, one, 0)


def forward_kernel(
    x, cot, gain1, gain2, tables, wq, wk, wv, w_out_shard, w_gate_shard, w_up_shard, w_down_shard,
    normed1_out, w_qkv_out, w_out_out, q_out, kv_out, attn_out, lse, hidden_out, branch_out, grad_hidden_out, grad_gain,
    result_out, g_gate_out, g_up_out, g_down_x, g_down_z,
    normed1_all, w_qkv_shard, w_qkv, w_out, kv_all, part, relay, near, over, qe, top, acc,
    w_gate, w_up, w_down, g_down, cot_all, normed2_all, gate_pre, up_pre, active, grad_gate, grad_up, branch,
    q, attn, hidden, grad_hidden, *rest,
):
    bufs, (send, recv) = rest[:14], rest[14:]
    place = Place()
    me = place.yl * 2 + place.co

    def prepare():
        rows = x[...].astype(F32)
        factor = lax.rsqrt(jnp.mean(rows * rows, -1, keepdims=True) + EPS)
        normed1_all[me] = (rows * factor * gain_row(gain1)).astype(BF16)
        w_qkv_shard[:, :512] = wq[...]
        w_qkv_shard[:, 512:640] = jnp.concatenate([wk[...], wv[...]], 1)

    greet(place.ctx_peers() + place.shard_peers(), prepare)
    copies = Copies(send, recv)
    ctx = lax.axis_index("ctx")
    order = [2 * (1 - place.yl) + 1 - place.co, 2 * (1 - place.yl) + place.co]
    order += [2 * place.yl + 1 - place.co, 2 * place.yl + place.co]
    starts = [pl.multiple_of(seq * 128, 128) for seq in order]
    engines = {
        "w": ctx_gathers(place, copies, w_qkv_shard, w_qkv),
        "o": ctx_gathers(place, copies, w_out_shard, w_out),
        "g": ctx_gathers(place, copies, w_gate_shard, w_gate),
        "u": ctx_gathers(place, copies, w_up_shard, w_up),
        "d": ctx_gathers(
            place, copies, w_down_shard.at[:, pl.ds(0, LATE)], w_down.at[:, :, :, :, pl.ds(0, LATE)], CtxGatherLate
        ),
        "h": ctx_gathers(
            place, copies, w_down_shard.at[:, pl.ds(LATE, 1408 - LATE)],
            w_down.at[:, :, :, :, pl.ds(LATE, 1408 - LATE)],
        ),
    }
    for k in range(4):
        engines[f"k{k}"] = [CtxGather(place, copies, None, kv_all, starts[k], 128, "xz"[k % 2])]
    normed = ShardGather(place, copies, normed1_all, 1)
    cots = ShardGather(place, copies, cot_all, 1)
    rows_out = ShardScatter(place, copies, part, (relay, near, over), CHUNKS)
    spread = ShardGather(place, copies, normed2_all, CHUNKS)
    thirds = [attend_seq(seq, ctx, q, kv_all, attn, lse, (qe, top, acc)) for seq in order]
    back = ShardScatterColumns(place, copies, part, (relay, near, over), CHUNKS)
    branches = ShardGather(place, copies, branch, CHUNKS)
    engines["e"] = [
        CtxScatter(place, copies, g_down, out, bufs[7 * h : 7 * h + 7], lo, rows, big, stop=True)
        for h, (out, (lo, rows, big)) in enumerate(zip((g_down_x, g_down_z), halves(64)))
    ]
    outgoing, normed_copy = [], []
    def normed_here():
        normed.finish()
        normed_copy.append(copies.local(normed1_all, normed1_out))

    def project_seq(k):
        at = pl.ds(starts[k], 128)
        tiles, kv = project_rows(normed1_all[order[k]], w_qkv[...].reshape(2048, 640), tables)
        for hp, tile in enumerate(tiles):
            q[at, hp * 128 : (hp + 1) * 128] = tile
        kv_all[place.x, place.z, place.y, at, :] = kv

    own_cot = []

    def send_cot():
        cots.send(0, cot)
        own_cot.append(copies.local(cot, cot_all.at[cots.me]))

    def cot_here():
        cots.finish()
        wait_all(own_cot)

    def project_out(k):
        part[order[k]] = nt(attn[pl.ds(starts[k], 128), :], w_out[...].reshape(2048, 512)).astype(BF16)

    def relay_rows():
        for c in range(CHUNKS):
            rows_out.relay_on(c)

    def second_norm():
        outgoing.extend(
            copies.local(*pair)
            for pair in ((w_qkv, w_qkv_out), (w_out, w_out_out), (kv_all, kv_out), (q, q_out), (attn, attn_out))
        )
        gain = gain_row(gain2)
        for c in range(CHUNKS):
            at = rows_out.at(c)
            here = x[at, :].astype(F32) + rows_out.total(c)
            hidden[at, :] = here
            factor = lax.rsqrt(jnp.mean(here * here, -1, keepdims=True) + EPS)
            normed2_all[spread.me, at, :] = (here * factor * gain).astype(BF16)
            spread.send(c)
        outgoing.append(copies.local(hidden, hidden_out))

    def spread_on():
        for c in range(CHUNKS):
            spread.forward(c)

    def columns_of(w, cols, width):
        return w[:, :, :, :, cols].reshape(2048, width)

    def grad_active_tiles():
        def tile(cols, width):
            rows = cot_all[...].reshape(512, 2048)
            here = jnp.dot(rows, columns_of(w_down, cols, width), preferred_element_type=F32)
            grad_up[:, cols] = here.astype(BF16)

        over_hidden_units(tile)

    def hidden_units():
        def tile(cols, width):
            rows = normed2_all[...].reshape(512, 2048)
            here = pl.ds(0, width)
            gate_pre[:, here] = jnp.dot(rows, columns_of(w_gate, cols, width), preferred_element_type=F32)
            up_pre[:, here] = jnp.dot(rows, columns_of(w_up, cols, width), preferred_element_type=F32)

            def some(r, _):
                at = pl.ds(pl.multiple_of(r * 64, 64), 64)
                gate, up, grad = gate_pre[at, here], up_pre[at, here], grad_up[at, cols].astype(F32)
                sigmoid = 1.0 / (1.0 + jnp.exp(-gate))
                silu = gate * sigmoid
                active[at, cols] = (silu * up).astype(BF16)
                grad_gate[at, cols] = (grad * up * sigmoid * (1.0 + gate * (1.0 - sigmoid))).astype(BF16)
                grad_up[at, cols] = (grad * silu).astype(BF16)
                return 0

            lax.fori_loop(0, 8, some, 0)

        over_hidden_units(tile)

    def result_tiles():
        wait_all(normed_copy)
        result_part = normed1_all

        def step(j, cols):
            rows = nt(active[...], w_down[j].reshape(512, 1408))
            result_part[:, :, cols] = rows.astype(BF16).reshape(4, 128, 512)

        over_width(step)
        outgoing.append(copies.local(result_part, result_out))

    def grad_normed_tile(j):
        rows = nt(grad_gate[...], w_gate[j].reshape(512, 1408)) + nt(grad_up[...], w_up[j].reshape(512, 1408))
        part[:, :, j * 512 : (j + 1) * 512] = rows.astype(BF16).reshape(4, 128, 512)
        back.begin(j)

    def weight_grad(left, right, w):
        def step(j, cols):
            block = tn(left[:, :, cols].reshape(512, 512), right[...])
            w[j] = block.astype(BF16).reshape(4, 2, 64, 1408)

        over_width(step)

    def gate_grad():
        weight_grad(normed2_all, grad_gate, w_gate)
        outgoing.append(copies.local(w_gate, g_gate_out))

    def up_grad():
        weight_grad(normed2_all, grad_up, w_up)
        outgoing.append(copies.local(w_up, g_up_out))

    def second_norm_back():
        gain = gain_row(gain2)
        for c in range(CHUNKS):
            at = back.at(c)
            grad, per_gain = norm_back_rows(back.total(c), hidden[at, :], gain)
            here = cot_all[branches.me, at, :].astype(F32) + grad
            grad_hidden[at, :] = here
            branch[branches.me, at, :] = here.astype(BF16)
            branches.send(c)
            grad_gain[...] = eight(per_gain) if c == 0 else grad_gain[...] + eight(per_gain)
        outgoing.append(copies.local(grad_hidden, grad_hidden_out))

    def branch_on():
        for c in range(CHUNKS):
            branches.forward(c)

    def branch_here():
        branches.finish()
        outgoing.append(copies.local(branch, branch_out))

    actions = {
        "N1": lambda: normed.send(0), "NF": lambda: normed.forward(0), "NW": normed_here,
        "CB": send_cot, "CF": lambda: cots.forward(0), "CW": cot_here,
        "RF": rows_out.begin_far, "RR": relay_rows, "RN": rows_out.begin_near,
        "NT": second_norm, "SF": spread_on, "SW": spread.finish,
        "DA": grad_active_tiles, "FU": hidden_units, "RP": result_tiles,
        "GD": lambda: weight_grad(cot_all, active, g_down), "GG": gate_grad, "GU": up_grad, "XT": second_norm_back,
        "XF": branch_on, "XW": branch_here,
    }
    for k in range(4):
        actions[f"T{k}"] = partial(grad_normed_tile, k)
        actions[f"XR{k}"] = partial(back.relay_on, k)
        actions[f"J{k}"] = partial(project_seq, k)
        actions[f"OP{k}"] = partial(project_out, k)
        for third in range(3):
            actions[f"A{k}{third}"] = partial(next, thirds[k], None)
    run_steps(FORWARD, engines, actions)
    wait_all(outgoing + [copy for e in engines["e"] for copy in e.live])


def forward(cid, x, cot, gain1, gain2, tables, w_qkv, shards):
    tokens, width = x.shape
    every = (4, tokens, width)
    ffn_width = shards[1].shape[1]

    def full(n):
        return (4, 4, 2, 64, n)

    kv_all, totals = (4, 4, 2, 512, 128), (4, 2, 32, ffn_width)
    outs = [
        (ANY, every, BF16), (ANY, full(640), BF16), (ANY, full(512), BF16), (ANY, (512, 512), BF16),
        (ANY, kv_all, BF16), (ANY, (512, 512), BF16), (VMEM, (8, 512), F32), (ANY, (tokens, width), F32),
        (ANY, every, BF16), (ANY, (tokens, width), F32), (VMEM, (8, width), F32), (ANY, every, BF16),
        (ANY, full(ffn_width), BF16), (ANY, full(ffn_width), BF16), (ANY, totals, BF16), (ANY, totals, BF16),
    ]
    return pl.pallas_call(
        forward_kernel,
        out_shape=[jax.ShapeDtypeStruct(shape, dtype) for _, shape, dtype in outs],
        in_specs=[VMEM, ANY, VMEM, VMEM, VMEM, VMEM, VMEM, VMEM] + [ANY] * 4,
        out_specs=[space for space, _, _ in outs],
        scratch_shapes=[
            pltpu.VMEM(every, BF16),
            pltpu.VMEM((64, 640), BF16),
            pltpu.VMEM(full(640), BF16),
            pltpu.VMEM(full(512), BF16),
            pltpu.VMEM(kv_all, BF16),
            pltpu.VMEM(every, BF16),
            *ShardScatter.scratch(tokens, width),
            *attend_scratch(),
            *[pltpu.VMEM(full(ffn_width), BF16)] * 4,
            pltpu.VMEM(every, BF16),
            pltpu.VMEM(every, BF16),
            *[pltpu.VMEM((512, 512), F32)] * 2,
            *[pltpu.VMEM((512, ffn_width), BF16)] * 3,
            pltpu.VMEM(every, BF16),
            *[pltpu.VMEM((512, 512), BF16)] * 2,
            *[pltpu.VMEM((tokens, width), F32)] * 2,
            *CtxScatter.scratch(32, ffn_width),
            *CtxScatter.scratch(32, ffn_width),
            *sems(16 * CtxGather.COPIES + 2 * CtxScatter.COPIES + 12 * CHUNKS + 28),
        ],
        compiler_params=params(cid),
        name="forward",
    )(x, cot, gain1.reshape(16, 128), gain2.reshape(16, 128), tables, *w_qkv, *shards)


def backward_kernel(*refs):
    (
        branch_in, result_in, w_out_in, w_qkv_in, normed_in, g_gate, g_up, g_down_x, g_down_z,
        q_in, kv_in, attn_in, hidden_in, grad_hidden_in, x_in, grad_gain, lse, tables, gain1,
    ) = refs[:19]
    grad_inputs, gains, outputs, out_q, out_kv, out_o, out_gate, out_up, out_down = refs[19:28]
    normed, result_part, w_out, w_qkv, branch, dkv_send, relay, near, over = refs[28:37]
    grad_lin, grad_kv, g_query, g_kv, q, kv, attn, hidden, grad_hidden, x = refs[37:47]
    scratch, gain_bufs, bufs, (free, send, recv) = refs[47:51], refs[51:57], refs[57:-3], refs[-3:]
    place = Place()
    copies = Copies(send, recv)
    loads = [copies.local(a, b) for a, b in (
        (branch_in, branch), (w_out_in, w_out), (q_in, q), (kv_in, kv), (attn_in, attn)
    )]
    greet(place.ctx_peers() + place.shard_peers() + place.far_peers())
    ctx = lax.axis_index("ctx")
    me, co = 2 * place.yl + place.co, 2 * place.yl + 1 - place.co
    far, far_co = 2 * (1 - place.yl) + place.co, 2 * (1 - place.yl) + 1 - place.co
    order = [me, far_co, far, co]
    taken = 0

    def take(n):
        nonlocal taken
        taken += n
        return bufs[taken - n : taken]

    def rows_of(seq):
        return pl.ds(pl.multiple_of(seq * 128, 128), 128)

    engines = {}
    for name, src, out, count in (
        ("g", g_gate, out_gate, 9), ("o", w_out, out_o, 7), ("q", g_query, out_q, 7), ("v", g_kv, out_kv, 7),
    ):
        engines[name] = [
            CtxScatter(place, copies, src, out, take(count), lo, rows, big) for lo, rows, big in halves(64)
        ]
    for k in range(4):
        engines[f"k{k}"] = [
            CtxScatter(place, copies, dkv_send.at[k], grad_kv.at[rows_of(order[k])], take(7), 0, 128, "xz"[k % 2])
        ]
    engines["u"] = [
        CtxScatterLate(place, copies, g_up, out_up, take(8), lo, rows, big) for lo, rows, big in halves(64)
    ]
    engines["d"] = []
    for (lo, rows, big), totals in zip(halves(64), (g_down_x, g_down_z)):
        pos, far2, pos2, neg2, last = take(5)
        load = copies.local(totals, pos)
        engines["d"].append(
            CtxScatter(
                place, copies, None, out_down, (None, pos, None, far2, pos2, neg2, last), lo, rows, big, resumed=load
            )
        )
    gain_sum = GainScatter(place, copies, gains, gain_bufs)
    engines["n"] = [gain_sum]
    result = ShardScatter(place, copies, result_part, (relay, near, over), 1)
    last = ShardScatter(place, copies, branch, (relay, near, over), CHUNKS)
    thirds = [
        attend_back_seq(
            order[k], ctx, q, kv, grad_lin, attn, lse, tables, grad_lin, dkv_send.at[k], scratch
        )
        for k in range(4)
    ]

    def relay_rows(rows_scatter):
        for c in range(CHUNKS):
            rows_scatter.relay_on(c)

    def grad_rows(seq):
        w = w_out[...].reshape(2048, 512)
        grad_lin[rows_of(seq), :512] = jnp.dot(branch[seq], w, preferred_element_type=F32).astype(BF16)

    def grad_mixed_own():
        wait_all(loads)
        loads.extend(copies.local(a, b) for a, b in (
            (result_in, result_part), (w_qkv_in, w_qkv), (normed_in, normed), (hidden_in, hidden),
            (grad_hidden_in, grad_hidden), (x_in, x),
        ))
        grad_rows(me)

    def grad_mixed():
        for seq in order[1:]:
            grad_rows(seq)

    def begin_result():
        loads[5].wait()
        result.begin()

    def grad_of_out():
        rows = branch[...].reshape(512, 2048)
        for j in range(8):
            block = tn(rows[:, j * 256 : (j + 1) * 256], attn[...]).astype(BF16)
            w_out[j // 2, pl.ds((j % 2) * 2, 2)] = block.reshape(2, 2, 64, 512)

    def result_rows():
        loads[8].wait()
        outputs[...] = (hidden[...] + result.total(0)).astype(BF16)
        for device in place.shard_peers():
            pl.semaphore_signal(free, inc=1, device_id=device, device_id_type=MESH)

    def input_rows(k):
        if k == FIRST_INPUT_ROWS:
            loads[6].wait()
        at = rows_of(order[k])
        grad_lin[at, 512:640] = unrotate_tile(grad_kv[at, :], tables[2], tables[3]).astype(BF16)
        branch[order[k]] = nt(grad_lin[at, :], w_qkv[...].reshape(2048, 640)).astype(BF16)
        if k == 1:
            pl.semaphore_wait(free, 2)
            last.begin_far()
        elif k == 2:
            relay_rows(last)
        elif k == 3:
            last.begin_near()

    def weight_grad(w, start, width):
        def step(j, cols):
            block = tn(normed[:, :, cols].reshape(512, 512), grad_lin[:, start : start + width])
            w[j] = block.astype(BF16).reshape(4, 2, 64, width)

        over_width(step)

    def grad_of_query():
        loads[7].wait()
        weight_grad(g_query, 0, 512)

    def first_norm_back():
        wait_all(loads[9:])
        gain = gain_row(gain1)
        for c in range(CHUNKS):
            rows = last.at(c)
            back, per_gain = norm_back_rows(last.total(c), x[rows, :].astype(F32), gain)
            grad_inputs[rows, :] = (grad_hidden[rows, :] + back).astype(BF16)
            total = eight(per_gain) if c == 0 else total + eight(per_gain)
        row = lax.broadcasted_iota(jnp.int32, total.shape, 0)
        one, two = jnp.sum(total, 0, keepdims=True), jnp.sum(grad_gain[...], 0, keepdims=True)
        gain_sum.vec[...] = jnp.where(row == 0, one, jnp.where(row == 1, two, 0.0))

    actions = {
        "DO": grad_mixed_own, "DP": grad_mixed, "GO": grad_of_out, "RESB": begin_result,
        "RESR": lambda: result.relay_on(0), "RES": result_rows, "QG": grad_of_query,
        "VG": lambda: weight_grad(g_kv, 512, 128), "TOT": first_norm_back,
    }
    for k in range(4):
        actions[f"I{k}"] = partial(input_rows, k)
        for third in range(3):
            actions[f"A{k}{third}"] = partial(next, thirds[k], None)
    run_steps(BACKWARD, engines, actions)


def backward(cid, in_hbm, in_vmem):
    tokens, width = in_hbm[-1].shape
    ffn_width = in_hbm[5].shape[4]
    in_vmem = [a.reshape(16, 128) if a.ndim == 1 else a for a in in_vmem]
    scratch = []
    for _ in range(2):
        scratch += CtxScatter.scratch(32, ffn_width, True)
    for _ in range(4):
        scratch += CtxScatter.scratch(32, 512)
    for _ in range(2):
        scratch += CtxScatter.scratch(32, 128)
    for _ in range(4):
        scratch += CtxScatter.scratch(128, 128)
    for _ in range(2):
        scratch += CtxScatterLate.scratch(32, ffn_width)
    for _ in range(2):
        whole = CtxScatter.scratch(32, ffn_width)
        scratch += whole[1:2] + whole[3:]
    shapes = [
        ((tokens, width), BF16), ((8, 128), F32), ((tokens, width), BF16), ((64, 512), F32), ((64, 128), F32),
        ((64, 512), F32), ((64, ffn_width), F32), ((64, ffn_width), F32), ((64, ffn_width), F32),
    ]
    return pl.pallas_call(
        backward_kernel,
        out_shape=[jax.ShapeDtypeStruct(*shape) for shape in shapes],
        in_specs=[ANY] * len(in_hbm) + [VMEM] * len(in_vmem),
        out_specs=[VMEM] * len(shapes),
        scratch_shapes=[
            pltpu.VMEM((4, tokens, width), BF16),
            pltpu.VMEM((4, tokens, width), BF16),
            pltpu.VMEM((4, 4, 2, 64, 512), BF16),
            pltpu.VMEM((4, 4, 2, 64, 640), BF16),
            pltpu.VMEM((4, tokens, width), BF16),
            pltpu.VMEM((4, 4, 4, 2, 128, 128), BF16),
            *ShardScatter.scratch(tokens, width),
            pltpu.VMEM((512, 640), BF16),
            pltpu.VMEM((512, 128), F32),
            pltpu.VMEM((4, 4, 2, 64, 512), BF16),
            pltpu.VMEM((4, 4, 2, 64, 128), BF16),
            *[pltpu.VMEM(a.shape, a.dtype) for a in in_hbm[9:]],
            *attend_back_scratch(),
            *GainScatter.scratch(),
            *scratch,
            pltpu.SemaphoreType.REGULAR,
            *sems(16 * CtxScatter.COPIES + 2 * CtxScatterLate.COPIES + 6 * CHUNKS + GainScatter.COPIES + 20),
        ],
        compiler_params=params(cid),
        name="backward",
    )(*in_hbm, *in_vmem)


FIRST_INPUT_ROWS = int([step for step in BACKWARD if step[0] == "I"][0][1])


def finish_kernel(gains, grad_in, out_in, g_query, g_kv, g_out, g_gate, g_up, g_down, *outs):
    first, second, grad_inputs, outputs, query, key, value, out, gate, up, down = outs
    start = (lax.axis_index("ctx") % 2) * 64 + lax.axis_index("wshard") * 16
    own = pltpu.roll(gains[...], 128 - start, 1)
    first[...] = own[0:1, :16]
    second[...] = own[1:2, :16]
    grad_inputs[...] = grad_in[...]
    outputs[...] = out_in[...]
    query[...] = g_query[...]
    key[...] = g_kv[:, :HD]
    value[...] = g_kv[:, HD:]
    out[...] = g_out[...]
    gate[...] = g_gate[...]
    up[...] = g_up[...]
    down[...] = g_down[...]


def finish(*arrays):
    shapes = [((1, 16), F32)] * 2 + [(a.shape, a.dtype) for a in arrays[1:4]] + [((64, HD), F32)] * 2
    shapes += [(a.shape, a.dtype) for a in arrays[5:]]
    return pl.pallas_call(
        finish_kernel,
        out_shape=[jax.ShapeDtypeStruct(*shape) for shape in shapes],
        in_specs=[VMEM] * len(arrays),
        out_specs=[VMEM] * len(shapes),
        compiler_params=pltpu.CompilerParams(vmem_limit_bytes=VMEM_LIMIT),
        name="finish",
    )(*arrays)


def rope_tables(positions):
    freqs = 10000.0 ** (-jnp.arange(HD // 2, dtype=F32) * 2.0 / HD)
    angles = positions[:, None] * freqs[None]
    cosine, sine = jnp.cos(angles), jnp.sin(angles)
    one, zero = jnp.ones_like(cosine), jnp.zeros_like(cosine)
    return jnp.stack(
        [
            jnp.concatenate([cosine] * 4, -1),
            jnp.concatenate([sine] * 4, -1),
            jnp.concatenate([cosine, cosine, one, one], -1),
            jnp.concatenate([sine, sine, zero, zero], -1),
        ]
    )


def per_device(
    inputs, cotangent, norm_attn, w_query, w_key, w_value, w_out, norm_mlp, w_gate, w_up, w_down
):
    width = inputs.shape[-1]
    half_len = inputs.shape[2]
    tokens = 2 * half_len
    ctx_count = lax.axis_size("ctx")
    ctx_index = lax.axis_index("ctx")
    length = tokens * ctx_count
    x = inputs.reshape(tokens, width)
    cot = cotangent.reshape(tokens, width)
    rows_local = jnp.arange(tokens)
    positions = jnp.where(
        rows_local < half_len,
        ctx_index * half_len + rows_local,
        length - (ctx_index + 1) * half_len + (rows_local - half_len),
    ).astype(F32)
    tables = rope_tables(positions)

    (
        normed_all, w_qkv, w_out_t, q, kv_all, attn, lse, hidden, branch_all, grad_hidden, gain2_part, result_part,
        g_gate, g_up, g_down_x, g_down_z,
    ) = forward(
        0, x, cot, norm_attn, norm_mlp, tables, [w_query, w_key, w_value], [w_out.T, w_gate, w_up, w_down.T]
    )
    grad_inputs, gains, outputs, g_query, g_kv, g_out, g_gate, g_up, g_down = backward(
        1,
        [branch_all, result_part, w_out_t, w_qkv, normed_all, g_gate, g_up, g_down_x, g_down_z]
        + [q, kv_all, attn, hidden, grad_hidden, x],
        [gain2_part, lse, tables, norm_attn],
    )
    gain1, gain2, grad_inputs, outputs, g_query, g_key, g_value, g_out, g_gate, g_up, g_down = finish(
        gains, grad_inputs, outputs, g_query, g_kv, g_out, g_gate, g_up, g_down
    )
    return (
        outputs.reshape(inputs.shape),
        grad_inputs.reshape(inputs.shape),
        gain1.reshape(16),
        g_query,
        g_key,
        g_value,
        g_out.T,
        gain2.reshape(16),
        g_gate,
        g_up,
        g_down.T,
    )


def solution(mesh):
    return jax.shard_map(
        per_device,
        mesh=mesh,
        in_specs=(
            P("wshard", None, "ctx", None),
            P("wshard", None, "ctx", None),
            P(),
            P("ctx", "wshard"),
            P("ctx", "wshard"),
            P("ctx", "wshard"),
            P("wshard", "ctx"),
            P(),
            P("ctx", "wshard"),
            P("ctx", "wshard"),
            P("wshard", "ctx"),
        ),
        out_specs=(
            P("wshard", None, "ctx", None),
            P("wshard", None, "ctx", None),
            P(("ctx", "wshard")),
            P("ctx", "wshard"),
            P("ctx", "wshard"),
            P("ctx", "wshard"),
            P("wshard", "ctx"),
            P(("ctx", "wshard")),
            P("ctx", "wshard"),
            P("ctx", "wshard"),
            P("wshard", "ctx"),
        ),
        check_vma=False,
    )
```

```python
from functools import partial

import jax
import jax.numpy as jnp
from jax import lax
from jax.experimental import pallas as pl
from jax.experimental.pallas import tpu as pltpu
from jax.sharding import PartitionSpec as P

MESH = pl.DeviceIdType.MESH
HD = 64
EPS = 1e-05
NEG = -1e30
F32 = jnp.float32
BF16 = jnp.bfloat16
VMEM_LIMIT = 63 * 2**20
ANY = pl.BlockSpec(memory_space=pl.ANY)
VMEM = pl.BlockSpec(memory_space=pltpu.VMEM)


class Place:
    def __init__(self):
        ctx, shard = lax.axis_index("ctx"), lax.axis_index("wshard")
        self.x, self.z, self.y = ctx // 8, (ctx // 2) % 4, ctx % 2
        self.yl, self.co = shard // 2, shard % 2

    def at(self, x=None, z=None, y=None, yl=None, co=None):
        x, z, y = (self.x if x is None else x), (self.z if z is None else z), (self.y if y is None else y)
        yl, co = (self.yl if yl is None else yl), (self.co if co is None else co)
        return (x * 8 + z * 2 + y, yl * 2 + co)

    def step(self, axis, by):
        return self.at(**{axis: (getattr(self, axis) + by) % 4})

    def pair(self, axis):
        return self.at(**{axis: 1 - getattr(self, axis)})

    def ctx_peers(self):
        return [self.step("x", 1), self.step("x", 3), self.step("z", 1), self.step("z", 3), self.pair("y")]

    def shard_peers(self):
        return [self.pair("co"), self.pair("yl")]

    def far_peers(self):
        return [self.step("x", 2), self.step("z", 2)]


def greet(peers, meanwhile=None):
    barrier = pltpu.get_barrier_semaphore()
    for device in peers:
        pl.semaphore_signal(barrier, inc=1, device_id=device, device_id_type=MESH)
    if meanwhile is not None:
        meanwhile()
    pl.semaphore_wait(barrier, len(peers))


class Copies:
    def __init__(self, send, recv):
        self.send, self.recv, self.used = send, recv, 0

    def start(self, src, dst, device):
        k = self.used
        self.used += 1
        copy = pltpu.make_async_remote_copy(
            src_ref=src, dst_ref=dst, send_sem=self.send.at[k], recv_sem=self.recv.at[k],
            device_id=device, device_id_type=MESH,
        )
        copy.start()
        return copy

    def local(self, src, dst):
        k = self.used
        self.used += 1
        copy = pltpu.make_async_copy(src, dst, self.send.at[k])
        copy.start()
        return copy


def wait_all(copies):
    for copy in copies:
        copy.wait()


class CtxGather:
    COPIES = 10
    STAGES = 6

    def __init__(self, place, copies, shard, full, lo, n, big):
        self.p, self.c, self.shard, self.full = place, copies, shard, full
        self.lo, self.n, self.big, self.small = lo, n, big, ("z" if big == "x" else "x")
        self.live = []

    def block(self, o, i, y):
        x, z = (o, i) if self.big == "x" else (i, o)
        return self.full.at[x, z, y, pl.ds(self.lo, self.n)]

    def send(self, part, axis, by):
        dev = self.p.pair("y") if axis == "y" else self.p.step(axis, by)
        self.live.append(self.c.start(part, part, dev))

    def stage(self, s):
        p = self.p
        o, i, y = getattr(p, self.big), getattr(p, self.small), p.y
        wait_all(self.live)
        self.live = []
        every, both = pl.ds(0, 4), pl.ds(0, 2)
        if s == 0 and self.shard is None:
            self.send(self.block(o, i, y), "y", 0)
        elif s == 0:
            own = self.shard.at[pl.ds(self.lo, self.n)]
            self.live.append(self.c.start(own, self.block(o, i, y), p.pair("y")))
            self.live.append(self.c.local(own, self.block(o, i, y)))
        elif s == 1:
            self.send(self.block(o, i, both), self.small, 1)
            self.send(self.block(o, i, both), self.small, 3)
        elif s == 2:
            self.send(self.block(o, (i + 3) % 4, 0), self.small, 1)
            self.send(self.block(o, (i + 1) % 4, 1), self.small, 3)
        elif s == 3:
            self.send(self.block(o, every, both), self.big, 1)
            self.send(self.block(o, every, both), self.big, 3)
        elif s == 4:
            self.send(self.block((o + 3) % 4, pl.ds(0, 2), both), self.big, 1)
            self.send(self.block((o + 1) % 4, pl.ds(2, 2), both), self.big, 3)


class CtxGatherLate(CtxGather):
    def block(self, o, i, y, lo=None, n=None):
        x, z = (o, i) if self.big == "x" else (i, o)
        return self.full.at[x, z, y, pl.ds(self.lo if lo is None else lo, self.n if n is None else n)]

    def stage(self, s):
        p = self.p
        o, i, y = getattr(p, self.big), getattr(p, self.small), p.y
        wait_all(self.live)
        self.live = []
        every, half = pl.ds(0, 4), self.n // 2
        if s == 0:
            own = self.shard.at[pl.ds(self.lo, self.n)]
            for by in (1, 3):
                self.live.append(self.c.start(own, self.block(o, i, y), p.step(self.big, by)))
            self.live.append(self.c.local(own, self.block(o, i, y)))
        elif s == 1:
            self.send(self.block((o + 3) % 4, i, y, self.lo, half), self.big, 1)
            self.send(self.block((o + 1) % 4, i, y, self.lo + half, half), self.big, 3)
        elif s == 2:
            self.send(self.block(every, i, y), self.small, 1)
            self.send(self.block(every, i, y), self.small, 3)
        elif s == 3:
            self.send(self.block(pl.ds(0, 2), (i + 3) % 4, y), self.small, 1)
            self.send(self.block(pl.ds(2, 2), (i + 1) % 4, y), self.small, 3)
        elif s == 4:
            self.send(self.block(every, every, y), "y", 0)


class CtxScatter:
    COPIES = 17
    STAGES = 7

    @staticmethod
    def scratch(n, width, staged=False):
        shapes = [(2, 2, 2), (4, 2), (4, 2), (2,), (2,), (2,), ()]
        if staged:
            shapes += [(2, 2), (2, 2)]
        return [pltpu.VMEM(shape + (n, width), BF16) for shape in shapes]

    def __init__(self, place, copies, src, out, bufs, lo, n, big, stop=False, resumed=None):
        self.p, self.c, self.src, self.out = place, copies, src, out
        self.far, self.pos, self.neg, self.far2, self.pos2, self.neg2, self.last = bufs[:7]
        self.staged = bufs[7:]
        self.lo, self.n, self.big, self.small = lo, n, big, ("z" if big == "x" else "x")
        self.first, self.live = [], []
        self.stop, self.resumed = stop, resumed
        if resumed is not None:
            self.live = [resumed]

    def part(self, o, i):
        x, z = (o, i) if self.big == "x" else (i, o)
        return self.src.at[x, z, pl.ds(0, 2), pl.ds(self.lo, self.n)]

    def load(self, o, i, y, which):
        if self.staged:
            return self.staged[which][i % 2, y].astype(F32)
        x, z = (o, i) if self.big == "x" else (i, o)
        return self.src[x, z, y, pl.ds(self.lo, self.n), :].astype(F32)

    def send(self, src, dst, axis, by):
        dev = self.p.pair("y") if axis == "y" else self.p.step(axis, by)
        copy = self.c.start(src, dst, dev)
        self.live.append(copy)
        return copy

    def stage(self, s):
        p, big, small = self.p, self.big, self.small
        o, i, y = getattr(p, big), getattr(p, small), p.y
        up, down, across = (o + 1) % 4, (o + 3) % 4, (o + 2) % 4
        iup, idown, iacross = (i + 1) % 4, (i + 3) % 4, (i + 2) % 4
        low, high = pl.ds(0, 2), pl.ds(2, 2)
        if s == 2:
            wait_all(self.first)
        elif s > 2:
            wait_all(self.live)
            self.live = []
        if s == 0:
            for src, dst, by in (
                (self.part(across, low), self.far.at[0], 1), (self.part(across, high), self.far.at[1], 3)
            ):
                self.first.append(self.c.start(src, dst, p.step(big, by)))
            if self.staged:
                self.first.append(self.c.local(self.part(up, low), self.staged[0]))
                self.first.append(self.c.local(self.part(down, high), self.staged[1]))
        elif s == 1:
            self.send(self.part(up, high), self.pos.at[high], big, 1)
            self.send(self.part(down, low), self.neg.at[low], big, 3)
        elif s == 2:

            def fold(k, _):
                b, q = k // 2, k % 2
                self.far[0, b, q] = (self.far[0, b, q].astype(F32) + self.load(up, b, q, 0)).astype(BF16)
                self.far[1, b, q] = (self.far[1, b, q].astype(F32) + self.load(down, b + 2, q, 1)).astype(BF16)
                return 0

            lax.fori_loop(0, 4, fold, 0)
            self.send(self.far.at[0], self.pos.at[low], big, 1)
            self.send(self.far.at[1], self.neg.at[high], big, 3)
            if self.staged:
                self.live.append(self.c.local(self.part(o, low), self.staged[0]))
                self.live.append(self.c.local(self.part(o, high), self.staged[1]))
        elif s == 3:

            def total(k, _):
                b, q = k // 2, k % 2
                for which in range(2):
                    at = b + 2 * which
                    here = self.load(o, at, q, which) + self.pos[at, q].astype(F32) + self.neg[at, q].astype(F32)
                    self.pos[at, q] = here.astype(BF16)
                return 0

            if self.resumed is None:
                lax.fori_loop(0, 4, total, 0)
            if self.stop:
                self.live = [self.c.local(self.pos, self.out)]
                return
            self.first = [
                self.c.start(self.pos.at[iacross, 0], self.far2.at[0], p.step(small, 1)),
                self.c.start(self.pos.at[iacross, 1], self.far2.at[1], p.step(small, 3)),
            ]
            self.send(self.pos.at[iup, 1], self.pos2.at[1], small, 1)
            self.send(self.pos.at[idown, 0], self.neg2.at[0], small, 3)
        elif s == 4:
            wait_all(self.first)
            self.far2[0] = (self.far2[0].astype(F32) + self.pos[iup, 0].astype(F32)).astype(BF16)
            self.far2[1] = (self.far2[1].astype(F32) + self.pos[idown, 1].astype(F32)).astype(BF16)
            self.send(self.far2.at[0], self.pos2.at[0], small, 1)
            self.send(self.far2.at[1], self.neg2.at[1], small, 3)
        elif s == 5:
            for q in range(2):
                here = self.pos[i, q].astype(F32) + self.pos2[q].astype(F32) + self.neg2[q].astype(F32)
                self.pos2[q] = here.astype(BF16)
            self.send(self.pos2.at[1 - y], self.last, "y", 0)
        elif s == 6:
            total = self.pos2[y].astype(F32) + self.last[...].astype(F32)
            self.out[pl.ds(self.lo, self.n), :] = total.astype(self.out.dtype)


class CtxScatterLate:
    COPIES = 19
    STAGES = 6

    @staticmethod
    def scratch(n, width):
        shapes = [(4, 4, n), (4, 4, n), (2, 2, n), (4, n), (4, n), (2, n // 2), (2, n // 2), (2, n // 2)]
        return [pltpu.VMEM(shape + (width,), BF16) for shape in shapes]

    def __init__(self, place, copies, src, out, bufs, lo, n, big):
        self.p, self.c, self.src, self.out = place, copies, src, out
        self.all, self.staged, self.far, self.pos, self.neg, self.far2, self.pos2, self.neg2 = bufs
        self.lo, self.n, self.big, self.small = lo, n, big, ("z" if big == "x" else "x")
        self.first, self.live, self.loads = [], [], []

    def part(self, o, i):
        x, z = (o, i) if self.big == "x" else (i, o)
        return self.all.at[x, z]

    def load(self, o, i):
        x, z = (o, i) if self.big == "x" else (i, o)
        return self.all[x, z].astype(F32)

    def start(self, src, dst, axis, by):
        return self.c.start(src, dst, self.p.pair("y") if axis == "y" else self.p.step(axis, by))

    def stage_own(self, o):
        every, rows = pl.ds(0, 4), pl.ds(self.lo, self.n)
        x, z = (o, every) if self.big == "x" else (every, o)
        self.loads.append(self.c.local(self.src.at[x, z, self.p.y, rows], self.staged.at[o]))

    def stage(self, s):
        p, big, small, n = self.p, self.big, self.small, self.n
        o, i = getattr(p, big), getattr(p, small)
        up, down, across = (o + 1) % 4, (o + 3) % 4, (o + 2) % 4
        iup, idown, iacross = (i + 1) % 4, (i + 3) % 4, (i + 2) % 4
        low, high, every = pl.ds(0, 2), pl.ds(2, 2), pl.ds(0, 4)
        rows = [pl.ds(0, n // 2), pl.ds(n // 2, n // 2)]
        if s in (2, 4):
            wait_all(self.first)
        else:
            wait_all(self.live)
            self.live = []
        if s == 0:
            theirs = self.src.at[every, every, 1 - p.y, pl.ds(self.lo, n)]
            self.live = [self.start(theirs, self.all, "y", 0)]
            for slab in range(4):
                self.stage_own(slab)
        elif s == 1:
            for slab in range(4):
                self.loads[slab].wait()

                def add(k, _):
                    x, z = (slab, k) if big == "x" else (k, slab)
                    here = self.all[x, z].astype(F32) + self.staged[slab, k].astype(F32)
                    self.all[x, z] = here.astype(BF16)
                    return 0

                lax.fori_loop(0, 4, add, 0)
            self.first = [
                self.start(self.part(across, low), self.far.at[0], big, 1),
                self.start(self.part(across, high), self.far.at[1], big, 3),
            ]
            self.live = [
                self.start(self.part(up, high), self.pos.at[high], big, 1),
                self.start(self.part(down, low), self.neg.at[low], big, 3),
            ]
        elif s == 2:
            for b in range(2):
                self.far[0, b] = (self.far[0, b].astype(F32) + self.load(up, b)).astype(BF16)
                self.far[1, b] = (self.far[1, b].astype(F32) + self.load(down, b + 2)).astype(BF16)
            self.live += [
                self.start(self.far.at[0], self.pos.at[low], big, 1),
                self.start(self.far.at[1], self.neg.at[high], big, 3),
            ]
        elif s == 3:
            for b in range(4):
                here = self.load(o, b) + self.pos[b].astype(F32) + self.neg[b].astype(F32)
                self.pos[b] = here.astype(BF16)
            self.first = [
                self.start(self.pos.at[iacross, rows[0]], self.far2.at[0], small, 1),
                self.start(self.pos.at[iacross, rows[1]], self.far2.at[1], small, 3),
            ]
            self.live = [
                self.start(self.pos.at[iup, rows[1]], self.pos2.at[1], small, 1),
                self.start(self.pos.at[idown, rows[0]], self.neg2.at[0], small, 3),
            ]
        elif s == 4:
            self.far2[0] = (self.far2[0].astype(F32) + self.pos[iup, rows[0], :].astype(F32)).astype(BF16)
            self.far2[1] = (self.far2[1].astype(F32) + self.pos[idown, rows[1], :].astype(F32)).astype(BF16)
            self.live += [
                self.start(self.far2.at[0], self.pos2.at[0], small, 1),
                self.start(self.far2.at[1], self.neg2.at[1], small, 3),
            ]
        elif s == 5:
            for h in range(2):
                here = self.pos[i, rows[h], :].astype(F32) + self.pos2[h].astype(F32) + self.neg2[h].astype(F32)
                self.out[pl.ds(self.lo + h * (n // 2), n // 2), :] = here


class ShardGather:
    def __init__(self, place, copies, full, chunks):
        self.p, self.c, self.full, self.chunks = place, copies, full, chunks
        self.rows = full.shape[1] // chunks
        self.me, self.over = place.yl * 2 + place.co, (1 - place.yl) * 2 + place.co
        self.far, self.near = [], []

    COPIES = 3

    def part(self, who, k):
        return self.full.at[who, pl.ds(k * self.rows, self.rows)]

    def send(self, k, src=None):
        src = self.part(self.me, k) if src is None else src
        self.far.append(self.c.start(src, self.part(self.me, k), self.p.pair("yl")))
        self.near.append(self.c.start(src, self.part(self.me, k), self.p.pair("co")))

    def forward(self, k):
        self.far[k].wait()
        self.near.append(self.c.start(self.part(self.over, k), self.part(self.over, k), self.p.pair("co")))

    def finish(self):
        wait_all(self.near)


class ShardScatter:
    COPIES = 3

    @staticmethod
    def scratch(rows, width):
        return [pltpu.VMEM((rows, width), BF16)] * 3

    def __init__(self, place, copies, part, bufs, chunks):
        self.p, self.c, self.part, self.chunks = place, copies, part, chunks
        self.relay, self.near, self.over = bufs
        self.rows = part.shape[1] // chunks
        self.first, self.second, self.third = [], [], []

    def at(self, k):
        return pl.ds(k * self.rows, self.rows)

    def begin(self):
        self.begin_far()
        self.begin_near()

    def begin_far(self):
        p = self.p
        for k in range(self.chunks):
            src = self.part.at[(1 - p.yl) * 2 + 1 - p.co, self.at(k)]
            self.first.append(self.c.start(src, self.relay.at[self.at(k)], p.pair("co")))

    def begin_near(self):
        p = self.p
        for k in range(self.chunks):
            src = self.part.at[p.yl * 2 + 1 - p.co, self.at(k)]
            self.second.append(self.c.start(src, self.near.at[self.at(k)], p.pair("co")))

    def relay_on(self, k):
        p = self.p
        self.first[k].wait()
        here = self.part[(1 - p.yl) * 2 + p.co, self.at(k), :].astype(F32)
        self.relay[self.at(k), :] = (self.relay[self.at(k), :].astype(F32) + here).astype(BF16)
        self.third.append(self.c.start(self.relay.at[self.at(k)], self.over.at[self.at(k)], p.pair("yl")))

    def total(self, k):
        p = self.p
        self.second[k].wait()
        self.third[k].wait()
        here = self.part[p.yl * 2 + p.co, self.at(k), :].astype(F32)
        return here + self.near[self.at(k), :].astype(F32) + self.over[self.at(k), :].astype(F32)


class ShardScatterColumns(ShardScatter):
    def __init__(self, place, copies, part, bufs, chunks):
        super().__init__(place, copies, part, bufs, chunks)
        self.columns = part.shape[2] // chunks

    def begin(self, k):
        p, cols = self.p, pl.ds(k * self.columns, self.columns)
        far, near = (1 - p.yl) * 2 + 1 - p.co, p.yl * 2 + 1 - p.co
        self.first.append(self.c.start(self.part.at[far, :, cols], self.relay.at[:, cols], p.pair("co")))
        self.second.append(self.c.start(self.part.at[near, :, cols], self.near.at[:, cols], p.pair("co")))

    def relay_on(self, k):
        p, cols = self.p, pl.ds(k * self.columns, self.columns)
        self.first[k].wait()
        here = self.part[(1 - p.yl) * 2 + p.co, :, cols].astype(F32)
        self.relay[:, cols] = (self.relay[:, cols].astype(F32) + here).astype(BF16)
        self.third.append(self.c.start(self.relay.at[:, cols], self.over.at[:, cols], p.pair("yl")))

    def total(self, k):
        if k == 0:
            wait_all(self.second + self.third)
        here = self.part[self.p.yl * 2 + self.p.co, self.at(k), :].astype(F32)
        return here + self.near[self.at(k), :].astype(F32) + self.over[self.at(k), :].astype(F32)


class GainScatter:
    COPIES = 9
    STAGES = 6

    @staticmethod
    def scratch():
        return [
            pltpu.VMEM((8, 2048), F32),
            pltpu.VMEM((3, 8, 512), F32),
            pltpu.VMEM((8, 512), F32),
            pltpu.VMEM((3, 8, 128), F32),
            pltpu.VMEM((3, 8, 128), F32),
            pltpu.VMEM((3, 8, 128), F32),
        ]

    def __init__(self, place, copies, out, bufs):
        self.p, self.c, self.out = place, copies, out
        self.vec, self.xs, self.mid, self.zs, self.own, self.rest = bufs
        self.live = []

    def stage(self, s):
        p = self.p
        wait_all(self.live)
        self.live = []
        if s == 0:
            for by in (1, 2, 3):
                cols = pl.ds(pl.multiple_of(((p.x + by) % 4) * 512, 512), 512)
                self.live.append(self.c.start(self.vec.at[:, cols], self.xs.at[by - 1], p.step("x", by)))
        elif s == 1:
            cols = pl.ds(pl.multiple_of(p.x * 512, 512), 512)
            self.mid[...] = self.vec[:, cols] + self.xs[0] + self.xs[1] + self.xs[2]
            for by in (1, 2, 3):
                cols = pl.ds(pl.multiple_of(((p.z + by) % 4) * 128, 128), 128)
                self.live.append(self.c.start(self.mid.at[:, cols], self.zs.at[by - 1], p.step("z", by)))
        elif s == 2:
            cols = pl.ds(pl.multiple_of(p.z * 128, 128), 128)
            self.own[0] = self.mid[:, cols] + self.zs[0] + self.zs[1] + self.zs[2]
            self.live.append(self.c.start(self.own.at[0], self.rest.at[0], p.pair("y")))
        elif s == 3:
            self.own[1] = self.own[0] + self.rest[0]
            self.live.append(self.c.start(self.own.at[1], self.rest.at[1], p.pair("co")))
        elif s == 4:
            self.own[2] = self.own[1] + self.rest[1]
            self.live.append(self.c.start(self.own.at[2], self.rest.at[2], p.pair("yl")))
        elif s == 5:
            self.out[...] = self.own[2] + self.rest[2]


def sems(n):
    return [pltpu.SemaphoreType.DMA((n,)), pltpu.SemaphoreType.DMA((n,))]


def params(cid):
    return pltpu.CompilerParams(collective_id=cid, has_side_effects=True, vmem_limit_bytes=VMEM_LIMIT)


def halves(rows):
    return ((0, rows // 2, "x"), (rows // 2, rows // 2, "z"))


CHUNKS = 4
LATE = 1280


def norm_back_rows(grad, resid, gain):
    factor = lax.rsqrt(jnp.mean(resid * resid, -1, keepdims=True) + EPS)
    weighted = grad * gain
    per_gain = grad * resid * factor
    back = factor * weighted - resid * (factor * factor * factor) * jnp.mean(weighted * resid, -1, keepdims=True)
    return back, per_gain


def eight(rows):
    return jnp.sum(rows.reshape(rows.shape[0] // 8, 8, rows.shape[1]), 0)


KEYS = 256
KB = 4


def lane_iota(rows):
    return lax.broadcasted_iota(jnp.int32, (rows, 128), 1)


def rotate_tile(u, cosine, sine):
    low = lane_iota(u.shape[0]) % HD < HD // 2
    turned = jnp.where(low, -pltpu.roll(u, 128 - HD // 2, 1), pltpu.roll(u, HD // 2, 1))
    return u * cosine + turned * sine


def unrotate_tile(w, cosine, sine):
    low = lane_iota(w.shape[0]) % HD < HD // 2
    s = w * sine
    return w * cosine + jnp.where(low, pltpu.roll(s, 128 - HD // 2, 1), -pltpu.roll(s, HD // 2, 1))


def project_rows(rows, w_qkv, tables):
    lin = jnp.dot(rows, w_qkv, preferred_element_type=F32)
    tiles = []
    for hp in range(4):
        tile = lin[:, hp * 128 : (hp + 1) * 128]
        tiles.append((rotate_tile(tile, tables[0], tables[1])).astype(BF16) * jnp.asarray(HD**-0.5, BF16))
    kv = rotate_tile(lin[:, 512:640], tables[2], tables[3]).astype(BF16)
    return tiles, kv


def head_rows(ref, start, keep_low):
    low = lane_iota(64) < HD
    keep = low if keep_low else ~low
    pieces = []
    for hp in range(4):
        tile = ref[pl.ds(start, 64), hp * 128 : (hp + 1) * 128].astype(F32)
        turned = pltpu.roll(tile, HD, 1)
        even, odd = (tile, turned) if keep_low else (turned, tile)
        pieces += [jnp.where(keep, even, 0.0), jnp.where(keep, odd, 0.0)]
    return pieces


def key_chunk(kv, seq, chunk, half):
    start = pl.multiple_of(seq * 128 + half * 64, 64)
    z = pl.ds((chunk % 2) * 2, 2)
    return kv[chunk // 2, z, :, pl.ds(start, 64), :].reshape(KEYS, 128)


def diagonal(block, here):
    key = lax.broadcasted_iota(jnp.int32, (KEYS, 512), 0)
    query = lax.broadcasted_iota(jnp.int32, (KEYS, 512), 1) % 64
    ahead = key // 64 - here
    return key % 64 - query <= (-ahead if block == 0 else ahead) * 64


def pick(u, own_chunk):
    late = u - 8
    block = jnp.where(u < 8, 1, jnp.where(late >= own_chunk, 1, 0))
    half = jnp.where(u < 8, 0, block)
    chunk = jnp.where(u < 8, u, late + half)
    return block, chunk, half


def nt(a, b):
    return lax.dot_general(a, b, (((1,), (1,)), ((), ())), preferred_element_type=F32)


def tn(a, b):
    return lax.dot_general(a, b, (((0,), (0,)), ((), ())), preferred_element_type=F32)


def attend_seq(seq, ctx, q, kv, attn, lse, scratch):
    qe, top, acc = scratch
    low = lane_iota(64) < HD
    ones_low = lane_iota(KEYS) < HD
    own_chunk, here = ctx // KB, ctx % KB

    def with_ones(keys):
        return jnp.where(ones_low, jnp.ones_like(keys), keys)

    for b in range(2):
        for h, piece in enumerate(head_rows(q, seq * 128 + b * 64, True)):
            qe[b, h * 64 : (h + 1) * 64, :] = piece.astype(BF16)
    for b in range(2):
        keys = key_chunk(kv, seq, own_chunk, b)
        scores = jnp.where(diagonal(b, here), nt(keys, qe[b]), NEG)
        m = jnp.max(scores, 0, keepdims=True)
        p = jnp.exp(scores - m).astype(BF16)
        top[b] = m
        acc[b] = tn(with_ones(keys), p)

    def step(u, _):
        b, chunk, half = pick(u, own_chunk)
        keys = key_chunk(kv, seq, chunk, half)
        scores = nt(keys, qe[b])
        before = top[b]
        m = jnp.maximum(before, jnp.max(scores, 0, keepdims=True))
        p = jnp.exp(scores - m).astype(BF16)
        top[b] = m
        acc[b] = acc[b] * jnp.exp(before - m) + tn(with_ones(keys), p)
        return 0

    for k in range(3):
        lax.fori_loop(5 * k, 5 * k + 5, step, 0, unroll=True)
        if k < 2:
            yield
    for b in range(2):
        here_acc = acc[b]
        total = here_acc[0:1, :]
        lse[pl.ds(seq * 2 + b, 1), :] = top[b] + jnp.log(total)
        out = (here_acc * (1.0 / total)).T
        for hp in range(4):
            even, odd = out[hp * 128 : hp * 128 + 64, :], out[hp * 128 + 64 : hp * 128 + 128, :]
            tile = jnp.where(low, pltpu.roll(even, HD, 1), odd)
            attn[pl.ds(seq * 128 + b * 64, 64), hp * 128 : (hp + 1) * 128] = tile.astype(BF16)


def attend_scratch():
    return [pltpu.VMEM((2, 512, 128), BF16), pltpu.VMEM((2, 1, 512), F32), pltpu.VMEM((2, 128, 512), F32)]


def attend_back_seq(seq, ctx, q, kv, grad, attn, lse, tables, grad_lin, grad_kv, scratch):
    qd, delta, dq, dkv = scratch
    low = lane_iota(64) < HD
    own_chunk, here = ctx // KB, ctx % KB
    for b in range(2):
        start = seq * 128 + b * 64
        q_rows, g_rows, o_rows = (
            head_rows(q, start, True), head_rows(grad, start, False), head_rows(attn, start, False)
        )
        for h in range(8):
            qd[b, h * 64 : (h + 1) * 64, :] = q_rows[h].astype(BF16)
            qd[b, 512 + h * 64 : 512 + (h + 1) * 64, :] = g_rows[h].astype(BF16)
        products = jnp.concatenate([g * o for g, o in zip(g_rows, o_rows)], 0)
        delta[b] = jnp.sum(products.T, 0, keepdims=True)

    def grads(b, keys, allowed):
        both = nt(keys, qd[b])
        p = jnp.exp(both[:, :512] - lse[pl.ds(seq * 2 + b, 1), :])
        if allowed is not None:
            p = jnp.where(allowed, p, 0.0)
        ds = (p * (both[:, 512:] - delta[b])).astype(BF16)
        joined = jnp.concatenate([ds, p.astype(BF16)], 1)
        return tn(keys, ds), jnp.dot(joined, qd[b], preferred_element_type=F32)

    dkv[...] = jnp.zeros_like(dkv)

    def add_keys(chunk, half, value):
        start = pl.multiple_of(half * 64, 64)
        dkv[pl.ds(chunk * KB, KB), pl.ds(start, 64), :] += value.reshape(KB, 64, 128)

    for b in range(2):
        dq_part, dkv_part = grads(b, key_chunk(kv, seq, own_chunk, b), diagonal(b, here))
        dq[b] = dq_part
        add_keys(own_chunk, b, dkv_part)

    def step(u, _):
        b, chunk, half = pick(u, own_chunk)
        dq_part, dkv_part = grads(b, key_chunk(kv, seq, chunk, half), None)
        dq[b] += dq_part
        add_keys(chunk, half, dkv_part)
        return 0

    for k in range(3):
        lax.fori_loop(5 * k, 5 * k + 5, step, 0, unroll=True)
        if k < 2:
            yield
    for b in range(2):
        out = (dq[b] * HD**-0.5).T
        cosine, sine = tables[0, b * 64 : (b + 1) * 64, :], tables[1, b * 64 : (b + 1) * 64, :]
        for hp in range(4):
            even, odd = out[hp * 128 : hp * 128 + 64, :], out[hp * 128 + 64 : hp * 128 + 128, :]
            tile = jnp.where(low, even, pltpu.roll(odd, HD, 1))
            tile = unrotate_tile(tile, cosine, sine)
            grad_lin[pl.ds(seq * 128 + b * 64, 64), hp * 128 : (hp + 1) * 128] = tile.astype(BF16)
    grad_kv[...] = dkv[...].reshape(4, 4, 2, 128, 128).astype(BF16)


def attend_back_scratch():
    return [
        pltpu.VMEM((2, 1024, 128), BF16),
        pltpu.VMEM((2, 1, 512), F32),
        pltpu.VMEM((2, 128, 512), F32),
        pltpu.VMEM((32, 128, 128), F32),
    ]


def ctx_gathers(place, copies, src, full, kind=CtxGather):
    return [kind(place, copies, src, full, lo, rows, big) for lo, rows, big in halves(src.shape[0])]


FORWARD = [
    "w0", "o0", "h0", "u0", "d0", "w1", "d1", "g0", "o1", "N1", "w2", "d2", "w3", "o2", "u1", "NF", "w4", "d3",
    "CB", "o3", "NW", "w5", "J1", "J2", "k20", "k10", "J0", "k00", "J3", "k30", "d4", "g1", "k01", "k11", "k21",
    "k31", "o4", "k02", "h1", "k32", "k22", "k12", "u2", "k03", "g2", "k23", "k13", "k33", "h2", "k04", "k14",
    "k24", "h3", "g3", "k05", "k15", "CF", "A00", "A01", "A02", "h4", "k25", "A10", "o5", "OP0", "A11", "A12",
    "k34", "CW", "u3", "A20", "A21", "RF", "A22", "g4", "OP2", "OP1", "k35", "RR", "A30", "A31", "RN", "A32", "OP3",
    "NT", "u4", "d5", "h5", "DA", "SF", "u5", "SW", "g5", "FU", "T0", "T1", "XR0", "GD", "e0", "XR1", "T2", "T3",
    "e1", "XR2", "XR3", "GU", "e2", "XT", "GG", "RP", "XF", "e3", "XW",
]

BACKWARD = [
    "u0", "g0", "DO", "DP", "GO", "g1", "o0", "A00", "A01", "o1", "A02", "k00", "A10", "A11", "o2", "g2", "d3",
    "k01", "A12", "k02", "RESB", "A20", "A21", "k10", "k11", "A22", "k20", "A30", "k12", "g3", "k21", "A31", "d4",
    "A32", "k30", "QG", "k31", "k22", "k03", "k13", "RESR", "k32", "k04", "g4", "k33", "k23", "k14", "q0", "k34",
    "k24", "q1", "k15", "u1", "q2", "k25", "RES", "k16", "I1", "k26", "k35", "k05", "I2", "d5", "o3", "k06", "k36",
    "I3", "I0", "VG", "v0", "v1", "g5", "q3", "u2", "v2", "TOT", "n0", "q4", "o4", "v3", "n1", "u3", "n2", "v4",
    "q5", "o5", "u4", "n3", "v5", "q6", "n4", "v6", "u5", "o6", "g6", "d6", "n5",
]


def run_steps(steps, engines, actions):
    for step in steps:
        if step in actions:
            actions[step]()
        else:
            for e in engines[step[:-1]]:
                e.stage(int(step[-1]))


def gain_row(ref):
    gain = ref[...].astype(F32)
    return jnp.concatenate([gain[k : k + 1, :] for k in range(16)], 1)


def over_hidden_units(tile):
    def one(j, _):
        tile(pl.ds(pl.multiple_of(j * 512, 512), 512), 512)
        return 0

    lax.fori_loop(0, 2, one, 0)
    tile(pl.ds(1024, 384), 384)


def over_width(step):
    def one(j, _):
        step(j, pl.ds(pl.multiple_of(j * 512, 512), 512))
        return 0

    lax.fori_loop(0, 4, one, 0)


def forward_kernel(
    x, cot, gain1, gain2, tables, wq, wk, wv, w_out_shard, w_gate_shard, w_up_shard, w_down_shard,
    normed1_out, w_qkv_out, w_out_out, q_out, kv_out, attn_out, lse, hidden_out, branch_out, grad_hidden_out, grad_gain,
    result_out, g_gate_out, g_up_out, g_down_x, g_down_z,
    normed1_all, w_qkv_shard, w_qkv, w_out, kv_all, part, relay, near, over, qe, top, acc,
    w_gate, w_up, w_down, g_down, cot_all, normed2_all, gate_pre, up_pre, active, grad_gate, grad_up, branch,
    q, attn, hidden, grad_hidden, *rest,
):
    bufs, (send, recv) = rest[:14], rest[14:]
    place = Place()
    me = place.yl * 2 + place.co

    def prepare():
        rows = x[...].astype(F32)
        factor = lax.rsqrt(jnp.mean(rows * rows, -1, keepdims=True) + EPS)
        normed1_all[me] = (rows * factor * gain_row(gain1)).astype(BF16)
        w_qkv_shard[:, :512] = wq[...]
        w_qkv_shard[:, 512:640] = jnp.concatenate([wk[...], wv[...]], 1)

    greet(place.ctx_peers() + place.shard_peers(), prepare)
    copies = Copies(send, recv)
    ctx = lax.axis_index("ctx")
    order = [2 * (1 - place.yl) + 1 - place.co, 2 * (1 - place.yl) + place.co]
    order += [2 * place.yl + 1 - place.co, 2 * place.yl + place.co]
    starts = [pl.multiple_of(seq * 128, 128) for seq in order]
    engines = {
        "w": ctx_gathers(place, copies, w_qkv_shard, w_qkv),
        "o": ctx_gathers(place, copies, w_out_shard, w_out),
        "g": ctx_gathers(place, copies, w_gate_shard, w_gate),
        "u": ctx_gathers(place, copies, w_up_shard, w_up),
        "d": ctx_gathers(
            place, copies, w_down_shard.at[:, pl.ds(0, LATE)], w_down.at[:, :, :, :, pl.ds(0, LATE)], CtxGatherLate
        ),
        "h": ctx_gathers(
            place, copies, w_down_shard.at[:, pl.ds(LATE, 1408 - LATE)],
            w_down.at[:, :, :, :, pl.ds(LATE, 1408 - LATE)],
        ),
    }
    for k in range(4):
        engines[f"k{k}"] = [CtxGather(place, copies, None, kv_all, starts[k], 128, "xz"[k % 2])]
    normed = ShardGather(place, copies, normed1_all, 1)
    cots = ShardGather(place, copies, cot_all, 1)
    rows_out = ShardScatter(place, copies, part, (relay, near, over), CHUNKS)
    spread = ShardGather(place, copies, normed2_all, CHUNKS)
    thirds = [attend_seq(seq, ctx, q, kv_all, attn, lse, (qe, top, acc)) for seq in order]
    back = ShardScatterColumns(place, copies, part, (relay, near, over), CHUNKS)
    branches = ShardGather(place, copies, branch, CHUNKS)
    engines["e"] = [
        CtxScatter(place, copies, g_down, out, bufs[7 * h : 7 * h + 7], lo, rows, big, stop=True)
        for h, (out, (lo, rows, big)) in enumerate(zip((g_down_x, g_down_z), halves(64)))
    ]
    outgoing, normed_copy = [], []
    def normed_here():
        normed.finish()
        normed_copy.append(copies.local(normed1_all, normed1_out))

    def project_seq(k):
        at = pl.ds(starts[k], 128)
        tiles, kv = project_rows(normed1_all[order[k]], w_qkv[...].reshape(2048, 640), tables)
        for hp, tile in enumerate(tiles):
            q[at, hp * 128 : (hp + 1) * 128] = tile
        kv_all[place.x, place.z, place.y, at, :] = kv

    own_cot = []

    def send_cot():
        cots.send(0, cot)
        own_cot.append(copies.local(cot, cot_all.at[cots.me]))

    def cot_here():
        cots.finish()
        wait_all(own_cot)

    def project_out(k):
        part[order[k]] = nt(attn[pl.ds(starts[k], 128), :], w_out[...].reshape(2048, 512)).astype(BF16)

    def relay_rows():
        for c in range(CHUNKS):
            rows_out.relay_on(c)

    def second_norm():
        outgoing.extend(
            copies.local(*pair)
            for pair in ((w_qkv, w_qkv_out), (w_out, w_out_out), (kv_all, kv_out), (q, q_out), (attn, attn_out))
        )
        gain = gain_row(gain2)
        for c in range(CHUNKS):
            at = rows_out.at(c)
            here = x[at, :].astype(F32) + rows_out.total(c)
            hidden[at, :] = here
            factor = lax.rsqrt(jnp.mean(here * here, -1, keepdims=True) + EPS)
            normed2_all[spread.me, at, :] = (here * factor * gain).astype(BF16)
            spread.send(c)
        outgoing.append(copies.local(hidden, hidden_out))

    def spread_on():
        for c in range(CHUNKS):
            spread.forward(c)

    def columns_of(w, cols, width):
        return w[:, :, :, :, cols].reshape(2048, width)

    def grad_active_tiles():
        def tile(cols, width):
            rows = cot_all[...].reshape(512, 2048)
            here = jnp.dot(rows, columns_of(w_down, cols, width), preferred_element_type=F32)
            grad_up[:, cols] = here.astype(BF16)

        over_hidden_units(tile)

    def hidden_units():
        def tile(cols, width):
            rows = normed2_all[...].reshape(512, 2048)
            here = pl.ds(0, width)
            gate_pre[:, here] = jnp.dot(rows, columns_of(w_gate, cols, width), preferred_element_type=F32)
            up_pre[:, here] = jnp.dot(rows, columns_of(w_up, cols, width), preferred_element_type=F32)

            def some(r, _):
                at = pl.ds(pl.multiple_of(r * 64, 64), 64)
                gate, up, grad = gate_pre[at, here], up_pre[at, here], grad_up[at, cols].astype(F32)
                sigmoid = 1.0 / (1.0 + jnp.exp(-gate))
                silu = gate * sigmoid
                active[at, cols] = (silu * up).astype(BF16)
                grad_gate[at, cols] = (grad * up * sigmoid * (1.0 + gate * (1.0 - sigmoid))).astype(BF16)
                grad_up[at, cols] = (grad * silu).astype(BF16)
                return 0

            lax.fori_loop(0, 8, some, 0)

        over_hidden_units(tile)

    def result_tiles():
        wait_all(normed_copy)
        result_part = normed1_all

        def step(j, cols):
            rows = nt(active[...], w_down[j].reshape(512, 1408))
            result_part[:, :, cols] = rows.astype(BF16).reshape(4, 128, 512)

        over_width(step)
        outgoing.append(copies.local(result_part, result_out))

    def grad_normed_tile(j):
        rows = nt(grad_gate[...], w_gate[j].reshape(512, 1408)) + nt(grad_up[...], w_up[j].reshape(512, 1408))
        part[:, :, j * 512 : (j + 1) * 512] = rows.astype(BF16).reshape(4, 128, 512)
        back.begin(j)

    def weight_grad(left, right, w):
        def step(j, cols):
            block = tn(left[:, :, cols].reshape(512, 512), right[...])
            w[j] = block.astype(BF16).reshape(4, 2, 64, 1408)

        over_width(step)

    def gate_grad():
        weight_grad(normed2_all, grad_gate, w_gate)
        outgoing.append(copies.local(w_gate, g_gate_out))

    def up_grad():
        weight_grad(normed2_all, grad_up, w_up)
        outgoing.append(copies.local(w_up, g_up_out))

    def second_norm_back():
        gain = gain_row(gain2)
        for c in range(CHUNKS):
            at = back.at(c)
            grad, per_gain = norm_back_rows(back.total(c), hidden[at, :], gain)
            here = cot_all[branches.me, at, :].astype(F32) + grad
            grad_hidden[at, :] = here
            branch[branches.me, at, :] = here.astype(BF16)
            branches.send(c)
            grad_gain[...] = eight(per_gain) if c == 0 else grad_gain[...] + eight(per_gain)
        outgoing.append(copies.local(grad_hidden, grad_hidden_out))

    def branch_on():
        for c in range(CHUNKS):
            branches.forward(c)

    def branch_here():
        branches.finish()
        outgoing.append(copies.local(branch, branch_out))

    actions = {
        "N1": lambda: normed.send(0), "NF": lambda: normed.forward(0), "NW": normed_here,
        "CB": send_cot, "CF": lambda: cots.forward(0), "CW": cot_here,
        "RF": rows_out.begin_far, "RR": relay_rows, "RN": rows_out.begin_near,
        "NT": second_norm, "SF": spread_on, "SW": spread.finish,
        "DA": grad_active_tiles, "FU": hidden_units, "RP": result_tiles,
        "GD": lambda: weight_grad(cot_all, active, g_down), "GG": gate_grad, "GU": up_grad, "XT": second_norm_back,
        "XF": branch_on, "XW": branch_here,
    }
    for k in range(4):
        actions[f"T{k}"] = partial(grad_normed_tile, k)
        actions[f"XR{k}"] = partial(back.relay_on, k)
        actions[f"J{k}"] = partial(project_seq, k)
        actions[f"OP{k}"] = partial(project_out, k)
        for third in range(3):
            actions[f"A{k}{third}"] = partial(next, thirds[k], None)
    run_steps(FORWARD, engines, actions)
    wait_all(outgoing + [copy for e in engines["e"] for copy in e.live])


def forward(cid, x, cot, gain1, gain2, tables, w_qkv, shards):
    tokens, width = x.shape
    every = (4, tokens, width)
    ffn_width = shards[1].shape[1]

    def full(n):
        return (4, 4, 2, 64, n)

    kv_all, totals = (4, 4, 2, 512, 128), (4, 2, 32, ffn_width)
    outs = [
        (ANY, every, BF16), (ANY, full(640), BF16), (ANY, full(512), BF16), (ANY, (512, 512), BF16),
        (ANY, kv_all, BF16), (ANY, (512, 512), BF16), (VMEM, (8, 512), F32), (ANY, (tokens, width), F32),
        (ANY, every, BF16), (ANY, (tokens, width), F32), (VMEM, (8, width), F32), (ANY, every, BF16),
        (ANY, full(ffn_width), BF16), (ANY, full(ffn_width), BF16), (ANY, totals, BF16), (ANY, totals, BF16),
    ]
    return pl.pallas_call(
        forward_kernel,
        out_shape=[jax.ShapeDtypeStruct(shape, dtype) for _, shape, dtype in outs],
        in_specs=[VMEM, ANY, VMEM, VMEM, VMEM, VMEM, VMEM, VMEM] + [ANY] * 4,
        out_specs=[space for space, _, _ in outs],
        scratch_shapes=[
            pltpu.VMEM(every, BF16),
            pltpu.VMEM((64, 640), BF16),
            pltpu.VMEM(full(640), BF16),
            pltpu.VMEM(full(512), BF16),
            pltpu.VMEM(kv_all, BF16),
            pltpu.VMEM(every, BF16),
            *ShardScatter.scratch(tokens, width),
            *attend_scratch(),
            *[pltpu.VMEM(full(ffn_width), BF16)] * 4,
            pltpu.VMEM(every, BF16),
            pltpu.VMEM(every, BF16),
            *[pltpu.VMEM((512, 512), F32)] * 2,
            *[pltpu.VMEM((512, ffn_width), BF16)] * 3,
            pltpu.VMEM(every, BF16),
            *[pltpu.VMEM((512, 512), BF16)] * 2,
            *[pltpu.VMEM((tokens, width), F32)] * 2,
            *CtxScatter.scratch(32, ffn_width),
            *CtxScatter.scratch(32, ffn_width),
            *sems(16 * CtxGather.COPIES + 2 * CtxScatter.COPIES + 12 * CHUNKS + 28),
        ],
        compiler_params=params(cid),
        name="forward",
    )(x, cot, gain1.reshape(16, 128), gain2.reshape(16, 128), tables, *w_qkv, *shards)


def backward_kernel(*refs):
    (
        branch_in, result_in, w_out_in, w_qkv_in, normed_in, g_gate, g_up, g_down_x, g_down_z,
        q_in, kv_in, attn_in, hidden_in, grad_hidden_in, x_in, grad_gain, lse, tables, gain1,
    ) = refs[:19]
    grad_inputs, gains, outputs, out_q, out_kv, out_o, out_gate, out_up, out_down = refs[19:28]
    normed, result_part, w_out, w_qkv, branch, dkv_send, relay, near, over = refs[28:37]
    grad_lin, grad_kv, g_query, g_kv, q, kv, attn, hidden, grad_hidden, x = refs[37:47]
    scratch, gain_bufs, bufs, (free, send, recv) = refs[47:51], refs[51:57], refs[57:-3], refs[-3:]
    place = Place()
    copies = Copies(send, recv)
    loads = [copies.local(a, b) for a, b in (
        (branch_in, branch), (w_out_in, w_out), (q_in, q), (kv_in, kv), (attn_in, attn)
    )]
    greet(place.ctx_peers() + place.shard_peers() + place.far_peers())
    ctx = lax.axis_index("ctx")
    me, co = 2 * place.yl + place.co, 2 * place.yl + 1 - place.co
    far, far_co = 2 * (1 - place.yl) + place.co, 2 * (1 - place.yl) + 1 - place.co
    order = [me, far_co, far, co]
    taken = 0

    def take(n):
        nonlocal taken
        taken += n
        return bufs[taken - n : taken]

    def rows_of(seq):
        return pl.ds(pl.multiple_of(seq * 128, 128), 128)

    engines = {}
    for name, src, out, count in (
        ("g", g_gate, out_gate, 9), ("o", w_out, out_o, 7), ("q", g_query, out_q, 7), ("v", g_kv, out_kv, 7),
    ):
        engines[name] = [
            CtxScatter(place, copies, src, out, take(count), lo, rows, big) for lo, rows, big in halves(64)
        ]
    for k in range(4):
        engines[f"k{k}"] = [
            CtxScatter(place, copies, dkv_send.at[k], grad_kv.at[rows_of(order[k])], take(7), 0, 128, "xz"[k % 2])
        ]
    engines["u"] = [
        CtxScatterLate(place, copies, g_up, out_up, take(8), lo, rows, big) for lo, rows, big in halves(64)
    ]
    engines["d"] = []
    for (lo, rows, big), totals in zip(halves(64), (g_down_x, g_down_z)):
        pos, far2, pos2, neg2, last = take(5)
        load = copies.local(totals, pos)
        engines["d"].append(
            CtxScatter(
                place, copies, None, out_down, (None, pos, None, far2, pos2, neg2, last), lo, rows, big, resumed=load
            )
        )
    gain_sum = GainScatter(place, copies, gains, gain_bufs)
    engines["n"] = [gain_sum]
    result = ShardScatter(place, copies, result_part, (relay, near, over), 1)
    last = ShardScatter(place, copies, branch, (relay, near, over), CHUNKS)
    thirds = [
        attend_back_seq(
            order[k], ctx, q, kv, grad_lin, attn, lse, tables, grad_lin, dkv_send.at[k], scratch
        )
        for k in range(4)
    ]

    def relay_rows(rows_scatter):
        for c in range(CHUNKS):
            rows_scatter.relay_on(c)

    def grad_rows(seq):
        w = w_out[...].reshape(2048, 512)
        grad_lin[rows_of(seq), :512] = jnp.dot(branch[seq], w, preferred_element_type=F32).astype(BF16)

    def grad_mixed_own():
        wait_all(loads)
        loads.extend(copies.local(a, b) for a, b in (
            (result_in, result_part), (w_qkv_in, w_qkv), (normed_in, normed), (hidden_in, hidden),
            (grad_hidden_in, grad_hidden), (x_in, x),
        ))
        grad_rows(me)

    def grad_mixed():
        for seq in order[1:]:
            grad_rows(seq)

    def begin_result():
        loads[5].wait()
        result.begin()

    def grad_of_out():
        rows = branch[...].reshape(512, 2048)
        for j in range(8):
            block = tn(rows[:, j * 256 : (j + 1) * 256], attn[...]).astype(BF16)
            w_out[j // 2, pl.ds((j % 2) * 2, 2)] = block.reshape(2, 2, 64, 512)

    def result_rows():
        loads[8].wait()
        outputs[...] = (hidden[...] + result.total(0)).astype(BF16)
        for device in place.shard_peers():
            pl.semaphore_signal(free, inc=1, device_id=device, device_id_type=MESH)

    def input_rows(k):
        if k == FIRST_INPUT_ROWS:
            loads[6].wait()
        at = rows_of(order[k])
        grad_lin[at, 512:640] = unrotate_tile(grad_kv[at, :], tables[2], tables[3]).astype(BF16)
        branch[order[k]] = nt(grad_lin[at, :], w_qkv[...].reshape(2048, 640)).astype(BF16)
        if k == 1:
            pl.semaphore_wait(free, 2)
            last.begin_far()
        elif k == 2:
            relay_rows(last)
        elif k == 3:
            last.begin_near()

    def weight_grad(w, start, width):
        def step(j, cols):
            block = tn(normed[:, :, cols].reshape(512, 512), grad_lin[:, start : start + width])
            w[j] = block.astype(BF16).reshape(4, 2, 64, width)

        over_width(step)

    def grad_of_query():
        loads[7].wait()
        weight_grad(g_query, 0, 512)

    def first_norm_back():
        wait_all(loads[9:])
        gain = gain_row(gain1)
        for c in range(CHUNKS):
            rows = last.at(c)
            back, per_gain = norm_back_rows(last.total(c), x[rows, :].astype(F32), gain)
            grad_inputs[rows, :] = (grad_hidden[rows, :] + back).astype(BF16)
            total = eight(per_gain) if c == 0 else total + eight(per_gain)
        row = lax.broadcasted_iota(jnp.int32, total.shape, 0)
        one, two = jnp.sum(total, 0, keepdims=True), jnp.sum(grad_gain[...], 0, keepdims=True)
        gain_sum.vec[...] = jnp.where(row == 0, one, jnp.where(row == 1, two, 0.0))

    actions = {
        "DO": grad_mixed_own, "DP": grad_mixed, "GO": grad_of_out, "RESB": begin_result,
        "RESR": lambda: result.relay_on(0), "RES": result_rows, "QG": grad_of_query,
        "VG": lambda: weight_grad(g_kv, 512, 128), "TOT": first_norm_back,
    }
    for k in range(4):
        actions[f"I{k}"] = partial(input_rows, k)
        for third in range(3):
            actions[f"A{k}{third}"] = partial(next, thirds[k], None)
    run_steps(BACKWARD, engines, actions)


def backward(cid, in_hbm, in_vmem):
    tokens, width = in_hbm[-1].shape
    ffn_width = in_hbm[5].shape[4]
    in_vmem = [a.reshape(16, 128) if a.ndim == 1 else a for a in in_vmem]
    scratch = []
    for _ in range(2):
        scratch += CtxScatter.scratch(32, ffn_width, True)
    for _ in range(4):
        scratch += CtxScatter.scratch(32, 512)
    for _ in range(2):
        scratch += CtxScatter.scratch(32, 128)
    for _ in range(4):
        scratch += CtxScatter.scratch(128, 128)
    for _ in range(2):
        scratch += CtxScatterLate.scratch(32, ffn_width)
    for _ in range(2):
        whole = CtxScatter.scratch(32, ffn_width)
        scratch += whole[1:2] + whole[3:]
    shapes = [
        ((tokens, width), BF16), ((8, 128), F32), ((tokens, width), BF16), ((64, 512), F32), ((64, 128), F32),
        ((64, 512), F32), ((64, ffn_width), F32), ((64, ffn_width), F32), ((64, ffn_width), F32),
    ]
    return pl.pallas_call(
        backward_kernel,
        out_shape=[jax.ShapeDtypeStruct(*shape) for shape in shapes],
        in_specs=[ANY] * len(in_hbm) + [VMEM] * len(in_vmem),
        out_specs=[VMEM] * len(shapes),
        scratch_shapes=[
            pltpu.VMEM((4, tokens, width), BF16),
            pltpu.VMEM((4, tokens, width), BF16),
            pltpu.VMEM((4, 4, 2, 64, 512), BF16),
            pltpu.VMEM((4, 4, 2, 64, 640), BF16),
            pltpu.VMEM((4, tokens, width), BF16),
            pltpu.VMEM((4, 4, 4, 2, 128, 128), BF16),
            *ShardScatter.scratch(tokens, width),
            pltpu.VMEM((512, 640), BF16),
            pltpu.VMEM((512, 128), F32),
            pltpu.VMEM((4, 4, 2, 64, 512), BF16),
            pltpu.VMEM((4, 4, 2, 64, 128), BF16),
            *[pltpu.VMEM(a.shape, a.dtype) for a in in_hbm[9:]],
            *attend_back_scratch(),
            *GainScatter.scratch(),
            *scratch,
            pltpu.SemaphoreType.REGULAR,
            *sems(16 * CtxScatter.COPIES + 2 * CtxScatterLate.COPIES + 6 * CHUNKS + GainScatter.COPIES + 20),
        ],
        compiler_params=params(cid),
        name="backward",
    )(*in_hbm, *in_vmem)


FIRST_INPUT_ROWS = int([step for step in BACKWARD if step[0] == "I"][0][1])


def finish_kernel(gains, g_kv, *refs):
    ins, (first, second, key, value), outs, held, (load, store) = refs[:7], refs[7:11], refs[11:18], refs[18:25], refs[25:]
    loads = [pltpu.make_async_copy(a, b, load.at[k]) for k, (a, b) in enumerate(zip(ins, held))]
    stores = [pltpu.make_async_copy(a, b, store.at[k]) for k, (a, b) in enumerate(zip(held, outs))]
    for copy in loads:
        copy.start()
    start = (lax.axis_index("ctx") % 2) * 64 + lax.axis_index("wshard") * 16
    own = pltpu.roll(gains[...], 128 - start, 1)
    first[...] = own[0:1, :16]
    second[...] = own[1:2, :16]
    key[...] = g_kv[:, :HD]
    value[...] = g_kv[:, HD:]
    for arrive, leave in zip(loads, stores):
        arrive.wait()
        leave.start()
    wait_all(stores)


def finish(gains, g_kv, *arrays):
    shapes = [((1, 16), F32)] * 2 + [((64, HD), F32)] * 2 + [(a.shape, a.dtype) for a in arrays]
    return pl.pallas_call(
        finish_kernel,
        out_shape=[jax.ShapeDtypeStruct(*shape) for shape in shapes],
        in_specs=[VMEM] * 2 + [ANY] * 7,
        out_specs=[VMEM] * 4 + [ANY] * 7,
        scratch_shapes=[pltpu.VMEM(a.shape, a.dtype) for a in arrays] + sems(7),
        compiler_params=pltpu.CompilerParams(vmem_limit_bytes=VMEM_LIMIT),
        name="finish",
    )(gains, g_kv, *arrays)


def rope_tables(positions):
    freqs = 10000.0 ** (-jnp.arange(HD // 2, dtype=F32) * 2.0 / HD)
    angles = positions[:, None] * freqs[None]
    cosine, sine = jnp.cos(angles), jnp.sin(angles)
    one, zero = jnp.ones_like(cosine), jnp.zeros_like(cosine)
    return jnp.stack(
        [
            jnp.concatenate([cosine] * 4, -1),
            jnp.concatenate([sine] * 4, -1),
            jnp.concatenate([cosine, cosine, one, one], -1),
            jnp.concatenate([sine, sine, zero, zero], -1),
        ]
    )


def per_device(
    inputs, cotangent, norm_attn, w_query, w_key, w_value, w_out, norm_mlp, w_gate, w_up, w_down
):
    width = inputs.shape[-1]
    half_len = inputs.shape[2]
    tokens = 2 * half_len
    ctx_count = lax.axis_size("ctx")
    ctx_index = lax.axis_index("ctx")
    length = tokens * ctx_count
    x = inputs.reshape(tokens, width)
    cot = cotangent.reshape(tokens, width)
    rows_local = jnp.arange(tokens)
    positions = jnp.where(
        rows_local < half_len,
        ctx_index * half_len + rows_local,
        length - (ctx_index + 1) * half_len + (rows_local - half_len),
    ).astype(F32)
    tables = rope_tables(positions)

    (
        normed_all, w_qkv, w_out_t, q, kv_all, attn, lse, hidden, branch_all, grad_hidden, gain2_part, result_part,
        g_gate, g_up, g_down_x, g_down_z,
    ) = forward(
        0, x, cot, norm_attn, norm_mlp, tables, [w_query, w_key, w_value], [w_out.T, w_gate, w_up, w_down.T]
    )
    grad_inputs, gains, outputs, g_query, g_kv, g_out, g_gate, g_up, g_down = backward(
        1,
        [branch_all, result_part, w_out_t, w_qkv, normed_all, g_gate, g_up, g_down_x, g_down_z]
        + [q, kv_all, attn, hidden, grad_hidden, x],
        [gain2_part, lse, tables, norm_attn],
    )
    gain1, gain2, g_key, g_value, grad_inputs, outputs, g_query, g_out, g_gate, g_up, g_down = finish(
        gains, g_kv, grad_inputs, outputs, g_query, g_out, g_gate, g_up, g_down
    )
    return (
        outputs.reshape(inputs.shape),
        grad_inputs.reshape(inputs.shape),
        gain1.reshape(16),
        g_query,
        g_key,
        g_value,
        g_out.T,
        gain2.reshape(16),
        g_gate,
        g_up,
        g_down.T,
    )


def solution(mesh):
    return jax.shard_map(
        per_device,
        mesh=mesh,
        in_specs=(
            P("wshard", None, "ctx", None),
            P("wshard", None, "ctx", None),
            P(),
            P("ctx", "wshard"),
            P("ctx", "wshard"),
            P("ctx", "wshard"),
            P("wshard", "ctx"),
            P(),
            P("ctx", "wshard"),
            P("ctx", "wshard"),
            P("wshard", "ctx"),
        ),
        out_specs=(
            P("wshard", None, "ctx", None),
            P("wshard", None, "ctx", None),
            P(("ctx", "wshard")),
            P("ctx", "wshard"),
            P("ctx", "wshard"),
            P("ctx", "wshard"),
            P("wshard", "ctx"),
            P(("ctx", "wshard")),
            P("ctx", "wshard"),
            P("ctx", "wshard"),
            P("wshard", "ctx"),
        ),
        check_vma=False,
    )
```
